32 devices in a mesh: gx: 8 (over z, x), gy: 4 (over y, core).
Axes of the slice: x: 2, y: 2, z: 4, core: 2. Of those that a mesh axis runs over, the one named last changes fastest.
Arguments:
- density: float32 [4, 32, 64, 128], P(None, 'gx', 'gy'), may hold values from 0 to 12, as said below
- rate_table: float32 [4, 9], replicated, may hold values from 0 to 80, as said below
Outputs:
- propagated: float32 [4, 32, 64, 128], P(None, 'gx', 'gy')
- step_entries: float32 [4, 5], replicated
The draws below stay inside these ranges and needn't reach their ends.
Inputs may be any that keep to these rules, and one draw needn't show every extreme that they name: `density`: every entry is positive. `rate_table`: all entries positive; entry r of a row is the constant cr of the steps.
All inputs are finite; a program needn't handle non-finite values.
Results may differ from the reference program's by a relative error of at most 0.0006.
Values sent between devices are 32-bit elements; how exact they have to be, the bound alone decides.
No kernel may reach another device: no remote copies, remote signals or barrier semaphores. Data moves between devices by JAX's collectives and lax.ppermute only.
A program may use at most 64 MiB of HBM per device.

```python
import jax
import jax.numpy as jnp
from jax import lax

CI = 4
NK = 128
MEMBERS = 4
NI = 32
NJ = 64
N_GX = 8


def draw_density(key, part):
    full_shape = (MEMBERS, NI, NJ, NK)
    place_i = (jnp.arange(NI, dtype=jnp.float32) / NI)[:, None, None]
    place_j = (jnp.arange(NJ, dtype=jnp.float32) / NJ)[None, :, None]
    roughness = jnp.exp(jax.random.uniform(key, full_shape, jnp.float32, -0.6931, 0.6931))
    profile = jnp.power(10.0, place_i - 0.5) * jnp.power(3.0, place_j - 0.5)
    return roughness * profile[None]


def draw_rate_table(key, part):
    base_rates = jnp.array([40.0, 25.0 / NI, 40.0, 30.0 / NJ, 52.0 / (NI * NI), 13.0 / NK, 13.0 / NK, NJ / 4.0, NK / 4.0], dtype=jnp.float32)
    factor = jnp.exp(jax.random.uniform(key, (MEMBERS, 9), jnp.float32, -0.6931, 0.6931))
    return base_rates[None, :] * factor


def setup_inputs(seed: int = 0) -> dict:
    splits = jax.random.split(jax.random.key(seed), 3)
    density = draw_density(jax.random.fold_in(splits[2], 71), 0)
    rate_table = draw_rate_table(jax.random.fold_in(splits[2], 71), 0)
    return dict(density=density, rate_table=rate_table)


tau_step = 0.01
taylor_terms = 16
squarings = 4

def shift_down(vector_field):
    return jnp.concatenate([jnp.zeros_like(vector_field[..., :1]), vector_field[..., :-1]], axis=-1)

def shift_up(vector_field):
    return jnp.concatenate([vector_field[..., 1:], jnp.zeros_like(vector_field[..., :1])], axis=-1)

def generator_apply(padded, first_i, first_j, member_rates):
    row_count = padded.shape[0] - 4
    col_count = padded.shape[1] - 2
    lattice_depth = padded.shape[2]
    amount_i = (first_i + jnp.arange(row_count, dtype=jnp.int32)).astype(jnp.float32)[:, None, None]
    amount_j = (first_j + jnp.arange(col_count, dtype=jnp.int32)).astype(jnp.float32)[None, :, None]
    amount_k = jnp.arange(lattice_depth, dtype=jnp.int32).astype(jnp.float32)[None, None, :]
    ratio_j = amount_j / member_rates[7]
    ratio_k = amount_k / member_rates[8]
    make_u = member_rates[0] / (1.0 + ratio_j * ratio_j)
    make_v = member_rates[2] / (1.0 + ratio_k * ratio_k)
    outflow = make_u + member_rates[1] * amount_i + make_v + member_rates[3] * amount_j
    outflow = outflow + 0.5 * member_rates[4] * amount_i * (amount_i - 1.0) + (member_rates[5] + member_rates[6]) * amount_k
    centre = padded[2:-2, 1:-1]
    inflow = make_u * padded[1:-3, 1:-1]
    inflow = inflow + member_rates[1] * (amount_i + 1.0) * padded[3:-1, 1:-1]
    inflow = inflow + make_v * padded[2:-2, :-2]
    inflow = inflow + member_rates[3] * (amount_j + 1.0) * padded[2:-2, 2:]
    inflow = inflow + 0.5 * member_rates[4] * (amount_i + 2.0) * (amount_i + 1.0) * shift_down(padded[4:, 1:-1])
    inflow = inflow + member_rates[5] * (amount_k + 1.0) * shift_up(padded[:-4, 1:-1])
    inflow = inflow + member_rates[6] * (amount_k + 1.0) * shift_up(centre)
    return inflow - outflow * centre

def matrix_exponential(small):
    scaled = small * (tau_step / 2.0 ** squarings)
    identity = jnp.eye(3, dtype=jnp.float32)
    series = identity + jnp.zeros_like(scaled)
    for term_index in range(taylor_terms, 0, -1):
        series = identity + jnp.einsum('...ab,...bc->...ac', scaled, series, precision=lax.Precision.HIGHEST) / term_index
    for square_index in range(squarings):
        series = jnp.einsum('...ab,...bc->...ac', series, series, precision=lax.Precision.HIGHEST)
    return series

def apply_member(vector_field, member_rates):
    padded_full = jnp.pad(vector_field, ((2, 2), (1, 1), (0, 0)))
    starts = jnp.arange(N_GX, dtype=jnp.int32) * CI

    def one_block(block_start):
        slab_rows = lax.dynamic_slice_in_dim(padded_full, block_start, CI + 4, 0)
        return generator_apply(slab_rows, block_start, jnp.int32(0), member_rates)
    return lax.map(one_block, starts).reshape(vector_field.shape)

def one_member(pair):
    field_one, member_rates = pair
    basis_scale = jnp.sqrt(jnp.sum(field_one * field_one))
    basis_zero = field_one / basis_scale
    candidate = apply_member(basis_zero, member_rates)
    entry_00 = jnp.sum(basis_zero * candidate)
    candidate = candidate - entry_00 * basis_zero
    entry_10 = jnp.sqrt(jnp.sum(candidate * candidate))
    basis_one = candidate / entry_10
    candidate = apply_member(basis_one, member_rates)
    entry_01 = jnp.sum(basis_zero * candidate)
    entry_11 = jnp.sum(basis_one * candidate)
    candidate = candidate - entry_01 * basis_zero - entry_11 * basis_one
    entry_21 = jnp.sqrt(jnp.sum(candidate * candidate))
    basis_two = candidate / entry_21
    zeros = jnp.zeros_like(entry_00)
    small = jnp.stack([jnp.stack([entry_00, entry_01, zeros], -1), jnp.stack([entry_10, entry_11, zeros], -1), jnp.stack([zeros, entry_21, zeros], -1)], -2)
    propagator = matrix_exponential(small)
    propagated = basis_scale * (propagator[0, 0] * basis_zero + propagator[1, 0] * basis_one + propagator[2, 0] * basis_two)
    entries = tau_step * jnp.stack([entry_00, entry_10, entry_01, entry_11, entry_21], -1)
    return (propagated, entries)

def reference(density, rate_table):
    propagated_all, entries_all = lax.map(one_member, (density, rate_table))
    return (propagated_all, entries_all)
```

```python
import functools

import jax
import jax.numpy as jnp
from jax import lax
from jax.experimental import pallas as pl
from jax.experimental.pallas import tpu as pltpu
from jax.sharding import PartitionSpec as P

tau_step = 0.01
taylor_terms = 16
squarings = 4
HIGHEST = lax.Precision.HIGHEST
REACH = 4
HALF = 2
GAP = 8


def images_kernel(
    lattice, place, rates, field, above, below, left, right, image_one, image_two, message, wide, wide_image, parts
):
    members, rows, cols, depth = field.shape
    span = cols + 2 * GAP
    first_i, first_j = place[0], place[1]
    count_i, count_j = lattice

    wide[:, HALF : HALF + rows, GAP : GAP + cols] = field[...]
    wide[:, :HALF, GAP : GAP + cols] = above[:, REACH - HALF :]
    wide[:, HALF + rows :, GAP : GAP + cols] = below[:, :HALF]
    wide[:, :, GAP - 2 : GAP] = left[...]
    wide[:, :, GAP + cols : GAP + cols + 2] = right[...]

    lane = lax.broadcasted_iota(jnp.int32, (1, depth), 1)
    amount_k = lane.astype(jnp.float32)
    above_k = jnp.where(lane < depth - 1, amount_k + 1.0, 0.0)
    inner_k = jnp.where(lane > 0, 1.0, 0.0)
    sublane = lax.broadcasted_iota(jnp.int32, (span, 1), 0)
    amount_j = (first_j - GAP + sublane).astype(jnp.float32)

    def source(member, row):
        if row < -HALF:
            return above, row + REACH, 0
        if row >= rows + HALF:
            return below, row - rows, 0
        return wide, row + HALF, GAP

    for member in range(members):
        c = [rates[member, r] for r in range(9)]
        ratio_j = amount_j / jnp.full((span, 1), c[7])
        ratio_k = amount_k / jnp.full((1, depth), c[8])
        make_u = jnp.broadcast_to(c[0] / (1.0 + ratio_j * ratio_j), (span, depth))
        make_v = c[2] / (1.0 + ratio_k * ratio_k)
        lose_v = jnp.broadcast_to(c[3] * (amount_j + 1.0), (span, depth))
        rest = make_u + make_v + (c[3] * amount_j + (c[5] + c[6]) * amount_k)

        def apply(read, row, start, size):
            i = (first_i + row).astype(jnp.float32)
            cut = slice(GAP + start, GAP + start + size)
            centre = read(row, start, size)
            value = make_u[cut] * read(row - 1, start, size)
            value = value + (c[1] * (i + 1.0)) * read(row + 1, start, size)
            value = value + make_v * read(row, start - 1, size)
            value = value + lose_v[cut] * read(row, start + 1, size)
            pair = (0.5 * c[4] * (i + 2.0) * (i + 1.0)) * read(row + 2, start, size)
            value = value + inner_k * pltpu.roll(pair, 1, 1)
            split = c[5] * read(row - 2, start, size) + c[6] * centre
            value = value + above_k * pltpu.roll(split, depth - 1, 1)
            out = rest[cut] + (c[1] * i + 0.5 * c[4] * i * (i - 1.0))
            return value - out * centre

        def read_field(row, start, size):
            ref, index, offset = source(member, row)
            return ref[member, index, pl.ds(offset + start, size), :]

        def read_image(row, start, size):
            return wide_image[member, row + HALF, pl.ds(GAP + start, size), :]

        for row in range(-HALF, rows + HALF):
            inside = (first_i + row >= 0) & (first_i + row < count_i)
            value = apply(read_field, row, 0, cols)
            if row < 0 or row >= rows:
                value = jnp.where(inside, value, 0.0)
            else:
                image_one[member, row] = value
            wide_image[member, row + HALF, GAP : GAP + cols] = value
            if 0 <= row < rows:
                value = apply(read_field, row, -1, 1)
                wide_image[member, row + HALF, GAP - 1 : GAP] = jnp.where(first_j > 0, value, 0.0)
                value = apply(read_field, row, cols, 1)
                wide_image[member, row + HALF, GAP + cols : GAP + cols + 1] = jnp.where(
                    first_j + cols < count_j, value, 0.0
                )

        products = [jnp.zeros((cols, depth), jnp.float32) for _ in range(6)]
        for row in range(rows):
            zero = field[member, row]
            one = image_one[member, row]
            two = apply(read_image, row, 0, cols)
            image_two[member, row] = two
            terms = (zero * zero, zero * one, zero * two, one * one, one * two, two * two)
            products = [total + term for total, term in zip(products, terms)]
        for index, total in enumerate(products):
            parts[8 * index + member : 8 * index + member + 1, :] = jnp.sum(total, axis=0, keepdims=True)

    for index in range(6):
        parts[8 * index + members : 8 * index + 8, :] = jnp.zeros((8 - members, depth), jnp.float32)
    parts[48:, :] = jnp.zeros((parts.shape[0] - 48, depth), jnp.float32)
    ones = jnp.ones(message.shape[:1] + (depth,), jnp.float32)
    message[...] = lax.dot_general(
        ones, parts[...], (((1,), (1,)), ((), ())), precision=HIGHEST, preferred_element_type=jnp.float32
    )


def first_column(h00, s01, h11):
    scale = tau_step / 2.0**squarings
    a, b, d = scale * h00, scale * s01, scale * h11
    c = scale
    zero, one = jnp.zeros_like(a), jnp.ones_like(a)
    p00, p01, p10, p11, q0, q1 = one, zero, zero, one, zero, zero
    for term in range(taylor_terms, 0, -1):
        inverse = 1.0 / term
        p00, p01, p10, p11, q0, q1 = (
            1.0 + (a * p00 + b * p10) * inverse,
            (a * p01 + b * p11) * inverse,
            (c * p00 + d * p10) * inverse,
            1.0 + (c * p01 + d * p11) * inverse,
            p10 * (c * inverse),
            p11 * (c * inverse),
        )
    for _ in range(squarings):
        p00, p01, p10, p11, q0, q1 = (
            p00 * p00 + p01 * p10,
            p00 * p01 + p01 * p11,
            p10 * p00 + p11 * p10,
            p10 * p01 + p11 * p11,
            q0 * p00 + q1 * p10 + q0,
            q0 * p01 + q1 * p11 + q1,
        )
    return p00, p10, q0


def combine_kernel(gathered, field, image_one, image_two, propagated, entries):
    members, rows, cols, depth = field.shape
    ones = jnp.ones((gathered.shape[0], 128), jnp.float32)
    sums = lax.dot_general(
        gathered[...], ones, (((0,), (0,)), ((), ())), precision=HIGHEST, preferred_element_type=jnp.float32
    )
    g00, g01, g02, g11, g12, g22 = [sums[8 * index : 8 * index + 8] for index in range(6)]
    tiny = jnp.finfo(jnp.float32).tiny
    h00 = g01 / g00
    square_10 = jnp.maximum(g11 / g00 - h00 * h00, tiny)
    s01 = (g02 - h00 * g01) / g00
    h11 = ((g12 - h00 * g02) - h00 * (g11 - h00 * g01)) / (g00 * square_10)
    norm_2 = ((g22 - h00 * g12) - h00 * (g12 - h00 * g11)) / (g00 * square_10)
    h10 = jnp.sqrt(square_10)
    h01 = s01 / h10
    h21 = jnp.sqrt(jnp.maximum(norm_2 - h01 * h01 - h11 * h11, 0.0))
    e0, e1, e2 = first_column(h00, s01, h11)
    a2 = e2
    a1 = e1 - e2 * (h00 + h11)
    a0 = e0 - e1 * h00 - e2 * (s01 - h11 * h00)
    lane = lax.broadcasted_iota(jnp.int32, h00.shape, 1)
    table = h21
    for index, entry in enumerate((h00, h10, h01, h11)):
        table = jnp.where(lane == index, entry, table)
    entries[...] = (tau_step * table)[: entries.shape[0], : entries.shape[1]]
    for member in range(members):
        b0, b1, b2 = [jnp.broadcast_to(a[member : member + 1], (cols, depth)) for a in (a0, a1, a2)]
        for row in range(rows):
            propagated[member, row] = (
                b0 * field[member, row] + b1 * image_one[member, row] + b2 * image_two[member, row]
            )


def shards(density, rate_table):
    members, rows, cols, depth = density.shape
    size_x, size_y = lax.axis_size("gx"), lax.axis_size("gy")
    devices = size_x * size_y
    place = jnp.stack([lax.axis_index("gx") * rows, lax.axis_index("gy") * cols]).astype(jnp.int32)

    def neighbours(axis, size, last, initial):
        up = [(i, i + 1) for i in range(size - 1)]
        down = [(j, i) for i, j in up]
        return lax.ppermute(last, axis, up), lax.ppermute(initial, axis, down)

    above, below = neighbours("gx", size_x, density[:, rows - REACH :], density[:, :REACH])

    def edge(start):
        cut = slice(start, start + 2)
        return jnp.concatenate(
            [above[:, REACH - HALF :, cut], density[:, :, cut], below[:, :HALF, cut]], axis=1
        )

    left, right = neighbours("gy", size_y, edge(cols - 2), edge(0))

    vmem = pl.BlockSpec(memory_space=pltpu.VMEM)
    smem = pl.BlockSpec(memory_space=pltpu.SMEM)
    block = jax.ShapeDtypeStruct(density.shape, jnp.float32)
    image_one, image_two, message = pl.pallas_call(
        functools.partial(images_kernel, (size_x * rows, size_y * cols)),
        out_shape=[block, block, jax.ShapeDtypeStruct((devices, 128), jnp.float32)],
        in_specs=[smem, smem, vmem, vmem, vmem, vmem, vmem],
        out_specs=[vmem, vmem, vmem],
        scratch_shapes=[
            pltpu.VMEM((members, rows + 2 * HALF, cols + 2 * GAP, depth), jnp.float32),
            pltpu.VMEM((members, rows + 2 * HALF, cols + 2 * GAP, depth), jnp.float32),
            pltpu.VMEM((128, depth), jnp.float32),
        ],
        compiler_params=pltpu.CompilerParams(vmem_limit_bytes=8 * 2**20),
        name="images",
    )(place, rate_table, density, above, below, left, right)

    gathered = lax.all_to_all(message, ("gx", "gy"), 0, 0, tiled=True)

    return pl.pallas_call(
        combine_kernel,
        out_shape=[block, jax.ShapeDtypeStruct((members, 5), jnp.float32)],
        in_specs=[vmem] * 4,
        out_specs=[vmem, vmem],
        compiler_params=pltpu.CompilerParams(vmem_limit_bytes=8 * 2**20),
        name="combine",
    )(gathered, density, image_one, image_two)


def solution(mesh):
    in_specs = (P(None, "gx", "gy", None), P())
    out_specs = (P(None, "gx", "gy", None), P())
    return jax.shard_map(shards, mesh=mesh, in_specs=in_specs, out_specs=out_specs, check_vma=False)
```

```python
import functools

import jax
import jax.numpy as jnp
from jax import lax
from jax.experimental import pallas as pl
from jax.experimental.pallas import tpu as pltpu
from jax.sharding import PartitionSpec as P

tau_step = 0.01
taylor_terms = 16
squarings = 4
HIGHEST = lax.Precision.HIGHEST
REACH = 4
HALF = 2
GAP = 8


def images_kernel(
    lattice,
    place,
    rates,
    field,
    above,
    below,
    left,
    right,
    corners_above,
    corners_below,
    image_one,
    image_two,
    message,
    wide,
    wide_image,
    parts,
):
    members, rows, cols, depth = field.shape
    span = cols + 2 * GAP
    first_i, first_j = place[0], place[1]
    count_i, count_j = lattice

    wide[:, HALF : HALF + rows, GAP : GAP + cols] = field[...]
    wide[:, :HALF, GAP : GAP + cols] = above[:, REACH - HALF :]
    wide[:, HALF + rows :, GAP : GAP + cols] = below[:, :HALF]
    wide[:, HALF : HALF + rows, GAP - 2 : GAP] = left[...]
    wide[:, HALF : HALF + rows, GAP + cols : GAP + cols + 2] = right[...]
    for corners, at in ((corners_above, 0), (corners_below, HALF + rows)):
        wide[:, at : at + HALF, GAP - 1 : GAP] = corners[:, :, :1]
        wide[:, at : at + HALF, GAP + cols : GAP + cols + 1] = corners[:, :, 1:]

    lane = lax.broadcasted_iota(jnp.int32, (1, depth), 1)
    amount_k = lane.astype(jnp.float32)
    above_k = jnp.where(lane < depth - 1, amount_k + 1.0, 0.0)
    inner_k = jnp.where(lane > 0, 1.0, 0.0)
    sublane = lax.broadcasted_iota(jnp.int32, (span, 1), 0)
    amount_j = (first_j - GAP + sublane).astype(jnp.float32)

    def source(member, row):
        if row < -HALF:
            return above, row + REACH, 0
        if row >= rows + HALF:
            return below, row - rows, 0
        return wide, row + HALF, GAP

    for member in range(members):
        c = [rates[member, r] for r in range(9)]
        ratio_j = amount_j / jnp.full((span, 1), c[7])
        ratio_k = amount_k / jnp.full((1, depth), c[8])
        make_u = jnp.broadcast_to(c[0] / (1.0 + ratio_j * ratio_j), (span, depth))
        make_v = c[2] / (1.0 + ratio_k * ratio_k)
        lose_v = jnp.broadcast_to(c[3] * (amount_j + 1.0), (span, depth))
        rest = make_u + make_v + (c[3] * amount_j + (c[5] + c[6]) * amount_k)

        def apply(read, row, start, size):
            i = (first_i + row).astype(jnp.float32)
            cut = slice(GAP + start, GAP + start + size)
            centre = read(row, start, size)
            value = make_u[cut] * read(row - 1, start, size)
            value = value + (c[1] * (i + 1.0)) * read(row + 1, start, size)
            value = value + make_v * read(row, start - 1, size)
            value = value + lose_v[cut] * read(row, start + 1, size)
            pair = (0.5 * c[4] * (i + 2.0) * (i + 1.0)) * read(row + 2, start, size)
            value = value + inner_k * pltpu.roll(pair, 1, 1)
            split = c[5] * read(row - 2, start, size) + c[6] * centre
            value = value + above_k * pltpu.roll(split, depth - 1, 1)
            out = rest[cut] + (c[1] * i + 0.5 * c[4] * i * (i - 1.0))
            return value - out * centre

        def read_field(row, start, size):
            ref, index, offset = source(member, row)
            return ref[member, index, pl.ds(offset + start, size), :]

        def read_image(row, start, size):
            return wide_image[member, row + HALF, pl.ds(GAP + start, size), :]

        for row in range(-HALF, rows + HALF):
            inside = (first_i + row >= 0) & (first_i + row < count_i)
            value = apply(read_field, row, 0, cols)
            if row < 0 or row >= rows:
                value = jnp.where(inside, value, 0.0)
            else:
                image_one[member, row] = value
            wide_image[member, row + HALF, GAP : GAP + cols] = value
            if 0 <= row < rows:
                value = apply(read_field, row, -1, 1)
                wide_image[member, row + HALF, GAP - 1 : GAP] = jnp.where(first_j > 0, value, 0.0)
                value = apply(read_field, row, cols, 1)
                wide_image[member, row + HALF, GAP + cols : GAP + cols + 1] = jnp.where(
                    first_j + cols < count_j, value, 0.0
                )

        products = [jnp.zeros((cols, depth), jnp.float32) for _ in range(6)]
        for row in range(rows):
            zero = field[member, row]
            one = image_one[member, row]
            two = apply(read_image, row, 0, cols)
            image_two[member, row] = two
            terms = (zero * zero, zero * one, zero * two, one * one, one * two, two * two)
            products = [total + term for total, term in zip(products, terms)]
        for index, total in enumerate(products):
            parts[8 * index + member : 8 * index + member + 1, :] = jnp.sum(total, axis=0, keepdims=True)

    for index in range(6):
        parts[8 * index + members : 8 * index + 8, :] = jnp.zeros((8 - members, depth), jnp.float32)
    parts[48:, :] = jnp.zeros((parts.shape[0] - 48, depth), jnp.float32)
    ones = jnp.ones(message.shape[:1] + (depth,), jnp.float32)
    message[...] = lax.dot_general(
        ones, parts[...], (((1,), (1,)), ((), ())), precision=HIGHEST, preferred_element_type=jnp.float32
    )


def first_column(h00, s01, h11):
    scale = tau_step / 2.0**squarings
    a, b, d = scale * h00, scale * s01, scale * h11
    c = scale
    zero, one = jnp.zeros_like(a), jnp.ones_like(a)
    p00, p01, p10, p11, q0, q1 = one, zero, zero, one, zero, zero
    for term in range(taylor_terms, 0, -1):
        inverse = 1.0 / term
        p00, p01, p10, p11, q0, q1 = (
            1.0 + (a * p00 + b * p10) * inverse,
            (a * p01 + b * p11) * inverse,
            (c * p00 + d * p10) * inverse,
            1.0 + (c * p01 + d * p11) * inverse,
            p10 * (c * inverse),
            p11 * (c * inverse),
        )
    for _ in range(squarings):
        p00, p01, p10, p11, q0, q1 = (
            p00 * p00 + p01 * p10,
            p00 * p01 + p01 * p11,
            p10 * p00 + p11 * p10,
            p10 * p01 + p11 * p11,
            q0 * p00 + q1 * p10 + q0,
            q0 * p01 + q1 * p11 + q1,
        )
    return p00, p10, q0


def combine_kernel(gathered, field, image_one, image_two, propagated, entries):
    members, rows, cols, depth = field.shape
    ones = jnp.ones((gathered.shape[0], 128), jnp.float32)
    sums = lax.dot_general(
        gathered[...], ones, (((0,), (0,)), ((), ())), precision=HIGHEST, preferred_element_type=jnp.float32
    )
    g00, g01, g02, g11, g12, g22 = [sums[8 * index : 8 * index + 8] for index in range(6)]
    tiny = jnp.finfo(jnp.float32).tiny
    h00 = g01 / g00
    square_10 = jnp.maximum(g11 / g00 - h00 * h00, tiny)
    s01 = (g02 - h00 * g01) / g00
    h11 = ((g12 - h00 * g02) - h00 * (g11 - h00 * g01)) / (g00 * square_10)
    norm_2 = ((g22 - h00 * g12) - h00 * (g12 - h00 * g11)) / (g00 * square_10)
    h10 = jnp.sqrt(square_10)
    h01 = s01 / h10
    h21 = jnp.sqrt(jnp.maximum(norm_2 - h01 * h01 - h11 * h11, 0.0))
    e0, e1, e2 = first_column(h00, s01, h11)
    a2 = e2
    a1 = e1 - e2 * (h00 + h11)
    a0 = e0 - e1 * h00 - e2 * (s01 - h11 * h00)
    lane = lax.broadcasted_iota(jnp.int32, h00.shape, 1)
    table = h21
    for index, entry in enumerate((h00, h10, h01, h11)):
        table = jnp.where(lane == index, entry, table)
    entries[...] = (tau_step * table)[: entries.shape[0], : entries.shape[1]]
    for member in range(members):
        b0, b1, b2 = [jnp.broadcast_to(a[member : member + 1], (cols, depth)) for a in (a0, a1, a2)]
        for row in range(rows):
            propagated[member, row] = (
                b0 * field[member, row] + b1 * image_one[member, row] + b2 * image_two[member, row]
            )


def shards(density, rate_table):
    members, rows, cols, depth = density.shape
    size_x, size_y = lax.axis_size("gx"), lax.axis_size("gy")
    devices = size_x * size_y
    place = jnp.stack([lax.axis_index("gx") * rows, lax.axis_index("gy") * cols]).astype(jnp.int32)

    def neighbours(axis, size, last, initial):
        up = [(i, i + 1) for i in range(size - 1)]
        down = [(j, i) for i, j in up]
        return lax.ppermute(last, axis, up), lax.ppermute(initial, axis, down)

    left, right = neighbours("gy", size_y, density[:, :, cols - 2 :], density[:, :, :2])
    above, below = neighbours("gx", size_x, density[:, rows - REACH :], density[:, :REACH])

    def corners(first):
        cut = slice(first, first + HALF)
        return jnp.concatenate([left[:, cut, 1:], right[:, cut, :1]], axis=2)

    corners_above, corners_below = neighbours("gx", size_x, corners(rows - HALF), corners(0))

    vmem = pl.BlockSpec(memory_space=pltpu.VMEM)
    smem = pl.BlockSpec(memory_space=pltpu.SMEM)
    block = jax.ShapeDtypeStruct(density.shape, jnp.float32)
    image_one, image_two, message = pl.pallas_call(
        functools.partial(images_kernel, (size_x * rows, size_y * cols)),
        out_shape=[block, block, jax.ShapeDtypeStruct((devices, 128), jnp.float32)],
        in_specs=[smem, smem] + [vmem] * 7,
        out_specs=[vmem, vmem, vmem],
        scratch_shapes=[
            pltpu.VMEM((members, rows + 2 * HALF, cols + 2 * GAP, depth), jnp.float32),
            pltpu.VMEM((members, rows + 2 * HALF, cols + 2 * GAP, depth), jnp.float32),
            pltpu.VMEM((128, depth), jnp.float32),
        ],
        compiler_params=pltpu.CompilerParams(vmem_limit_bytes=8 * 2**20),
        name="images",
    )(place, rate_table, density, above, below, left, right, corners_above, corners_below)

    gathered = lax.all_to_all(message, ("gx", "gy"), 0, 0, tiled=True)

    return pl.pallas_call(
        combine_kernel,
        out_shape=[block, jax.ShapeDtypeStruct((members, 5), jnp.float32)],
        in_specs=[vmem] * 4,
        out_specs=[vmem, vmem],
        compiler_params=pltpu.CompilerParams(vmem_limit_bytes=8 * 2**20),
        name="combine",
    )(gathered, density, image_one, image_two)


def solution(mesh):
    in_specs = (P(None, "gx", "gy", None), P())
    out_specs = (P(None, "gx", "gy", None), P())
    return jax.shard_map(shards, mesh=mesh, in_specs=in_specs, out_specs=out_specs, check_vma=False)
```

```python
import functools

import jax
import jax.numpy as jnp
from jax import lax
from jax.experimental import pallas as pl
from jax.experimental.pallas import tpu as pltpu
from jax.sharding import PartitionSpec as P

tau_step = 0.01
taylor_terms = 16
squarings = 4
HIGHEST = lax.Precision.HIGHEST
REACH = 4
HALF = 2
GAP = 8


def images_kernel(
    lattice, place, rates, field, even_x, odd_x, even_y, odd_y, image_one, image_two, message, wide, wide_image, parts
):
    members, rows, cols, depth = field.shape
    span = cols + 2 * GAP
    first_i, first_j = place[0], place[1]
    count_i, count_j = lattice

    def sides(even, odd, is_even):
        return jnp.where(is_even, odd, even), jnp.where(is_even, even, odd)

    wide[:, REACH : REACH + rows, GAP : GAP + cols] = field[...]
    above, below = sides(even_x[...], odd_x[...], place[2] == 0)
    wide[:, :REACH, GAP : GAP + cols] = above
    wide[:, REACH + rows :, GAP : GAP + cols] = below
    left, right = sides(even_y[...], odd_y[...], place[3] == 0)
    wide[:, REACH - HALF : REACH + rows + HALF, GAP - 2 : GAP] = left
    wide[:, REACH - HALF : REACH + rows + HALF, GAP + cols : GAP + cols + 2] = right

    lane = lax.broadcasted_iota(jnp.int32, (1, depth), 1)
    amount_k = lane.astype(jnp.float32)
    above_k = jnp.where(lane < depth - 1, amount_k + 1.0, 0.0)
    inner_k = jnp.where(lane > 0, 1.0, 0.0)
    sublane = lax.broadcasted_iota(jnp.int32, (span, 1), 0)
    amount_j = (first_j - GAP + sublane).astype(jnp.float32)

    for member in range(members):
        c = [rates[member, r] for r in range(9)]
        ratio_j = amount_j / jnp.full((span, 1), c[7])
        ratio_k = amount_k / jnp.full((1, depth), c[8])
        make_u = jnp.broadcast_to(c[0] / (1.0 + ratio_j * ratio_j), (span, depth))
        make_v = c[2] / (1.0 + ratio_k * ratio_k)
        lose_v = jnp.broadcast_to(c[3] * (amount_j + 1.0), (span, depth))
        rest = make_u + make_v + (c[3] * amount_j + (c[5] + c[6]) * amount_k)

        def apply(read, row, start, size):
            i = (first_i + row).astype(jnp.float32)
            cut = slice(GAP + start, GAP + start + size)
            centre = read(row, start, size)
            value = make_u[cut] * read(row - 1, start, size)
            value = value + (c[1] * (i + 1.0)) * read(row + 1, start, size)
            value = value + make_v * read(row, start - 1, size)
            value = value + lose_v[cut] * read(row, start + 1, size)
            pair = (0.5 * c[4] * (i + 2.0) * (i + 1.0)) * read(row + 2, start, size)
            value = value + inner_k * pltpu.roll(pair, 1, 1)
            split = c[5] * read(row - 2, start, size) + c[6] * centre
            value = value + above_k * pltpu.roll(split, depth - 1, 1)
            out = rest[cut] + (c[1] * i + 0.5 * c[4] * i * (i - 1.0))
            return value - out * centre

        def read_field(row, start, size):
            return wide[member, row + REACH, pl.ds(GAP + start, size), :]

        def read_image(row, start, size):
            return wide_image[member, row + HALF, pl.ds(GAP + start, size), :]

        for row in range(-HALF, rows + HALF):
            inside = (first_i + row >= 0) & (first_i + row < count_i)
            value = apply(read_field, row, 0, cols)
            if row < 0 or row >= rows:
                value = jnp.where(inside, value, 0.0)
            else:
                image_one[member, row] = value
            wide_image[member, row + HALF, GAP : GAP + cols] = value
            if 0 <= row < rows:
                value = apply(read_field, row, -1, 1)
                wide_image[member, row + HALF, GAP - 1 : GAP] = jnp.where(first_j > 0, value, 0.0)
                value = apply(read_field, row, cols, 1)
                wide_image[member, row + HALF, GAP + cols : GAP + cols + 1] = jnp.where(
                    first_j + cols < count_j, value, 0.0
                )

        products = [jnp.zeros((cols, depth), jnp.float32) for _ in range(6)]
        for row in range(rows):
            zero = field[member, row]
            one = image_one[member, row]
            two = apply(read_image, row, 0, cols)
            image_two[member, row] = two
            terms = (zero * zero, zero * one, zero * two, one * one, one * two, two * two)
            products = [total + term for total, term in zip(products, terms)]
        for index, total in enumerate(products):
            parts[8 * index + member : 8 * index + member + 1, :] = jnp.sum(total, axis=0, keepdims=True)

    for index in range(6):
        parts[8 * index + members : 8 * index + 8, :] = jnp.zeros((8 - members, depth), jnp.float32)
    parts[48:, :] = jnp.zeros((parts.shape[0] - 48, depth), jnp.float32)
    ones = jnp.ones(message.shape[:1] + (depth,), jnp.float32)
    message[...] = lax.dot_general(
        ones, parts[...], (((1,), (1,)), ((), ())), precision=HIGHEST, preferred_element_type=jnp.float32
    )


def first_column(h00, s01, h11):
    scale = tau_step / 2.0**squarings
    a, b, d = scale * h00, scale * s01, scale * h11
    c = scale
    zero, one = jnp.zeros_like(a), jnp.ones_like(a)
    p00, p01, p10, p11, q0, q1 = one, zero, zero, one, zero, zero
    for term in range(taylor_terms, 0, -1):
        inverse = 1.0 / term
        p00, p01, p10, p11, q0, q1 = (
            1.0 + (a * p00 + b * p10) * inverse,
            (a * p01 + b * p11) * inverse,
            (c * p00 + d * p10) * inverse,
            1.0 + (c * p01 + d * p11) * inverse,
            p10 * (c * inverse),
            p11 * (c * inverse),
        )
    for _ in range(squarings):
        p00, p01, p10, p11, q0, q1 = (
            p00 * p00 + p01 * p10,
            p00 * p01 + p01 * p11,
            p10 * p00 + p11 * p10,
            p10 * p01 + p11 * p11,
            q0 * p00 + q1 * p10 + q0,
            q0 * p01 + q1 * p11 + q1,
        )
    return p00, p10, q0


def combine_kernel(gathered, field, image_one, image_two, propagated, entries):
    members, rows, cols, depth = field.shape
    ones = jnp.ones((gathered.shape[0], 128), jnp.float32)
    sums = lax.dot_general(
        gathered[...], ones, (((0,), (0,)), ((), ())), precision=HIGHEST, preferred_element_type=jnp.float32
    )
    g00, g01, g02, g11, g12, g22 = [sums[8 * index : 8 * index + 8] for index in range(6)]
    tiny = jnp.finfo(jnp.float32).tiny
    h00 = g01 / g00
    square_10 = jnp.maximum(g11 / g00 - h00 * h00, tiny)
    s01 = (g02 - h00 * g01) / g00
    h11 = ((g12 - h00 * g02) - h00 * (g11 - h00 * g01)) / (g00 * square_10)
    norm_2 = ((g22 - h00 * g12) - h00 * (g12 - h00 * g11)) / (g00 * square_10)
    h10 = jnp.sqrt(square_10)
    h01 = s01 / h10
    h21 = jnp.sqrt(jnp.maximum(norm_2 - h01 * h01 - h11 * h11, 0.0))
    e0, e1, e2 = first_column(h00, s01, h11)
    a2 = e2
    a1 = e1 - e2 * (h00 + h11)
    a0 = e0 - e1 * h00 - e2 * (s01 - h11 * h00)
    lane = lax.broadcasted_iota(jnp.int32, h00.shape, 1)
    table = h21
    for index, entry in enumerate((h00, h10, h01, h11)):
        table = jnp.where(lane == index, entry, table)
    entries[...] = (tau_step * table)[: entries.shape[0], : entries.shape[1]]
    for member in range(members):
        b0, b1, b2 = [jnp.broadcast_to(a[member : member + 1], (cols, depth)) for a in (a0, a1, a2)]
        for row in range(rows):
            propagated[member, row] = (
                b0 * field[member, row] + b1 * image_one[member, row] + b2 * image_two[member, row]
            )


def shards(density, rate_table):
    members, rows, cols, depth = density.shape
    size_x, size_y = lax.axis_size("gx"), lax.axis_size("gy")
    devices = size_x * size_y
    index_x, index_y = lax.axis_index("gx"), lax.axis_index("gy")
    parity_x, parity_y = index_x % 2, index_y % 2
    place = jnp.stack([index_x * rows, index_y * cols, parity_x, parity_y]).astype(jnp.int32)

    def swap(axis, size, first, value):
        pairs = [(i, i + 1) for i in range(first, size - 1, 2)]
        return lax.ppermute(value, axis, pairs + [(j, i) for i, j in pairs])

    def swaps(axis, size, parity, initial, last):
        if initial is last:
            return swap(axis, size, 0, last), swap(axis, size, 1, last)
        is_even = parity == 0
        return (
            swap(axis, size, 0, jnp.where(is_even, last, initial)),
            swap(axis, size, 1, jnp.where(is_even, initial, last)),
        )

    if rows == REACH:
        even_x, odd_x = swaps("gx", size_x, parity_x, density, density)
    else:
        even_x, odd_x = swaps("gx", size_x, parity_x, density[:, :REACH], density[:, rows - REACH :])

    def edge(start):
        cut = slice(start, start + 2)
        first, second = even_x[:, :, cut], odd_x[:, :, cut]
        above = jnp.where(parity_x == 0, second[:, REACH - HALF :], first[:, REACH - HALF :])
        below = jnp.where(parity_x == 0, first[:, :HALF], second[:, :HALF])
        return jnp.concatenate([above, density[:, :, cut], below], axis=1)

    even_y, odd_y = swaps("gy", size_y, parity_y, edge(0), edge(cols - 2))

    vmem = pl.BlockSpec(memory_space=pltpu.VMEM)
    smem = pl.BlockSpec(memory_space=pltpu.SMEM)
    block = jax.ShapeDtypeStruct(density.shape, jnp.float32)
    image_one, image_two, message = pl.pallas_call(
        functools.partial(images_kernel, (size_x * rows, size_y * cols)),
        out_shape=[block, block, jax.ShapeDtypeStruct((devices, 128), jnp.float32)],
        in_specs=[smem, smem, vmem, vmem, vmem, vmem, vmem],
        out_specs=[vmem, vmem, vmem],
        scratch_shapes=[
            pltpu.VMEM((members, rows + 2 * REACH, cols + 2 * GAP, depth), jnp.float32),
            pltpu.VMEM((members, rows + 2 * HALF, cols + 2 * GAP, depth), jnp.float32),
            pltpu.VMEM((128, depth), jnp.float32),
        ],
        compiler_params=pltpu.CompilerParams(vmem_limit_bytes=8 * 2**20),
        name="images",
    )(place, rate_table, density, even_x, odd_x, even_y, odd_y)

    gathered = lax.all_to_all(message, ("gx", "gy"), 0, 0, tiled=True)

    return pl.pallas_call(
        combine_kernel,
        out_shape=[block, jax.ShapeDtypeStruct((members, 5), jnp.float32)],
        in_specs=[vmem] * 4,
        out_specs=[vmem, vmem],
        compiler_params=pltpu.CompilerParams(vmem_limit_bytes=8 * 2**20),
        name="combine",
    )(gathered, density, image_one, image_two)


def solution(mesh):
    in_specs = (P(None, "gx", "gy", None), P())
    out_specs = (P(None, "gx", "gy", None), P())
    return jax.shard_map(shards, mesh=mesh, in_specs=in_specs, out_specs=out_specs, check_vma=False)
```

```python
import functools

import jax
import jax.numpy as jnp
from jax import lax
from jax.experimental import pallas as pl
from jax.experimental.pallas import tpu as pltpu
from jax.sharding import PartitionSpec as P

tau_step = 0.01
taylor_terms = 16
squarings = 4
HIGHEST = lax.Precision.HIGHEST
REACH = 4
HALF = 2
GAP = 8


def images_kernel(
    lattice,
    place,
    rates,
    field,
    even_x,
    odd_x,
    even_y,
    odd_y,
    even_corners,
    odd_corners,
    image_one,
    image_two,
    message,
    wide,
    wide_image,
    parts,
):
    members, rows, cols, depth = field.shape
    span = cols + 2 * GAP
    first_i, first_j = place[0], place[1]
    count_i, count_j = lattice

    def sides(even, odd, is_even):
        return jnp.where(is_even, odd, even), jnp.where(is_even, even, odd)

    wide[:, REACH : REACH + rows, GAP : GAP + cols] = field[...]
    above, below = sides(even_x[...], odd_x[...], place[2] == 0)
    wide[:, :REACH, GAP : GAP + cols] = above
    wide[:, REACH + rows :, GAP : GAP + cols] = below
    left, right = sides(even_y[...], odd_y[...], place[3] == 0)
    wide[:, REACH : REACH + rows, GAP - 2 : GAP] = left
    wide[:, REACH : REACH + rows, GAP + cols : GAP + cols + 2] = right
    upper, lower = sides(even_corners[...], odd_corners[...], place[2] == 0)
    for corners, at in ((upper, REACH - HALF), (lower, REACH + rows)):
        wide[:, at : at + HALF, GAP - 1 : GAP] = corners[:, :, :1]
        wide[:, at : at + HALF, GAP + cols : GAP + cols + 1] = corners[:, :, 1:]

    lane = lax.broadcasted_iota(jnp.int32, (1, depth), 1)
    amount_k = lane.astype(jnp.float32)
    above_k = jnp.where(lane < depth - 1, amount_k + 1.0, 0.0)
    inner_k = jnp.where(lane > 0, 1.0, 0.0)
    sublane = lax.broadcasted_iota(jnp.int32, (span, 1), 0)
    amount_j = (first_j - GAP + sublane).astype(jnp.float32)

    for member in range(members):
        c = [rates[member, r] for r in range(9)]
        ratio_j = amount_j / jnp.full((span, 1), c[7])
        ratio_k = amount_k / jnp.full((1, depth), c[8])
        make_u = jnp.broadcast_to(c[0] / (1.0 + ratio_j * ratio_j), (span, depth))
        make_v = c[2] / (1.0 + ratio_k * ratio_k)
        lose_v = jnp.broadcast_to(c[3] * (amount_j + 1.0), (span, depth))
        rest = make_u + make_v + (c[3] * amount_j + (c[5] + c[6]) * amount_k)

        def apply(read, row, start, size):
            i = (first_i + row).astype(jnp.float32)
            cut = slice(GAP + start, GAP + start + size)
            centre = read(row, start, size)
            value = make_u[cut] * read(row - 1, start, size)
            value = value + (c[1] * (i + 1.0)) * read(row + 1, start, size)
            value = value + make_v * read(row, start - 1, size)
            value = value + lose_v[cut] * read(row, start + 1, size)
            pair = (0.5 * c[4] * (i + 2.0) * (i + 1.0)) * read(row + 2, start, size)
            value = value + inner_k * pltpu.roll(pair, 1, 1)
            split = c[5] * read(row - 2, start, size) + c[6] * centre
            value = value + above_k * pltpu.roll(split, depth - 1, 1)
            out = rest[cut] + (c[1] * i + 0.5 * c[4] * i * (i - 1.0))
            return value - out * centre

        def read_field(row, start, size):
            return wide[member, row + REACH, pl.ds(GAP + start, size), :]

        def read_image(row, start, size):
            return wide_image[member, row + HALF, pl.ds(GAP + start, size), :]

        for row in range(-HALF, rows + HALF):
            inside = (first_i + row >= 0) & (first_i + row < count_i)
            value = apply(read_field, row, 0, cols)
            if row < 0 or row >= rows:
                value = jnp.where(inside, value, 0.0)
            else:
                image_one[member, row] = value
            wide_image[member, row + HALF, GAP : GAP + cols] = value
            if 0 <= row < rows:
                value = apply(read_field, row, -1, 1)
                wide_image[member, row + HALF, GAP - 1 : GAP] = jnp.where(first_j > 0, value, 0.0)
                value = apply(read_field, row, cols, 1)
                wide_image[member, row + HALF, GAP + cols : GAP + cols + 1] = jnp.where(
                    first_j + cols < count_j, value, 0.0
                )

        products = [jnp.zeros((cols, depth), jnp.float32) for _ in range(6)]
        for row in range(rows):
            zero = field[member, row]
            one = image_one[member, row]
            two = apply(read_image, row, 0, cols)
            image_two[member, row] = two
            terms = (zero * zero, zero * one, zero * two, one * one, one * two, two * two)
            products = [total + term for total, term in zip(products, terms)]
        for index, total in enumerate(products):
            parts[8 * index + member : 8 * index + member + 1, :] = jnp.sum(total, axis=0, keepdims=True)

    for index in range(6):
        parts[8 * index + members : 8 * index + 8, :] = jnp.zeros((8 - members, depth), jnp.float32)
    parts[48:, :] = jnp.zeros((parts.shape[0] - 48, depth), jnp.float32)
    ones = jnp.ones(message.shape[:1] + (depth,), jnp.float32)
    message[...] = lax.dot_general(
        ones, parts[...], (((1,), (1,)), ((), ())), precision=HIGHEST, preferred_element_type=jnp.float32
    )


def first_column(h00, s01, h11):
    scale = tau_step / 2.0**squarings
    a, b, d = scale * h00, scale * s01, scale * h11
    c = scale
    zero, one = jnp.zeros_like(a), jnp.ones_like(a)
    p00, p01, p10, p11, q0, q1 = one, zero, zero, one, zero, zero
    for term in range(taylor_terms, 0, -1):
        inverse = 1.0 / term
        p00, p01, p10, p11, q0, q1 = (
            1.0 + (a * p00 + b * p10) * inverse,
            (a * p01 + b * p11) * inverse,
            (c * p00 + d * p10) * inverse,
            1.0 + (c * p01 + d * p11) * inverse,
            p10 * (c * inverse),
            p11 * (c * inverse),
        )
    for _ in range(squarings):
        p00, p01, p10, p11, q0, q1 = (
            p00 * p00 + p01 * p10,
            p00 * p01 + p01 * p11,
            p10 * p00 + p11 * p10,
            p10 * p01 + p11 * p11,
            q0 * p00 + q1 * p10 + q0,
            q0 * p01 + q1 * p11 + q1,
        )
    return p00, p10, q0


def combine_kernel(gathered, field, image_one, image_two, propagated, entries):
    members, rows, cols, depth = field.shape
    ones = jnp.ones((gathered.shape[0], 128), jnp.float32)
    sums = lax.dot_general(
        gathered[...], ones, (((0,), (0,)), ((), ())), precision=HIGHEST, preferred_element_type=jnp.float32
    )
    g00, g01, g02, g11, g12, g22 = [sums[8 * index : 8 * index + 8] for index in range(6)]
    tiny = jnp.finfo(jnp.float32).tiny
    h00 = g01 / g00
    square_10 = jnp.maximum(g11 / g00 - h00 * h00, tiny)
    s01 = (g02 - h00 * g01) / g00
    h11 = ((g12 - h00 * g02) - h00 * (g11 - h00 * g01)) / (g00 * square_10)
    norm_2 = ((g22 - h00 * g12) - h00 * (g12 - h00 * g11)) / (g00 * square_10)
    h10 = jnp.sqrt(square_10)
    h01 = s01 / h10
    h21 = jnp.sqrt(jnp.maximum(norm_2 - h01 * h01 - h11 * h11, 0.0))
    e0, e1, e2 = first_column(h00, s01, h11)
    a2 = e2
    a1 = e1 - e2 * (h00 + h11)
    a0 = e0 - e1 * h00 - e2 * (s01 - h11 * h00)
    lane = lax.broadcasted_iota(jnp.int32, h00.shape, 1)
    table = h21
    for index, entry in enumerate((h00, h10, h01, h11)):
        table = jnp.where(lane == index, entry, table)
    entries[...] = (tau_step * table)[: entries.shape[0], : entries.shape[1]]
    for member in range(members):
        b0, b1, b2 = [jnp.broadcast_to(a[member : member + 1], (cols, depth)) for a in (a0, a1, a2)]
        for row in range(rows):
            propagated[member, row] = (
                b0 * field[member, row] + b1 * image_one[member, row] + b2 * image_two[member, row]
            )


def shards(density, rate_table):
    members, rows, cols, depth = density.shape
    size_x, size_y = lax.axis_size("gx"), lax.axis_size("gy")
    devices = size_x * size_y
    index_x, index_y = lax.axis_index("gx"), lax.axis_index("gy")
    parity_x, parity_y = index_x % 2, index_y % 2
    place = jnp.stack([index_x * rows, index_y * cols, parity_x, parity_y]).astype(jnp.int32)

    def swap(axis, size, first, value):
        pairs = [(i, i + 1) for i in range(first, size - 1, 2)]
        return lax.ppermute(value, axis, pairs + [(j, i) for i, j in pairs])

    def swaps(axis, size, parity, initial, last):
        if initial is last:
            return swap(axis, size, 0, last), swap(axis, size, 1, last)
        is_even = parity == 0
        return (
            swap(axis, size, 0, jnp.where(is_even, last, initial)),
            swap(axis, size, 1, jnp.where(is_even, initial, last)),
        )

    if rows == REACH:
        even_x, odd_x = swaps("gx", size_x, parity_x, density, density)
    else:
        even_x, odd_x = swaps("gx", size_x, parity_x, density[:, :REACH], density[:, rows - REACH :])

    even_y, odd_y = swaps("gy", size_y, parity_y, density[:, :, :2], density[:, :, cols - 2 :])

    def corners(first):
        even, odd = even_y[:, first : first + HALF], odd_y[:, first : first + HALF]
        left = jnp.where(parity_y == 0, odd, even)[:, :, 1:]
        right = jnp.where(parity_y == 0, even, odd)[:, :, :1]
        return jnp.concatenate([left, right], axis=2)

    even_corners, odd_corners = swaps("gx", size_x, parity_x, corners(0), corners(rows - HALF))

    vmem = pl.BlockSpec(memory_space=pltpu.VMEM)
    smem = pl.BlockSpec(memory_space=pltpu.SMEM)
    block = jax.ShapeDtypeStruct(density.shape, jnp.float32)
    image_one, image_two, message = pl.pallas_call(
        functools.partial(images_kernel, (size_x * rows, size_y * cols)),
        out_shape=[block, block, jax.ShapeDtypeStruct((devices, 128), jnp.float32)],
        in_specs=[smem, smem] + [vmem] * 7,
        out_specs=[vmem, vmem, vmem],
        scratch_shapes=[
            pltpu.VMEM((members, rows + 2 * REACH, cols + 2 * GAP, depth), jnp.float32),
            pltpu.VMEM((members, rows + 2 * HALF, cols + 2 * GAP, depth), jnp.float32),
            pltpu.VMEM((128, depth), jnp.float32),
        ],
        compiler_params=pltpu.CompilerParams(vmem_limit_bytes=8 * 2**20),
        name="images",
    )(place, rate_table, density, even_x, odd_x, even_y, odd_y, even_corners, odd_corners)

    gathered = lax.all_to_all(message, ("gx", "gy"), 0, 0, tiled=True)

    return pl.pallas_call(
        combine_kernel,
        out_shape=[block, jax.ShapeDtypeStruct((members, 5), jnp.float32)],
        in_specs=[vmem] * 4,
        out_specs=[vmem, vmem],
        compiler_params=pltpu.CompilerParams(vmem_limit_bytes=8 * 2**20),
        name="combine",
    )(gathered, density, image_one, image_two)


def solution(mesh):
    in_specs = (P(None, "gx", "gy", None), P())
    out_specs = (P(None, "gx", "gy", None), P())
    return jax.shard_map(shards, mesh=mesh, in_specs=in_specs, out_specs=out_specs, check_vma=False)
```

```python
import functools

import jax
import jax.numpy as jnp
from jax import lax
from jax.experimental import pallas as pl
from jax.experimental.pallas import tpu as pltpu
from jax.sharding import PartitionSpec as P

tau_step = 0.01
taylor_terms = 16
squarings = 4
HIGHEST = lax.Precision.HIGHEST
REACH = 4
HALF = 2
GAP = 8


def images_kernel(
    lattice,
    place,
    rates,
    field,
    even_x,
    odd_x,
    even_y,
    odd_y,
    even_corners,
    odd_corners,
    image_one,
    image_two,
    message,
    wide,
    wide_image,
    parts,
):
    members, rows, cols, depth = field.shape
    span = cols + 2 * GAP
    first_i, first_j = place[0], place[1]
    count_i, count_j = lattice

    def sides(even, odd, is_even):
        return jnp.where(is_even, odd, even), jnp.where(is_even, even, odd)

    wide[:, REACH : REACH + rows, GAP : GAP + cols] = field[...]
    above, below = sides(even_x[...], odd_x[...], place[2] == 0)
    wide[:, :REACH, GAP : GAP + cols] = above
    wide[:, REACH + rows :, GAP : GAP + cols] = below
    left, right = sides(even_y[...], odd_y[...], place[3] == 0)
    wide[:, REACH : REACH + rows, GAP - 2 : GAP] = left
    wide[:, REACH : REACH + rows, GAP + cols : GAP + cols + 2] = right
    upper, lower = sides(even_corners[...], odd_corners[...], place[2] == 0)
    for corners, at in ((upper, REACH - HALF), (lower, REACH + rows)):
        wide[:, at : at + HALF, GAP - 1 : GAP] = corners[:, :, :1]
        wide[:, at : at + HALF, GAP + cols : GAP + cols + 1] = corners[:, :, 1:]

    lane = lax.broadcasted_iota(jnp.int32, (1, depth), 1)
    amount_k = lane.astype(jnp.float32)
    above_k = jnp.where(lane < depth - 1, amount_k + 1.0, 0.0)
    inner_k = jnp.where(lane > 0, 1.0, 0.0)
    sublane = lax.broadcasted_iota(jnp.int32, (span, 1), 0)
    amount_j = (first_j - GAP + sublane).astype(jnp.float32)

    for member in range(members):
        c = [rates[member, r] for r in range(9)]
        ratio_j = amount_j / jnp.full((span, 1), c[7])
        ratio_k = amount_k / jnp.full((1, depth), c[8])
        make_u = jnp.broadcast_to(c[0] / (1.0 + ratio_j * ratio_j), (span, depth))
        make_v = c[2] / (1.0 + ratio_k * ratio_k)
        lose_v = jnp.broadcast_to(c[3] * (amount_j + 1.0), (span, depth))
        rest = make_u + make_v + (c[3] * amount_j + (c[5] + c[6]) * amount_k)

        def apply(read, row, start, size):
            i = (first_i + row).astype(jnp.float32)
            cut = slice(GAP + start, GAP + start + size)
            centre = read(row, start, size)
            value = make_u[cut] * read(row - 1, start, size)
            value = value + (c[1] * (i + 1.0)) * read(row + 1, start, size)
            value = value + make_v * read(row, start - 1, size)
            value = value + lose_v[cut] * read(row, start + 1, size)
            pair = (0.5 * c[4] * (i + 2.0) * (i + 1.0)) * read(row + 2, start, size)
            value = value + inner_k * pltpu.roll(pair, 1, 1)
            split = c[5] * read(row - 2, start, size) + c[6] * centre
            value = value + above_k * pltpu.roll(split, depth - 1, 1)
            out = rest[cut] + (c[1] * i + 0.5 * c[4] * i * (i - 1.0))
            return value - out * centre

        def read_field(row, start, size):
            return wide[member, row + REACH, pl.ds(GAP + start, size), :]

        def read_image(row, start, size):
            return wide_image[member, row + HALF, pl.ds(GAP + start, size), :]

        for row in range(-HALF, rows + HALF):
            inside = (first_i + row >= 0) & (first_i + row < count_i)
            value = apply(read_field, row, 0, cols)
            if row < 0 or row >= rows:
                value = jnp.where(inside, value, 0.0)
            else:
                image_one[member, row] = value
            wide_image[member, row + HALF, GAP : GAP + cols] = value
            if 0 <= row < rows:
                value = apply(read_field, row, -1, 1)
                wide_image[member, row + HALF, GAP - 1 : GAP] = jnp.where(first_j > 0, value, 0.0)
                value = apply(read_field, row, cols, 1)
                wide_image[member, row + HALF, GAP + cols : GAP + cols + 1] = jnp.where(
                    first_j + cols < count_j, value, 0.0
                )

        products = [jnp.zeros((cols, depth), jnp.float32) for _ in range(6)]
        for row in range(rows):
            zero = field[member, row]
            one = image_one[member, row]
            two = apply(read_image, row, 0, cols)
            image_two[member, row] = two
            terms = (zero * zero, zero * one, zero * two, one * one, one * two, two * two)
            products = [total + term for total, term in zip(products, terms)]
        for index, total in enumerate(products):
            parts[8 * index + member : 8 * index + member + 1, :] = jnp.sum(total, axis=0, keepdims=True)

    for index in range(6):
        parts[8 * index + members : 8 * index + 8, :] = jnp.zeros((8 - members, depth), jnp.float32)
    parts[48:, :] = jnp.zeros((parts.shape[0] - 48, depth), jnp.float32)
    ones = jnp.ones((8, depth), jnp.float32)
    sums = lax.dot_general(
        ones, parts[...], (((1,), (1,)), ((), ())), precision=HIGHEST, preferred_element_type=jnp.float32
    )
    message[...] = sums[:1]


def first_column(h00, s01, h11):
    scale = tau_step / 2.0**squarings
    a, b, d = scale * h00, scale * s01, scale * h11
    c = scale
    zero, one = jnp.zeros_like(a), jnp.ones_like(a)
    p00, p01, p10, p11, q0, q1 = one, zero, zero, one, zero, zero
    for term in range(taylor_terms, 0, -1):
        inverse = 1.0 / term
        p00, p01, p10, p11, q0, q1 = (
            1.0 + (a * p00 + b * p10) * inverse,
            (a * p01 + b * p11) * inverse,
            (c * p00 + d * p10) * inverse,
            1.0 + (c * p01 + d * p11) * inverse,
            p10 * (c * inverse),
            p11 * (c * inverse),
        )
    for _ in range(squarings):
        p00, p01, p10, p11, q0, q1 = (
            p00 * p00 + p01 * p10,
            p00 * p01 + p01 * p11,
            p10 * p00 + p11 * p10,
            p10 * p01 + p11 * p11,
            q0 * p00 + q1 * p10 + q0,
            q0 * p01 + q1 * p11 + q1,
        )
    return p00, p10, q0


def combine_kernel(gathered, field, image_one, image_two, propagated, entries):
    members, rows, cols, depth = field.shape
    ones = jnp.ones((gathered.shape[0], 128), jnp.float32)
    sums = lax.dot_general(
        gathered[...], ones, (((0,), (0,)), ((), ())), precision=HIGHEST, preferred_element_type=jnp.float32
    )
    g00, g01, g02, g11, g12, g22 = [sums[8 * index : 8 * index + 8] for index in range(6)]
    tiny = jnp.finfo(jnp.float32).tiny
    h00 = g01 / g00
    square_10 = jnp.maximum(g11 / g00 - h00 * h00, tiny)
    s01 = (g02 - h00 * g01) / g00
    h11 = ((g12 - h00 * g02) - h00 * (g11 - h00 * g01)) / (g00 * square_10)
    norm_2 = ((g22 - h00 * g12) - h00 * (g12 - h00 * g11)) / (g00 * square_10)
    h10 = jnp.sqrt(square_10)
    h01 = s01 / h10
    h21 = jnp.sqrt(jnp.maximum(norm_2 - h01 * h01 - h11 * h11, 0.0))
    e0, e1, e2 = first_column(h00, s01, h11)
    a2 = e2
    a1 = e1 - e2 * (h00 + h11)
    a0 = e0 - e1 * h00 - e2 * (s01 - h11 * h00)
    lane = lax.broadcasted_iota(jnp.int32, h00.shape, 1)
    table = h21
    for index, entry in enumerate((h00, h10, h01, h11)):
        table = jnp.where(lane == index, entry, table)
    entries[...] = (tau_step * table)[: entries.shape[0], : entries.shape[1]]
    for member in range(members):
        b0, b1, b2 = [jnp.broadcast_to(a[member : member + 1], (cols, depth)) for a in (a0, a1, a2)]
        for row in range(rows):
            propagated[member, row] = (
                b0 * field[member, row] + b1 * image_one[member, row] + b2 * image_two[member, row]
            )


def shards(density, rate_table):
    members, rows, cols, depth = density.shape
    size_x, size_y = lax.axis_size("gx"), lax.axis_size("gy")
    index_x, index_y = lax.axis_index("gx"), lax.axis_index("gy")
    parity_x, parity_y = index_x % 2, index_y % 2
    place = jnp.stack([index_x * rows, index_y * cols, parity_x, parity_y]).astype(jnp.int32)

    def swap(axis, size, first, value):
        pairs = [(i, i + 1) for i in range(first, size - 1, 2)]
        return lax.ppermute(value, axis, pairs + [(j, i) for i, j in pairs])

    def swaps(axis, size, parity, initial, last):
        if initial is last:
            return swap(axis, size, 0, last), swap(axis, size, 1, last)
        is_even = parity == 0
        return (
            swap(axis, size, 0, jnp.where(is_even, last, initial)),
            swap(axis, size, 1, jnp.where(is_even, initial, last)),
        )

    if rows == REACH:
        even_x, odd_x = swaps("gx", size_x, parity_x, density, density)
    else:
        even_x, odd_x = swaps("gx", size_x, parity_x, density[:, :REACH], density[:, rows - REACH :])

    even_y, odd_y = swaps("gy", size_y, parity_y, density[:, :, :2], density[:, :, cols - 2 :])

    def corners(first):
        even, odd = even_y[:, first : first + HALF], odd_y[:, first : first + HALF]
        left = jnp.where(parity_y == 0, odd, even)[:, :, 1:]
        right = jnp.where(parity_y == 0, even, odd)[:, :, :1]
        return jnp.concatenate([left, right], axis=2)

    even_corners, odd_corners = swaps("gx", size_x, parity_x, corners(0), corners(rows - HALF))

    vmem = pl.BlockSpec(memory_space=pltpu.VMEM)
    smem = pl.BlockSpec(memory_space=pltpu.SMEM)
    block = jax.ShapeDtypeStruct(density.shape, jnp.float32)
    image_one, image_two, message = pl.pallas_call(
        functools.partial(images_kernel, (size_x * rows, size_y * cols)),
        out_shape=[block, block, jax.ShapeDtypeStruct((1, 128), jnp.float32)],
        in_specs=[smem, smem] + [vmem] * 7,
        out_specs=[vmem, vmem, vmem],
        scratch_shapes=[
            pltpu.VMEM((members, rows + 2 * REACH, cols + 2 * GAP, depth), jnp.float32),
            pltpu.VMEM((members, rows + 2 * HALF, cols + 2 * GAP, depth), jnp.float32),
            pltpu.VMEM((128, depth), jnp.float32),
        ],
        compiler_params=pltpu.CompilerParams(vmem_limit_bytes=8 * 2**20),
        name="images",
    )(place, rate_table, density, even_x, odd_x, even_y, odd_y, even_corners, odd_corners)

    gathered = lax.all_gather(message, ("gx", "gy"), axis=0, tiled=True)

    return pl.pallas_call(
        combine_kernel,
        out_shape=[block, jax.ShapeDtypeStruct((members, 5), jnp.float32)],
        in_specs=[vmem] * 4,
        out_specs=[vmem, vmem],
        compiler_params=pltpu.CompilerParams(vmem_limit_bytes=8 * 2**20),
        name="combine",
    )(gathered, density, image_one, image_two)


def solution(mesh):
    in_specs = (P(None, "gx", "gy", None), P())
    out_specs = (P(None, "gx", "gy", None), P())
    return jax.shard_map(shards, mesh=mesh, in_specs=in_specs, out_specs=out_specs, check_vma=False)
```

```python
import functools

import jax
import jax.numpy as jnp
from jax import lax
from jax.experimental import pallas as pl
from jax.experimental.pallas import tpu as pltpu
from jax.sharding import PartitionSpec as P

tau_step = 0.01
taylor_terms = 16
squarings = 4
HIGHEST = lax.Precision.HIGHEST
REACH = 4
HALF = 2
GAP = 8


def edges_kernel(place, field, far, low, high):
    rows, cols = field.shape[1:3]
    low[...] = field[:, :, :2]
    high[...] = field[:, :, cols - 2 :]
    far[...] = jnp.where(place[2] == 0, field[:, rows - REACH : rows - HALF], field[:, HALF:REACH])


def images_kernel(
    lattice,
    place,
    rates,
    field,
    odd_x,
    near,
    far,
    even_y,
    odd_y,
    image_one,
    image_two,
    message,
    wide,
    wide_image,
    parts,
):
    members, rows, cols, depth = field.shape
    span = cols + 2 * GAP
    first_i, first_j = place[0], place[1]
    count_i, count_j = lattice

    def sides(even, odd, is_even):
        return jnp.where(is_even, odd, even), jnp.where(is_even, even, odd)

    wide[:, REACH : REACH + rows, GAP : GAP + cols] = field[...]
    end = REACH + rows
    for low, high, part, first in ((0, end + HALF, far, 0), (HALF, end, near, HALF)):
        above, below = odd_x[:, first : first + HALF], odd_x[:, HALF - first : REACH - first]
        wide[:, low : low + HALF, GAP : GAP + cols] = jnp.where(place[2] == 0, above, part[...])
        wide[:, high : high + HALF, GAP : GAP + cols] = jnp.where(place[2] == 0, part[...], below)
    left, right = sides(even_y[...], odd_y[...], place[3] == 0)
    wide[:, REACH - HALF : REACH + rows + HALF, GAP - 2 : GAP] = left
    wide[:, REACH - HALF : REACH + rows + HALF, GAP + cols : GAP + cols + 2] = right

    lane = lax.broadcasted_iota(jnp.int32, (1, depth), 1)
    amount_k = lane.astype(jnp.float32)
    above_k = jnp.where(lane < depth - 1, amount_k + 1.0, 0.0)
    inner_k = jnp.where(lane > 0, 1.0, 0.0)
    sublane = lax.broadcasted_iota(jnp.int32, (span, 1), 0)
    amount_j = (first_j - GAP + sublane).astype(jnp.float32)

    for member in range(members):
        c = [rates[member, r] for r in range(9)]
        ratio_j = amount_j / jnp.full((span, 1), c[7])
        ratio_k = amount_k / jnp.full((1, depth), c[8])
        make_u = jnp.broadcast_to(c[0] / (1.0 + ratio_j * ratio_j), (span, depth))
        make_v = c[2] / (1.0 + ratio_k * ratio_k)
        lose_v = jnp.broadcast_to(c[3] * (amount_j + 1.0), (span, depth))
        rest = make_u + make_v + (c[3] * amount_j + (c[5] + c[6]) * amount_k)

        def apply(read, row, start, size):
            i = (first_i + row).astype(jnp.float32)
            cut = slice(GAP + start, GAP + start + size)
            centre = read(row, start, size)
            value = make_u[cut] * read(row - 1, start, size)
            value = value + (c[1] * (i + 1.0)) * read(row + 1, start, size)
            value = value + make_v * read(row, start - 1, size)
            value = value + lose_v[cut] * read(row, start + 1, size)
            pair = (0.5 * c[4] * (i + 2.0) * (i + 1.0)) * read(row + 2, start, size)
            value = value + inner_k * pltpu.roll(pair, 1, 1)
            split = c[5] * read(row - 2, start, size) + c[6] * centre
            value = value + above_k * pltpu.roll(split, depth - 1, 1)
            out = rest[cut] + (c[1] * i + 0.5 * c[4] * i * (i - 1.0))
            return value - out * centre

        def read_field(row, start, size):
            return wide[member, row + REACH, pl.ds(GAP + start, size), :]

        def read_image(row, start, size):
            return wide_image[member, row + HALF, pl.ds(GAP + start, size), :]

        for row in range(-HALF, rows + HALF):
            inside = (first_i + row >= 0) & (first_i + row < count_i)
            value = apply(read_field, row, 0, cols)
            if row < 0 or row >= rows:
                value = jnp.where(inside, value, 0.0)
            else:
                image_one[member, row] = value
            wide_image[member, row + HALF, GAP : GAP + cols] = value
            if 0 <= row < rows:
                value = apply(read_field, row, -1, 1)
                wide_image[member, row + HALF, GAP - 1 : GAP] = jnp.where(first_j > 0, value, 0.0)
                value = apply(read_field, row, cols, 1)
                wide_image[member, row + HALF, GAP + cols : GAP + cols + 1] = jnp.where(
                    first_j + cols < count_j, value, 0.0
                )

        products = [jnp.zeros((cols, depth), jnp.float32) for _ in range(6)]
        for row in range(rows):
            zero = field[member, row]
            one = image_one[member, row]
            two = apply(read_image, row, 0, cols)
            image_two[member, row] = two
            terms = (zero * zero, zero * one, zero * two, one * one, one * two, two * two)
            products = [total + term for total, term in zip(products, terms)]
        for index, total in enumerate(products):
            parts[8 * index + member : 8 * index + member + 1, :] = jnp.sum(total, axis=0, keepdims=True)

    for index in range(6):
        parts[8 * index + members : 8 * index + 8, :] = jnp.zeros((8 - members, depth), jnp.float32)
    parts[48:, :] = jnp.zeros((parts.shape[0] - 48, depth), jnp.float32)
    ones = jnp.ones(message.shape[:1] + (depth,), jnp.float32)
    message[...] = lax.dot_general(
        ones, parts[...], (((1,), (1,)), ((), ())), precision=HIGHEST, preferred_element_type=jnp.float32
    )


def first_column(h00, s01, h11):
    scale = tau_step / 2.0**squarings
    a, b, d = scale * h00, scale * s01, scale * h11
    c = scale
    zero, one = jnp.zeros_like(a), jnp.ones_like(a)
    p00, p01, p10, p11, q0, q1 = one, zero, zero, one, zero, zero
    for term in range(taylor_terms, 0, -1):
        inverse = 1.0 / term
        p00, p01, p10, p11, q0, q1 = (
            1.0 + (a * p00 + b * p10) * inverse,
            (a * p01 + b * p11) * inverse,
            (c * p00 + d * p10) * inverse,
            1.0 + (c * p01 + d * p11) * inverse,
            p10 * (c * inverse),
            p11 * (c * inverse),
        )
    for _ in range(squarings):
        p00, p01, p10, p11, q0, q1 = (
            p00 * p00 + p01 * p10,
            p00 * p01 + p01 * p11,
            p10 * p00 + p11 * p10,
            p10 * p01 + p11 * p11,
            q0 * p00 + q1 * p10 + q0,
            q0 * p01 + q1 * p11 + q1,
        )
    return p00, p10, q0


def combine_kernel(gathered, field, image_one, image_two, propagated, entries):
    members, rows, cols, depth = field.shape
    ones = jnp.ones((gathered.shape[0], 128), jnp.float32)
    sums = lax.dot_general(
        gathered[...], ones, (((0,), (0,)), ((), ())), precision=HIGHEST, preferred_element_type=jnp.float32
    )
    g00, g01, g02, g11, g12, g22 = [sums[8 * index : 8 * index + 8] for index in range(6)]
    tiny = jnp.finfo(jnp.float32).tiny
    h00 = g01 / g00
    square_10 = jnp.maximum(g11 / g00 - h00 * h00, tiny)
    s01 = (g02 - h00 * g01) / g00
    h11 = ((g12 - h00 * g02) - h00 * (g11 - h00 * g01)) / (g00 * square_10)
    norm_2 = ((g22 - h00 * g12) - h00 * (g12 - h00 * g11)) / (g00 * square_10)
    h10 = jnp.sqrt(square_10)
    h01 = s01 / h10
    h21 = jnp.sqrt(jnp.maximum(norm_2 - h01 * h01 - h11 * h11, 0.0))
    e0, e1, e2 = first_column(h00, s01, h11)
    a2 = e2
    a1 = e1 - e2 * (h00 + h11)
    a0 = e0 - e1 * h00 - e2 * (s01 - h11 * h00)
    lane = lax.broadcasted_iota(jnp.int32, h00.shape, 1)
    table = h21
    for index, entry in enumerate((h00, h10, h01, h11)):
        table = jnp.where(lane == index, entry, table)
    entries[...] = (tau_step * table)[: entries.shape[0], : entries.shape[1]]
    for member in range(members):
        b0, b1, b2 = [jnp.broadcast_to(a[member : member + 1], (cols, depth)) for a in (a0, a1, a2)]
        for row in range(rows):
            propagated[member, row] = (
                b0 * field[member, row] + b1 * image_one[member, row] + b2 * image_two[member, row]
            )


def shards(density, rate_table):
    members, rows, cols, depth = density.shape
    size_x, size_y = lax.axis_size("gx"), lax.axis_size("gy")
    devices = size_x * size_y
    index_x, index_y = lax.axis_index("gx"), lax.axis_index("gy")
    parity_x, parity_y = index_x % 2, index_y % 2
    place = jnp.stack([index_x * rows, index_y * cols, parity_x, parity_y]).astype(jnp.int32)

    vmem = pl.BlockSpec(memory_space=pltpu.VMEM)
    smem = pl.BlockSpec(memory_space=pltpu.SMEM)

    def swap(axis, size, first, value):
        pairs = [(i, i + 1) for i in range(first, size - 1, 2)]
        return lax.ppermute(value, axis, pairs + [(j, i) for i, j in pairs])

    def swaps(axis, size, parity, initial, last):
        is_even = parity == 0
        return (
            swap(axis, size, 0, jnp.where(is_even, last, initial)),
            swap(axis, size, 1, jnp.where(is_even, initial, last)),
        )

    is_even = parity_x == 0
    initial, last = density[:, :REACH], density[:, rows - REACH :]
    odd_x = swap("gx", size_x, 1, density if rows == REACH else jnp.where(is_even, initial, last))
    near = swap("gx", size_x, 0, jnp.where(is_even, last[:, HALF:], initial[:, :HALF]))
    far, low, high = pl.pallas_call(
        edges_kernel,
        out_shape=[
            jax.ShapeDtypeStruct((members, HALF, cols, depth), jnp.float32),
            jax.ShapeDtypeStruct((members, rows, 2, depth), jnp.float32),
            jax.ShapeDtypeStruct((members, rows, 2, depth), jnp.float32),
        ],
        in_specs=[smem, vmem],
        out_specs=[vmem] * 3,
        compiler_params=pltpu.CompilerParams(vmem_limit_bytes=4 * 2**20),
        name="edges",
    )(place, density)
    far = swap("gx", size_x, 0, far)

    def edge(own, start):
        cut = slice(start, start + 2)
        above = jnp.where(is_even, odd_x[:, HALF:, cut], near[:, :, cut])
        below = jnp.where(is_even, near[:, :, cut], odd_x[:, :HALF, cut])
        return jnp.concatenate([above, own, below], axis=1)

    even_y, odd_y = swaps("gy", size_y, parity_y, edge(low, 0), edge(high, cols - 2))

    block = jax.ShapeDtypeStruct(density.shape, jnp.float32)
    image_one, image_two, message = pl.pallas_call(
        functools.partial(images_kernel, (size_x * rows, size_y * cols)),
        out_shape=[block, block, jax.ShapeDtypeStruct((devices, 128), jnp.float32)],
        in_specs=[smem, smem] + [vmem] * 6,
        out_specs=[vmem, vmem, vmem],
        scratch_shapes=[
            pltpu.VMEM((members, rows + 2 * REACH, cols + 2 * GAP, depth), jnp.float32),
            pltpu.VMEM((members, rows + 2 * HALF, cols + 2 * GAP, depth), jnp.float32),
            pltpu.VMEM((128, depth), jnp.float32),
        ],
        compiler_params=pltpu.CompilerParams(vmem_limit_bytes=8 * 2**20),
        name="images",
    )(place, rate_table, density, odd_x, near, far, even_y, odd_y)

    gathered = lax.all_to_all(message, ("gx", "gy"), 0, 0, tiled=True)

    return pl.pallas_call(
        combine_kernel,
        out_shape=[block, jax.ShapeDtypeStruct((members, 5), jnp.float32)],
        in_specs=[vmem] * 4,
        out_specs=[vmem, vmem],
        compiler_params=pltpu.CompilerParams(vmem_limit_bytes=8 * 2**20),
        name="combine",
    )(gathered, density, image_one, image_two)


def solution(mesh):
    in_specs = (P(None, "gx", "gy", None), P())
    out_specs = (P(None, "gx", "gy", None), P())
    return jax.shard_map(shards, mesh=mesh, in_specs=in_specs, out_specs=out_specs, check_vma=False)
```

```python
import functools

import jax
import jax.numpy as jnp
from jax import lax
from jax.experimental import pallas as pl
from jax.experimental.pallas import tpu as pltpu
from jax.sharding import PartitionSpec as P

tau_step = 0.01
taylor_terms = 16
squarings = 4
HIGHEST = lax.Precision.HIGHEST
REACH = 4
HALF = 2
GAP = 8


def edges_kernel(place, field, far, low, high):
    rows, cols = field.shape[1:3]
    low[...] = field[:, :, :2]
    high[...] = field[:, :, cols - 2 :]
    far[...] = jnp.where(place[2] == 0, field[:, rows - REACH : rows - HALF], field[:, HALF:REACH])


def images_kernel(
    lattice,
    place,
    rates,
    field,
    odd_x,
    near,
    far,
    even_y,
    odd_y,
    image_one,
    image_two,
    message,
    wide,
    wide_image,
    parts,
):
    members, rows, cols, depth = field.shape
    span = cols + 2 * GAP
    first_i, first_j = place[0], place[1]
    count_i, count_j = lattice

    first_end, second_end = first_i + rows < count_i, first_j + cols < count_j

    def pick(inside, is_even, even, odd):
        return jnp.where(inside, jnp.where(is_even, even, odd), 0.0)

    wide[:, REACH : REACH + rows, GAP : GAP + cols] = field[...]
    end = REACH + rows
    even_i, even_j = place[2] == 0, place[3] == 0
    for low, high, part, first in ((0, end + HALF, far, 0), (HALF, end, near, HALF)):
        above, below = odd_x[:, first : first + HALF], odd_x[:, HALF - first : REACH - first]
        wide[:, low : low + HALF, GAP : GAP + cols] = pick(first_i > 0, even_i, above, part[...])
        wide[:, high : high + HALF, GAP : GAP + cols] = pick(first_end, even_i, part[...], below)
    left = pick(first_j > 0, even_j, odd_y[...], even_y[...])
    right = pick(second_end, even_j, even_y[...], odd_y[...])
    for at, values in ((GAP - 2, left), (GAP + cols, right)):
        wide[:, HALF:REACH, at : at + 2] = jnp.where(first_i > 0, values[:, :HALF], 0.0)
        wide[:, REACH:end, at : at + 2] = values[:, HALF : HALF + rows]
        wide[:, end : end + HALF, at : at + 2] = jnp.where(first_end, values[:, HALF + rows :], 0.0)

    lane = lax.broadcasted_iota(jnp.int32, (1, depth), 1)
    amount_k = lane.astype(jnp.float32)
    above_k = jnp.where(lane < depth - 1, amount_k + 1.0, 0.0)
    inner_k = jnp.where(lane > 0, 1.0, 0.0)
    sublane = lax.broadcasted_iota(jnp.int32, (span, 1), 0)
    amount_j = (first_j - GAP + sublane).astype(jnp.float32)

    for member in range(members):
        c = [rates[member, r] for r in range(9)]
        ratio_j = amount_j / jnp.full((span, 1), c[7])
        ratio_k = amount_k / jnp.full((1, depth), c[8])
        make_u = jnp.broadcast_to(c[0] / (1.0 + ratio_j * ratio_j), (span, depth))
        make_v = c[2] / (1.0 + ratio_k * ratio_k)
        lose_v = jnp.broadcast_to(c[3] * (amount_j + 1.0), (span, depth))
        rest = make_u + make_v + (c[3] * amount_j + (c[5] + c[6]) * amount_k)

        def apply(read, row, start, size):
            i = (first_i + row).astype(jnp.float32)
            cut = slice(GAP + start, GAP + start + size)
            centre = read(row, start, size)
            value = make_u[cut] * read(row - 1, start, size)
            value = value + (c[1] * (i + 1.0)) * read(row + 1, start, size)
            value = value + make_v * read(row, start - 1, size)
            value = value + lose_v[cut] * read(row, start + 1, size)
            pair = (0.5 * c[4] * (i + 2.0) * (i + 1.0)) * read(row + 2, start, size)
            value = value + inner_k * pltpu.roll(pair, 1, 1)
            split = c[5] * read(row - 2, start, size) + c[6] * centre
            value = value + above_k * pltpu.roll(split, depth - 1, 1)
            out = rest[cut] + (c[1] * i + 0.5 * c[4] * i * (i - 1.0))
            return value - out * centre

        def read_field(row, start, size):
            return wide[member, row + REACH, pl.ds(GAP + start, size), :]

        def read_image(row, start, size):
            return wide_image[member, row + HALF, pl.ds(GAP + start, size), :]

        for row in range(-HALF, rows + HALF):
            inside = (first_i + row >= 0) & (first_i + row < count_i)
            value = apply(read_field, row, 0, cols)
            if row < 0 or row >= rows:
                value = jnp.where(inside, value, 0.0)
            else:
                image_one[member, row] = value
            wide_image[member, row + HALF, GAP : GAP + cols] = value
            if 0 <= row < rows:
                value = apply(read_field, row, -1, 1)
                wide_image[member, row + HALF, GAP - 1 : GAP] = jnp.where(first_j > 0, value, 0.0)
                value = apply(read_field, row, cols, 1)
                wide_image[member, row + HALF, GAP + cols : GAP + cols + 1] = jnp.where(
                    first_j + cols < count_j, value, 0.0
                )

        products = [jnp.zeros((cols, depth), jnp.float32) for _ in range(6)]
        for row in range(rows):
            zero = field[member, row]
            one = image_one[member, row]
            two = apply(read_image, row, 0, cols)
            image_two[member, row] = two
            terms = (zero * zero, zero * one, zero * two, one * one, one * two, two * two)
            products = [total + term for total, term in zip(products, terms)]
        for index, total in enumerate(products):
            parts[8 * index + member : 8 * index + member + 1, :] = jnp.sum(total, axis=0, keepdims=True)

    for index in range(6):
        parts[8 * index + members : 8 * index + 8, :] = jnp.zeros((8 - members, depth), jnp.float32)
    parts[48:, :] = jnp.zeros((parts.shape[0] - 48, depth), jnp.float32)
    ones = jnp.ones(message.shape[:1] + (depth,), jnp.float32)
    message[...] = lax.dot_general(
        ones, parts[...], (((1,), (1,)), ((), ())), precision=HIGHEST, preferred_element_type=jnp.float32
    )


def first_column(h00, s01, h11):
    scale = tau_step / 2.0**squarings
    a, b, d = scale * h00, scale * s01, scale * h11
    c = scale
    zero, one = jnp.zeros_like(a), jnp.ones_like(a)
    p00, p01, p10, p11, q0, q1 = one, zero, zero, one, zero, zero
    for term in range(taylor_terms, 0, -1):
        inverse = 1.0 / term
        p00, p01, p10, p11, q0, q1 = (
            1.0 + (a * p00 + b * p10) * inverse,
            (a * p01 + b * p11) * inverse,
            (c * p00 + d * p10) * inverse,
            1.0 + (c * p01 + d * p11) * inverse,
            p10 * (c * inverse),
            p11 * (c * inverse),
        )
    for _ in range(squarings):
        p00, p01, p10, p11, q0, q1 = (
            p00 * p00 + p01 * p10,
            p00 * p01 + p01 * p11,
            p10 * p00 + p11 * p10,
            p10 * p01 + p11 * p11,
            q0 * p00 + q1 * p10 + q0,
            q0 * p01 + q1 * p11 + q1,
        )
    return p00, p10, q0


def combine_kernel(gathered, field, image_one, image_two, propagated, entries):
    members, rows, cols, depth = field.shape
    ones = jnp.ones((gathered.shape[0], 128), jnp.float32)
    sums = lax.dot_general(
        gathered[...], ones, (((0,), (0,)), ((), ())), precision=HIGHEST, preferred_element_type=jnp.float32
    )
    g00, g01, g02, g11, g12, g22 = [sums[8 * index : 8 * index + 8] for index in range(6)]
    tiny = jnp.finfo(jnp.float32).tiny
    h00 = g01 / g00
    square_10 = jnp.maximum(g11 / g00 - h00 * h00, tiny)
    s01 = (g02 - h00 * g01) / g00
    h11 = ((g12 - h00 * g02) - h00 * (g11 - h00 * g01)) / (g00 * square_10)
    norm_2 = ((g22 - h00 * g12) - h00 * (g12 - h00 * g11)) / (g00 * square_10)
    h10 = jnp.sqrt(square_10)
    h01 = s01 / h10
    h21 = jnp.sqrt(jnp.maximum(norm_2 - h01 * h01 - h11 * h11, 0.0))
    e0, e1, e2 = first_column(h00, s01, h11)
    a2 = e2
    a1 = e1 - e2 * (h00 + h11)
    a0 = e0 - e1 * h00 - e2 * (s01 - h11 * h00)
    lane = lax.broadcasted_iota(jnp.int32, h00.shape, 1)
    table = h21
    for index, entry in enumerate((h00, h10, h01, h11)):
        table = jnp.where(lane == index, entry, table)
    entries[...] = (tau_step * table)[: entries.shape[0], : entries.shape[1]]
    for member in range(members):
        b0, b1, b2 = [jnp.broadcast_to(a[member : member + 1], (cols, depth)) for a in (a0, a1, a2)]
        for row in range(rows):
            propagated[member, row] = (
                b0 * field[member, row] + b1 * image_one[member, row] + b2 * image_two[member, row]
            )


def shards(density, rate_table):
    members, rows, cols, depth = density.shape
    size_x, size_y = lax.axis_size("gx"), lax.axis_size("gy")
    devices = size_x * size_y
    index_x, index_y = lax.axis_index("gx"), lax.axis_index("gy")
    parity_x, parity_y = index_x % 2, index_y % 2
    place = jnp.stack([index_x * rows, index_y * cols, parity_x, parity_y]).astype(jnp.int32)

    vmem = pl.BlockSpec(memory_space=pltpu.VMEM)
    smem = pl.BlockSpec(memory_space=pltpu.SMEM)

    def swap(axis, size, first, value):
        pairs = [(i, i + 1) for i in range(first, size - 1, 2)]
        pairs = pairs + [(j, i) for i, j in pairs]
        met = [i for i, _ in pairs]
        return lax.ppermute(value, axis, pairs + [(i, i) for i in range(size) if i not in met])

    def swaps(axis, size, parity, initial, last):
        is_even = parity == 0
        return (
            swap(axis, size, 0, jnp.where(is_even, last, initial)),
            swap(axis, size, 1, jnp.where(is_even, initial, last)),
        )

    is_even = parity_x == 0
    initial, last = density[:, :REACH], density[:, rows - REACH :]
    odd_x = swap("gx", size_x, 1, density if rows == REACH else jnp.where(is_even, initial, last))
    near = swap("gx", size_x, 0, jnp.where(is_even, last[:, HALF:], initial[:, :HALF]))
    far, low, high = pl.pallas_call(
        edges_kernel,
        out_shape=[
            jax.ShapeDtypeStruct((members, HALF, cols, depth), jnp.float32),
            jax.ShapeDtypeStruct((members, rows, 2, depth), jnp.float32),
            jax.ShapeDtypeStruct((members, rows, 2, depth), jnp.float32),
        ],
        in_specs=[smem, vmem],
        out_specs=[vmem] * 3,
        compiler_params=pltpu.CompilerParams(vmem_limit_bytes=4 * 2**20),
        name="edges",
    )(place, density)
    far = swap("gx", size_x, 0, far)

    def edge(own, start):
        cut = slice(start, start + 2)
        above = jnp.where(is_even, odd_x[:, HALF:, cut], near[:, :, cut])
        below = jnp.where(is_even, near[:, :, cut], odd_x[:, :HALF, cut])
        return jnp.concatenate([above, own, below], axis=1)

    even_y, odd_y = swaps("gy", size_y, parity_y, edge(low, 0), edge(high, cols - 2))

    block = jax.ShapeDtypeStruct(density.shape, jnp.float32)
    image_one, image_two, message = pl.pallas_call(
        functools.partial(images_kernel, (size_x * rows, size_y * cols)),
        out_shape=[block, block, jax.ShapeDtypeStruct((devices, 128), jnp.float32)],
        in_specs=[smem, smem] + [vmem] * 6,
        out_specs=[vmem, vmem, vmem],
        scratch_shapes=[
            pltpu.VMEM((members, rows + 2 * REACH, cols + 2 * GAP, depth), jnp.float32),
            pltpu.VMEM((members, rows + 2 * HALF, cols + 2 * GAP, depth), jnp.float32),
            pltpu.VMEM((128, depth), jnp.float32),
        ],
        compiler_params=pltpu.CompilerParams(vmem_limit_bytes=8 * 2**20),
        name="images",
    )(place, rate_table, density, odd_x, near, far, even_y, odd_y)

    gathered = lax.all_to_all(message, ("gx", "gy"), 0, 0, tiled=True)

    return pl.pallas_call(
        combine_kernel,
        out_shape=[block, jax.ShapeDtypeStruct((members, 5), jnp.float32)],
        in_specs=[vmem] * 4,
        out_specs=[vmem, vmem],
        compiler_params=pltpu.CompilerParams(vmem_limit_bytes=8 * 2**20),
        name="combine",
    )(gathered, density, image_one, image_two)


def solution(mesh):
    in_specs = (P(None, "gx", "gy", None), P())
    out_specs = (P(None, "gx", "gy", None), P())
    return jax.shard_map(shards, mesh=mesh, in_specs=in_specs, out_specs=out_specs, check_vma=False)
```

```python
import functools

import jax
import jax.numpy as jnp
from jax import lax
from jax.experimental import pallas as pl
from jax.experimental.pallas import tpu as pltpu
from jax.sharding import PartitionSpec as P

tau_step = 0.01
taylor_terms = 16
squarings = 4
HIGHEST = lax.Precision.HIGHEST
REACH = 4
HALF = 2
GAP = 8


def edges_kernel(place, field, far_edge, near_edge):
    cols = field.shape[2]
    low, high = field[:, :, :2], field[:, :, cols - 2 :]
    far_edge[...] = jnp.where(place[3] == 0, low, high)
    near_edge[...] = jnp.where(place[3] == 0, high, low)


def images_kernel(
    lattice,
    place,
    rates,
    field,
    own_rows,
    relayed_rows,
    columns,
    corners,
    image_one,
    image_two,
    message,
    wide,
    wide_image,
    parts,
):
    members, rows, cols, depth = field.shape
    span = cols + 2 * GAP
    first_i, first_j = place[0], place[1]
    count_i, count_j = lattice

    def sides(own, relayed, is_even):
        return jnp.where(is_even, relayed, own), jnp.where(is_even, own, relayed)

    end = REACH + rows
    wide[:, REACH:end, GAP : GAP + cols] = field[...]
    above, below = sides(own_rows[...], relayed_rows[...], place[2] == 0)
    wide[:, :REACH, GAP : GAP + cols] = above
    wide[:, end:, GAP : GAP + cols] = below
    left, right = sides(columns[:, :rows], columns[:, rows:], place[3] == 0)
    wide[:, REACH:end, GAP - 2 : GAP] = left
    wide[:, REACH:end, GAP + cols : GAP + cols + 2] = right
    upper, lower = sides(corners[:, :HALF], corners[:, HALF:], place[2] == 0)
    for corner, at in ((upper, REACH - HALF), (lower, end)):
        wide[:, at : at + HALF, GAP - 1 : GAP] = corner[:, :, :1]
        wide[:, at : at + HALF, GAP + cols : GAP + cols + 1] = corner[:, :, 1:]

    lane = lax.broadcasted_iota(jnp.int32, (1, depth), 1)
    amount_k = lane.astype(jnp.float32)
    above_k = jnp.where(lane < depth - 1, amount_k + 1.0, 0.0)
    inner_k = jnp.where(lane > 0, 1.0, 0.0)
    sublane = lax.broadcasted_iota(jnp.int32, (span, 1), 0)
    amount_j = (first_j - GAP + sublane).astype(jnp.float32)

    for member in range(members):
        c = [rates[member, r] for r in range(9)]
        ratio_j = amount_j / jnp.full((span, 1), c[7])
        ratio_k = amount_k / jnp.full((1, depth), c[8])
        make_u = jnp.broadcast_to(c[0] / (1.0 + ratio_j * ratio_j), (span, depth))
        make_v = c[2] / (1.0 + ratio_k * ratio_k)
        lose_v = jnp.broadcast_to(c[3] * (amount_j + 1.0), (span, depth))
        rest = make_u + make_v + (c[3] * amount_j + (c[5] + c[6]) * amount_k)

        def apply(read, row, start, size):
            i = (first_i + row).astype(jnp.float32)
            cut = slice(GAP + start, GAP + start + size)
            centre = read(row, start, size)
            value = make_u[cut] * read(row - 1, start, size)
            value = value + (c[1] * (i + 1.0)) * read(row + 1, start, size)
            value = value + make_v * read(row, start - 1, size)
            value = value + lose_v[cut] * read(row, start + 1, size)
            pair = (0.5 * c[4] * (i + 2.0) * (i + 1.0)) * read(row + 2, start, size)
            value = value + inner_k * pltpu.roll(pair, 1, 1)
            split = c[5] * read(row - 2, start, size) + c[6] * centre
            value = value + above_k * pltpu.roll(split, depth - 1, 1)
            out = rest[cut] + (c[1] * i + 0.5 * c[4] * i * (i - 1.0))
            return value - out * centre

        def read_field(row, start, size):
            return wide[member, row + REACH, pl.ds(GAP + start, size), :]

        def read_image(row, start, size):
            return wide_image[member, row + HALF, pl.ds(GAP + start, size), :]

        for row in range(-HALF, rows + HALF):
            inside = (first_i + row >= 0) & (first_i + row < count_i)
            value = apply(read_field, row, 0, cols)
            if row < 0 or row >= rows:
                value = jnp.where(inside, value, 0.0)
            else:
                image_one[member, row] = value
            wide_image[member, row + HALF, GAP : GAP + cols] = value
            if 0 <= row < rows:
                value = apply(read_field, row, -1, 1)
                wide_image[member, row + HALF, GAP - 1 : GAP] = jnp.where(first_j > 0, value, 0.0)
                value = apply(read_field, row, cols, 1)
                wide_image[member, row + HALF, GAP + cols : GAP + cols + 1] = jnp.where(
                    first_j + cols < count_j, value, 0.0
                )

        products = [jnp.zeros((cols, depth), jnp.float32) for _ in range(6)]
        for row in range(rows):
            zero = field[member, row]
            one = image_one[member, row]
            two = apply(read_image, row, 0, cols)
            image_two[member, row] = two
            terms = (zero * zero, zero * one, zero * two, one * one, one * two, two * two)
            products = [total + term for total, term in zip(products, terms)]
        for index, total in enumerate(products):
            parts[8 * index + member : 8 * index + member + 1, :] = jnp.sum(total, axis=0, keepdims=True)

    for index in range(6):
        parts[8 * index + members : 8 * index + 8, :] = jnp.zeros((8 - members, depth), jnp.float32)
    parts[48:, :] = jnp.zeros((parts.shape[0] - 48, depth), jnp.float32)
    ones = jnp.ones(message.shape[:1] + (depth,), jnp.float32)
    message[...] = lax.dot_general(
        ones, parts[...], (((1,), (1,)), ((), ())), precision=HIGHEST, preferred_element_type=jnp.float32
    )


def first_column(h00, s01, h11):
    scale = tau_step / 2.0**squarings
    a, b, d = scale * h00, scale * s01, scale * h11
    c = scale
    zero, one = jnp.zeros_like(a), jnp.ones_like(a)
    p00, p01, p10, p11, q0, q1 = one, zero, zero, one, zero, zero
    for term in range(taylor_terms, 0, -1):
        inverse = 1.0 / term
        p00, p01, p10, p11, q0, q1 = (
            1.0 + (a * p00 + b * p10) * inverse,
            (a * p01 + b * p11) * inverse,
            (c * p00 + d * p10) * inverse,
            1.0 + (c * p01 + d * p11) * inverse,
            p10 * (c * inverse),
            p11 * (c * inverse),
        )
    for _ in range(squarings):
        p00, p01, p10, p11, q0, q1 = (
            p00 * p00 + p01 * p10,
            p00 * p01 + p01 * p11,
            p10 * p00 + p11 * p10,
            p10 * p01 + p11 * p11,
            q0 * p00 + q1 * p10 + q0,
            q0 * p01 + q1 * p11 + q1,
        )
    return p00, p10, q0


def combine_kernel(gathered, field, image_one, image_two, propagated, entries):
    members, rows, cols, depth = field.shape
    ones = jnp.ones((gathered.shape[0], 128), jnp.float32)
    sums = lax.dot_general(
        gathered[...], ones, (((0,), (0,)), ((), ())), precision=HIGHEST, preferred_element_type=jnp.float32
    )
    g00, g01, g02, g11, g12, g22 = [sums[8 * index : 8 * index + 8] for index in range(6)]
    tiny = jnp.finfo(jnp.float32).tiny
    h00 = g01 / g00
    square_10 = jnp.maximum(g11 / g00 - h00 * h00, tiny)
    s01 = (g02 - h00 * g01) / g00
    h11 = ((g12 - h00 * g02) - h00 * (g11 - h00 * g01)) / (g00 * square_10)
    norm_2 = ((g22 - h00 * g12) - h00 * (g12 - h00 * g11)) / (g00 * square_10)
    h10 = jnp.sqrt(square_10)
    h01 = s01 / h10
    h21 = jnp.sqrt(jnp.maximum(norm_2 - h01 * h01 - h11 * h11, 0.0))
    e0, e1, e2 = first_column(h00, s01, h11)
    a2 = e2
    a1 = e1 - e2 * (h00 + h11)
    a0 = e0 - e1 * h00 - e2 * (s01 - h11 * h00)
    lane = lax.broadcasted_iota(jnp.int32, h00.shape, 1)
    table = h21
    for index, entry in enumerate((h00, h10, h01, h11)):
        table = jnp.where(lane == index, entry, table)
    entries[...] = (tau_step * table)[: entries.shape[0], : entries.shape[1]]
    for member in range(members):
        b0, b1, b2 = [jnp.broadcast_to(a[member : member + 1], (cols, depth)) for a in (a0, a1, a2)]
        for row in range(rows):
            propagated[member, row] = (
                b0 * field[member, row] + b1 * image_one[member, row] + b2 * image_two[member, row]
            )


def shards(density, rate_table):
    members, rows, cols, depth = density.shape
    size_x, size_y = lax.axis_size("gx"), lax.axis_size("gy")
    devices = size_x * size_y
    index_x, index_y = lax.axis_index("gx"), lax.axis_index("gy")
    parity_x, parity_y = index_x % 2, index_y % 2
    place = jnp.stack([index_x * rows, index_y * cols, parity_x, parity_y]).astype(jnp.int32)

    vmem = pl.BlockSpec(memory_space=pltpu.VMEM)
    smem = pl.BlockSpec(memory_space=pltpu.SMEM)

    def swap(axis, size, value):
        return lax.ppermute(value, axis, [(i, i ^ 1) for i in range(size)])

    def pass_on(axis, size, value):
        pairs = [(i, i + 2 if i % 2 else i - 2) for i in range(size)]
        return lax.ppermute(value, axis, [(i, j) for i, j in pairs if 0 <= j < size])

    assert size_x % 2 == 0 and size_y % 2 == 0
    even_x, even_y = parity_x == 0, parity_y == 0
    initial, last = density[:, :REACH], density[:, rows - REACH :]
    same = rows == REACH
    relayed_rows = pass_on("gx", size_x, density if same else jnp.where(even_x, initial, last))
    own_rows = swap("gx", size_x, density if same else jnp.where(even_x, last, initial))

    edge = jax.ShapeDtypeStruct((members, rows, 2, depth), jnp.float32)
    far_edge, near_edge = pl.pallas_call(
        edges_kernel,
        out_shape=[edge, edge],
        in_specs=[smem, vmem],
        out_specs=[vmem, vmem],
        compiler_params=pltpu.CompilerParams(vmem_limit_bytes=4 * 2**20),
        name="edges",
    )(place, density)
    relayed = pass_on("gy", size_y, far_edge)
    relayed_rows, own_rows, relayed = lax.optimization_barrier((relayed_rows, own_rows, relayed))
    columns = swap("gy", size_y, jnp.concatenate([near_edge, relayed], axis=1))

    relayed_rows = swap("gx", size_x, relayed_rows)

    left = jnp.where(even_y, columns[:, rows:], columns[:, :rows])[:, :, 1:]
    right = jnp.where(even_y, columns[:, :rows], columns[:, rows:])[:, :, :1]
    nearest = jnp.concatenate([left, right], axis=2)
    first, final = nearest[:, :HALF], nearest[:, rows - HALF :]
    relayed = pass_on("gx", size_x, jnp.where(even_x, first, final))
    corners = swap("gx", size_x, jnp.concatenate([jnp.where(even_x, final, first), relayed], axis=1))

    block = jax.ShapeDtypeStruct(density.shape, jnp.float32)
    image_one, image_two, message = pl.pallas_call(
        functools.partial(images_kernel, (size_x * rows, size_y * cols)),
        out_shape=[block, block, jax.ShapeDtypeStruct((devices, 128), jnp.float32)],
        in_specs=[smem, smem] + [vmem] * 5,
        out_specs=[vmem, vmem, vmem],
        scratch_shapes=[
            pltpu.VMEM((members, rows + 2 * REACH, cols + 2 * GAP, depth), jnp.float32),
            pltpu.VMEM((members, rows + 2 * HALF, cols + 2 * GAP, depth), jnp.float32),
            pltpu.VMEM((128, depth), jnp.float32),
        ],
        compiler_params=pltpu.CompilerParams(vmem_limit_bytes=8 * 2**20),
        name="images",
    )(place, rate_table, density, own_rows, relayed_rows, columns, corners)

    gathered = lax.all_to_all(message, ("gx", "gy"), 0, 0, tiled=True)

    return pl.pallas_call(
        combine_kernel,
        out_shape=[block, jax.ShapeDtypeStruct((members, 5), jnp.float32)],
        in_specs=[vmem] * 4,
        out_specs=[vmem, vmem],
        compiler_params=pltpu.CompilerParams(vmem_limit_bytes=8 * 2**20),
        name="combine",
    )(gathered, density, image_one, image_two)


def solution(mesh):
    in_specs = (P(None, "gx", "gy", None), P())
    out_specs = (P(None, "gx", "gy", None), P())
    return jax.shard_map(shards, mesh=mesh, in_specs=in_specs, out_specs=out_specs, check_vma=False)
```

```python
import functools

import jax
import jax.numpy as jnp
from jax import lax
from jax.experimental import pallas as pl
from jax.experimental.pallas import tpu as pltpu
from jax.sharding import PartitionSpec as P

tau_step = 0.01
taylor_terms = 16
squarings = 4
HIGHEST = lax.Precision.HIGHEST
REACH = 4
HALF = 2
GAP = 8


def edges_kernel(place, field, far, low, high):
    rows, cols = field.shape[1:3]
    low[...] = field[:, :, :2]
    high[...] = field[:, :, cols - 2 :]
    far[...] = jnp.where(place[2] == 0, field[:, rows - REACH : rows - HALF], field[:, HALF:REACH])


def images_kernel(
    lattice,
    place,
    rates,
    field,
    odd_x,
    near,
    far,
    even_y,
    odd_y,
    image_one,
    image_two,
    message,
    wide,
    wide_image,
    parts,
):
    members, rows, cols, depth = field.shape
    span = cols + 2 * GAP
    first_i, first_j = place[0], place[1]
    count_i, count_j = lattice

    first_end, second_end = first_i + rows < count_i, first_j + cols < count_j

    def pick(inside, is_even, even, odd):
        return jnp.where(inside, jnp.where(is_even, even, odd), 0.0)

    wide[:, REACH : REACH + rows, GAP : GAP + cols] = field[...]
    end = REACH + rows
    even_i, even_j = place[2] == 0, place[3] == 0
    for low, high, part, first in ((0, end + HALF, far, 0), (HALF, end, near, HALF)):
        above, below = odd_x[:, first : first + HALF], odd_x[:, HALF - first : REACH - first]
        wide[:, low : low + HALF, GAP : GAP + cols] = pick(first_i > 0, even_i, above, part[...])
        wide[:, high : high + HALF, GAP : GAP + cols] = pick(first_end, even_i, part[...], below)
    left = pick(first_j > 0, even_j, odd_y[...], even_y[...])
    right = pick(second_end, even_j, even_y[...], odd_y[...])
    for at, values in ((GAP - 2, left), (GAP + cols, right)):
        wide[:, HALF:REACH, at : at + 2] = jnp.where(first_i > 0, values[:, :HALF], 0.0)
        wide[:, REACH:end, at : at + 2] = values[:, HALF : HALF + rows]
        wide[:, end : end + HALF, at : at + 2] = jnp.where(first_end, values[:, HALF + rows :], 0.0)

    lane = lax.broadcasted_iota(jnp.int32, (1, depth), 1)
    amount_k = lane.astype(jnp.float32)
    above_k = jnp.where(lane < depth - 1, amount_k + 1.0, 0.0)
    inner_k = jnp.where(lane > 0, 1.0, 0.0)
    sublane = lax.broadcasted_iota(jnp.int32, (span, 1), 0)
    amount_j = (first_j - GAP + sublane).astype(jnp.float32)

    for member in range(members):
        c = [rates[member, r] for r in range(9)]
        ratio_j = amount_j / jnp.full((span, 1), c[7])
        ratio_k = amount_k / jnp.full((1, depth), c[8])
        make_u = jnp.broadcast_to(c[0] / (1.0 + ratio_j * ratio_j), (span, depth))
        make_v = c[2] / (1.0 + ratio_k * ratio_k)
        lose_v = jnp.broadcast_to(c[3] * (amount_j + 1.0), (span, depth))
        rest = make_u + make_v + (c[3] * amount_j + (c[5] + c[6]) * amount_k)

        def apply(read, row, start, size):
            i = (first_i + row).astype(jnp.float32)
            cut = slice(GAP + start, GAP + start + size)
            centre = read(row, start, size)
            value = make_u[cut] * read(row - 1, start, size)
            value = value + (c[1] * (i + 1.0)) * read(row + 1, start, size)
            value = value + make_v * read(row, start - 1, size)
            value = value + lose_v[cut] * read(row, start + 1, size)
            pair = (0.5 * c[4] * (i + 2.0) * (i + 1.0)) * read(row + 2, start, size)
            value = value + inner_k * pltpu.roll(pair, 1, 1)
            split = c[5] * read(row - 2, start, size) + c[6] * centre
            value = value + above_k * pltpu.roll(split, depth - 1, 1)
            out = rest[cut] + (c[1] * i + 0.5 * c[4] * i * (i - 1.0))
            return value - out * centre

        def read_field(row, start, size):
            return wide[member, row + REACH, pl.ds(GAP + start, size), :]

        def read_image(row, start, size):
            return wide_image[member, row + HALF, pl.ds(GAP + start, size), :]

        for row in range(-HALF, rows + HALF):
            inside = (first_i + row >= 0) & (first_i + row < count_i)
            value = apply(read_field, row, 0, cols)
            if row < 0 or row >= rows:
                value = jnp.where(inside, value, 0.0)
            else:
                image_one[member, row] = value
            wide_image[member, row + HALF, GAP : GAP + cols] = value
            if 0 <= row < rows:
                value = apply(read_field, row, -1, 1)
                wide_image[member, row + HALF, GAP - 1 : GAP] = jnp.where(first_j > 0, value, 0.0)
                value = apply(read_field, row, cols, 1)
                wide_image[member, row + HALF, GAP + cols : GAP + cols + 1] = jnp.where(
                    first_j + cols < count_j, value, 0.0
                )

        products = [jnp.zeros((cols, depth), jnp.float32) for _ in range(6)]
        for row in range(rows):
            zero = field[member, row]
            one = image_one[member, row]
            two = apply(read_image, row, 0, cols)
            image_two[member, row] = two
            terms = (zero * zero, zero * one, zero * two, one * one, one * two, two * two)
            products = [total + term for total, term in zip(products, terms)]
        for index, total in enumerate(products):
            parts[8 * index + member : 8 * index + member + 1, :] = jnp.sum(total, axis=0, keepdims=True)

    for index in range(6):
        parts[8 * index + members : 8 * index + 8, :] = jnp.zeros((8 - members, depth), jnp.float32)
    parts[48:, :] = jnp.zeros((parts.shape[0] - 48, depth), jnp.float32)
    ones = jnp.ones(message.shape[:1] + (depth,), jnp.float32)
    message[...] = lax.dot_general(
        ones, parts[...], (((1,), (1,)), ((), ())), precision=HIGHEST, preferred_element_type=jnp.float32
    )


def first_column(h00, s01, h11):
    scale = tau_step / 2.0**squarings
    a, b, d = scale * h00, scale * s01, scale * h11
    c = scale
    zero, one = jnp.zeros_like(a), jnp.ones_like(a)
    p00, p01, p10, p11, q0, q1 = one, zero, zero, one, zero, zero
    for term in range(taylor_terms, 0, -1):
        inverse = 1.0 / term
        p00, p01, p10, p11, q0, q1 = (
            1.0 + (a * p00 + b * p10) * inverse,
            (a * p01 + b * p11) * inverse,
            (c * p00 + d * p10) * inverse,
            1.0 + (c * p01 + d * p11) * inverse,
            p10 * (c * inverse),
            p11 * (c * inverse),
        )
    for _ in range(squarings):
        p00, p01, p10, p11, q0, q1 = (
            p00 * p00 + p01 * p10,
            p00 * p01 + p01 * p11,
            p10 * p00 + p11 * p10,
            p10 * p01 + p11 * p11,
            q0 * p00 + q1 * p10 + q0,
            q0 * p01 + q1 * p11 + q1,
        )
    return p00, p10, q0


def combine_kernel(gathered, field, image_one, image_two, propagated, entries):
    members, rows, cols, depth = field.shape
    ones = jnp.ones((gathered.shape[0], 128), jnp.float32)
    sums = lax.dot_general(
        gathered[...], ones, (((0,), (0,)), ((), ())), precision=HIGHEST, preferred_element_type=jnp.float32
    )
    g00, g01, g02, g11, g12, g22 = [sums[8 * index : 8 * index + 8] for index in range(6)]
    tiny = jnp.finfo(jnp.float32).tiny
    h00 = g01 / g00
    square_10 = jnp.maximum(g11 / g00 - h00 * h00, tiny)
    s01 = (g02 - h00 * g01) / g00
    h11 = ((g12 - h00 * g02) - h00 * (g11 - h00 * g01)) / (g00 * square_10)
    norm_2 = ((g22 - h00 * g12) - h00 * (g12 - h00 * g11)) / (g00 * square_10)
    h10 = jnp.sqrt(square_10)
    h01 = s01 / h10
    h21 = jnp.sqrt(jnp.maximum(norm_2 - h01 * h01 - h11 * h11, 0.0))
    e0, e1, e2 = first_column(h00, s01, h11)
    a2 = e2
    a1 = e1 - e2 * (h00 + h11)
    a0 = e0 - e1 * h00 - e2 * (s01 - h11 * h00)
    lane = lax.broadcasted_iota(jnp.int32, h00.shape, 1)
    table = h21
    for index, entry in enumerate((h00, h10, h01, h11)):
        table = jnp.where(lane == index, entry, table)
    entries[...] = (tau_step * table)[: entries.shape[0], : entries.shape[1]]
    for member in range(members):
        b0, b1, b2 = [jnp.broadcast_to(a[member : member + 1], (cols, depth)) for a in (a0, a1, a2)]
        for row in range(rows):
            propagated[member, row] = (
                b0 * field[member, row] + b1 * image_one[member, row] + b2 * image_two[member, row]
            )


def shards(density, rate_table):
    members, rows, cols, depth = density.shape
    size_x, size_y = lax.axis_size("gx"), lax.axis_size("gy")
    devices = size_x * size_y
    index_x, index_y = lax.axis_index("gx"), lax.axis_index("gy")
    parity_x, parity_y = index_x % 2, index_y % 2
    place = jnp.stack([index_x * rows, index_y * cols, parity_x, parity_y]).astype(jnp.int32)

    vmem = pl.BlockSpec(memory_space=pltpu.VMEM)
    smem = pl.BlockSpec(memory_space=pltpu.SMEM)

    def swap(axis, size, first, value):
        pairs = [(i, (i + 1) % size) for i in range(first, size, 2)]
        return lax.ppermute(value, axis, pairs + [(j, i) for i, j in pairs])

    def swaps(axis, size, parity, initial, last):
        is_even = parity == 0
        return (
            swap(axis, size, 0, jnp.where(is_even, last, initial)),
            swap(axis, size, 1, jnp.where(is_even, initial, last)),
        )

    is_even = parity_x == 0
    initial, last = density[:, :REACH], density[:, rows - REACH :]
    odd_x = swap("gx", size_x, 1, density if rows == REACH else jnp.where(is_even, initial, last))
    near = swap("gx", size_x, 0, jnp.where(is_even, last[:, HALF:], initial[:, :HALF]))
    far, low, high = pl.pallas_call(
        edges_kernel,
        out_shape=[
            jax.ShapeDtypeStruct((members, HALF, cols, depth), jnp.float32),
            jax.ShapeDtypeStruct((members, rows, 2, depth), jnp.float32),
            jax.ShapeDtypeStruct((members, rows, 2, depth), jnp.float32),
        ],
        in_specs=[smem, vmem],
        out_specs=[vmem] * 3,
        compiler_params=pltpu.CompilerParams(vmem_limit_bytes=4 * 2**20),
        name="edges",
    )(place, density)
    far = swap("gx", size_x, 0, far)

    def edge(own, start):
        cut = slice(start, start + 2)
        above = jnp.where(is_even, odd_x[:, HALF:, cut], near[:, :, cut])
        below = jnp.where(is_even, near[:, :, cut], odd_x[:, :HALF, cut])
        return jnp.concatenate([above, own, below], axis=1)

    even_y, odd_y = swaps("gy", size_y, parity_y, edge(low, 0), edge(high, cols - 2))

    block = jax.ShapeDtypeStruct(density.shape, jnp.float32)
    image_one, image_two, message = pl.pallas_call(
        functools.partial(images_kernel, (size_x * rows, size_y * cols)),
        out_shape=[block, block, jax.ShapeDtypeStruct((devices, 128), jnp.float32)],
        in_specs=[smem, smem] + [vmem] * 6,
        out_specs=[vmem, vmem, vmem],
        scratch_shapes=[
            pltpu.VMEM((members, rows + 2 * REACH, cols + 2 * GAP, depth), jnp.float32),
            pltpu.VMEM((members, rows + 2 * HALF, cols + 2 * GAP, depth), jnp.float32),
            pltpu.VMEM((128, depth), jnp.float32),
        ],
        compiler_params=pltpu.CompilerParams(vmem_limit_bytes=8 * 2**20),
        name="images",
    )(place, rate_table, density, odd_x, near, far, even_y, odd_y)

    gathered = lax.all_to_all(message, ("gx", "gy"), 0, 0, tiled=True)

    return pl.pallas_call(
        combine_kernel,
        out_shape=[block, jax.ShapeDtypeStruct((members, 5), jnp.float32)],
        in_specs=[vmem] * 4,
        out_specs=[vmem, vmem],
        compiler_params=pltpu.CompilerParams(vmem_limit_bytes=8 * 2**20),
        name="combine",
    )(gathered, density, image_one, image_two)


def solution(mesh):
    in_specs = (P(None, "gx", "gy", None), P())
    out_specs = (P(None, "gx", "gy", None), P())
    return jax.shard_map(shards, mesh=mesh, in_specs=in_specs, out_specs=out_specs, check_vma=False)
```

```python
import functools

import jax
import jax.numpy as jnp
from jax import lax
from jax.experimental import pallas as pl
from jax.experimental.pallas import tpu as pltpu
from jax.sharding import PartitionSpec as P

tau_step = 0.01
taylor_terms = 16
squarings = 4
HIGHEST = lax.Precision.HIGHEST
REACH = 4
HALF = 2
GAP = 8


def images_kernel(
    lattice,
    place,
    rates,
    field,
    even_x,
    odd_x,
    even_y,
    odd_y,
    even_corners,
    odd_corners,
    image_one,
    image_two,
    message,
    wide,
    wide_image,
    parts,
):
    members, rows, cols, depth = field.shape
    span = cols + 2 * GAP
    first_i, first_j = place[0], place[1]
    count_i, count_j = lattice

    ends_i, ends_j = first_i + rows < count_i, first_j + cols < count_j

    def sides(even, odd, is_even, lower_inside, higher_inside):
        lower, higher = jnp.where(is_even, odd, even), jnp.where(is_even, even, odd)
        return jnp.where(lower_inside, lower, 0.0), jnp.where(higher_inside, higher, 0.0)

    wide[:, REACH : REACH + rows, GAP : GAP + cols] = field[...]
    above, below = sides(even_x[...], odd_x[...], place[2] == 0, first_i > 0, ends_i)
    wide[:, :REACH, GAP : GAP + cols] = above
    wide[:, REACH + rows :, GAP : GAP + cols] = below
    left, right = sides(even_y[...], odd_y[...], place[3] == 0, first_j > 0, ends_j)
    wide[:, REACH : REACH + rows, GAP - 2 : GAP] = left
    wide[:, REACH : REACH + rows, GAP + cols : GAP + cols + 2] = right
    upper, lower = sides(even_corners[...], odd_corners[...], place[2] == 0, first_i > 0, ends_i)
    for corners, at in ((upper, REACH - HALF), (lower, REACH + rows)):
        wide[:, at : at + HALF, GAP - 1 : GAP] = jnp.where(first_j > 0, corners[:, :, :1], 0.0)
        wide[:, at : at + HALF, GAP + cols : GAP + cols + 1] = jnp.where(ends_j, corners[:, :, 1:], 0.0)

    lane = lax.broadcasted_iota(jnp.int32, (1, depth), 1)
    amount_k = lane.astype(jnp.float32)
    above_k = jnp.where(lane < depth - 1, amount_k + 1.0, 0.0)
    inner_k = jnp.where(lane > 0, 1.0, 0.0)
    sublane = lax.broadcasted_iota(jnp.int32, (span, 1), 0)
    amount_j = (first_j - GAP + sublane).astype(jnp.float32)

    for member in range(members):
        c = [rates[member, r] for r in range(9)]
        ratio_j = amount_j / jnp.full((span, 1), c[7])
        ratio_k = amount_k / jnp.full((1, depth), c[8])
        make_u = jnp.broadcast_to(c[0] / (1.0 + ratio_j * ratio_j), (span, depth))
        make_v = c[2] / (1.0 + ratio_k * ratio_k)
        lose_v = jnp.broadcast_to(c[3] * (amount_j + 1.0), (span, depth))
        rest = make_u + make_v + (c[3] * amount_j + (c[5] + c[6]) * amount_k)

        def apply(read, row, start, size):
            i = (first_i + row).astype(jnp.float32)
            cut = slice(GAP + start, GAP + start + size)
            centre = read(row, start, size)
            value = make_u[cut] * read(row - 1, start, size)
            value = value + (c[1] * (i + 1.0)) * read(row + 1, start, size)
            value = value + make_v * read(row, start - 1, size)
            value = value + lose_v[cut] * read(row, start + 1, size)
            pair = (0.5 * c[4] * (i + 2.0) * (i + 1.0)) * read(row + 2, start, size)
            value = value + inner_k * pltpu.roll(pair, 1, 1)
            split = c[5] * read(row - 2, start, size) + c[6] * centre
            value = value + above_k * pltpu.roll(split, depth - 1, 1)
            out = rest[cut] + (c[1] * i + 0.5 * c[4] * i * (i - 1.0))
            return value - out * centre

        def read_field(row, start, size):
            return wide[member, row + REACH, pl.ds(GAP + start, size), :]

        def read_image(row, start, size):
            return wide_image[member, row + HALF, pl.ds(GAP + start, size), :]

        for row in range(-HALF, rows + HALF):
            inside = (first_i + row >= 0) & (first_i + row < count_i)
            value = apply(read_field, row, 0, cols)
            if row < 0 or row >= rows:
                value = jnp.where(inside, value, 0.0)
            else:
                image_one[member, row] = value
            wide_image[member, row + HALF, GAP : GAP + cols] = value
            if 0 <= row < rows:
                value = apply(read_field, row, -1, 1)
                wide_image[member, row + HALF, GAP - 1 : GAP] = jnp.where(first_j > 0, value, 0.0)
                value = apply(read_field, row, cols, 1)
                wide_image[member, row + HALF, GAP + cols : GAP + cols + 1] = jnp.where(
                    first_j + cols < count_j, value, 0.0
                )

        products = [jnp.zeros((cols, depth), jnp.float32) for _ in range(6)]
        for row in range(rows):
            zero = field[member, row]
            one = image_one[member, row]
            two = apply(read_image, row, 0, cols)
            image_two[member, row] = two
            terms = (zero * zero, zero * one, zero * two, one * one, one * two, two * two)
            products = [total + term for total, term in zip(products, terms)]
        for index, total in enumerate(products):
            parts[8 * index + member : 8 * index + member + 1, :] = jnp.sum(total, axis=0, keepdims=True)

    for index in range(6):
        parts[8 * index + members : 8 * index + 8, :] = jnp.zeros((8 - members, depth), jnp.float32)
    parts[48:, :] = jnp.zeros((parts.shape[0] - 48, depth), jnp.float32)
    ones = jnp.ones(message.shape[:1] + (depth,), jnp.float32)
    message[...] = lax.dot_general(
        ones, parts[...], (((1,), (1,)), ((), ())), precision=HIGHEST, preferred_element_type=jnp.float32
    )


def first_column(h00, s01, h11):
    scale = tau_step / 2.0**squarings
    a, b, d = scale * h00, scale * s01, scale * h11
    c = scale
    zero, one = jnp.zeros_like(a), jnp.ones_like(a)
    p00, p01, p10, p11, q0, q1 = one, zero, zero, one, zero, zero
    for term in range(taylor_terms, 0, -1):
        inverse = 1.0 / term
        p00, p01, p10, p11, q0, q1 = (
            1.0 + (a * p00 + b * p10) * inverse,
            (a * p01 + b * p11) * inverse,
            (c * p00 + d * p10) * inverse,
            1.0 + (c * p01 + d * p11) * inverse,
            p10 * (c * inverse),
            p11 * (c * inverse),
        )
    for _ in range(squarings):
        p00, p01, p10, p11, q0, q1 = (
            p00 * p00 + p01 * p10,
            p00 * p01 + p01 * p11,
            p10 * p00 + p11 * p10,
            p10 * p01 + p11 * p11,
            q0 * p00 + q1 * p10 + q0,
            q0 * p01 + q1 * p11 + q1,
        )
    return p00, p10, q0


def combine_kernel(gathered, field, image_one, image_two, propagated, entries):
    members, rows, cols, depth = field.shape
    ones = jnp.ones((gathered.shape[0], 128), jnp.float32)
    sums = lax.dot_general(
        gathered[...], ones, (((0,), (0,)), ((), ())), precision=HIGHEST, preferred_element_type=jnp.float32
    )
    g00, g01, g02, g11, g12, g22 = [sums[8 * index : 8 * index + 8] for index in range(6)]
    tiny = jnp.finfo(jnp.float32).tiny
    h00 = g01 / g00
    square_10 = jnp.maximum(g11 / g00 - h00 * h00, tiny)
    s01 = (g02 - h00 * g01) / g00
    h11 = ((g12 - h00 * g02) - h00 * (g11 - h00 * g01)) / (g00 * square_10)
    norm_2 = ((g22 - h00 * g12) - h00 * (g12 - h00 * g11)) / (g00 * square_10)
    h10 = jnp.sqrt(square_10)
    h01 = s01 / h10
    h21 = jnp.sqrt(jnp.maximum(norm_2 - h01 * h01 - h11 * h11, 0.0))
    e0, e1, e2 = first_column(h00, s01, h11)
    a2 = e2
    a1 = e1 - e2 * (h00 + h11)
    a0 = e0 - e1 * h00 - e2 * (s01 - h11 * h00)
    lane = lax.broadcasted_iota(jnp.int32, h00.shape, 1)
    table = h21
    for index, entry in enumerate((h00, h10, h01, h11)):
        table = jnp.where(lane == index, entry, table)
    entries[...] = (tau_step * table)[: entries.shape[0], : entries.shape[1]]
    for member in range(members):
        b0, b1, b2 = [jnp.broadcast_to(a[member : member + 1], (cols, depth)) for a in (a0, a1, a2)]
        for row in range(rows):
            propagated[member, row] = (
                b0 * field[member, row] + b1 * image_one[member, row] + b2 * image_two[member, row]
            )


def shards(density, rate_table):
    members, rows, cols, depth = density.shape
    size_x, size_y = lax.axis_size("gx"), lax.axis_size("gy")
    devices = size_x * size_y
    index_x, index_y = lax.axis_index("gx"), lax.axis_index("gy")
    parity_x, parity_y = index_x % 2, index_y % 2
    place = jnp.stack([index_x * rows, index_y * cols, parity_x, parity_y]).astype(jnp.int32)

    def swap(axis, size, first, value):
        def partner(x, y):
            at = x if axis == "gx" else y
            other = at + 1 if (at - first) % 2 == 0 else at - 1
            if not 0 <= other < size:
                return (x, y ^ 1) if axis == "gx" else (x ^ 1, y)
            return (other, y) if axis == "gx" else (x, other)

        pairs = [
            (x * size_y + y, partner(x, y)[0] * size_y + partner(x, y)[1])
            for x in range(size_x)
            for y in range(size_y)
        ]
        return lax.ppermute(value, ("gx", "gy"), pairs)

    assert size_x % 2 == 0 and size_y % 2 == 0

    def swaps(axis, size, parity, initial, last):
        if initial is last:
            return swap(axis, size, 0, last), swap(axis, size, 1, last)
        is_even = parity == 0
        return (
            swap(axis, size, 0, jnp.where(is_even, last, initial)),
            swap(axis, size, 1, jnp.where(is_even, initial, last)),
        )

    if rows == REACH:
        even_x, odd_x = swaps("gx", size_x, parity_x, density, density)
    else:
        even_x, odd_x = swaps("gx", size_x, parity_x, density[:, :REACH], density[:, rows - REACH :])

    even_y, odd_y = swaps("gy", size_y, parity_y, density[:, :, :2], density[:, :, cols - 2 :])

    def corners(first):
        even, odd = even_y[:, first : first + HALF], odd_y[:, first : first + HALF]
        left = jnp.where(parity_y == 0, odd, even)[:, :, 1:]
        right = jnp.where(parity_y == 0, even, odd)[:, :, :1]
        return jnp.concatenate([left, right], axis=2)

    even_corners, odd_corners = swaps("gx", size_x, parity_x, corners(0), corners(rows - HALF))

    vmem = pl.BlockSpec(memory_space=pltpu.VMEM)
    smem = pl.BlockSpec(memory_space=pltpu.SMEM)
    block = jax.ShapeDtypeStruct(density.shape, jnp.float32)
    image_one, image_two, message = pl.pallas_call(
        functools.partial(images_kernel, (size_x * rows, size_y * cols)),
        out_shape=[block, block, jax.ShapeDtypeStruct((devices, 128), jnp.float32)],
        in_specs=[smem, smem] + [vmem] * 7,
        out_specs=[vmem, vmem, vmem],
        scratch_shapes=[
            pltpu.VMEM((members, rows + 2 * REACH, cols + 2 * GAP, depth), jnp.float32),
            pltpu.VMEM((members, rows + 2 * HALF, cols + 2 * GAP, depth), jnp.float32),
            pltpu.VMEM((128, depth), jnp.float32),
        ],
        compiler_params=pltpu.CompilerParams(vmem_limit_bytes=8 * 2**20),
        name="images",
    )(place, rate_table, density, even_x, odd_x, even_y, odd_y, even_corners, odd_corners)

    gathered = lax.all_to_all(message, ("gx", "gy"), 0, 0, tiled=True)

    return pl.pallas_call(
        combine_kernel,
        out_shape=[block, jax.ShapeDtypeStruct((members, 5), jnp.float32)],
        in_specs=[vmem] * 4,
        out_specs=[vmem, vmem],
        compiler_params=pltpu.CompilerParams(vmem_limit_bytes=8 * 2**20),
        name="combine",
    )(gathered, density, image_one, image_two)


def solution(mesh):
    in_specs = (P(None, "gx", "gy", None), P())
    out_specs = (P(None, "gx", "gy", None), P())
    return jax.shard_map(shards, mesh=mesh, in_specs=in_specs, out_specs=out_specs, check_vma=False)
```

```python
import functools

import jax
import jax.numpy as jnp
from jax import lax
from jax.experimental import pallas as pl
from jax.experimental.pallas import tpu as pltpu
from jax.sharding import PartitionSpec as P

tau_step = 0.01
taylor_terms = 16
squarings = 4
HIGHEST = lax.Precision.HIGHEST
REACH = 4
HALF = 2
GAP = 8


def images_kernel(
    lattice,
    place,
    rates,
    field,
    even_x,
    odd_x,
    even_y,
    odd_y,
    even_corners,
    odd_corners,
    image_one,
    image_two,
    message,
    wide,
    wide_image,
    parts,
):
    members, rows, cols, depth = field.shape
    span = cols + 2 * GAP
    first_i, first_j = place[0], place[1]
    count_i, count_j = lattice

    ends_i, ends_j = first_i + rows < count_i, first_j + cols < count_j

    def sides(even, odd, is_even, lower_inside, higher_inside):
        lower, higher = jnp.where(is_even, odd, even), jnp.where(is_even, even, odd)
        return jnp.where(lower_inside, lower, 0.0), jnp.where(higher_inside, higher, 0.0)

    wide[:, REACH : REACH + rows, GAP : GAP + cols] = field[...]
    above, below = sides(even_x[...], odd_x[...], place[2] == 0, first_i > 0, ends_i)
    wide[:, :REACH, GAP : GAP + cols] = above
    wide[:, REACH + rows :, GAP : GAP + cols] = below
    left, right = sides(even_y[...], odd_y[...], place[3] == 0, first_j > 0, ends_j)
    wide[:, REACH : REACH + rows, GAP - 2 : GAP] = left
    wide[:, REACH : REACH + rows, GAP + cols : GAP + cols + 2] = right
    upper, lower = sides(even_corners[...], odd_corners[...], place[2] == 0, first_i > 0, ends_i)
    for corners, at in ((upper, REACH - HALF), (lower, REACH + rows)):
        wide[:, at : at + HALF, GAP - 1 : GAP] = jnp.where(first_j > 0, corners[:, :, :1], 0.0)
        wide[:, at : at + HALF, GAP + cols : GAP + cols + 1] = jnp.where(ends_j, corners[:, :, 1:], 0.0)

    lane = lax.broadcasted_iota(jnp.int32, (1, depth), 1)
    amount_k = lane.astype(jnp.float32)
    above_k = jnp.where(lane < depth - 1, amount_k + 1.0, 0.0)
    inner_k = jnp.where(lane > 0, 1.0, 0.0)
    sublane = lax.broadcasted_iota(jnp.int32, (span, 1), 0)
    amount_j = (first_j - GAP + sublane).astype(jnp.float32)

    for member in range(members):
        c = [rates[member, r] for r in range(9)]
        ratio_j = amount_j / jnp.full((span, 1), c[7])
        ratio_k = amount_k / jnp.full((1, depth), c[8])
        make_u = jnp.broadcast_to(c[0] / (1.0 + ratio_j * ratio_j), (span, depth))
        make_v = c[2] / (1.0 + ratio_k * ratio_k)
        lose_v = jnp.broadcast_to(c[3] * (amount_j + 1.0), (span, depth))
        rest = make_u + make_v + (c[3] * amount_j + (c[5] + c[6]) * amount_k)

        def apply(read, row, start, size):
            i = (first_i + row).astype(jnp.float32)
            cut = slice(GAP + start, GAP + start + size)
            centre = read(row, start, size)
            value = make_u[cut] * read(row - 1, start, size)
            value = value + (c[1] * (i + 1.0)) * read(row + 1, start, size)
            value = value + make_v * read(row, start - 1, size)
            value = value + lose_v[cut] * read(row, start + 1, size)
            pair = (0.5 * c[4] * (i + 2.0) * (i + 1.0)) * read(row + 2, start, size)
            value = value + inner_k * pltpu.roll(pair, 1, 1)
            split = c[5] * read(row - 2, start, size) + c[6] * centre
            value = value + above_k * pltpu.roll(split, depth - 1, 1)
            out = rest[cut] + (c[1] * i + 0.5 * c[4] * i * (i - 1.0))
            return value - out * centre

        def read_field(row, start, size):
            return wide[member, row + REACH, pl.ds(GAP + start, size), :]

        def read_image(row, start, size):
            return wide_image[member, row + HALF, pl.ds(GAP + start, size), :]

        for row in range(-HALF, rows + HALF):
            inside = (first_i + row >= 0) & (first_i + row < count_i)
            value = apply(read_field, row, 0, cols)
            if row < 0 or row >= rows:
                value = jnp.where(inside, value, 0.0)
            else:
                image_one[member, row] = value
            wide_image[member, row + HALF, GAP : GAP + cols] = value
            if 0 <= row < rows:
                value = apply(read_field, row, -1, 1)
                wide_image[member, row + HALF, GAP - 1 : GAP] = jnp.where(first_j > 0, value, 0.0)
                value = apply(read_field, row, cols, 1)
                wide_image[member, row + HALF, GAP + cols : GAP + cols + 1] = jnp.where(
                    first_j + cols < count_j, value, 0.0
                )

        products = [jnp.zeros((cols, depth), jnp.float32) for _ in range(6)]
        for row in range(rows):
            zero = field[member, row]
            one = image_one[member, row]
            two = apply(read_image, row, 0, cols)
            image_two[member, row] = two
            terms = (zero * zero, zero * one, zero * two, one * one, one * two, two * two)
            products = [total + term for total, term in zip(products, terms)]
        for index, total in enumerate(products):
            parts[8 * index + member : 8 * index + member + 1, :] = jnp.sum(total, axis=0, keepdims=True)

    for index in range(6):
        parts[8 * index + members : 8 * index + 8, :] = jnp.zeros((8 - members, depth), jnp.float32)
    parts[48:, :] = jnp.zeros((parts.shape[0] - 48, depth), jnp.float32)
    ones = jnp.ones(message.shape[:1] + (depth,), jnp.float32)
    message[...] = lax.dot_general(
        ones, parts[...], (((1,), (1,)), ((), ())), precision=HIGHEST, preferred_element_type=jnp.float32
    )


def first_column(h00, s01, h11):
    scale = tau_step / 2.0**squarings
    a, b, d = scale * h00, scale * s01, scale * h11
    c = scale
    zero, one = jnp.zeros_like(a), jnp.ones_like(a)
    p00, p01, p10, p11, q0, q1 = one, zero, zero, one, zero, zero
    for term in range(taylor_terms, 0, -1):
        inverse = 1.0 / term
        p00, p01, p10, p11, q0, q1 = (
            1.0 + (a * p00 + b * p10) * inverse,
            (a * p01 + b * p11) * inverse,
            (c * p00 + d * p10) * inverse,
            1.0 + (c * p01 + d * p11) * inverse,
            p10 * (c * inverse),
            p11 * (c * inverse),
        )
    for _ in range(squarings):
        p00, p01, p10, p11, q0, q1 = (
            p00 * p00 + p01 * p10,
            p00 * p01 + p01 * p11,
            p10 * p00 + p11 * p10,
            p10 * p01 + p11 * p11,
            q0 * p00 + q1 * p10 + q0,
            q0 * p01 + q1 * p11 + q1,
        )
    return p00, p10, q0


def combine_kernel(gathered, field, image_one, image_two, propagated, entries):
    members, rows, cols, depth = field.shape
    ones = jnp.ones((gathered.shape[0], 128), jnp.float32)
    sums = lax.dot_general(
        gathered[...], ones, (((0,), (0,)), ((), ())), precision=HIGHEST, preferred_element_type=jnp.float32
    )
    g00, g01, g02, g11, g12, g22 = [sums[8 * index : 8 * index + 8] for index in range(6)]
    tiny = jnp.finfo(jnp.float32).tiny
    h00 = g01 / g00
    square_10 = jnp.maximum(g11 / g00 - h00 * h00, tiny)
    s01 = (g02 - h00 * g01) / g00
    h11 = ((g12 - h00 * g02) - h00 * (g11 - h00 * g01)) / (g00 * square_10)
    norm_2 = ((g22 - h00 * g12) - h00 * (g12 - h00 * g11)) / (g00 * square_10)
    h10 = jnp.sqrt(square_10)
    h01 = s01 / h10
    h21 = jnp.sqrt(jnp.maximum(norm_2 - h01 * h01 - h11 * h11, 0.0))
    e0, e1, e2 = first_column(h00, s01, h11)
    a2 = e2
    a1 = e1 - e2 * (h00 + h11)
    a0 = e0 - e1 * h00 - e2 * (s01 - h11 * h00)
    lane = lax.broadcasted_iota(jnp.int32, h00.shape, 1)
    table = h21
    for index, entry in enumerate((h00, h10, h01, h11)):
        table = jnp.where(lane == index, entry, table)
    entries[...] = (tau_step * table)[: entries.shape[0], : entries.shape[1]]
    for member in range(members):
        b0, b1, b2 = [jnp.broadcast_to(a[member : member + 1], (cols, depth)) for a in (a0, a1, a2)]
        for row in range(rows):
            propagated[member, row] = (
                b0 * field[member, row] + b1 * image_one[member, row] + b2 * image_two[member, row]
            )


def shards(density, rate_table):
    members, rows, cols, depth = density.shape
    size_x, size_y = lax.axis_size("gx"), lax.axis_size("gy")
    devices = size_x * size_y
    index_x, index_y = lax.axis_index("gx"), lax.axis_index("gy")
    parity_x, parity_y = index_x % 2, index_y % 2
    place = jnp.stack([index_x * rows, index_y * cols, parity_x, parity_y]).astype(jnp.int32)

    def swap(axis, size, first, value):
        def partner(x, y):
            at = x if axis == "gx" else y
            other = at + 1 if (at - first) % 2 == 0 else at - 1
            if not 0 <= other < size:
                return (x, y ^ 1) if axis == "gx" else (x ^ 1, y)
            return (other, y) if axis == "gx" else (x, other)

        pairs = [
            (x * size_y + y, partner(x, y)[0] * size_y + partner(x, y)[1])
            for x in range(size_x)
            for y in range(size_y)
        ]
        return lax.ppermute(value, ("gx", "gy"), pairs)

    assert size_x % 2 == 0 and size_y % 2 == 0

    def swaps(axis, size, parity, initial, last):
        if initial is last:
            return swap(axis, size, 0, last), swap(axis, size, 1, last)
        is_even = parity == 0
        return (
            swap(axis, size, 0, jnp.where(is_even, last, initial)),
            swap(axis, size, 1, jnp.where(is_even, initial, last)),
        )

    if rows == REACH:
        even_x, odd_x = swaps("gx", size_x, parity_x, density, density)
    else:
        even_x, odd_x = swaps("gx", size_x, parity_x, density[:, :REACH], density[:, rows - REACH :])

    even_y, odd_y = swaps("gy", size_y, parity_y, density[:, :, :2], density[:, :, cols - 2 :])

    odd_x, even_y, odd_y = lax.optimization_barrier((odd_x, even_y, odd_y))

    def corners(first):
        even, odd = even_y[:, first : first + HALF], odd_y[:, first : first + HALF]
        left = jnp.where(parity_y == 0, odd, even)[:, :, 1:]
        right = jnp.where(parity_y == 0, even, odd)[:, :, :1]
        return jnp.concatenate([left, right], axis=2)

    even_corners, odd_corners = swaps("gx", size_x, parity_x, corners(0), corners(rows - HALF))

    vmem = pl.BlockSpec(memory_space=pltpu.VMEM)
    smem = pl.BlockSpec(memory_space=pltpu.SMEM)
    block = jax.ShapeDtypeStruct(density.shape, jnp.float32)
    image_one, image_two, message = pl.pallas_call(
        functools.partial(images_kernel, (size_x * rows, size_y * cols)),
        out_shape=[block, block, jax.ShapeDtypeStruct((devices, 128), jnp.float32)],
        in_specs=[smem, smem] + [vmem] * 7,
        out_specs=[vmem, vmem, vmem],
        scratch_shapes=[
            pltpu.VMEM((members, rows + 2 * REACH, cols + 2 * GAP, depth), jnp.float32),
            pltpu.VMEM((members, rows + 2 * HALF, cols + 2 * GAP, depth), jnp.float32),
            pltpu.VMEM((128, depth), jnp.float32),
        ],
        compiler_params=pltpu.CompilerParams(vmem_limit_bytes=8 * 2**20),
        name="images",
    )(place, rate_table, density, even_x, odd_x, even_y, odd_y, even_corners, odd_corners)

    gathered = lax.all_to_all(message, ("gx", "gy"), 0, 0, tiled=True)

    return pl.pallas_call(
        combine_kernel,
        out_shape=[block, jax.ShapeDtypeStruct((members, 5), jnp.float32)],
        in_specs=[vmem] * 4,
        out_specs=[vmem, vmem],
        compiler_params=pltpu.CompilerParams(vmem_limit_bytes=8 * 2**20),
        name="combine",
    )(gathered, density, image_one, image_two)


def solution(mesh):
    in_specs = (P(None, "gx", "gy", None), P())
    out_specs = (P(None, "gx", "gy", None), P())
    return jax.shard_map(shards, mesh=mesh, in_specs=in_specs, out_specs=out_specs, check_vma=False)
```

```python
import functools

import jax
import jax.numpy as jnp
from jax import lax
from jax.experimental import pallas as pl
from jax.experimental.pallas import tpu as pltpu
from jax.sharding import PartitionSpec as P

tau_step = 0.01
taylor_terms = 16
squarings = 4
HIGHEST = lax.Precision.HIGHEST
REACH = 4
HALF = 2
GAP = 8


def images_kernel(
    lattice,
    place,
    rates,
    field,
    even_x,
    odd_x,
    even_y,
    odd_y,
    even_corners,
    odd_corners,
    image_one,
    image_two,
    message,
    wide,
    wide_image,
    parts,
):
    members, rows, cols, depth = field.shape
    span = cols + 2 * GAP
    first_i, first_j = place[0], place[1]
    count_i, count_j = lattice

    ends_i, ends_j = first_i + rows < count_i, first_j + cols < count_j

    def sides(even, odd, is_even, lower_inside, higher_inside):
        lower, higher = jnp.where(is_even, odd, even), jnp.where(is_even, even, odd)
        return jnp.where(lower_inside, lower, 0.0), jnp.where(higher_inside, higher, 0.0)

    wide[:, REACH : REACH + rows, GAP : GAP + cols] = field[...]
    above, below = sides(even_x[...], odd_x[...], place[2] == 0, first_i > 0, ends_i)
    wide[:, :REACH, GAP : GAP + cols] = above
    wide[:, REACH + rows :, GAP : GAP + cols] = below
    left, right = sides(even_y[...], odd_y[...], place[3] == 0, first_j > 0, ends_j)
    wide[:, REACH : REACH + rows, GAP - 2 : GAP] = left
    wide[:, REACH : REACH + rows, GAP + cols : GAP + cols + 2] = right
    upper, lower = sides(even_corners[...], odd_corners[...], place[2] == 0, first_i > 0, ends_i)
    for corners, at in ((upper, REACH - HALF), (lower, REACH + rows)):
        wide[:, at : at + HALF, GAP - 1 : GAP] = jnp.where(first_j > 0, corners[:, :, :1], 0.0)
        wide[:, at : at + HALF, GAP + cols : GAP + cols + 1] = jnp.where(ends_j, corners[:, :, 1:], 0.0)

    lane = lax.broadcasted_iota(jnp.int32, (1, depth), 1)
    amount_k = lane.astype(jnp.float32)
    above_k = jnp.where(lane < depth - 1, amount_k + 1.0, 0.0)
    inner_k = jnp.where(lane > 0, 1.0, 0.0)
    sublane = lax.broadcasted_iota(jnp.int32, (span, 1), 0)
    amount_j = (first_j - GAP + sublane).astype(jnp.float32)

    for member in range(members):
        c = [rates[member, r] for r in range(9)]
        ratio_j = amount_j / jnp.full((span, 1), c[7])
        ratio_k = amount_k / jnp.full((1, depth), c[8])
        make_u = jnp.broadcast_to(c[0] / (1.0 + ratio_j * ratio_j), (span, depth))
        make_v = c[2] / (1.0 + ratio_k * ratio_k)
        lose_v = jnp.broadcast_to(c[3] * (amount_j + 1.0), (span, depth))
        rest = make_u + make_v + (c[3] * amount_j + (c[5] + c[6]) * amount_k)

        def apply(read, row, start, size):
            i = (first_i + row).astype(jnp.float32)
            cut = slice(GAP + start, GAP + start + size)
            centre = read(row, start, size)
            value = make_u[cut] * read(row - 1, start, size)
            value = value + (c[1] * (i + 1.0)) * read(row + 1, start, size)
            value = value + make_v * read(row, start - 1, size)
            value = value + lose_v[cut] * read(row, start + 1, size)
            pair = (0.5 * c[4] * (i + 2.0) * (i + 1.0)) * read(row + 2, start, size)
            value = value + inner_k * pltpu.roll(pair, 1, 1)
            split = c[5] * read(row - 2, start, size) + c[6] * centre
            value = value + above_k * pltpu.roll(split, depth - 1, 1)
            out = rest[cut] + (c[1] * i + 0.5 * c[4] * i * (i - 1.0))
            return value - out * centre

        def read_field(row, start, size):
            return wide[member, row + REACH, pl.ds(GAP + start, size), :]

        def read_image(row, start, size):
            return wide_image[member, row + HALF, pl.ds(GAP + start, size), :]

        for row in range(-HALF, rows + HALF):
            inside = (first_i + row >= 0) & (first_i + row < count_i)
            value = apply(read_field, row, 0, cols)
            if row < 0 or row >= rows:
                value = jnp.where(inside, value, 0.0)
            else:
                image_one[member, row] = value
            wide_image[member, row + HALF, GAP : GAP + cols] = value
            if 0 <= row < rows:
                value = apply(read_field, row, -1, 1)
                wide_image[member, row + HALF, GAP - 1 : GAP] = jnp.where(first_j > 0, value, 0.0)
                value = apply(read_field, row, cols, 1)
                wide_image[member, row + HALF, GAP + cols : GAP + cols + 1] = jnp.where(
                    first_j + cols < count_j, value, 0.0
                )

        products = [jnp.zeros((cols, depth), jnp.float32) for _ in range(6)]
        for row in range(rows):
            zero = field[member, row]
            one = image_one[member, row]
            two = apply(read_image, row, 0, cols)
            image_two[member, row] = two
            terms = (zero * zero, zero * one, zero * two, one * one, one * two, two * two)
            products = [total + term for total, term in zip(products, terms)]
        for index, total in enumerate(products):
            parts[8 * index + member : 8 * index + member + 1, :] = jnp.sum(total, axis=0, keepdims=True)

    for index in range(6):
        parts[8 * index + members : 8 * index + 8, :] = jnp.zeros((8 - members, depth), jnp.float32)
    parts[48:, :] = jnp.zeros((parts.shape[0] - 48, depth), jnp.float32)
    ones = jnp.ones(message.shape[:1] + (depth,), jnp.float32)
    message[...] = lax.dot_general(
        ones, parts[...], (((1,), (1,)), ((), ())), precision=HIGHEST, preferred_element_type=jnp.float32
    )


def first_column(h00, s01, h11):
    scale = tau_step / 2.0**squarings
    a, b, d = scale * h00, scale * s01, scale * h11
    c = scale
    zero, one = jnp.zeros_like(a), jnp.ones_like(a)
    p00, p01, p10, p11, q0, q1 = one, zero, zero, one, zero, zero
    for term in range(taylor_terms, 0, -1):
        inverse = 1.0 / term
        p00, p01, p10, p11, q0, q1 = (
            1.0 + (a * p00 + b * p10) * inverse,
            (a * p01 + b * p11) * inverse,
            (c * p00 + d * p10) * inverse,
            1.0 + (c * p01 + d * p11) * inverse,
            p10 * (c * inverse),
            p11 * (c * inverse),
        )
    for _ in range(squarings):
        p00, p01, p10, p11, q0, q1 = (
            p00 * p00 + p01 * p10,
            p00 * p01 + p01 * p11,
            p10 * p00 + p11 * p10,
            p10 * p01 + p11 * p11,
            q0 * p00 + q1 * p10 + q0,
            q0 * p01 + q1 * p11 + q1,
        )
    return p00, p10, q0


def combine_kernel(gathered, field, image_one, image_two, propagated, entries):
    members, rows, cols, depth = field.shape
    ones = jnp.ones((gathered.shape[0], 128), jnp.float32)
    sums = lax.dot_general(
        gathered[...], ones, (((0,), (0,)), ((), ())), precision=HIGHEST, preferred_element_type=jnp.float32
    )
    g00, g01, g02, g11, g12, g22 = [sums[8 * index : 8 * index + 8] for index in range(6)]
    tiny = jnp.finfo(jnp.float32).tiny
    h00 = g01 / g00
    square_10 = jnp.maximum(g11 / g00 - h00 * h00, tiny)
    s01 = (g02 - h00 * g01) / g00
    h11 = ((g12 - h00 * g02) - h00 * (g11 - h00 * g01)) / (g00 * square_10)
    norm_2 = ((g22 - h00 * g12) - h00 * (g12 - h00 * g11)) / (g00 * square_10)
    h10 = jnp.sqrt(square_10)
    h01 = s01 / h10
    h21 = jnp.sqrt(jnp.maximum(norm_2 - h01 * h01 - h11 * h11, 0.0))
    e0, e1, e2 = first_column(h00, s01, h11)
    a2 = e2
    a1 = e1 - e2 * (h00 + h11)
    a0 = e0 - e1 * h00 - e2 * (s01 - h11 * h00)
    lane = lax.broadcasted_iota(jnp.int32, h00.shape, 1)
    table = h21
    for index, entry in enumerate((h00, h10, h01, h11)):
        table = jnp.where(lane == index, entry, table)
    entries[...] = (tau_step * table)[: entries.shape[0], : entries.shape[1]]
    for member in range(members):
        b0, b1, b2 = [jnp.broadcast_to(a[member : member + 1], (cols, depth)) for a in (a0, a1, a2)]
        for row in range(rows):
            propagated[member, row] = (
                b0 * field[member, row] + b1 * image_one[member, row] + b2 * image_two[member, row]
            )


def shards(density, rate_table):
    members, rows, cols, depth = density.shape
    size_x, size_y = lax.axis_size("gx"), lax.axis_size("gy")
    index_x, index_y = lax.axis_index("gx"), lax.axis_index("gy")
    parity_x, parity_y = index_x % 2, index_y % 2
    place = jnp.stack([index_x * rows, index_y * cols, parity_x, parity_y]).astype(jnp.int32)

    def swap(axis, size, first, value):
        def partner(x, y):
            at = x if axis == "gx" else y
            other = at + 1 if (at - first) % 2 == 0 else at - 1
            if not 0 <= other < size:
                return (x, y ^ 1) if axis == "gx" else (x ^ 1, y)
            return (other, y) if axis == "gx" else (x, other)

        pairs = [
            (x * size_y + y, partner(x, y)[0] * size_y + partner(x, y)[1])
            for x in range(size_x)
            for y in range(size_y)
        ]
        return lax.ppermute(value, ("gx", "gy"), pairs)

    assert size_x % 2 == 0 and size_y % 2 == 0

    def swaps(axis, size, parity, initial, last):
        if initial is last:
            return swap(axis, size, 0, last), swap(axis, size, 1, last)
        is_even = parity == 0
        return (
            swap(axis, size, 0, jnp.where(is_even, last, initial)),
            swap(axis, size, 1, jnp.where(is_even, initial, last)),
        )

    if rows == REACH:
        even_x, odd_x = swaps("gx", size_x, parity_x, density, density)
    else:
        even_x, odd_x = swaps("gx", size_x, parity_x, density[:, :REACH], density[:, rows - REACH :])

    even_y, odd_y = swaps("gy", size_y, parity_y, density[:, :, :2], density[:, :, cols - 2 :])

    def corners(first):
        even, odd = even_y[:, first : first + HALF], odd_y[:, first : first + HALF]
        left = jnp.where(parity_y == 0, odd, even)[:, :, 1:]
        right = jnp.where(parity_y == 0, even, odd)[:, :, :1]
        return jnp.concatenate([left, right], axis=2)

    even_corners, odd_corners = swaps("gx", size_x, parity_x, corners(0), corners(rows - HALF))

    vmem = pl.BlockSpec(memory_space=pltpu.VMEM)
    smem = pl.BlockSpec(memory_space=pltpu.SMEM)
    block = jax.ShapeDtypeStruct(density.shape, jnp.float32)
    image_one, image_two, message = pl.pallas_call(
        functools.partial(images_kernel, (size_x * rows, size_y * cols)),
        out_shape=[block, block, jax.ShapeDtypeStruct((size_y, 128), jnp.float32)],
        in_specs=[smem, smem] + [vmem] * 7,
        out_specs=[vmem, vmem, vmem],
        scratch_shapes=[
            pltpu.VMEM((members, rows + 2 * REACH, cols + 2 * GAP, depth), jnp.float32),
            pltpu.VMEM((members, rows + 2 * HALF, cols + 2 * GAP, depth), jnp.float32),
            pltpu.VMEM((128, depth), jnp.float32),
        ],
        compiler_params=pltpu.CompilerParams(vmem_limit_bytes=8 * 2**20),
        name="images",
    )(place, rate_table, density, even_x, odd_x, even_y, odd_y, even_corners, odd_corners)

    message = lax.all_to_all(message, "gy", 0, 0, tiled=True)
    message = jnp.broadcast_to(jnp.sum(message, axis=0, keepdims=True), (size_x, 128))
    gathered = lax.all_to_all(message, "gx", 0, 0, tiled=True)

    return pl.pallas_call(
        combine_kernel,
        out_shape=[block, jax.ShapeDtypeStruct((members, 5), jnp.float32)],
        in_specs=[vmem] * 4,
        out_specs=[vmem, vmem],
        compiler_params=pltpu.CompilerParams(vmem_limit_bytes=8 * 2**20),
        name="combine",
    )(gathered, density, image_one, image_two)


def solution(mesh):
    in_specs = (P(None, "gx", "gy", None), P())
    out_specs = (P(None, "gx", "gy", None), P())
    return jax.shard_map(shards, mesh=mesh, in_specs=in_specs, out_specs=out_specs, check_vma=False)
```

```python
import functools

import jax
import jax.numpy as jnp
from jax import lax
from jax.experimental import pallas as pl
from jax.experimental.pallas import tpu as pltpu
from jax.sharding import PartitionSpec as P

tau_step = 0.01
taylor_terms = 16
squarings = 4
HIGHEST = lax.Precision.HIGHEST
REACH = 4
HALF = 2
GAP = 8


def images_kernel(
    lattice,
    place,
    rates,
    field,
    even_x,
    odd_x,
    even_y,
    odd_y,
    even_corners,
    odd_corners,
    image_one,
    image_two,
    message,
    wide,
    wide_image,
    parts,
):
    members, rows, cols, depth = field.shape
    span = cols + 2 * GAP
    first_i, first_j = place[0], place[1]
    count_i, count_j = lattice

    ends_i, ends_j = first_i + rows < count_i, first_j + cols < count_j

    def sides(even, odd, is_even, lower_inside, higher_inside):
        lower, higher = jnp.where(is_even, odd, even), jnp.where(is_even, even, odd)
        return jnp.where(lower_inside, lower, 0.0), jnp.where(higher_inside, higher, 0.0)

    wide[:, REACH : REACH + rows, GAP : GAP + cols] = field[...]
    above, below = sides(even_x[...], odd_x[...], place[2] == 0, first_i > 0, ends_i)
    wide[:, :REACH, GAP : GAP + cols] = above
    wide[:, REACH + rows :, GAP : GAP + cols] = below
    left, right = sides(even_y[...], odd_y[...], place[3] == 0, first_j > 0, ends_j)
    wide[:, REACH : REACH + rows, GAP - 2 : GAP] = left
    wide[:, REACH : REACH + rows, GAP + cols : GAP + cols + 2] = right
    upper, lower = sides(even_corners[...], odd_corners[...], place[2] == 0, first_i > 0, ends_i)
    for corners, at in ((upper, REACH - HALF), (lower, REACH + rows)):
        wide[:, at : at + HALF, GAP - 1 : GAP] = jnp.where(first_j > 0, corners[:, :, :1], 0.0)
        wide[:, at : at + HALF, GAP + cols : GAP + cols + 1] = jnp.where(ends_j, corners[:, :, 1:], 0.0)

    lane = lax.broadcasted_iota(jnp.int32, (1, depth), 1)
    amount_k = lane.astype(jnp.float32)
    above_k = jnp.where(lane < depth - 1, amount_k + 1.0, 0.0)
    inner_k = jnp.where(lane > 0, 1.0, 0.0)
    sublane = lax.broadcasted_iota(jnp.int32, (span, 1), 0)
    amount_j = (first_j - GAP + sublane).astype(jnp.float32)

    for member in range(members):
        c = [rates[member, r] for r in range(9)]
        ratio_j = amount_j / jnp.full((span, 1), c[7])
        ratio_k = amount_k / jnp.full((1, depth), c[8])
        make_u = jnp.broadcast_to(c[0] / (1.0 + ratio_j * ratio_j), (span, depth))
        make_v = c[2] / (1.0 + ratio_k * ratio_k)
        lose_v = jnp.broadcast_to(c[3] * (amount_j + 1.0), (span, depth))
        rest = make_u + make_v + (c[3] * amount_j + (c[5] + c[6]) * amount_k)

        def apply(read, row, start, size):
            i = (first_i + row).astype(jnp.float32)
            cut = slice(GAP + start, GAP + start + size)
            centre = read(row, start, size)
            value = make_u[cut] * read(row - 1, start, size)
            value = value + (c[1] * (i + 1.0)) * read(row + 1, start, size)
            value = value + make_v * read(row, start - 1, size)
            value = value + lose_v[cut] * read(row, start + 1, size)
            pair = (0.5 * c[4] * (i + 2.0) * (i + 1.0)) * read(row + 2, start, size)
            value = value + inner_k * pltpu.roll(pair, 1, 1)
            split = c[5] * read(row - 2, start, size) + c[6] * centre
            value = value + above_k * pltpu.roll(split, depth - 1, 1)
            out = rest[cut] + (c[1] * i + 0.5 * c[4] * i * (i - 1.0))
            return value - out * centre

        def read_field(row, start, size):
            return wide[member, row + REACH, pl.ds(GAP + start, size), :]

        def read_image(row, start, size):
            return wide_image[member, row + HALF, pl.ds(GAP + start, size), :]

        for row in range(-HALF, rows + HALF):
            inside = (first_i + row >= 0) & (first_i + row < count_i)
            value = apply(read_field, row, 0, cols)
            if row < 0 or row >= rows:
                value = jnp.where(inside, value, 0.0)
            else:
                image_one[member, row] = value
            wide_image[member, row + HALF, GAP : GAP + cols] = value
            if 0 <= row < rows:
                value = apply(read_field, row, -1, 1)
                wide_image[member, row + HALF, GAP - 1 : GAP] = jnp.where(first_j > 0, value, 0.0)
                value = apply(read_field, row, cols, 1)
                wide_image[member, row + HALF, GAP + cols : GAP + cols + 1] = jnp.where(
                    first_j + cols < count_j, value, 0.0
                )

        products = [jnp.zeros((cols, depth), jnp.float32) for _ in range(6)]
        for row in range(rows):
            zero = field[member, row]
            one = image_one[member, row]
            two = apply(read_image, row, 0, cols)
            image_two[member, row] = two
            terms = (zero * zero, zero * one, zero * two, one * one, one * two, two * two)
            products = [total + term for total, term in zip(products, terms)]
        for index, total in enumerate(products):
            parts[8 * index + member : 8 * index + member + 1, :] = jnp.sum(total, axis=0, keepdims=True)

    for index in range(6):
        parts[8 * index + members : 8 * index + 8, :] = jnp.zeros((8 - members, depth), jnp.float32)
    parts[48:, :] = jnp.zeros((parts.shape[0] - 48, depth), jnp.float32)
    ones = jnp.ones(message.shape[:1] + (depth,), jnp.float32)
    message[...] = lax.dot_general(
        ones, parts[...], (((1,), (1,)), ((), ())), precision=HIGHEST, preferred_element_type=jnp.float32
    )


def first_column(h00, s01, h11):
    scale = tau_step / 2.0**squarings
    a, b, d = scale * h00, scale * s01, scale * h11
    c = scale
    zero, one = jnp.zeros_like(a), jnp.ones_like(a)
    p00, p01, p10, p11, q0, q1 = one, zero, zero, one, zero, zero
    for term in range(taylor_terms, 0, -1):
        inverse = 1.0 / term
        p00, p01, p10, p11, q0, q1 = (
            1.0 + (a * p00 + b * p10) * inverse,
            (a * p01 + b * p11) * inverse,
            (c * p00 + d * p10) * inverse,
            1.0 + (c * p01 + d * p11) * inverse,
            p10 * (c * inverse),
            p11 * (c * inverse),
        )
    for _ in range(squarings):
        p00, p01, p10, p11, q0, q1 = (
            p00 * p00 + p01 * p10,
            p00 * p01 + p01 * p11,
            p10 * p00 + p11 * p10,
            p10 * p01 + p11 * p11,
            q0 * p00 + q1 * p10 + q0,
            q0 * p01 + q1 * p11 + q1,
        )
    return p00, p10, q0


def combine_kernel(gathered, field, image_one, image_two, propagated, entries):
    members, rows, cols, depth = field.shape
    ones = jnp.ones((gathered.shape[0], 128), jnp.float32)
    sums = lax.dot_general(
        gathered[...], ones, (((0,), (0,)), ((), ())), precision=HIGHEST, preferred_element_type=jnp.float32
    )
    g00, g01, g02, g11, g12, g22 = [sums[8 * index : 8 * index + 8] for index in range(6)]
    tiny = jnp.finfo(jnp.float32).tiny
    h00 = g01 / g00
    square_10 = jnp.maximum(g11 / g00 - h00 * h00, tiny)
    s01 = (g02 - h00 * g01) / g00
    h11 = ((g12 - h00 * g02) - h00 * (g11 - h00 * g01)) / (g00 * square_10)
    norm_2 = ((g22 - h00 * g12) - h00 * (g12 - h00 * g11)) / (g00 * square_10)
    h10 = jnp.sqrt(square_10)
    h01 = s01 / h10
    h21 = jnp.sqrt(jnp.maximum(norm_2 - h01 * h01 - h11 * h11, 0.0))
    e0, e1, e2 = first_column(h00, s01, h11)
    a2 = e2
    a1 = e1 - e2 * (h00 + h11)
    a0 = e0 - e1 * h00 - e2 * (s01 - h11 * h00)
    lane = lax.broadcasted_iota(jnp.int32, h00.shape, 1)
    table = h21
    for index, entry in enumerate((h00, h10, h01, h11)):
        table = jnp.where(lane == index, entry, table)
    entries[...] = (tau_step * table)[: entries.shape[0], : entries.shape[1]]
    for member in range(members):
        b0, b1, b2 = [jnp.broadcast_to(a[member : member + 1], (cols, depth)) for a in (a0, a1, a2)]
        for row in range(rows):
            propagated[member, row] = (
                b0 * field[member, row] + b1 * image_one[member, row] + b2 * image_two[member, row]
            )


def shards(density, rate_table):
    members, rows, cols, depth = density.shape
    size_x, size_y = lax.axis_size("gx"), lax.axis_size("gy")
    devices = size_x * size_y
    index_x, index_y = lax.axis_index("gx"), lax.axis_index("gy")
    parity_x, parity_y = index_x % 2, index_y % 2
    place = jnp.stack([index_x * rows, index_y * cols, parity_x, parity_y]).astype(jnp.int32)

    def swap(axis, size, first, value):
        def partner(x, y):
            at = x if axis == "gx" else y
            other = at + 1 if (at - first) % 2 == 0 else at - 1
            if not 0 <= other < size:
                return (x, y ^ 1) if axis == "gx" else (x ^ 1, y)
            return (other, y) if axis == "gx" else (x, other)

        pairs = [
            (x * size_y + y, partner(x, y)[0] * size_y + partner(x, y)[1])
            for x in range(size_x)
            for y in range(size_y)
        ]
        return lax.ppermute(value, ("gx", "gy"), pairs)

    assert size_x % 2 == 0 and size_y % 2 == 0

    def swaps(axis, size, parity, initial, last):
        if initial is last:
            return swap(axis, size, 0, last), swap(axis, size, 1, last)
        is_even = parity == 0
        return (
            swap(axis, size, 0, jnp.where(is_even, last, initial)),
            swap(axis, size, 1, jnp.where(is_even, initial, last)),
        )

    if rows == REACH:
        even_x, odd_x = swaps("gx", size_x, parity_x, density, density)
    else:
        even_x, odd_x = swaps("gx", size_x, parity_x, density[:, :REACH], density[:, rows - REACH :])

    even_y, odd_y = swaps("gy", size_y, parity_y, density[:, :, :2], density[:, :, cols - 2 :])

    even_x, even_y, odd_y = lax.optimization_barrier((even_x, even_y, odd_y))

    def corners(first):
        even, odd = even_y[:, first : first + HALF], odd_y[:, first : first + HALF]
        left = jnp.where(parity_y == 0, odd, even)[:, :, 1:]
        right = jnp.where(parity_y == 0, even, odd)[:, :, :1]
        return jnp.concatenate([left, right], axis=2)

    even_corners, odd_corners = swaps("gx", size_x, parity_x, corners(0), corners(rows - HALF))

    vmem = pl.BlockSpec(memory_space=pltpu.VMEM)
    smem = pl.BlockSpec(memory_space=pltpu.SMEM)
    block = jax.ShapeDtypeStruct(density.shape, jnp.float32)
    image_one, image_two, message = pl.pallas_call(
        functools.partial(images_kernel, (size_x * rows, size_y * cols)),
        out_shape=[block, block, jax.ShapeDtypeStruct((devices, 128), jnp.float32)],
        in_specs=[smem, smem] + [vmem] * 7,
        out_specs=[vmem, vmem, vmem],
        scratch_shapes=[
            pltpu.VMEM((members, rows + 2 * REACH, cols + 2 * GAP, depth), jnp.float32),
            pltpu.VMEM((members, rows + 2 * HALF, cols + 2 * GAP, depth), jnp.float32),
            pltpu.VMEM((128, depth), jnp.float32),
        ],
        compiler_params=pltpu.CompilerParams(vmem_limit_bytes=8 * 2**20),
        name="images",
    )(place, rate_table, density, even_x, odd_x, even_y, odd_y, even_corners, odd_corners)

    gathered = lax.all_to_all(message, ("gx", "gy"), 0, 0, tiled=True)

    return pl.pallas_call(
        combine_kernel,
        out_shape=[block, jax.ShapeDtypeStruct((members, 5), jnp.float32)],
        in_specs=[vmem] * 4,
        out_specs=[vmem, vmem],
        compiler_params=pltpu.CompilerParams(vmem_limit_bytes=8 * 2**20),
        name="combine",
    )(gathered, density, image_one, image_two)


def solution(mesh):
    in_specs = (P(None, "gx", "gy", None), P())
    out_specs = (P(None, "gx", "gy", None), P())
    return jax.shard_map(shards, mesh=mesh, in_specs=in_specs, out_specs=out_specs, check_vma=False)
```

```python
import functools

import jax
import jax.numpy as jnp
from jax import lax
from jax.experimental import pallas as pl
from jax.experimental.pallas import tpu as pltpu
from jax.sharding import PartitionSpec as P

tau_step = 0.01
taylor_terms = 16
squarings = 4
REACH = 4
HALF = 2
GAP = 8


def own_lane(first):
    row = lax.broadcasted_iota(jnp.int32, (8, 128), 0)
    return lax.broadcasted_iota(jnp.int32, (8, 128), 1) == first + row


def images_kernel(
    lattice,
    rates,
    field,
    even_x,
    odd_x,
    even_y,
    odd_y,
    even_corners,
    odd_corners,
    image_one,
    image_two,
    message,
    wide,
    wide_image,
    parts,
):
    members, rows, cols, depth = field.shape
    span = cols + 2 * GAP
    index_i, index_j = lax.axis_index("gx"), lax.axis_index("gy")
    first_i, first_j = index_i * rows, index_j * cols
    even_i, even_j = index_i % 2 == 0, index_j % 2 == 0
    count_i, count_j = lattice

    ends_i, ends_j = first_i + rows < count_i, first_j + cols < count_j

    def sides(even, odd, is_even, lower_inside, higher_inside):
        lower, higher = jnp.where(is_even, odd, even), jnp.where(is_even, even, odd)
        return jnp.where(lower_inside, lower, 0.0), jnp.where(higher_inside, higher, 0.0)

    wide[:, REACH : REACH + rows, GAP : GAP + cols] = field[...]
    above, below = sides(even_x[...], odd_x[...], even_i, first_i > 0, ends_i)
    wide[:, :REACH, GAP : GAP + cols] = above
    wide[:, REACH + rows :, GAP : GAP + cols] = below
    left, right = sides(even_y[...], odd_y[...], even_j, first_j > 0, ends_j)
    wide[:, REACH : REACH + rows, GAP - 2 : GAP] = left
    wide[:, REACH : REACH + rows, GAP + cols : GAP + cols + 2] = right
    upper, lower = sides(even_corners[...], odd_corners[...], even_i, first_i > 0, ends_i)
    for corners, at in ((upper, REACH - HALF), (lower, REACH + rows)):
        wide[:, at : at + HALF, GAP - 1 : GAP] = jnp.where(first_j > 0, corners[:, :, :1], 0.0)
        wide[:, at : at + HALF, GAP + cols : GAP + cols + 1] = jnp.where(ends_j, corners[:, :, 1:], 0.0)

    lane = lax.broadcasted_iota(jnp.int32, (1, depth), 1)
    amount_k = lane.astype(jnp.float32)
    above_k = jnp.where(lane < depth - 1, amount_k + 1.0, 0.0)
    inner_k = jnp.where(lane > 0, 1.0, 0.0)
    sublane = lax.broadcasted_iota(jnp.int32, (span, 1), 0)
    amount_j = (first_j - GAP + sublane).astype(jnp.float32)

    for member in range(members):
        c = [jnp.broadcast_to(rates[member : member + 1, r : r + 1], (1, depth)) for r in range(9)]
        ratio_j = amount_j / c[7]
        ratio_k = amount_k / c[8]
        make_u = c[0] / (1.0 + ratio_j * ratio_j)
        make_v = c[2] / (1.0 + ratio_k * ratio_k)
        lose_v = c[3] * (amount_j + 1.0)
        rest = make_u + make_v + (c[3] * amount_j + (c[5] + c[6]) * amount_k)

        def apply(read, row, start, size):
            i = (first_i + row).astype(jnp.float32)
            cut = slice(GAP + start, GAP + start + size)
            centre = read(row, start, size)
            value = make_u[cut] * read(row - 1, start, size)
            value = value + (c[1] * (i + 1.0)) * read(row + 1, start, size)
            value = value + make_v * read(row, start - 1, size)
            value = value + lose_v[cut] * read(row, start + 1, size)
            pair = (0.5 * c[4] * (i + 2.0) * (i + 1.0)) * read(row + 2, start, size)
            value = value + inner_k * pltpu.roll(pair, 1, 1)
            split = c[5] * read(row - 2, start, size) + c[6] * centre
            value = value + above_k * pltpu.roll(split, depth - 1, 1)
            out = rest[cut] + (c[1] * i + 0.5 * c[4] * i * (i - 1.0))
            return value - out * centre

        def read_field(row, start, size):
            return wide[member, row + REACH, pl.ds(GAP + start, size), :]

        def read_image(row, start, size):
            return wide_image[member, row + HALF, pl.ds(GAP + start, size), :]

        for row in range(-HALF, rows + HALF):
            inside = (first_i + row >= 0) & (first_i + row < count_i)
            value = apply(read_field, row, 0, cols)
            if row < 0 or row >= rows:
                value = jnp.where(inside, value, 0.0)
            else:
                image_one[member, row] = value
            wide_image[member, row + HALF, GAP : GAP + cols] = value
            if 0 <= row < rows:
                value = apply(read_field, row, -1, 1)
                wide_image[member, row + HALF, GAP - 1 : GAP] = jnp.where(first_j > 0, value, 0.0)
                value = apply(read_field, row, cols, 1)
                wide_image[member, row + HALF, GAP + cols : GAP + cols + 1] = jnp.where(
                    first_j + cols < count_j, value, 0.0
                )

        products = [jnp.zeros((cols, depth), jnp.float32) for _ in range(6)]
        for row in range(rows):
            zero = field[member, row]
            one = image_one[member, row]
            two = apply(read_image, row, 0, cols)
            image_two[member, row] = two
            terms = (zero * zero, zero * one, zero * two, one * one, one * two, two * two)
            products = [total + term for total, term in zip(products, terms)]
        for index, total in enumerate(products):
            parts[8 * index + member : 8 * index + member + 1, :] = jnp.sum(total, axis=0, keepdims=True)

    for index in range(6):
        parts[8 * index + members : 8 * index + 8, :] = jnp.zeros((8 - members, depth), jnp.float32)
    row = jnp.zeros((8, depth), jnp.float32)
    for index in range(6):
        total = jnp.sum(parts[8 * index : 8 * index + 8], axis=1, keepdims=True)
        row = row + jnp.where(own_lane(8 * index), total, 0.0)
    message[...] = jnp.broadcast_to(jnp.sum(row, axis=0, keepdims=True), message.shape)


def first_column(h00, s01, h11):
    scale = tau_step / 2.0**squarings
    a, b, d = scale * h00, scale * s01, scale * h11
    c = scale
    zero, one = jnp.zeros_like(a), jnp.ones_like(a)
    p00, p01, p10, p11, q0, q1 = one, zero, zero, one, zero, zero
    for term in range(taylor_terms, 0, -1):
        inverse = 1.0 / term
        p00, p01, p10, p11, q0, q1 = (
            1.0 + (a * p00 + b * p10) * inverse,
            (a * p01 + b * p11) * inverse,
            (c * p00 + d * p10) * inverse,
            1.0 + (c * p01 + d * p11) * inverse,
            p10 * (c * inverse),
            p11 * (c * inverse),
        )
    for _ in range(squarings):
        p00, p01, p10, p11, q0, q1 = (
            p00 * p00 + p01 * p10,
            p00 * p01 + p01 * p11,
            p10 * p00 + p11 * p10,
            p10 * p01 + p11 * p11,
            q0 * p00 + q1 * p10 + q0,
            q0 * p01 + q1 * p11 + q1,
        )
    return p00, p10, q0


def combine_kernel(gathered, field, image_one, image_two, propagated, entries):
    members, rows, cols, depth = field.shape
    sums = jnp.broadcast_to(jnp.sum(gathered[...], axis=0, keepdims=True), (8, 128))
    g00, g01, g02, g11, g12, g22 = [
        jnp.broadcast_to(jnp.sum(jnp.where(own_lane(8 * index), sums, 0.0), axis=1, keepdims=True), (8, 128))
        for index in range(6)
    ]
    tiny = jnp.finfo(jnp.float32).tiny
    h00 = g01 / g00
    square_10 = jnp.maximum(g11 / g00 - h00 * h00, tiny)
    s01 = (g02 - h00 * g01) / g00
    h11 = ((g12 - h00 * g02) - h00 * (g11 - h00 * g01)) / (g00 * square_10)
    norm_2 = ((g22 - h00 * g12) - h00 * (g12 - h00 * g11)) / (g00 * square_10)
    h10 = jnp.sqrt(square_10)
    h01 = s01 / h10
    h21 = jnp.sqrt(jnp.maximum(norm_2 - h01 * h01 - h11 * h11, 0.0))
    e0, e1, e2 = first_column(h00, s01, h11)
    a2 = e2
    a1 = e1 - e2 * (h00 + h11)
    a0 = e0 - e1 * h00 - e2 * (s01 - h11 * h00)
    lane = lax.broadcasted_iota(jnp.int32, h00.shape, 1)
    table = h21
    for index, entry in enumerate((h00, h10, h01, h11)):
        table = jnp.where(lane == index, entry, table)
    entries[...] = (tau_step * table)[: entries.shape[0], : entries.shape[1]]
    for member in range(members):
        b0, b1, b2 = [jnp.broadcast_to(a[member : member + 1], (cols, depth)) for a in (a0, a1, a2)]
        for row in range(rows):
            propagated[member, row] = (
                b0 * field[member, row] + b1 * image_one[member, row] + b2 * image_two[member, row]
            )


def shards(density, rate_table):
    members, rows, cols, depth = density.shape
    size_x, size_y = lax.axis_size("gx"), lax.axis_size("gy")
    devices = size_x * size_y
    parity_x, parity_y = lax.axis_index("gx") % 2, lax.axis_index("gy") % 2

    def swap(axis, size, first, value):
        def partner(x, y):
            at = x if axis == "gx" else y
            other = at + 1 if (at - first) % 2 == 0 else at - 1
            if not 0 <= other < size:
                return (x, y ^ 1) if axis == "gx" else (x ^ 1, y)
            return (other, y) if axis == "gx" else (x, other)

        pairs = [
            (x * size_y + y, partner(x, y)[0] * size_y + partner(x, y)[1])
            for x in range(size_x)
            for y in range(size_y)
        ]
        return lax.ppermute(value, ("gx", "gy"), pairs)

    assert size_x % 2 == 0 and size_y % 2 == 0

    def swaps(axis, size, parity, initial, last):
        if initial is last:
            return swap(axis, size, 0, last), swap(axis, size, 1, last)
        is_even = parity == 0
        return (
            swap(axis, size, 0, jnp.where(is_even, last, initial)),
            swap(axis, size, 1, jnp.where(is_even, initial, last)),
        )

    if rows == REACH:
        even_x, odd_x = swaps("gx", size_x, parity_x, density, density)
    else:
        even_x, odd_x = swaps("gx", size_x, parity_x, density[:, :REACH], density[:, rows - REACH :])

    even_y, odd_y = swaps("gy", size_y, parity_y, density[:, :, :2], density[:, :, cols - 2 :])

    even_x, even_y, odd_y = lax.optimization_barrier((even_x, even_y, odd_y))

    def corners(first):
        even, odd = even_y[:, first : first + HALF], odd_y[:, first : first + HALF]
        left = jnp.where(parity_y == 0, odd, even)[:, :, 1:]
        right = jnp.where(parity_y == 0, even, odd)[:, :, :1]
        return jnp.concatenate([left, right], axis=2)

    even_corners, odd_corners = swaps("gx", size_x, parity_x, corners(0), corners(rows - HALF))

    vmem = pl.BlockSpec(memory_space=pltpu.VMEM)
    block = jax.ShapeDtypeStruct(density.shape, jnp.float32)
    image_one, image_two, message = pl.pallas_call(
        functools.partial(images_kernel, (size_x * rows, size_y * cols)),
        out_shape=[block, block, jax.ShapeDtypeStruct((devices, 128), jnp.float32)],
        in_specs=[vmem] * 8,
        out_specs=[vmem, vmem, vmem],
        scratch_shapes=[
            pltpu.VMEM((members, rows + 2 * REACH, cols + 2 * GAP, depth), jnp.float32),
            pltpu.VMEM((members, rows + 2 * HALF, cols + 2 * GAP, depth), jnp.float32),
            pltpu.VMEM((48, depth), jnp.float32),
        ],
        compiler_params=pltpu.CompilerParams(vmem_limit_bytes=8 * 2**20),
        name="images",
    )(rate_table, density, even_x, odd_x, even_y, odd_y, even_corners, odd_corners)

    gathered = lax.all_to_all(message, ("gx", "gy"), 0, 0, tiled=True)

    return pl.pallas_call(
        combine_kernel,
        out_shape=[block, jax.ShapeDtypeStruct((members, 5), jnp.float32)],
        in_specs=[vmem] * 4,
        out_specs=[vmem, vmem],
        compiler_params=pltpu.CompilerParams(vmem_limit_bytes=8 * 2**20),
        name="combine",
    )(gathered, density, image_one, image_two)


def solution(mesh):
    in_specs = (P(None, "gx", "gy", None), P())
    out_specs = (P(None, "gx", "gy", None), P())
    return jax.shard_map(shards, mesh=mesh, in_specs=in_specs, out_specs=out_specs, check_vma=False)
```

```python
import functools

import jax
import jax.numpy as jnp
from jax import lax
from jax.experimental import pallas as pl
from jax.experimental.pallas import tpu as pltpu
from jax.sharding import PartitionSpec as P

tau_step = 0.01
taylor_terms = 16
squarings = 4
REACH = 4
HALF = 2
GAP = 8


def own_lane(first):
    row = lax.broadcasted_iota(jnp.int32, (8, 128), 0)
    return lax.broadcasted_iota(jnp.int32, (8, 128), 1) == first + row


def images_kernel(
    lattice,
    rates,
    field,
    even_x,
    odd_x,
    even_y,
    odd_y,
    even_corners,
    odd_corners,
    image_one,
    image_two,
    message,
    wide,
    wide_image,
    parts,
):
    members, rows, cols, depth = field.shape
    span = cols + 2 * GAP
    index_i, index_j = lax.axis_index("gx"), lax.axis_index("gy")
    first_i, first_j = index_i * rows, index_j * cols
    even_i, even_j = index_i % 2 == 0, index_j % 2 == 0
    count_i, count_j = lattice

    ends_i, ends_j = first_i + rows < count_i, first_j + cols < count_j

    def sides(even, odd, is_even, lower_inside, higher_inside):
        lower, higher = jnp.where(is_even, odd, even), jnp.where(is_even, even, odd)
        return jnp.where(lower_inside, lower, 0.0), jnp.where(higher_inside, higher, 0.0)

    wide[:, REACH : REACH + rows, GAP : GAP + cols] = field[...]
    above, below = sides(even_x[...], odd_x[...], even_i, first_i > 0, ends_i)
    wide[:, :REACH, GAP : GAP + cols] = above
    wide[:, REACH + rows :, GAP : GAP + cols] = below
    left, right = sides(even_y[...], odd_y[...], even_j, first_j > 0, ends_j)
    wide[:, REACH : REACH + rows, GAP - 2 : GAP] = left
    wide[:, REACH : REACH + rows, GAP + cols : GAP + cols + 2] = right
    upper, lower = sides(even_corners[...], odd_corners[...], even_i, first_i > 0, ends_i)
    for corners, at in ((upper, REACH - HALF), (lower, REACH + rows)):
        wide[:, at : at + HALF, GAP - 1 : GAP] = jnp.where(first_j > 0, corners[:, :, :1], 0.0)
        wide[:, at : at + HALF, GAP + cols : GAP + cols + 1] = jnp.where(ends_j, corners[:, :, 1:], 0.0)

    lane = lax.broadcasted_iota(jnp.int32, (1, depth), 1)
    amount_k = lane.astype(jnp.float32)
    above_k = jnp.where(lane < depth - 1, amount_k + 1.0, 0.0)
    inner_k = jnp.where(lane > 0, 1.0, 0.0)
    sublane = lax.broadcasted_iota(jnp.int32, (span, 1), 0)
    amount_j = (first_j - GAP + sublane).astype(jnp.float32)

    for member in range(members):
        c = [jnp.broadcast_to(rates[member : member + 1, r : r + 1], (1, depth)) for r in range(9)]
        ratio_j = amount_j / c[7]
        ratio_k = amount_k / c[8]
        make_u = c[0] / (1.0 + ratio_j * ratio_j)
        make_v = c[2] / (1.0 + ratio_k * ratio_k)
        lose_v = c[3] * (amount_j + 1.0)
        rest = make_u + make_v + (c[3] * amount_j + (c[5] + c[6]) * amount_k)

        def apply(read, row, start, size):
            i = (first_i + row).astype(jnp.float32)
            cut = slice(GAP + start, GAP + start + size)
            centre = read(row, start, size)
            value = make_u[cut] * read(row - 1, start, size)
            value = value + (c[1] * (i + 1.0)) * read(row + 1, start, size)
            value = value + make_v * read(row, start - 1, size)
            value = value + lose_v[cut] * read(row, start + 1, size)
            pair = (0.5 * c[4] * (i + 2.0) * (i + 1.0)) * read(row + 2, start, size)
            value = value + inner_k * pltpu.roll(pair, 1, 1)
            split = c[5] * read(row - 2, start, size) + c[6] * centre
            value = value + above_k * pltpu.roll(split, depth - 1, 1)
            out = rest[cut] + (c[1] * i + 0.5 * c[4] * i * (i - 1.0))
            return value - out * centre

        def read_field(row, start, size):
            return wide[member, row + REACH, pl.ds(GAP + start, size), :]

        def read_image(row, start, size):
            return wide_image[member, row + HALF, pl.ds(GAP + start, size), :]

        for row in range(-HALF, rows + HALF):
            inside = (first_i + row >= 0) & (first_i + row < count_i)
            value = apply(read_field, row, 0, cols)
            if row < 0 or row >= rows:
                value = jnp.where(inside, value, 0.0)
            else:
                image_one[member, row] = value
            wide_image[member, row + HALF, GAP : GAP + cols] = value
            if 0 <= row < rows:
                value = apply(read_field, row, -1, 1)
                wide_image[member, row + HALF, GAP - 1 : GAP] = jnp.where(first_j > 0, value, 0.0)
                value = apply(read_field, row, cols, 1)
                wide_image[member, row + HALF, GAP + cols : GAP + cols + 1] = jnp.where(
                    first_j + cols < count_j, value, 0.0
                )

        products = [jnp.zeros((cols, depth), jnp.float32) for _ in range(6)]
        for row in range(rows):
            zero = field[member, row]
            one = image_one[member, row]
            two = apply(read_image, row, 0, cols)
            image_two[member, row] = two
            terms = (zero * zero, zero * one, zero * two, one * one, one * two, two * two)
            products = [total + term for total, term in zip(products, terms)]
        for index, total in enumerate(products):
            parts[8 * index + member : 8 * index + member + 1, :] = jnp.sum(total, axis=0, keepdims=True)

    for index in range(6):
        parts[8 * index + members : 8 * index + 8, :] = jnp.zeros((8 - members, depth), jnp.float32)
    row = jnp.zeros((8, depth), jnp.float32)
    for index in range(6):
        total = jnp.sum(parts[8 * index : 8 * index + 8], axis=1, keepdims=True)
        row = row + jnp.where(own_lane(8 * index), total, 0.0)
    message[...] = jnp.broadcast_to(jnp.sum(row, axis=0, keepdims=True), message.shape)


def first_column(h00, s01, h11):
    scale = tau_step / 2.0**squarings
    a, b, d = scale * h00, scale * s01, scale * h11
    c = scale
    zero, one = jnp.zeros_like(a), jnp.ones_like(a)
    p00, p01, p10, p11, q0, q1 = one, zero, zero, one, zero, zero
    for term in range(taylor_terms, 0, -1):
        inverse = 1.0 / term
        p00, p01, p10, p11, q0, q1 = (
            1.0 + (a * p00 + b * p10) * inverse,
            (a * p01 + b * p11) * inverse,
            (c * p00 + d * p10) * inverse,
            1.0 + (c * p01 + d * p11) * inverse,
            p10 * (c * inverse),
            p11 * (c * inverse),
        )
    for _ in range(squarings):
        p00, p01, p10, p11, q0, q1 = (
            p00 * p00 + p01 * p10,
            p00 * p01 + p01 * p11,
            p10 * p00 + p11 * p10,
            p10 * p01 + p11 * p11,
            q0 * p00 + q1 * p10 + q0,
            q0 * p01 + q1 * p11 + q1,
        )
    return p00, p10, q0


def combine_kernel(gathered, field, image_one, image_two, propagated, entries):
    members, rows, cols, depth = field.shape
    sums = jnp.broadcast_to(jnp.sum(gathered[...], axis=0, keepdims=True), (8, 128))
    g00, g01, g02, g11, g12, g22 = [
        jnp.broadcast_to(jnp.sum(jnp.where(own_lane(8 * index), sums, 0.0), axis=1, keepdims=True), (8, 128))
        for index in range(6)
    ]
    tiny = jnp.finfo(jnp.float32).tiny
    h00 = g01 / g00
    square_10 = jnp.maximum(g11 / g00 - h00 * h00, tiny)
    s01 = (g02 - h00 * g01) / g00
    h11 = ((g12 - h00 * g02) - h00 * (g11 - h00 * g01)) / (g00 * square_10)
    norm_2 = ((g22 - h00 * g12) - h00 * (g12 - h00 * g11)) / (g00 * square_10)
    h10 = jnp.sqrt(square_10)
    h01 = s01 / h10
    h21 = jnp.sqrt(jnp.maximum(norm_2 - h01 * h01 - h11 * h11, 0.0))
    e0, e1, e2 = first_column(h00, s01, h11)
    a2 = e2
    a1 = e1 - e2 * (h00 + h11)
    a0 = e0 - e1 * h00 - e2 * (s01 - h11 * h00)
    lane = lax.broadcasted_iota(jnp.int32, h00.shape, 1)
    table = h21
    for index, entry in enumerate((h00, h10, h01, h11)):
        table = jnp.where(lane == index, entry, table)
    entries[...] = (tau_step * table)[: entries.shape[0], : entries.shape[1]]
    for member in range(members):
        b0, b1, b2 = [jnp.broadcast_to(a[member : member + 1], (cols, depth)) for a in (a0, a1, a2)]
        for row in range(rows):
            propagated[member, row] = (
                b0 * field[member, row] + b1 * image_one[member, row] + b2 * image_two[member, row]
            )


def shards(density, rate_table):
    members, rows, cols, depth = density.shape
    size_x, size_y = lax.axis_size("gx"), lax.axis_size("gy")
    devices = size_x * size_y
    parity_x, parity_y = lax.axis_index("gx") % 2, lax.axis_index("gy") % 2

    def swap(axis, size, first, value):
        spare = 2 if size_x % 4 == 0 else 1

        def partner(x, y):
            at = x if axis == "gx" else y
            other = at + 1 if (at - first) % 2 == 0 else at - 1
            if not 0 <= other < size:
                return (x, y ^ 1) if axis == "gx" else (x ^ spare, y)
            return (other, y) if axis == "gx" else (x, other)

        pairs = [
            (x * size_y + y, partner(x, y)[0] * size_y + partner(x, y)[1])
            for x in range(size_x)
            for y in range(size_y)
        ]
        return lax.ppermute(value, ("gx", "gy"), pairs)

    assert size_x % 2 == 0 and size_y % 2 == 0

    def swaps(axis, size, parity, initial, last):
        if initial is last:
            return swap(axis, size, 0, last), swap(axis, size, 1, last)
        is_even = parity == 0
        return (
            swap(axis, size, 0, jnp.where(is_even, last, initial)),
            swap(axis, size, 1, jnp.where(is_even, initial, last)),
        )

    if rows == REACH:
        even_x, odd_x = swaps("gx", size_x, parity_x, density, density)
    else:
        even_x, odd_x = swaps("gx", size_x, parity_x, density[:, :REACH], density[:, rows - REACH :])

    even_y, odd_y = swaps("gy", size_y, parity_y, density[:, :, :2], density[:, :, cols - 2 :])

    even_x, even_y, odd_y = lax.optimization_barrier((even_x, even_y, odd_y))

    def corners(first):
        even, odd = even_y[:, first : first + HALF], odd_y[:, first : first + HALF]
        left = jnp.where(parity_y == 0, odd, even)[:, :, 1:]
        right = jnp.where(parity_y == 0, even, odd)[:, :, :1]
        return jnp.concatenate([left, right], axis=2)

    even_corners, odd_corners = swaps("gx", size_x, parity_x, corners(0), corners(rows - HALF))

    vmem = pl.BlockSpec(memory_space=pltpu.VMEM)
    block = jax.ShapeDtypeStruct(density.shape, jnp.float32)
    image_one, image_two, message = pl.pallas_call(
        functools.partial(images_kernel, (size_x * rows, size_y * cols)),
        out_shape=[block, block, jax.ShapeDtypeStruct((devices, 128), jnp.float32)],
        in_specs=[vmem] * 8,
        out_specs=[vmem, vmem, vmem],
        scratch_shapes=[
            pltpu.VMEM((members, rows + 2 * REACH, cols + 2 * GAP, depth), jnp.float32),
            pltpu.VMEM((members, rows + 2 * HALF, cols + 2 * GAP, depth), jnp.float32),
            pltpu.VMEM((48, depth), jnp.float32),
        ],
        compiler_params=pltpu.CompilerParams(vmem_limit_bytes=8 * 2**20),
        name="images",
    )(rate_table, density, even_x, odd_x, even_y, odd_y, even_corners, odd_corners)

    gathered = lax.all_to_all(message, ("gx", "gy"), 0, 0, tiled=True)

    return pl.pallas_call(
        combine_kernel,
        out_shape=[block, jax.ShapeDtypeStruct((members, 5), jnp.float32)],
        in_specs=[vmem] * 4,
        out_specs=[vmem, vmem],
        compiler_params=pltpu.CompilerParams(vmem_limit_bytes=8 * 2**20),
        name="combine",
    )(gathered, density, image_one, image_two)


def solution(mesh):
    in_specs = (P(None, "gx", "gy", None), P())
    out_specs = (P(None, "gx", "gy", None), P())
    return jax.shard_map(shards, mesh=mesh, in_specs=in_specs, out_specs=out_specs, check_vma=False)
```

```python
import functools

import jax
import jax.numpy as jnp
from jax import lax
from jax.experimental import pallas as pl
from jax.experimental.pallas import tpu as pltpu
from jax.sharding import PartitionSpec as P

tau_step = 0.01
taylor_terms = 16
squarings = 4
REACH = 4
HALF = 2
GAP = 8


def own_lane(first):
    row = lax.broadcasted_iota(jnp.int32, (8, 128), 0)
    return lax.broadcasted_iota(jnp.int32, (8, 128), 1) == first + row


def images_kernel(
    lattice,
    rates,
    field,
    even_x,
    odd_x,
    even_y,
    odd_y,
    image_one,
    image_two,
    message,
    wide,
    wide_image,
    parts,
):
    members, rows, cols, depth = field.shape
    span = cols + 2 * GAP
    index_i, index_j = lax.axis_index("gx"), lax.axis_index("gy")
    first_i, first_j = index_i * rows, index_j * cols
    even_i, even_j = index_i % 2 == 0, index_j % 2 == 0
    count_i, count_j = lattice

    ends_i, ends_j = first_i + rows < count_i, first_j + cols < count_j

    def sides(even, odd, is_even, lower_inside, higher_inside):
        lower, higher = jnp.where(is_even, odd, even), jnp.where(is_even, even, odd)
        return jnp.where(lower_inside, lower, 0.0), jnp.where(higher_inside, higher, 0.0)

    wide[:, REACH : REACH + rows, GAP : GAP + cols] = field[...]
    above, below = sides(even_x[...], odd_x[...], even_i, first_i > 0, ends_i)
    wide[:, :REACH, GAP : GAP + cols] = above
    wide[:, REACH + rows :, GAP : GAP + cols] = below
    left, right = sides(even_y[...], odd_y[...], even_j, first_j > 0, ends_j)
    end = REACH + rows
    for columns, at in ((left, GAP - 2), (right, GAP + cols)):
        wide[:, HALF:REACH, at : at + 2] = jnp.where(first_i > 0, columns[:, :HALF], 0.0)
        wide[:, REACH:end, at : at + 2] = columns[:, HALF : HALF + rows]
        wide[:, end : end + HALF, at : at + 2] = jnp.where(ends_i, columns[:, HALF + rows :], 0.0)

    lane = lax.broadcasted_iota(jnp.int32, (1, depth), 1)
    amount_k = lane.astype(jnp.float32)
    above_k = jnp.where(lane < depth - 1, amount_k + 1.0, 0.0)
    inner_k = jnp.where(lane > 0, 1.0, 0.0)
    sublane = lax.broadcasted_iota(jnp.int32, (span, 1), 0)
    amount_j = (first_j - GAP + sublane).astype(jnp.float32)

    for member in range(members):
        c = [jnp.broadcast_to(rates[member : member + 1, r : r + 1], (1, depth)) for r in range(9)]
        ratio_j = amount_j / c[7]
        ratio_k = amount_k / c[8]
        make_u = c[0] / (1.0 + ratio_j * ratio_j)
        make_v = c[2] / (1.0 + ratio_k * ratio_k)
        lose_v = c[3] * (amount_j + 1.0)
        rest = make_u + make_v + (c[3] * amount_j + (c[5] + c[6]) * amount_k)

        def apply(read, row, start, size):
            i = (first_i + row).astype(jnp.float32)
            cut = slice(GAP + start, GAP + start + size)
            centre = read(row, start, size)
            value = make_u[cut] * read(row - 1, start, size)
            value = value + (c[1] * (i + 1.0)) * read(row + 1, start, size)
            value = value + make_v * read(row, start - 1, size)
            value = value + lose_v[cut] * read(row, start + 1, size)
            pair = (0.5 * c[4] * (i + 2.0) * (i + 1.0)) * read(row + 2, start, size)
            value = value + inner_k * pltpu.roll(pair, 1, 1)
            split = c[5] * read(row - 2, start, size) + c[6] * centre
            value = value + above_k * pltpu.roll(split, depth - 1, 1)
            out = rest[cut] + (c[1] * i + 0.5 * c[4] * i * (i - 1.0))
            return value - out * centre

        def read_field(row, start, size):
            return wide[member, row + REACH, pl.ds(GAP + start, size), :]

        def read_image(row, start, size):
            return wide_image[member, row + HALF, pl.ds(GAP + start, size), :]

        for row in range(-HALF, rows + HALF):
            inside = (first_i + row >= 0) & (first_i + row < count_i)
            value = apply(read_field, row, 0, cols)
            if row < 0 or row >= rows:
                value = jnp.where(inside, value, 0.0)
            else:
                image_one[member, row] = value
            wide_image[member, row + HALF, GAP : GAP + cols] = value
            if 0 <= row < rows:
                value = apply(read_field, row, -1, 1)
                wide_image[member, row + HALF, GAP - 1 : GAP] = jnp.where(first_j > 0, value, 0.0)
                value = apply(read_field, row, cols, 1)
                wide_image[member, row + HALF, GAP + cols : GAP + cols + 1] = jnp.where(
                    first_j + cols < count_j, value, 0.0
                )

        products = [jnp.zeros((cols, depth), jnp.float32) for _ in range(6)]
        for row in range(rows):
            zero = field[member, row]
            one = image_one[member, row]
            two = apply(read_image, row, 0, cols)
            image_two[member, row] = two
            terms = (zero * zero, zero * one, zero * two, one * one, one * two, two * two)
            products = [total + term for total, term in zip(products, terms)]
        for index, total in enumerate(products):
            parts[8 * index + member : 8 * index + member + 1, :] = jnp.sum(total, axis=0, keepdims=True)

    for index in range(6):
        parts[8 * index + members : 8 * index + 8, :] = jnp.zeros((8 - members, depth), jnp.float32)
    row = jnp.zeros((8, depth), jnp.float32)
    for index in range(6):
        total = jnp.sum(parts[8 * index : 8 * index + 8], axis=1, keepdims=True)
        row = row + jnp.where(own_lane(8 * index), total, 0.0)
    message[...] = jnp.broadcast_to(jnp.sum(row, axis=0, keepdims=True), message.shape)


def first_column(h00, s01, h11):
    scale = tau_step / 2.0**squarings
    a, b, d = scale * h00, scale * s01, scale * h11
    c = scale
    zero, one = jnp.zeros_like(a), jnp.ones_like(a)
    p00, p01, p10, p11, q0, q1 = one, zero, zero, one, zero, zero
    for term in range(taylor_terms, 0, -1):
        inverse = 1.0 / term
        p00, p01, p10, p11, q0, q1 = (
            1.0 + (a * p00 + b * p10) * inverse,
            (a * p01 + b * p11) * inverse,
            (c * p00 + d * p10) * inverse,
            1.0 + (c * p01 + d * p11) * inverse,
            p10 * (c * inverse),
            p11 * (c * inverse),
        )
    for _ in range(squarings):
        p00, p01, p10, p11, q0, q1 = (
            p00 * p00 + p01 * p10,
            p00 * p01 + p01 * p11,
            p10 * p00 + p11 * p10,
            p10 * p01 + p11 * p11,
            q0 * p00 + q1 * p10 + q0,
            q0 * p01 + q1 * p11 + q1,
        )
    return p00, p10, q0


def combine_kernel(gathered, field, image_one, image_two, propagated, entries):
    members, rows, cols, depth = field.shape
    sums = jnp.broadcast_to(jnp.sum(gathered[...], axis=0, keepdims=True), (8, 128))
    g00, g01, g02, g11, g12, g22 = [
        jnp.broadcast_to(jnp.sum(jnp.where(own_lane(8 * index), sums, 0.0), axis=1, keepdims=True), (8, 128))
        for index in range(6)
    ]
    tiny = jnp.finfo(jnp.float32).tiny
    h00 = g01 / g00
    square_10 = jnp.maximum(g11 / g00 - h00 * h00, tiny)
    s01 = (g02 - h00 * g01) / g00
    h11 = ((g12 - h00 * g02) - h00 * (g11 - h00 * g01)) / (g00 * square_10)
    norm_2 = ((g22 - h00 * g12) - h00 * (g12 - h00 * g11)) / (g00 * square_10)
    h10 = jnp.sqrt(square_10)
    h01 = s01 / h10
    h21 = jnp.sqrt(jnp.maximum(norm_2 - h01 * h01 - h11 * h11, 0.0))
    e0, e1, e2 = first_column(h00, s01, h11)
    a2 = e2
    a1 = e1 - e2 * (h00 + h11)
    a0 = e0 - e1 * h00 - e2 * (s01 - h11 * h00)
    lane = lax.broadcasted_iota(jnp.int32, h00.shape, 1)
    table = h21
    for index, entry in enumerate((h00, h10, h01, h11)):
        table = jnp.where(lane == index, entry, table)
    entries[...] = (tau_step * table)[: entries.shape[0], : entries.shape[1]]
    for member in range(members):
        b0, b1, b2 = [jnp.broadcast_to(a[member : member + 1], (cols, depth)) for a in (a0, a1, a2)]
        for row in range(rows):
            propagated[member, row] = (
                b0 * field[member, row] + b1 * image_one[member, row] + b2 * image_two[member, row]
            )


def shards(density, rate_table):
    members, rows, cols, depth = density.shape
    size_x, size_y = lax.axis_size("gx"), lax.axis_size("gy")
    devices = size_x * size_y
    parity_x, parity_y = lax.axis_index("gx") % 2, lax.axis_index("gy") % 2

    def swap(axis, size, first, value):
        def partner(x, y):
            at = x if axis == "gx" else y
            other = at + 1 if (at - first) % 2 == 0 else at - 1
            if not 0 <= other < size:
                return (x, y ^ 1) if axis == "gx" else (x ^ 1, y)
            return (other, y) if axis == "gx" else (x, other)

        pairs = [
            (x * size_y + y, partner(x, y)[0] * size_y + partner(x, y)[1])
            for x in range(size_x)
            for y in range(size_y)
        ]
        return lax.ppermute(value, ("gx", "gy"), pairs)

    assert size_x % 2 == 0 and size_y % 2 == 0

    def swaps(axis, size, parity, initial, last):
        if initial is last:
            return swap(axis, size, 0, last), swap(axis, size, 1, last)
        is_even = parity == 0
        return (
            swap(axis, size, 0, jnp.where(is_even, last, initial)),
            swap(axis, size, 1, jnp.where(is_even, initial, last)),
        )

    if rows == REACH:
        even_x, odd_x = swaps("gx", size_x, parity_x, density, density)
    else:
        even_x, odd_x = swaps("gx", size_x, parity_x, density[:, :REACH], density[:, rows - REACH :])

    low, high = density[:, :, :2], density[:, :, cols - 2 :]
    sides = jnp.concatenate([low, high], axis=2)
    even_near, odd_near = swaps("gx", size_x, parity_x, sides[:, :HALF], sides[:, rows - HALF :])
    even_x, even_near, odd_near = lax.optimization_barrier((even_x, even_near, odd_near))
    above = jnp.where(parity_x == 0, odd_near, even_near)
    below = jnp.where(parity_x == 0, even_near, odd_near)

    def edge(own, cut):
        return jnp.concatenate([above[:, :, cut], own, below[:, :, cut]], axis=1)

    even_y, odd_y = swaps("gy", size_y, parity_y, edge(low, slice(0, 2)), edge(high, slice(2, 4)))

    vmem = pl.BlockSpec(memory_space=pltpu.VMEM)
    block = jax.ShapeDtypeStruct(density.shape, jnp.float32)
    image_one, image_two, message = pl.pallas_call(
        functools.partial(images_kernel, (size_x * rows, size_y * cols)),
        out_shape=[block, block, jax.ShapeDtypeStruct((devices, 128), jnp.float32)],
        in_specs=[vmem] * 6,
        out_specs=[vmem, vmem, vmem],
        scratch_shapes=[
            pltpu.VMEM((members, rows + 2 * REACH, cols + 2 * GAP, depth), jnp.float32),
            pltpu.VMEM((members, rows + 2 * HALF, cols + 2 * GAP, depth), jnp.float32),
            pltpu.VMEM((48, depth), jnp.float32),
        ],
        compiler_params=pltpu.CompilerParams(vmem_limit_bytes=8 * 2**20),
        name="images",
    )(rate_table, density, even_x, odd_x, even_y, odd_y)

    gathered = lax.all_to_all(message, ("gx", "gy"), 0, 0, tiled=True)

    return pl.pallas_call(
        combine_kernel,
        out_shape=[block, jax.ShapeDtypeStruct((members, 5), jnp.float32)],
        in_specs=[vmem] * 4,
        out_specs=[vmem, vmem],
        compiler_params=pltpu.CompilerParams(vmem_limit_bytes=8 * 2**20),
        name="combine",
    )(gathered, density, image_one, image_two)


def solution(mesh):
    in_specs = (P(None, "gx", "gy", None), P())
    out_specs = (P(None, "gx", "gy", None), P())
    return jax.shard_map(shards, mesh=mesh, in_specs=in_specs, out_specs=out_specs, check_vma=False)
```

```python
import functools
import math

import jax
import jax.numpy as jnp
from jax import lax
from jax.experimental import pallas as pl
from jax.experimental.pallas import tpu as pltpu
from jax.sharding import PartitionSpec as P

tau_step = 0.01
taylor_terms = 16
squarings = 4
REACH = 4
HALF = 2
GAP = 8


def edges_kernel(field, for_odd, for_even, block, arrived):
    copy = pltpu.make_async_copy(field, block, arrived)
    copy.start()
    is_even = lax.axis_index("gy") % 2 == 0
    cols = block.shape[2]
    copy.wait()
    low, high = block[:, :, :2], block[:, :, cols - 2 :]
    for_even[...] = jnp.where(is_even, high, low)
    for_odd[...] = jnp.where(is_even, low, high)


def own_lane(first):
    row = lax.broadcasted_iota(jnp.int32, (8, 128), 0)
    return lax.broadcasted_iota(jnp.int32, (8, 128), 1) == first + row


def images_kernel(
    lattice,
    rates,
    field,
    even_x,
    odd_x,
    even_y,
    odd_y,
    even_corners,
    odd_corners,
    image_one,
    image_two,
    message,
    wide,
    wide_image,
    parts,
):
    members, rows, cols, depth = field.shape
    span = cols + 2 * GAP
    index_i, index_j = lax.axis_index("gx"), lax.axis_index("gy")
    first_i, first_j = index_i * rows, index_j * cols
    even_i, even_j = index_i % 2 == 0, index_j % 2 == 0
    count_i, count_j = lattice

    ends_i, ends_j = first_i + rows < count_i, first_j + cols < count_j

    def sides(even, odd, is_even, lower_inside, higher_inside):
        lower, higher = jnp.where(is_even, odd, even), jnp.where(is_even, even, odd)
        return jnp.where(lower_inside, lower, 0.0), jnp.where(higher_inside, higher, 0.0)

    def place(row, start, values):
        for at in range(values.shape[1]):
            first = (row + REACH + at) * span + GAP + start
            wide[:, first : first + values.shape[2]] = values[:, at]

    def column(ref, member, row, at):
        return ref[member, pl.ds(row * span + at, rows, stride=span), :]

    place(0, 0, field[...])
    above, below = sides(even_x[...], odd_x[...], even_i, first_i > 0, ends_i)
    place(-REACH, 0, above)
    place(rows, 0, below)
    left, right = sides(even_y[...], odd_y[...], even_j, first_j > 0, ends_j)
    place(0, -2, left)
    place(0, cols, right)
    upper, lower = sides(even_corners[...], odd_corners[...], even_i, first_i > 0, ends_i)
    for corners, row in ((upper, -HALF), (lower, rows)):
        place(row, -1, jnp.where(first_j > 0, corners[:, :, :1], 0.0))
        place(row, cols, jnp.where(ends_j, corners[:, :, 1:], 0.0))

    lane = lax.broadcasted_iota(jnp.int32, (1, depth), 1)
    amount_k = lane.astype(jnp.float32)
    above_k = jnp.where(lane < depth - 1, amount_k + 1.0, 0.0)
    inner_k = jnp.where(lane > 0, 1.0, 0.0)
    sublane = lax.broadcasted_iota(jnp.int32, (span, 1), 0)
    amount_j = (first_j - GAP + sublane).astype(jnp.float32)

    for member in range(members):
        c = [jnp.broadcast_to(rates[member : member + 1, r : r + 1], (1, depth)) for r in range(9)]
        ratio_j = amount_j / c[7]
        ratio_k = amount_k / c[8]
        make_u = c[0] / (1.0 + ratio_j * ratio_j)
        make_v = c[2] / (1.0 + ratio_k * ratio_k)
        lose_v = c[3] * (amount_j + 1.0)
        rest = make_u + make_v + (c[3] * amount_j + (c[5] + c[6]) * amount_k)

        def apply(read, row, start, size, i=None):
            if i is None:
                i = (first_i + row).astype(jnp.float32)
            cut = slice(GAP + start, GAP + start + size)
            centre = read(row, start, size)
            value = make_u[cut] * read(row - 1, start, size)
            value = value + (c[1] * (i + 1.0)) * read(row + 1, start, size)
            value = value + make_v * read(row, start - 1, size)
            value = value + lose_v[cut] * read(row, start + 1, size)
            pair = pltpu.roll(read(row + 2, start, size), 1, 1)
            value = value + (inner_k * (0.5 * c[4] * (i + 2.0) * (i + 1.0))) * pair
            split = c[5] * read(row - 2, start, size) + c[6] * centre
            value = value + above_k * pltpu.roll(split, depth - 1, 1)
            out = rest[cut] + (c[1] * i + 0.5 * c[4] * i * (i - 1.0))
            return value - out * centre

        def read_field(row, start, size):
            return wide[member, pl.ds((row + REACH) * span + GAP + start, size), :]

        def read_image(row, start, size):
            return wide_image[member, pl.ds((row + HALF) * span + GAP + start, size), :]

        for row in range(-HALF, rows + HALF):
            inside = (first_i + row >= 0) & (first_i + row < count_i)
            value = apply(read_field, row, 0, cols)
            if row < 0 or row >= rows:
                value = jnp.where(inside, value, 0.0)
            else:
                image_one[member, row] = value
            wide_image[member, pl.ds((row + HALF) * span + GAP, cols), :] = value

        def read_side(row, start, size):
            return column(wide, member, row + REACH, GAP + start)

        i = (first_i + lax.broadcasted_iota(jnp.int32, (rows, depth), 0)).astype(jnp.float32)
        for start, inside in ((-1, first_j > 0), (cols, ends_j)):
            value = jnp.where(inside, apply(read_side, 0, start, 1, i), 0.0)
            wide_image[member, pl.ds(HALF * span + GAP + start, rows, stride=span), :] = value

        products = [jnp.zeros((cols, depth), jnp.float32) for _ in range(6)]
        for row in range(rows):
            zero = field[member, row]
            one = image_one[member, row]
            two = apply(read_image, row, 0, cols)
            image_two[member, row] = two
            terms = (zero * zero, zero * one, zero * two, one * one, one * two, two * two)
            products = [total + term for total, term in zip(products, terms)]
        for index, total in enumerate(products):
            parts[8 * index + member : 8 * index + member + 1, :] = jnp.sum(total, axis=0, keepdims=True)

    for index in range(6):
        parts[8 * index + members : 8 * index + 8, :] = jnp.zeros((8 - members, depth), jnp.float32)
    row = jnp.zeros((8, depth), jnp.float32)
    for index in range(6):
        total = jnp.sum(parts[8 * index : 8 * index + 8], axis=1, keepdims=True)
        row = row + jnp.where(own_lane(8 * index), total, 0.0)
    message[...] = jnp.broadcast_to(jnp.sum(row, axis=0, keepdims=True), message.shape)


def product(left, right):
    a, b, c, d = left
    e, f, g, h = right
    return a * e + b * g, a * f + b * h, c * e + d * g, c * f + d * h


def first_column(h00, s01, h11):
    scale = tau_step / 2.0**squarings
    one = jnp.ones_like(h00)
    z1 = (scale * h00, scale * s01, scale * one, scale * h11)
    z2 = product(z1, z1)
    z3, z4 = product(z2, z1), product(z2, z2)
    weights = [1.0 / math.factorial(k + 1) for k in range(taylor_terms)]

    def block(first):
        w0, w1, w2, w3 = weights[first : first + 4]
        terms = [w1 * p + w2 * q + w3 * r for p, q, r in zip(z1, z2, z3)]
        return terms[0] + w0, terms[1], terms[2], terms[3] + w0

    phi = block(taylor_terms - 4)
    for first in range(taylor_terms - 8, -1, -4):
        phi = tuple(p + q for p, q in zip(product(z4, phi), block(first)))
    p00, p01, p10, p11 = product(z1, phi)
    p00, p11 = 1.0 + p00, 1.0 + p11
    q0, q1 = scale * phi[2], scale * phi[3]
    for _ in range(squarings):
        p00, p01, p10, p11, q0, q1 = (
            p00 * p00 + p01 * p10,
            p00 * p01 + p01 * p11,
            p10 * p00 + p11 * p10,
            p10 * p01 + p11 * p11,
            q0 * p00 + q1 * p10 + q0,
            q0 * p01 + q1 * p11 + q1,
        )
    return p00, p10, q0


def combine_kernel(gathered, field, image_one, image_two, propagated, entries):
    members, rows, cols, depth = field.shape
    sums = jnp.broadcast_to(jnp.sum(gathered[...], axis=0, keepdims=True), (8, 128))
    g00, g01, g02, g11, g12, g22 = [
        jnp.broadcast_to(jnp.sum(jnp.where(own_lane(8 * index), sums, 0.0), axis=1, keepdims=True), (8, 128))
        for index in range(6)
    ]
    tiny = jnp.finfo(jnp.float32).tiny
    h00 = g01 / g00
    square_10 = jnp.maximum(g11 / g00 - h00 * h00, tiny)
    s01 = (g02 - h00 * g01) / g00
    h11 = ((g12 - h00 * g02) - h00 * (g11 - h00 * g01)) / (g00 * square_10)
    norm_2 = ((g22 - h00 * g12) - h00 * (g12 - h00 * g11)) / (g00 * square_10)
    h10 = jnp.sqrt(square_10)
    h01 = s01 / h10
    h21 = jnp.sqrt(jnp.maximum(norm_2 - h01 * h01 - h11 * h11, 0.0))
    e0, e1, e2 = first_column(h00, s01, h11)
    a2 = e2
    a1 = e1 - e2 * (h00 + h11)
    a0 = e0 - e1 * h00 - e2 * (s01 - h11 * h00)
    lane = lax.broadcasted_iota(jnp.int32, h00.shape, 1)
    table = h21
    for index, entry in enumerate((h00, h10, h01, h11)):
        table = jnp.where(lane == index, entry, table)
    entries[...] = (tau_step * table)[: entries.shape[0], : entries.shape[1]]
    for member in range(members):
        b0, b1, b2 = [jnp.broadcast_to(a[member : member + 1], (cols, depth)) for a in (a0, a1, a2)]
        for row in range(rows):
            propagated[member, row] = (
                b0 * field[member, row] + b1 * image_one[member, row] + b2 * image_two[member, row]
            )


def shards(density, rate_table):
    members, rows, cols, depth = density.shape
    size_x, size_y = lax.axis_size("gx"), lax.axis_size("gy")
    devices = size_x * size_y
    vmem = pl.BlockSpec(memory_space=pltpu.VMEM)
    parity_x, parity_y = lax.axis_index("gx") % 2, lax.axis_index("gy") % 2

    def swap(axis, size, first, value):
        def partner(x, y):
            at = x if axis == "gx" else y
            other = at + 1 if (at - first) % 2 == 0 else at - 1
            if not 0 <= other < size:
                return (x, y ^ 1) if axis == "gx" else (x ^ 1, y)
            return (other, y) if axis == "gx" else (x, other)

        pairs = [
            (x * size_y + y, partner(x, y)[0] * size_y + partner(x, y)[1])
            for x in range(size_x)
            for y in range(size_y)
        ]
        return lax.ppermute(value, ("gx", "gy"), pairs)

    assert size_x % 2 == 0 and size_y % 2 == 0

    def swaps(axis, size, parity, initial, last):
        if initial is last:
            return swap(axis, size, 0, last), swap(axis, size, 1, last)
        is_even = parity == 0
        return (
            swap(axis, size, 0, jnp.where(is_even, last, initial)),
            swap(axis, size, 1, jnp.where(is_even, initial, last)),
        )

    if rows == REACH:
        even_x, odd_x = swaps("gx", size_x, parity_x, density, density)
    else:
        even_x, odd_x = swaps("gx", size_x, parity_x, density[:, :REACH], density[:, rows - REACH :])

    edge = jax.ShapeDtypeStruct((members, rows, 2, depth), jnp.float32)
    block = jax.ShapeDtypeStruct(density.shape, jnp.float32)
    for_odd, for_even, field = pl.pallas_call(
        edges_kernel,
        out_shape=[edge, edge, block],
        in_specs=[pl.BlockSpec(memory_space=pl.ANY)],
        out_specs=[vmem] * 3,
        scratch_shapes=[pltpu.SemaphoreType.DMA],
        compiler_params=pltpu.CompilerParams(vmem_limit_bytes=4 * 2**20),
        name="edges",
    )(density)
    odd_y = swap("gy", size_y, 1, for_odd)
    even_y = swap("gy", size_y, 0, for_even)

    even_x, odd_y, even_y = lax.optimization_barrier((even_x, odd_y, even_y))

    def corners(first):
        even, odd = even_y[:, first : first + HALF], odd_y[:, first : first + HALF]
        left = jnp.where(parity_y == 0, odd, even)[:, :, 1:]
        right = jnp.where(parity_y == 0, even, odd)[:, :, :1]
        return jnp.concatenate([left, right], axis=2)

    even_corners, odd_corners = swaps("gx", size_x, parity_x, corners(0), corners(rows - HALF))

    image_one, image_two, message = pl.pallas_call(
        functools.partial(images_kernel, (size_x * rows, size_y * cols)),
        out_shape=[block, block, jax.ShapeDtypeStruct((devices, 128), jnp.float32)],
        in_specs=[vmem] * 8,
        out_specs=[vmem, vmem, vmem],
        scratch_shapes=[
            pltpu.VMEM((members, (rows + 2 * REACH) * (cols + 2 * GAP), depth), jnp.float32),
            pltpu.VMEM((members, (rows + 2 * HALF) * (cols + 2 * GAP), depth), jnp.float32),
            pltpu.VMEM((48, depth), jnp.float32),
        ],
        compiler_params=pltpu.CompilerParams(vmem_limit_bytes=8 * 2**20),
        name="images",
    )(rate_table, field, even_x, odd_x, even_y, odd_y, even_corners, odd_corners)

    gathered = lax.all_to_all(message, ("gx", "gy"), 0, 0, tiled=True)

    return pl.pallas_call(
        combine_kernel,
        out_shape=[block, jax.ShapeDtypeStruct((members, 5), jnp.float32)],
        in_specs=[vmem] * 4,
        out_specs=[vmem, vmem],
        compiler_params=pltpu.CompilerParams(vmem_limit_bytes=8 * 2**20),
        name="combine",
    )(gathered, field, image_one, image_two)


def solution(mesh):
    in_specs = (P(None, "gx", "gy", None), P())
    out_specs = (P(None, "gx", "gy", None), P())
    return jax.shard_map(shards, mesh=mesh, in_specs=in_specs, out_specs=out_specs, check_vma=False)
```

```python
import functools
import math

import jax
import jax.numpy as jnp
from jax import lax
from jax.experimental import pallas as pl
from jax.experimental.pallas import tpu as pltpu
from jax.sharding import PartitionSpec as P

tau_step = 0.01
taylor_terms = 16
squarings = 4
REACH = 4
HALF = 2
GAP = 8


def edges_kernel(field, for_odd, for_even, block, arrived):
    copy = pltpu.make_async_copy(field, block, arrived)
    copy.start()
    is_even = lax.axis_index("gy") % 2 == 0
    cols = block.shape[2]
    copy.wait()
    low, high = block[:, :, :2], block[:, :, cols - 2 :]
    for_even[...] = jnp.where(is_even, high, low)
    for_odd[...] = jnp.where(is_even, low, high)


def own_lane(first):
    row = lax.broadcasted_iota(jnp.int32, (8, 128), 0)
    return lax.broadcasted_iota(jnp.int32, (8, 128), 1) == first + row


def lanes(depth):
    lane = lax.broadcasted_iota(jnp.int32, (1, depth), 1)
    amount_k = lane.astype(jnp.float32)
    return amount_k, jnp.where(lane < depth - 1, amount_k + 1.0, 0.0), jnp.where(lane > 0, 1.0, 0.0)


def apply(c, depth, i, make_u, make_v, lose_v, rest, centre, rows_by, left, right):
    _, above_k, inner_k = lanes(depth)
    value = make_u * rows_by(-1) + (c[1] * (i + 1.0)) * rows_by(1)
    value = value + make_v * left
    value = value + lose_v * right
    pair = pltpu.roll(rows_by(2), 1, 1)
    value = value + (inner_k * (0.5 * c[4] * (i + 2.0) * (i + 1.0))) * pair
    split = c[5] * rows_by(-2) + c[6] * centre
    value = value + above_k * pltpu.roll(split, depth - 1, 1)
    out = rest + (c[1] * i + 0.5 * c[4] * i * (i - 1.0))
    return value - out * centre


def constants(rates, member, depth, amount_j):
    c = [jnp.broadcast_to(rates[member : member + 1, r : r + 1], (1, depth)) for r in range(9)]
    amount_k = lanes(depth)[0]
    ratio_j, ratio_k = amount_j / c[7], amount_k / c[8]
    make_u = c[0] / (1.0 + ratio_j * ratio_j)
    make_v = c[2] / (1.0 + ratio_k * ratio_k)
    lose_v = c[3] * (amount_j + 1.0)
    rest = make_u + make_v + (c[3] * amount_j + (c[5] + c[6]) * amount_k)
    return c, make_u, make_v, lose_v, rest


def sides(even, odd, is_even, lower_inside, higher_inside):
    lower, higher = jnp.where(is_even, odd, even), jnp.where(is_even, even, odd)
    return jnp.where(lower_inside, lower, 0.0), jnp.where(higher_inside, higher, 0.0)


def images_kernel(
    lattice,
    rates,
    field,
    even_x,
    odd_x,
    even_y,
    odd_y,
    image_one,
    image_two,
    lines,
    parts,
    wide,
    wide_image,
):
    members, rows, cols, depth = field.shape
    span = cols + 2 * GAP
    tall = rows + 2 * HALF
    index_i, index_j = lax.axis_index("gx"), lax.axis_index("gy")
    first_i, first_j = index_i * rows, index_j * cols
    even_i, even_j = index_i % 2 == 0, index_j % 2 == 0
    count_i, count_j = lattice

    def place(row, start, values):
        for at in range(values.shape[1]):
            first = (row + REACH + at) * span + GAP + start
            wide[:, first : first + values.shape[2]] = values[:, at]

    place(0, 0, field[...])
    above, below = sides(even_x[...], odd_x[...], even_i, first_i > 0, first_i + rows < count_i)
    place(-REACH, 0, above)
    place(rows, 0, below)
    left, right = sides(even_y[...], odd_y[...], even_j, first_j > 0, first_j + cols < count_j)
    place(0, -2, left)
    place(0, cols, right)
    corner = jnp.zeros((members, HALF, 1, depth), jnp.float32)
    for row in (-HALF, rows):
        place(row, -1, corner)
        place(row, cols, corner)

    sublane = lax.broadcasted_iota(jnp.int32, (span, 1), 0)
    amount_j = (first_j - GAP + sublane).astype(jnp.float32)
    place_j = lax.broadcasted_iota(jnp.int32, (cols, depth), 0)
    inner_j = (place_j > 0) & (place_j < cols - 1)

    for member in range(members):
        c, make_u, make_v, lose_v, rest = constants(rates, member, depth, amount_j)
        make_u, lose_v, rest = [term[GAP : GAP + cols] for term in (make_u, lose_v, rest)]

        def image(read, row):
            i = (first_i + row).astype(jnp.float32)
            rows_by = lambda by: read(row + by, 0)
            return apply(c, depth, i, make_u, make_v, lose_v, rest, read(row, 0), rows_by, read(row, -1), read(row, 1))

        def read_field(row, start):
            return wide[member, pl.ds((row + REACH) * span + GAP + start, cols), :]

        def read_image(row, start):
            return wide_image[member, pl.ds((row + HALF) * span + GAP + start, cols), :]

        for row in range(-HALF, rows + HALF):
            inside = (first_i + row >= 0) & (first_i + row < count_i)
            value = image(read_field, row)
            if row < 0 or row >= rows:
                value = jnp.where(inside, value, 0.0)
            else:
                image_one[member, row] = value
            wide_image[member, pl.ds((row + HALF) * span + GAP, cols), :] = value

        products = [jnp.zeros((cols, depth), jnp.float32) for _ in range(6)]
        for row in range(rows):
            zero = field[member, row]
            one = image_one[member, row]
            two = jnp.where(inner_j, image(read_image, row), 0.0)
            image_two[member, row] = two
            terms = (zero * zero, zero * one, zero * two, one * one, one * two, two * two)
            products = [total + term for total, term in zip(products, terms)]
        for index, total in enumerate(products):
            parts[8 * index + member : 8 * index + member + 1, :] = jnp.sum(total, axis=0, keepdims=True)

        for at, column in enumerate((0, cols - 1, 1, cols - 2)):
            lines[member, at] = wide_image[member, pl.ds(GAP + column, tall, stride=span), :]
        for at, column in enumerate((0, cols - 1, -1, cols, -2, cols + 1)):
            lines[member, 4 + at] = wide[member, pl.ds(HALF * span + GAP + column, tall, stride=span), :]

    for index in range(6):
        parts[8 * index + members : 8 * index + 8, :] = jnp.zeros((8 - members, depth), jnp.float32)


def corners_kernel(lattice, cols, rates, lines, odd_corners, even_corners, parts, columns_two, message, edge, total):
    members, _, tall, depth = lines.shape
    rows = tall - 2 * HALF
    index_i, index_j = lax.axis_index("gx"), lax.axis_index("gy")
    first_i, first_j = index_i * rows, index_j * cols
    count_i, count_j = lattice
    upper, lower = sides(
        even_corners[...], odd_corners[...], index_i % 2 == 0, first_i > 0, first_i + rows < count_i
    )
    i = (first_i + lax.broadcasted_iota(jnp.int32, (rows, depth), 0)).astype(jnp.float32)
    total[...] = parts[...]
    for member in range(members):

        def line(at):
            return lines[member, at, pl.ds(HALF, rows), :]

        sums = [jnp.zeros((rows, depth), jnp.float32) for _ in range(3)]
        for side, column, beyond, inside in (
            (0, 0, -1, first_j > 0),
            (1, cols - 1, cols, first_j + cols < count_j),
        ):

            def at_column(column):
                amount_j = jnp.broadcast_to((first_j + column).astype(jnp.float32), (1, depth))
                return constants(rates, member, depth, amount_j)

            outer, fixed = edge.at[member, side, 0], edge.at[member, side, 1]
            outer[HALF : HALF + rows, :] = line(6 + side)
            for row in range(HALF):
                for first, corner in ((0, upper), (HALF + rows, lower)):
                    value = corner[member, row, side : side + 1, :]
                    outer[first + row : first + row + 1, :] = jnp.where(inside, value, 0.0)

            c, make_u, make_v, lose_v, rest = at_column(beyond)
            rows_by = lambda by: outer[pl.ds(HALF + by, rows), :]
            beside = (line(8), line(4)) if side == 0 else (line(5), line(9))
            value = apply(c, depth, i, make_u, make_v, lose_v, rest, rows_by(0), rows_by, *beside)
            image_beyond = jnp.where(inside, value, 0.0)

            c, make_u, make_v, lose_v, rest = at_column(column)
            gain = make_v if side == 0 else lose_v
            fixed[...] = lines[member, side]
            for first in (0, HALF + rows):
                fixed[first : first + HALF, :] = fixed[first : first + HALF, :] + gain * outer[first : first + HALF, :]

            rows_by = lambda by: fixed[pl.ds(HALF + by, rows), :]
            beside = (image_beyond, line(2)) if side == 0 else (line(3), image_beyond)
            two = apply(c, depth, i, make_u, make_v, lose_v, rest, rows_by(0), rows_by, *beside)
            columns_two[member, side] = two
            terms = (line(4 + side) * two, line(side) * two, two * two)
            sums = [value + term for value, term in zip(sums, terms)]
        for index, value in zip((2, 4, 5), sums):
            at = 8 * index + member
            total[at : at + 1, :] = total[at : at + 1, :] + jnp.sum(value, axis=0, keepdims=True)

    row = jnp.zeros((8, depth), jnp.float32)
    for index in range(6):
        value = jnp.sum(total[8 * index : 8 * index + 8], axis=1, keepdims=True)
        row = row + jnp.where(own_lane(8 * index), value, 0.0)
    message[...] = jnp.broadcast_to(jnp.sum(row, axis=0, keepdims=True), message.shape)


def product(left, right):
    a, b, c, d = left
    e, f, g, h = right
    return a * e + b * g, a * f + b * h, c * e + d * g, c * f + d * h


def first_column(h00, s01, h11):
    scale = tau_step / 2.0**squarings
    one = jnp.ones_like(h00)
    z1 = (scale * h00, scale * s01, scale * one, scale * h11)
    z2 = product(z1, z1)
    z3, z4 = product(z2, z1), product(z2, z2)
    weights = [1.0 / math.factorial(k + 1) for k in range(taylor_terms)]

    def block(first):
        w0, w1, w2, w3 = weights[first : first + 4]
        terms = [w1 * p + w2 * q + w3 * r for p, q, r in zip(z1, z2, z3)]
        return terms[0] + w0, terms[1], terms[2], terms[3] + w0

    phi = block(taylor_terms - 4)
    for first in range(taylor_terms - 8, -1, -4):
        phi = tuple(p + q for p, q in zip(product(z4, phi), block(first)))
    p00, p01, p10, p11 = product(z1, phi)
    p00, p11 = 1.0 + p00, 1.0 + p11
    q0, q1 = scale * phi[2], scale * phi[3]
    for _ in range(squarings):
        p00, p01, p10, p11, q0, q1 = (
            p00 * p00 + p01 * p10,
            p00 * p01 + p01 * p11,
            p10 * p00 + p11 * p10,
            p10 * p01 + p11 * p11,
            q0 * p00 + q1 * p10 + q0,
            q0 * p01 + q1 * p11 + q1,
        )
    return p00, p10, q0


def combine_kernel(gathered, field, image_one, image_two, columns_two, propagated, entries):
    members, rows, cols, depth = field.shape
    sums = jnp.broadcast_to(jnp.sum(gathered[...], axis=0, keepdims=True), (8, 128))
    g00, g01, g02, g11, g12, g22 = [
        jnp.broadcast_to(jnp.sum(jnp.where(own_lane(8 * index), sums, 0.0), axis=1, keepdims=True), (8, 128))
        for index in range(6)
    ]
    tiny = jnp.finfo(jnp.float32).tiny
    h00 = g01 / g00
    square_10 = jnp.maximum(g11 / g00 - h00 * h00, tiny)
    s01 = (g02 - h00 * g01) / g00
    h11 = ((g12 - h00 * g02) - h00 * (g11 - h00 * g01)) / (g00 * square_10)
    norm_2 = ((g22 - h00 * g12) - h00 * (g12 - h00 * g11)) / (g00 * square_10)
    h10 = jnp.sqrt(square_10)
    h01 = s01 / h10
    h21 = jnp.sqrt(jnp.maximum(norm_2 - h01 * h01 - h11 * h11, 0.0))
    e0, e1, e2 = first_column(h00, s01, h11)
    a2 = e2
    a1 = e1 - e2 * (h00 + h11)
    a0 = e0 - e1 * h00 - e2 * (s01 - h11 * h00)
    lane = lax.broadcasted_iota(jnp.int32, h00.shape, 1)
    table = h21
    for index, entry in enumerate((h00, h10, h01, h11)):
        table = jnp.where(lane == index, entry, table)
    entries[...] = (tau_step * table)[: entries.shape[0], : entries.shape[1]]
    place_j = lax.broadcasted_iota(jnp.int32, (cols, depth), 0)
    for member in range(members):
        b0, b1, b2 = [jnp.broadcast_to(a[member : member + 1], (cols, depth)) for a in (a0, a1, a2)]
        for row in range(rows):
            two = jnp.where(place_j == 0, columns_two[member, 0, row : row + 1], image_two[member, row])
            two = jnp.where(place_j == cols - 1, columns_two[member, 1, row : row + 1], two)
            propagated[member, row] = b0 * field[member, row] + b1 * image_one[member, row] + b2 * two


def shards(density, rate_table):
    members, rows, cols, depth = density.shape
    size_x, size_y = lax.axis_size("gx"), lax.axis_size("gy")
    devices = size_x * size_y
    vmem = pl.BlockSpec(memory_space=pltpu.VMEM)
    parity_x, parity_y = lax.axis_index("gx") % 2, lax.axis_index("gy") % 2

    def swap(axis, size, first, value):
        def partner(x, y):
            at = x if axis == "gx" else y
            other = at + 1 if (at - first) % 2 == 0 else at - 1
            if not 0 <= other < size:
                return (x, y ^ 1) if axis == "gx" else (x ^ 1, y)
            return (other, y) if axis == "gx" else (x, other)

        pairs = [
            (x * size_y + y, partner(x, y)[0] * size_y + partner(x, y)[1])
            for x in range(size_x)
            for y in range(size_y)
        ]
        return lax.ppermute(value, ("gx", "gy"), pairs)

    assert size_x % 2 == 0 and size_y % 2 == 0

    def swaps(axis, size, parity, initial, last):
        if initial is last:
            return swap(axis, size, 0, last), swap(axis, size, 1, last)
        is_even = parity == 0
        return (
            swap(axis, size, 0, jnp.where(is_even, last, initial)),
            swap(axis, size, 1, jnp.where(is_even, initial, last)),
        )

    if rows == REACH:
        even_x, odd_x = swaps("gx", size_x, parity_x, density, density)
    else:
        even_x, odd_x = swaps("gx", size_x, parity_x, density[:, :REACH], density[:, rows - REACH :])

    edge = jax.ShapeDtypeStruct((members, rows, 2, depth), jnp.float32)
    block = jax.ShapeDtypeStruct(density.shape, jnp.float32)
    for_odd, for_even, field = pl.pallas_call(
        edges_kernel,
        out_shape=[edge, edge, block],
        in_specs=[pl.BlockSpec(memory_space=pl.ANY)],
        out_specs=[vmem] * 3,
        scratch_shapes=[pltpu.SemaphoreType.DMA],
        compiler_params=pltpu.CompilerParams(vmem_limit_bytes=4 * 2**20),
        name="edges",
    )(density)
    odd_y = swap("gy", size_y, 1, for_odd)
    even_y = swap("gy", size_y, 0, for_even)

    even_x, odd_y, even_y = lax.optimization_barrier((even_x, odd_y, even_y))

    def corners(first):
        even, odd = even_y[:, first : first + HALF], odd_y[:, first : first + HALF]
        left = jnp.where(parity_y == 0, odd, even)[:, :, 1:]
        right = jnp.where(parity_y == 0, even, odd)[:, :, :1]
        return jnp.concatenate([left, right], axis=2)

    even_corners, odd_corners = swaps("gx", size_x, parity_x, corners(0), corners(rows - HALF))

    lattice = (size_x * rows, size_y * cols)
    tall, span = rows + 2 * HALF, cols + 2 * GAP
    image_one, image_two, lines, parts = pl.pallas_call(
        functools.partial(images_kernel, lattice),
        out_shape=[
            block,
            block,
            jax.ShapeDtypeStruct((members, 10, tall, depth), jnp.float32),
            jax.ShapeDtypeStruct((48, depth), jnp.float32),
        ],
        in_specs=[vmem] * 6,
        out_specs=[vmem] * 4,
        scratch_shapes=[
            pltpu.VMEM((members, (rows + 2 * REACH) * span, depth), jnp.float32),
            pltpu.VMEM((members, tall * span, depth), jnp.float32),
        ],
        compiler_params=pltpu.CompilerParams(vmem_limit_bytes=8 * 2**20),
        name="images",
    )(rate_table, field, even_x, odd_x, even_y, odd_y)

    columns_two, message = pl.pallas_call(
        functools.partial(corners_kernel, lattice, cols),
        out_shape=[
            jax.ShapeDtypeStruct((members, 2, rows, depth), jnp.float32),
            jax.ShapeDtypeStruct((devices, 128), jnp.float32),
        ],
        in_specs=[vmem] * 5,
        out_specs=[vmem, vmem],
        scratch_shapes=[
            pltpu.VMEM((members, 2, 2, tall, depth), jnp.float32),
            pltpu.VMEM((48, depth), jnp.float32),
        ],
        compiler_params=pltpu.CompilerParams(vmem_limit_bytes=4 * 2**20),
        name="corners",
    )(rate_table, lines, odd_corners, even_corners, parts)

    gathered = lax.all_to_all(message, ("gx", "gy"), 0, 0, tiled=True)

    return pl.pallas_call(
        combine_kernel,
        out_shape=[block, jax.ShapeDtypeStruct((members, 5), jnp.float32)],
        in_specs=[vmem] * 5,
        out_specs=[vmem, vmem],
        compiler_params=pltpu.CompilerParams(vmem_limit_bytes=8 * 2**20),
        name="combine",
    )(gathered, field, image_one, image_two, columns_two)


def solution(mesh):
    in_specs = (P(None, "gx", "gy", None), P())
    out_specs = (P(None, "gx", "gy", None), P())
    return jax.shard_map(shards, mesh=mesh, in_specs=in_specs, out_specs=out_specs, check_vma=False)
```

```python
import functools
import math

import jax
import jax.numpy as jnp
from jax import lax
from jax.experimental import pallas as pl
from jax.experimental.pallas import tpu as pltpu
from jax.sharding import PartitionSpec as P

tau_step = 0.01
taylor_terms = 16
squarings = 4
REACH = 4
HALF = 2
GAP = 8


def edges_kernel(field, for_odd, for_even, block, arrived):
    copy = pltpu.make_async_copy(field, block, arrived)
    copy.start()
    is_even = lax.axis_index("gy") % 2 == 0
    cols = block.shape[2]
    copy.wait()
    low, high = block[:, :, :2], block[:, :, cols - 2 :]
    for_even[...] = jnp.where(is_even, high, low)
    for_odd[...] = jnp.where(is_even, low, high)


def own_lane(first):
    row = lax.broadcasted_iota(jnp.int32, (8, 128), 0)
    return lax.broadcasted_iota(jnp.int32, (8, 128), 1) == first + row


def lanes(depth):
    lane = lax.broadcasted_iota(jnp.int32, (1, depth), 1)
    amount_k = lane.astype(jnp.float32)
    return amount_k, jnp.where(lane < depth - 1, amount_k + 1.0, 0.0), jnp.where(lane > 0, 1.0, 0.0)


def apply(c, depth, i, make_u, make_v, lose_v, rest, centre, rows_by, left, right):
    _, above_k, inner_k = lanes(depth)
    value = make_u * rows_by(-1) + (c[1] * (i + 1.0)) * rows_by(1)
    value = value + make_v * left
    value = value + lose_v * right
    pair = pltpu.roll(rows_by(2), 1, 1)
    value = value + (inner_k * (0.5 * c[4] * (i + 2.0) * (i + 1.0))) * pair
    split = c[5] * rows_by(-2) + c[6] * centre
    value = value + above_k * pltpu.roll(split, depth - 1, 1)
    out = rest + (c[1] * i + 0.5 * c[4] * i * (i - 1.0))
    return value - out * centre


def constants(rates, member, depth, amount_j):
    row = rates[pl.ds(member, 1), :]
    c = [jnp.broadcast_to(row[:, r : r + 1], (1, depth)) for r in range(9)]
    amount_k = lanes(depth)[0]
    ratio_j, ratio_k = amount_j / c[7], amount_k / c[8]
    make_u = c[0] / (1.0 + ratio_j * ratio_j)
    make_v = c[2] / (1.0 + ratio_k * ratio_k)
    lose_v = c[3] * (amount_j + 1.0)
    rest = make_u + make_v + (c[3] * amount_j + (c[5] + c[6]) * amount_k)
    return c, make_u, make_v, lose_v, rest


def sides(even, odd, is_even, lower_inside, higher_inside):
    lower, higher = jnp.where(is_even, odd, even), jnp.where(is_even, even, odd)
    return jnp.where(lower_inside, lower, 0.0), jnp.where(higher_inside, higher, 0.0)


def images_kernel(
    lattice,
    rates,
    field,
    even_x,
    odd_x,
    even_y,
    odd_y,
    image_one,
    image_two,
    lines,
    parts,
    wide,
    wide_image,
):
    members, rows, cols, depth = field.shape
    span = cols + 2 * GAP
    tall = rows + 2 * HALF
    index_i, index_j = lax.axis_index("gx"), lax.axis_index("gy")
    first_i, first_j = index_i * rows, index_j * cols
    even_i, even_j = index_i % 2 == 0, index_j % 2 == 0
    count_i, count_j = lattice

    def place(row, start, values):
        for at in range(values.shape[1]):
            first = (row + REACH + at) * span + GAP + start
            wide[:, first : first + values.shape[2]] = values[:, at]

    place(0, 0, field[...])
    above, below = sides(even_x[...], odd_x[...], even_i, first_i > 0, first_i + rows < count_i)
    place(-REACH, 0, above)
    place(rows, 0, below)
    left, right = sides(even_y[...], odd_y[...], even_j, first_j > 0, first_j + cols < count_j)
    place(0, -2, left)
    place(0, cols, right)
    corner = jnp.zeros((members, HALF, 1, depth), jnp.float32)
    for row in (-HALF, rows):
        place(row, -1, corner)
        place(row, cols, corner)

    sublane = lax.broadcasted_iota(jnp.int32, (span, 1), 0)
    amount_j = (first_j - GAP + sublane).astype(jnp.float32)
    place_j = lax.broadcasted_iota(jnp.int32, (cols, depth), 0)
    inner_j = (place_j > 0) & (place_j < cols - 1)

    @pl.loop(0, members)
    def _(member):
        c, make_u, make_v, lose_v, rest = constants(rates, member, depth, amount_j)
        make_u, lose_v, rest = [term[GAP : GAP + cols] for term in (make_u, lose_v, rest)]

        def image(read, row):
            i = (first_i + row).astype(jnp.float32)
            rows_by = lambda by: read(row + by, 0)
            return apply(c, depth, i, make_u, make_v, lose_v, rest, read(row, 0), rows_by, read(row, -1), read(row, 1))

        def read_field(row, start):
            return wide[member, pl.ds((row + REACH) * span + GAP + start, cols), :]

        def read_image(row, start):
            return wide_image[member, pl.ds((row + HALF) * span + GAP + start, cols), :]

        for row in range(-HALF, rows + HALF):
            inside = (first_i + row >= 0) & (first_i + row < count_i)
            value = image(read_field, row)
            if row < 0 or row >= rows:
                value = jnp.where(inside, value, 0.0)
            else:
                image_one[member, row] = value
            wide_image[member, pl.ds((row + HALF) * span + GAP, cols), :] = value

        products = [jnp.zeros((cols, depth), jnp.float32) for _ in range(6)]
        for row in range(rows):
            zero = field[member, row]
            one = image_one[member, row]
            two = jnp.where(inner_j, image(read_image, row), 0.0)
            image_two[member, row] = two
            terms = (zero * zero, zero * one, zero * two, one * one, one * two, two * two)
            products = [total + term for total, term in zip(products, terms)]
        for index, total in enumerate(products):
            parts[pl.ds(8 * index + member, 1), :] = jnp.sum(total, axis=0, keepdims=True)

        for at, column in enumerate((0, cols - 1, 1, cols - 2)):
            lines[member, at] = wide_image[member, pl.ds(GAP + column, tall, stride=span), :]
        for at, column in enumerate((0, cols - 1, -1, cols, -2, cols + 1)):
            lines[member, 4 + at] = wide[member, pl.ds(HALF * span + GAP + column, tall, stride=span), :]

    for index in range(6):
        parts[8 * index + members : 8 * index + 8, :] = jnp.zeros((8 - members, depth), jnp.float32)


def corners_kernel(lattice, cols, rates, lines, odd_corners, even_corners, parts, columns_two, message, edge, total):
    members, _, tall, depth = lines.shape
    rows = tall - 2 * HALF
    index_i, index_j = lax.axis_index("gx"), lax.axis_index("gy")
    first_i, first_j = index_i * rows, index_j * cols
    count_i, count_j = lattice
    upper, lower = sides(
        even_corners[...], odd_corners[...], index_i % 2 == 0, first_i > 0, first_i + rows < count_i
    )
    i = (first_i + lax.broadcasted_iota(jnp.int32, (rows, depth), 0)).astype(jnp.float32)
    total[...] = parts[...]
    for member in range(members):

        def line(at):
            return lines[member, at, pl.ds(HALF, rows), :]

        sums = [jnp.zeros((rows, depth), jnp.float32) for _ in range(3)]
        for side, column, beyond, inside in (
            (0, 0, -1, first_j > 0),
            (1, cols - 1, cols, first_j + cols < count_j),
        ):

            def at_column(column):
                amount_j = jnp.broadcast_to((first_j + column).astype(jnp.float32), (1, depth))
                return constants(rates, member, depth, amount_j)

            outer, fixed = edge.at[member, side, 0], edge.at[member, side, 1]
            outer[HALF : HALF + rows, :] = line(6 + side)
            for row in range(HALF):
                for first, corner in ((0, upper), (HALF + rows, lower)):
                    value = corner[member, row, side : side + 1, :]
                    outer[first + row : first + row + 1, :] = jnp.where(inside, value, 0.0)

            c, make_u, make_v, lose_v, rest = at_column(beyond)
            rows_by = lambda by: outer[pl.ds(HALF + by, rows), :]
            beside = (line(8), line(4)) if side == 0 else (line(5), line(9))
            value = apply(c, depth, i, make_u, make_v, lose_v, rest, rows_by(0), rows_by, *beside)
            image_beyond = jnp.where(inside, value, 0.0)

            c, make_u, make_v, lose_v, rest = at_column(column)
            gain = make_v if side == 0 else lose_v
            fixed[...] = lines[member, side]
            for first in (0, HALF + rows):
                fixed[first : first + HALF, :] = fixed[first : first + HALF, :] + gain * outer[first : first + HALF, :]

            rows_by = lambda by: fixed[pl.ds(HALF + by, rows), :]
            beside = (image_beyond, line(2)) if side == 0 else (line(3), image_beyond)
            two = apply(c, depth, i, make_u, make_v, lose_v, rest, rows_by(0), rows_by, *beside)
            columns_two[member, side] = two
            terms = (line(4 + side) * two, line(side) * two, two * two)
            sums = [value + term for value, term in zip(sums, terms)]
        for index, value in zip((2, 4, 5), sums):
            at = 8 * index + member
            total[at : at + 1, :] = total[at : at + 1, :] + jnp.sum(value, axis=0, keepdims=True)

    row = jnp.zeros((8, depth), jnp.float32)
    for index in range(6):
        value = jnp.sum(total[8 * index : 8 * index + 8], axis=1, keepdims=True)
        row = row + jnp.where(own_lane(8 * index), value, 0.0)
    message[...] = jnp.broadcast_to(jnp.sum(row, axis=0, keepdims=True), message.shape)


def product(left, right):
    a, b, c, d = left
    e, f, g, h = right
    return a * e + b * g, a * f + b * h, c * e + d * g, c * f + d * h


def first_column(h00, s01, h11):
    scale = tau_step / 2.0**squarings
    one = jnp.ones_like(h00)
    z1 = (scale * h00, scale * s01, scale * one, scale * h11)
    z2 = product(z1, z1)
    z3, z4 = product(z2, z1), product(z2, z2)
    weights = [1.0 / math.factorial(k + 1) for k in range(taylor_terms)]

    def block(first):
        w0, w1, w2, w3 = weights[first : first + 4]
        terms = [w1 * p + w2 * q + w3 * r for p, q, r in zip(z1, z2, z3)]
        return terms[0] + w0, terms[1], terms[2], terms[3] + w0

    phi = block(taylor_terms - 4)
    for first in range(taylor_terms - 8, -1, -4):
        phi = tuple(p + q for p, q in zip(product(z4, phi), block(first)))
    p00, p01, p10, p11 = product(z1, phi)
    p00, p11 = 1.0 + p00, 1.0 + p11
    q0, q1 = scale * phi[2], scale * phi[3]
    for _ in range(squarings):
        p00, p01, p10, p11, q0, q1 = (
            p00 * p00 + p01 * p10,
            p00 * p01 + p01 * p11,
            p10 * p00 + p11 * p10,
            p10 * p01 + p11 * p11,
            q0 * p00 + q1 * p10 + q0,
            q0 * p01 + q1 * p11 + q1,
        )
    return p00, p10, q0


def combine_kernel(gathered, field, image_one, image_two, columns_two, propagated, entries):
    members, rows, cols, depth = field.shape
    sums = jnp.broadcast_to(jnp.sum(gathered[...], axis=0, keepdims=True), (8, 128))
    g00, g01, g02, g11, g12, g22 = [
        jnp.broadcast_to(jnp.sum(jnp.where(own_lane(8 * index), sums, 0.0), axis=1, keepdims=True), (8, 128))
        for index in range(6)
    ]
    tiny = jnp.finfo(jnp.float32).tiny
    h00 = g01 / g00
    square_10 = jnp.maximum(g11 / g00 - h00 * h00, tiny)
    s01 = (g02 - h00 * g01) / g00
    h11 = ((g12 - h00 * g02) - h00 * (g11 - h00 * g01)) / (g00 * square_10)
    norm_2 = ((g22 - h00 * g12) - h00 * (g12 - h00 * g11)) / (g00 * square_10)
    h10 = jnp.sqrt(square_10)
    h01 = s01 / h10
    h21 = jnp.sqrt(jnp.maximum(norm_2 - h01 * h01 - h11 * h11, 0.0))
    e0, e1, e2 = first_column(h00, s01, h11)
    a2 = e2
    a1 = e1 - e2 * (h00 + h11)
    a0 = e0 - e1 * h00 - e2 * (s01 - h11 * h00)
    lane = lax.broadcasted_iota(jnp.int32, h00.shape, 1)
    table = h21
    for index, entry in enumerate((h00, h10, h01, h11)):
        table = jnp.where(lane == index, entry, table)
    entries[...] = (tau_step * table)[: entries.shape[0], : entries.shape[1]]
    place_j = lax.broadcasted_iota(jnp.int32, (cols, depth), 0)
    for member in range(members):
        b0, b1, b2 = [jnp.broadcast_to(a[member : member + 1], (cols, depth)) for a in (a0, a1, a2)]
        for row in range(rows):
            two = jnp.where(place_j == 0, columns_two[member, 0, row : row + 1], image_two[member, row])
            two = jnp.where(place_j == cols - 1, columns_two[member, 1, row : row + 1], two)
            propagated[member, row] = b0 * field[member, row] + b1 * image_one[member, row] + b2 * two


def shards(density, rate_table):
    members, rows, cols, depth = density.shape
    size_x, size_y = lax.axis_size("gx"), lax.axis_size("gy")
    devices = size_x * size_y
    vmem = pl.BlockSpec(memory_space=pltpu.VMEM)
    parity_x, parity_y = lax.axis_index("gx") % 2, lax.axis_index("gy") % 2

    def swap(axis, size, first, value):
        def partner(x, y):
            at = x if axis == "gx" else y
            other = at + 1 if (at - first) % 2 == 0 else at - 1
            if not 0 <= other < size:
                return (x, y ^ 1) if axis == "gx" else (x ^ 1, y)
            return (other, y) if axis == "gx" else (x, other)

        pairs = [
            (x * size_y + y, partner(x, y)[0] * size_y + partner(x, y)[1])
            for x in range(size_x)
            for y in range(size_y)
        ]
        return lax.ppermute(value, ("gx", "gy"), pairs)

    assert size_x % 2 == 0 and size_y % 2 == 0

    def swaps(axis, size, parity, initial, last):
        if initial is last:
            return swap(axis, size, 0, last), swap(axis, size, 1, last)
        is_even = parity == 0
        return (
            swap(axis, size, 0, jnp.where(is_even, last, initial)),
            swap(axis, size, 1, jnp.where(is_even, initial, last)),
        )

    if rows == REACH:
        even_x, odd_x = swaps("gx", size_x, parity_x, density, density)
    else:
        even_x, odd_x = swaps("gx", size_x, parity_x, density[:, :REACH], density[:, rows - REACH :])

    edge = jax.ShapeDtypeStruct((members, rows, 2, depth), jnp.float32)
    block = jax.ShapeDtypeStruct(density.shape, jnp.float32)
    for_odd, for_even, field = pl.pallas_call(
        edges_kernel,
        out_shape=[edge, edge, block],
        in_specs=[pl.BlockSpec(memory_space=pl.ANY)],
        out_specs=[vmem] * 3,
        scratch_shapes=[pltpu.SemaphoreType.DMA],
        compiler_params=pltpu.CompilerParams(vmem_limit_bytes=4 * 2**20),
        name="edges",
    )(density)
    odd_y = swap("gy", size_y, 1, for_odd)
    even_y = swap("gy", size_y, 0, for_even)

    even_x, odd_y, even_y = lax.optimization_barrier((even_x, odd_y, even_y))

    def corners(first):
        even, odd = even_y[:, first : first + HALF], odd_y[:, first : first + HALF]
        left = jnp.where(parity_y == 0, odd, even)[:, :, 1:]
        right = jnp.where(parity_y == 0, even, odd)[:, :, :1]
        return jnp.concatenate([left, right], axis=2)

    even_corners, odd_corners = swaps("gx", size_x, parity_x, corners(0), corners(rows - HALF))

    lattice = (size_x * rows, size_y * cols)
    tall, span = rows + 2 * HALF, cols + 2 * GAP
    image_one, image_two, lines, parts = pl.pallas_call(
        functools.partial(images_kernel, lattice),
        out_shape=[
            block,
            block,
            jax.ShapeDtypeStruct((members, 10, tall, depth), jnp.float32),
            jax.ShapeDtypeStruct((48, depth), jnp.float32),
        ],
        in_specs=[vmem] * 6,
        out_specs=[vmem] * 4,
        scratch_shapes=[
            pltpu.VMEM((members, (rows + 2 * REACH) * span, depth), jnp.float32),
            pltpu.VMEM((members, tall * span, depth), jnp.float32),
        ],
        compiler_params=pltpu.CompilerParams(vmem_limit_bytes=8 * 2**20),
        name="images",
    )(rate_table, field, even_x, odd_x, even_y, odd_y)

    columns_two, message = pl.pallas_call(
        functools.partial(corners_kernel, lattice, cols),
        out_shape=[
            jax.ShapeDtypeStruct((members, 2, rows, depth), jnp.float32),
            jax.ShapeDtypeStruct((devices, 128), jnp.float32),
        ],
        in_specs=[vmem] * 5,
        out_specs=[vmem, vmem],
        scratch_shapes=[
            pltpu.VMEM((members, 2, 2, tall, depth), jnp.float32),
            pltpu.VMEM((48, depth), jnp.float32),
        ],
        compiler_params=pltpu.CompilerParams(vmem_limit_bytes=4 * 2**20),
        name="corners",
    )(rate_table, lines, odd_corners, even_corners, parts)

    gathered = lax.all_to_all(message, ("gx", "gy"), 0, 0, tiled=True)

    return pl.pallas_call(
        combine_kernel,
        out_shape=[block, jax.ShapeDtypeStruct((members, 5), jnp.float32)],
        in_specs=[vmem] * 5,
        out_specs=[vmem, vmem],
        compiler_params=pltpu.CompilerParams(vmem_limit_bytes=8 * 2**20),
        name="combine",
    )(gathered, field, image_one, image_two, columns_two)


def solution(mesh):
    in_specs = (P(None, "gx", "gy", None), P())
    out_specs = (P(None, "gx", "gy", None), P())
    return jax.shard_map(shards, mesh=mesh, in_specs=in_specs, out_specs=out_specs, check_vma=False)
```

```python
import functools
import math

import jax
import jax.numpy as jnp
from jax import lax
from jax.experimental import pallas as pl
from jax.experimental.pallas import tpu as pltpu
from jax.sharding import PartitionSpec as P

tau_step = 0.01
taylor_terms = 16
squarings = 4
REACH = 4
HALF = 2
GAP = 8


def edges_kernel(field, for_odd, for_even, block, arrived):
    copy = pltpu.make_async_copy(field, block, arrived)
    copy.start()
    is_even = lax.axis_index("gy") % 2 == 0
    cols = block.shape[2]
    copy.wait()
    low, high = block[:, :, :2], block[:, :, cols - 2 :]
    for_even[...] = jnp.where(is_even, high, low)
    for_odd[...] = jnp.where(is_even, low, high)


def own_lane(first):
    row = lax.broadcasted_iota(jnp.int32, (8, 128), 0)
    return lax.broadcasted_iota(jnp.int32, (8, 128), 1) == first + row


def lanes(depth):
    lane = lax.broadcasted_iota(jnp.int32, (1, depth), 1)
    amount_k = lane.astype(jnp.float32)
    return amount_k, jnp.where(lane < depth - 1, amount_k + 1.0, 0.0), jnp.where(lane > 0, 1.0, 0.0)


def apply(c, depth, i, make_u, make_v, lose_v, rest, centre, rows_by, left, right):
    _, above_k, inner_k = lanes(depth)
    value = make_u * rows_by(-1) + (c[1] * (i + 1.0)) * rows_by(1)
    value = value + make_v * left
    value = value + lose_v * right
    pair = pltpu.roll(rows_by(2), 1, 1)
    value = value + (inner_k * (0.5 * c[4] * (i + 2.0) * (i + 1.0))) * pair
    split = c[5] * rows_by(-2) + c[6] * centre
    value = value + above_k * pltpu.roll(split, depth - 1, 1)
    out = rest + (c[1] * i + 0.5 * c[4] * i * (i - 1.0))
    return value - out * centre


def constants(rates, member, depth, amount_j):
    c = [jnp.broadcast_to(rates[member : member + 1, r : r + 1], (1, depth)) for r in range(9)]
    amount_k = lanes(depth)[0]
    ratio_j, ratio_k = amount_j / c[7], amount_k / c[8]
    make_u = c[0] / (1.0 + ratio_j * ratio_j)
    make_v = c[2] / (1.0 + ratio_k * ratio_k)
    lose_v = c[3] * (amount_j + 1.0)
    rest = make_u + make_v + (c[3] * amount_j + (c[5] + c[6]) * amount_k)
    return c, make_u, make_v, lose_v, rest


def sides(even, odd, is_even, lower_inside, higher_inside):
    lower, higher = jnp.where(is_even, odd, even), jnp.where(is_even, even, odd)
    return jnp.where(lower_inside, lower, 0.0), jnp.where(higher_inside, higher, 0.0)


def images_kernel(
    lattice,
    rates,
    field,
    even_x,
    odd_x,
    even_y,
    odd_y,
    image_one,
    image_two,
    lines,
    parts,
    wide,
    wide_image,
):
    members, rows, cols, depth = field.shape
    span = cols + 2 * GAP
    tall = rows + 2 * HALF
    index_i, index_j = lax.axis_index("gx"), lax.axis_index("gy")
    first_i, first_j = index_i * rows, index_j * cols
    even_i, even_j = index_i % 2 == 0, index_j % 2 == 0
    count_i, count_j = lattice

    def place(row, start, values):
        for at in range(values.shape[1]):
            first = (row + REACH + at) * span + GAP + start
            wide[:, first : first + values.shape[2]] = values[:, at]

    place(0, 0, field[...])
    above, below = sides(even_x[...], odd_x[...], even_i, first_i > 0, first_i + rows < count_i)
    place(-REACH, 0, above)
    place(rows, 0, below)
    left, right = sides(even_y[...], odd_y[...], even_j, first_j > 0, first_j + cols < count_j)
    place(0, -2, left)
    place(0, cols, right)
    corner = jnp.zeros((members, HALF, 1, depth), jnp.float32)
    for row in (-HALF, rows):
        place(row, -1, corner)
        place(row, cols, corner)

    sublane = lax.broadcasted_iota(jnp.int32, (span, 1), 0)
    amount_j = (first_j - GAP + sublane).astype(jnp.float32)
    place_j = lax.broadcasted_iota(jnp.int32, (cols, depth), 0)
    inner_j = (place_j > 0) & (place_j < cols - 1)

    for member in range(members):
        c, make_u, make_v, lose_v, rest = constants(rates, member, depth, amount_j)
        make_u, lose_v, rest = [term[GAP : GAP + cols] for term in (make_u, lose_v, rest)]

        def image(read, row):
            i = (first_i + row).astype(jnp.float32)
            rows_by = lambda by: read(row + by, 0)
            return apply(c, depth, i, make_u, make_v, lose_v, rest, read(row, 0), rows_by, read(row, -1), read(row, 1))

        def read_field(row, start):
            return wide[member, pl.ds((row + REACH) * span + GAP + start, cols), :]

        def read_image(row, start):
            return wide_image[member, pl.ds((row + HALF) * span + GAP + start, cols), :]

        for row in range(-HALF, rows + HALF):
            inside = (first_i + row >= 0) & (first_i + row < count_i)
            value = image(read_field, row)
            if row < 0 or row >= rows:
                value = jnp.where(inside, value, 0.0)
            else:
                image_one[member, row] = value
            wide_image[member, pl.ds((row + HALF) * span + GAP, cols), :] = value

        products = [jnp.zeros((cols, depth), jnp.float32) for _ in range(6)]
        for row in range(rows):
            zero = field[member, row]
            one = image_one[member, row]
            two = jnp.where(inner_j, image(read_image, row), 0.0)
            image_two[member, row] = two
            terms = (zero * zero, zero * one, zero * two, one * one, one * two, two * two)
            products = [total + term for total, term in zip(products, terms)]
        for index, total in enumerate(products):
            parts[8 * index + member : 8 * index + member + 1, :] = jnp.sum(total, axis=0, keepdims=True)

        for at, column in enumerate((0, cols - 1, 1, cols - 2)):
            lines[member, at] = wide_image[member, pl.ds(GAP + column, tall, stride=span), :]
        for at, column in enumerate((0, cols - 1, -1, cols, -2, cols + 1)):
            lines[member, 4 + at] = wide[member, pl.ds(HALF * span + GAP + column, tall, stride=span), :]

    for index in range(6):
        parts[8 * index + members : 8 * index + 8, :] = jnp.zeros((8 - members, depth), jnp.float32)


def corners_kernel(lattice, cols, rates, lines, odd_corners, even_corners, parts, columns_two, message, edge, total):
    members, _, tall, depth = lines.shape
    rows = tall - 2 * HALF
    index_i, index_j = lax.axis_index("gx"), lax.axis_index("gy")
    first_i, first_j = index_i * rows, index_j * cols
    count_i, count_j = lattice
    upper, lower = sides(
        even_corners[...], odd_corners[...], index_i % 2 == 0, first_i > 0, first_i + rows < count_i
    )
    i = (first_i + lax.broadcasted_iota(jnp.int32, (rows, depth), 0)).astype(jnp.float32)
    total[...] = parts[...]
    for member in range(members):

        def line(at):
            return lines[member, at, pl.ds(HALF, rows), :]

        sums = [jnp.zeros((rows, depth), jnp.float32) for _ in range(3)]
        for side, column, beyond, inside in (
            (0, 0, -1, first_j > 0),
            (1, cols - 1, cols, first_j + cols < count_j),
        ):

            def at_column(column):
                amount_j = jnp.broadcast_to((first_j + column).astype(jnp.float32), (1, depth))
                return constants(rates, member, depth, amount_j)

            outer, fixed = edge.at[member, side, 0], edge.at[member, side, 1]
            outer[HALF : HALF + rows, :] = line(6 + side)
            for row in range(HALF):
                for first, corner in ((0, upper), (HALF + rows, lower)):
                    value = corner[member, row, side : side + 1, :]
                    outer[first + row : first + row + 1, :] = jnp.where(inside, value, 0.0)

            c, make_u, make_v, lose_v, rest = at_column(beyond)
            rows_by = lambda by: outer[pl.ds(HALF + by, rows), :]
            beside = (line(8), line(4)) if side == 0 else (line(5), line(9))
            value = apply(c, depth, i, make_u, make_v, lose_v, rest, rows_by(0), rows_by, *beside)
            image_beyond = jnp.where(inside, value, 0.0)

            c, make_u, make_v, lose_v, rest = at_column(column)
            gain = make_v if side == 0 else lose_v
            fixed[...] = lines[member, side]
            for first in (0, HALF + rows):
                fixed[first : first + HALF, :] = fixed[first : first + HALF, :] + gain * outer[first : first + HALF, :]

            rows_by = lambda by: fixed[pl.ds(HALF + by, rows), :]
            beside = (image_beyond, line(2)) if side == 0 else (line(3), image_beyond)
            two = apply(c, depth, i, make_u, make_v, lose_v, rest, rows_by(0), rows_by, *beside)
            columns_two[member, side] = two
            terms = (line(4 + side) * two, line(side) * two, two * two)
            sums = [value + term for value, term in zip(sums, terms)]
        for index, value in zip((2, 4, 5), sums):
            at = 8 * index + member
            total[at : at + 1, :] = total[at : at + 1, :] + jnp.sum(value, axis=0, keepdims=True)

    row = jnp.zeros((8, depth), jnp.float32)
    for index in range(6):
        value = jnp.sum(total[8 * index : 8 * index + 8], axis=1, keepdims=True)
        row = row + jnp.where(own_lane(8 * index), value, 0.0)
    message[...] = jnp.broadcast_to(jnp.sum(row, axis=0, keepdims=True), message.shape)


def product(left, right):
    a, b, c, d = left
    e, f, g, h = right
    return a * e + b * g, a * f + b * h, c * e + d * g, c * f + d * h


def first_column(h00, s01, h11):
    scale = tau_step / 2.0**squarings
    one = jnp.ones_like(h00)
    z1 = (scale * h00, scale * s01, scale * one, scale * h11)
    z2 = product(z1, z1)
    z3, z4 = product(z2, z1), product(z2, z2)
    weights = [1.0 / math.factorial(k + 1) for k in range(taylor_terms)]

    def block(first):
        w0, w1, w2, w3 = weights[first : first + 4]
        terms = [w1 * p + w2 * q + w3 * r for p, q, r in zip(z1, z2, z3)]
        return terms[0] + w0, terms[1], terms[2], terms[3] + w0

    phi = block(taylor_terms - 4)
    for first in range(taylor_terms - 8, -1, -4):
        phi = tuple(p + q for p, q in zip(product(z4, phi), block(first)))
    p00, p01, p10, p11 = product(z1, phi)
    p00, p11 = 1.0 + p00, 1.0 + p11
    q0, q1 = scale * phi[2], scale * phi[3]
    for _ in range(squarings):
        p00, p01, p10, p11, q0, q1 = (
            p00 * p00 + p01 * p10,
            p00 * p01 + p01 * p11,
            p10 * p00 + p11 * p10,
            p10 * p01 + p11 * p11,
            q0 * p00 + q1 * p10 + q0,
            q0 * p01 + q1 * p11 + q1,
        )
    return p00, p10, q0


def combine_kernel(gathered, field, image_one, image_two, columns_two, propagated, entries):
    members, rows, cols, depth = field.shape
    sums = jnp.broadcast_to(jnp.sum(gathered[...], axis=0, keepdims=True), (8, 128))
    g00, g01, g02, g11, g12, g22 = [
        jnp.broadcast_to(jnp.sum(jnp.where(own_lane(8 * index), sums, 0.0), axis=1, keepdims=True), (8, 128))
        for index in range(6)
    ]
    tiny = jnp.finfo(jnp.float32).tiny
    h00 = g01 / g00
    square_10 = jnp.maximum(g11 / g00 - h00 * h00, tiny)
    s01 = (g02 - h00 * g01) / g00
    h11 = ((g12 - h00 * g02) - h00 * (g11 - h00 * g01)) / (g00 * square_10)
    norm_2 = ((g22 - h00 * g12) - h00 * (g12 - h00 * g11)) / (g00 * square_10)
    h10 = jnp.sqrt(square_10)
    h01 = s01 / h10
    h21 = jnp.sqrt(jnp.maximum(norm_2 - h01 * h01 - h11 * h11, 0.0))
    e0, e1, e2 = first_column(h00, s01, h11)
    a2 = e2
    a1 = e1 - e2 * (h00 + h11)
    a0 = e0 - e1 * h00 - e2 * (s01 - h11 * h00)
    lane = lax.broadcasted_iota(jnp.int32, h00.shape, 1)
    table = h21
    for index, entry in enumerate((h00, h10, h01, h11)):
        table = jnp.where(lane == index, entry, table)
    entries[...] = (tau_step * table)[: entries.shape[0], : entries.shape[1]]
    place_j = lax.broadcasted_iota(jnp.int32, (cols, depth), 0)
    for member in range(members):
        b0, b1, b2 = [jnp.broadcast_to(a[member : member + 1], (cols, depth)) for a in (a0, a1, a2)]
        for row in range(rows):
            two = jnp.where(place_j == 0, columns_two[member, 0, row : row + 1], image_two[member, row])
            two = jnp.where(place_j == cols - 1, columns_two[member, 1, row : row + 1], two)
            propagated[member, row] = b0 * field[member, row] + b1 * image_one[member, row] + b2 * two


def shards(density, rate_table):
    members, rows, cols, depth = density.shape
    size_x, size_y = lax.axis_size("gx"), lax.axis_size("gy")
    devices = size_x * size_y
    vmem = pl.BlockSpec(memory_space=pltpu.VMEM)
    parity_x, parity_y = lax.axis_index("gx") % 2, lax.axis_index("gy") % 2

    def swap(axis, size, first, value):
        def partner(x, y):
            at = x if axis == "gx" else y
            other = at + 1 if (at - first) % 2 == 0 else at - 1
            if not 0 <= other < size:
                return (x, y ^ 1) if axis == "gx" else (x ^ 1, y)
            return (other, y) if axis == "gx" else (x, other)

        pairs = [
            (x * size_y + y, partner(x, y)[0] * size_y + partner(x, y)[1])
            for x in range(size_x)
            for y in range(size_y)
        ]
        return lax.ppermute(value, ("gx", "gy"), pairs)

    assert size_x % 2 == 0 and size_y % 2 == 0

    def swaps(axis, size, parity, initial, last):
        if initial is last:
            return swap(axis, size, 0, last), swap(axis, size, 1, last)
        is_even = parity == 0
        return (
            swap(axis, size, 0, jnp.where(is_even, last, initial)),
            swap(axis, size, 1, jnp.where(is_even, initial, last)),
        )

    if rows == REACH:
        even_x, odd_x = swaps("gx", size_x, parity_x, density, density)
    else:
        even_x, odd_x = swaps("gx", size_x, parity_x, density[:, :REACH], density[:, rows - REACH :])

    edge = jax.ShapeDtypeStruct((members, rows, 2, depth), jnp.float32)
    block = jax.ShapeDtypeStruct(density.shape, jnp.float32)
    for_odd, for_even, field = pl.pallas_call(
        edges_kernel,
        out_shape=[edge, edge, block],
        in_specs=[pl.BlockSpec(memory_space=pl.ANY)],
        out_specs=[vmem] * 3,
        scratch_shapes=[pltpu.SemaphoreType.DMA],
        compiler_params=pltpu.CompilerParams(vmem_limit_bytes=4 * 2**20),
        name="edges",
    )(density)
    odd_y = swap("gy", size_y, 1, for_odd)
    even_y = swap("gy", size_y, 0, for_even)

    even_x, odd_y, even_y = lax.optimization_barrier((even_x, odd_y, even_y))

    def corners(first):
        even, odd = even_y[:, first : first + HALF], odd_y[:, first : first + HALF]
        left = jnp.where(parity_y == 0, odd, even)[:, :, 1:]
        right = jnp.where(parity_y == 0, even, odd)[:, :, :1]
        return jnp.concatenate([left, right], axis=2)

    even_corners, odd_corners = swaps("gx", size_x, parity_x, corners(0), corners(rows - HALF))

    lattice = (size_x * rows, size_y * cols)
    tall, span = rows + 2 * HALF, cols + 2 * GAP
    image_one, image_two, lines, parts = pl.pallas_call(
        functools.partial(images_kernel, lattice),
        out_shape=[
            block,
            block,
            jax.ShapeDtypeStruct((members, 10, tall, depth), jnp.float32),
            jax.ShapeDtypeStruct((48, depth), jnp.float32),
        ],
        in_specs=[vmem] * 6,
        out_specs=[vmem] * 4,
        scratch_shapes=[
            pltpu.VMEM((members, (rows + 2 * REACH) * span, depth), jnp.float32),
            pltpu.VMEM((members, tall * span, depth), jnp.float32),
        ],
        compiler_params=pltpu.CompilerParams(vmem_limit_bytes=8 * 2**20),
        name="images",
    )(rate_table, field, even_x, odd_x, even_y, odd_y)

    columns_two, message = pl.pallas_call(
        functools.partial(corners_kernel, lattice, cols),
        out_shape=[
            jax.ShapeDtypeStruct((members, 2, rows, depth), jnp.float32),
            jax.ShapeDtypeStruct((devices, 128), jnp.float32),
        ],
        in_specs=[vmem] * 5,
        out_specs=[vmem, vmem],
        scratch_shapes=[
            pltpu.VMEM((members, 2, 2, tall, depth), jnp.float32),
            pltpu.VMEM((48, depth), jnp.float32),
        ],
        compiler_params=pltpu.CompilerParams(vmem_limit_bytes=4 * 2**20),
        name="corners",
    )(rate_table, lines, odd_corners, even_corners, parts)

    gathered = lax.all_to_all(message, ("gy", "gx"), 0, 0, tiled=True)

    return pl.pallas_call(
        combine_kernel,
        out_shape=[block, jax.ShapeDtypeStruct((members, 5), jnp.float32)],
        in_specs=[vmem] * 5,
        out_specs=[vmem, vmem],
        compiler_params=pltpu.CompilerParams(vmem_limit_bytes=8 * 2**20),
        name="combine",
    )(gathered, field, image_one, image_two, columns_two)


def solution(mesh):
    in_specs = (P(None, "gx", "gy", None), P())
    out_specs = (P(None, "gx", "gy", None), P())
    return jax.shard_map(shards, mesh=mesh, in_specs=in_specs, out_specs=out_specs, check_vma=False)
```

```python
import functools
import math

import jax
import jax.numpy as jnp
from jax import lax
from jax.experimental import pallas as pl
from jax.experimental.pallas import tpu as pltpu
from jax.sharding import PartitionSpec as P

tau_step = 0.01
taylor_terms = 16
squarings = 4
REACH = 4
HALF = 2
GAP = 8


def edges_kernel(field, for_odd, for_even, block, arrived):
    copy = pltpu.make_async_copy(field, block, arrived)
    copy.start()
    is_even = lax.axis_index("gy") % 2 == 0
    cols = block.shape[2]
    copy.wait()
    low, high = block[:, :, :2], block[:, :, cols - 2 :]
    for_even[...] = jnp.where(is_even, high, low)
    for_odd[...] = jnp.where(is_even, low, high)


def own_lane(first):
    row = lax.broadcasted_iota(jnp.int32, (8, 128), 0)
    return lax.broadcasted_iota(jnp.int32, (8, 128), 1) == first + row


def lanes(depth):
    lane = lax.broadcasted_iota(jnp.int32, (1, depth), 1)
    amount_k = lane.astype(jnp.float32)
    return amount_k, jnp.where(lane < depth - 1, amount_k + 1.0, 0.0), jnp.where(lane > 0, 1.0, 0.0)


def apply(c, depth, i, make_u, make_v, lose_v, rest, centre, rows_by, left, right):
    _, above_k, inner_k = lanes(depth)
    value = make_u * rows_by(-1) + (c[1] * (i + 1.0)) * rows_by(1)
    value = value + make_v * left
    value = value + lose_v * right
    pair = pltpu.roll(rows_by(2), 1, 1)
    value = value + (inner_k * (0.5 * c[4] * (i + 2.0) * (i + 1.0))) * pair
    split = c[5] * rows_by(-2) + c[6] * centre
    value = value + above_k * pltpu.roll(split, depth - 1, 1)
    out = rest + (c[1] * i + 0.5 * c[4] * i * (i - 1.0))
    return value - out * centre


def constants(rates, member, depth, amount_j):
    c = [jnp.broadcast_to(rates[member : member + 1, r : r + 1], (1, depth)) for r in range(9)]
    amount_k = lanes(depth)[0]
    ratio_j, ratio_k = amount_j / c[7], amount_k / c[8]
    make_u = c[0] / (1.0 + ratio_j * ratio_j)
    make_v = c[2] / (1.0 + ratio_k * ratio_k)
    lose_v = c[3] * (amount_j + 1.0)
    rest = make_u + make_v + (c[3] * amount_j + (c[5] + c[6]) * amount_k)
    return c, make_u, make_v, lose_v, rest


def sides(even, odd, is_even, lower_inside, higher_inside):
    lower, higher = jnp.where(is_even, odd, even), jnp.where(is_even, even, odd)
    return jnp.where(lower_inside, lower, 0.0), jnp.where(higher_inside, higher, 0.0)


def images_kernel(
    lattice,
    rates,
    field,
    even_x,
    odd_x,
    even_y,
    odd_y,
    image_one,
    image_two,
    lines,
    parts,
    wide,
    wide_image,
):
    members, rows, cols, depth = field.shape
    span = cols + 2 * GAP
    tall = rows + 2 * HALF
    index_i, index_j = lax.axis_index("gx"), lax.axis_index("gy")
    first_i, first_j = index_i * rows, index_j * cols
    even_i, even_j = index_i % 2 == 0, index_j % 2 == 0
    count_i, count_j = lattice

    def place(row, start, values):
        for at in range(values.shape[1]):
            first = (row + REACH + at) * span + GAP + start
            wide[:, first : first + values.shape[2]] = values[:, at]

    place(0, 0, field[...])
    above, below = sides(even_x[...], odd_x[...], even_i, first_i > 0, first_i + rows < count_i)
    place(-REACH, 0, above)
    place(rows, 0, below)
    left, right = sides(even_y[...], odd_y[...], even_j, first_j > 0, first_j + cols < count_j)
    place(0, -2, left)
    place(0, cols, right)
    corner = jnp.zeros((members, HALF, 1, depth), jnp.float32)
    for row in (-HALF, rows):
        place(row, -1, corner)
        place(row, cols, corner)

    sublane = lax.broadcasted_iota(jnp.int32, (span, 1), 0)
    amount_j = (first_j - GAP + sublane).astype(jnp.float32)
    place_j = lax.broadcasted_iota(jnp.int32, (cols, depth), 0)
    inner_j = (place_j > 0) & (place_j < cols - 1)

    for member in range(members):
        c, make_u, make_v, lose_v, rest = constants(rates, member, depth, amount_j)
        make_u, lose_v, rest = [term[GAP : GAP + cols] for term in (make_u, lose_v, rest)]

        def image(read, row):
            i = (first_i + row).astype(jnp.float32)
            rows_by = lambda by: read(row + by, 0)
            return apply(c, depth, i, make_u, make_v, lose_v, rest, read(row, 0), rows_by, read(row, -1), read(row, 1))

        def read_field(row, start):
            return wide[member, pl.ds((row + REACH) * span + GAP + start, cols), :]

        def read_image(row, start):
            return wide_image[member, pl.ds((row + HALF) * span + GAP + start, cols), :]

        for row in range(-HALF, rows + HALF):
            inside = (first_i + row >= 0) & (first_i + row < count_i)
            value = image(read_field, row)
            if row < 0 or row >= rows:
                value = jnp.where(inside, value, 0.0)
            else:
                image_one[member, row] = value
            wide_image[member, pl.ds((row + HALF) * span + GAP, cols), :] = value

        products = [jnp.zeros((cols, depth), jnp.float32) for _ in range(6)]
        for row in range(rows):
            zero = field[member, row]
            one = image_one[member, row]
            two = jnp.where(inner_j, image(read_image, row), 0.0)
            image_two[member, row] = two
            terms = (zero * zero, zero * one, zero * two, one * one, one * two, two * two)
            products = [total + term for total, term in zip(products, terms)]
        for index, total in enumerate(products):
            parts[8 * index + member : 8 * index + member + 1, :] = jnp.sum(total, axis=0, keepdims=True)

        for at, column in enumerate((0, cols - 1, 1, cols - 2)):
            lines[member, at] = wide_image[member, pl.ds(GAP + column, tall, stride=span), :]
        for at, column in enumerate((0, cols - 1, -1, cols, -2, cols + 1)):
            lines[member, 4 + at] = wide[member, pl.ds(HALF * span + GAP + column, tall, stride=span), :]

    for index in range(6):
        parts[8 * index + members : 8 * index + 8, :] = jnp.zeros((8 - members, depth), jnp.float32)


def corners_kernel(lattice, cols, rates, lines, odd_corners, even_corners, parts, columns_two, message, edge, total):
    members, _, tall, depth = lines.shape
    rows = tall - 2 * HALF
    index_i, index_j = lax.axis_index("gx"), lax.axis_index("gy")
    first_i, first_j = index_i * rows, index_j * cols
    count_i, count_j = lattice
    upper, lower = sides(
        even_corners[...], odd_corners[...], index_i % 2 == 0, first_i > 0, first_i + rows < count_i
    )
    i = (first_i + lax.broadcasted_iota(jnp.int32, (rows, depth), 0)).astype(jnp.float32)
    total[...] = parts[...]
    for member in range(members):

        def line(at):
            return lines[member, at, pl.ds(HALF, rows), :]

        sums = [jnp.zeros((rows, depth), jnp.float32) for _ in range(3)]
        for side, column, beyond, inside in (
            (0, 0, -1, first_j > 0),
            (1, cols - 1, cols, first_j + cols < count_j),
        ):

            def at_column(column):
                amount_j = jnp.broadcast_to((first_j + column).astype(jnp.float32), (1, depth))
                return constants(rates, member, depth, amount_j)

            outer, fixed = edge.at[member, side, 0], edge.at[member, side, 1]
            outer[HALF : HALF + rows, :] = line(6 + side)
            for row in range(HALF):
                for first, corner in ((0, upper), (HALF + rows, lower)):
                    value = corner[member, row, side : side + 1, :]
                    outer[first + row : first + row + 1, :] = jnp.where(inside, value, 0.0)

            c, make_u, make_v, lose_v, rest = at_column(beyond)
            rows_by = lambda by: outer[pl.ds(HALF + by, rows), :]
            beside = (line(8), line(4)) if side == 0 else (line(5), line(9))
            value = apply(c, depth, i, make_u, make_v, lose_v, rest, rows_by(0), rows_by, *beside)
            image_beyond = jnp.where(inside, value, 0.0)

            c, make_u, make_v, lose_v, rest = at_column(column)
            gain = make_v if side == 0 else lose_v
            fixed[...] = lines[member, side]
            for first in (0, HALF + rows):
                fixed[first : first + HALF, :] = fixed[first : first + HALF, :] + gain * outer[first : first + HALF, :]

            rows_by = lambda by: fixed[pl.ds(HALF + by, rows), :]
            beside = (image_beyond, line(2)) if side == 0 else (line(3), image_beyond)
            two = apply(c, depth, i, make_u, make_v, lose_v, rest, rows_by(0), rows_by, *beside)
            columns_two[member, side] = two
            terms = (line(4 + side) * two, line(side) * two, two * two)
            sums = [value + term for value, term in zip(sums, terms)]
        for index, value in zip((2, 4, 5), sums):
            at = 8 * index + member
            total[at : at + 1, :] = total[at : at + 1, :] + jnp.sum(value, axis=0, keepdims=True)

    row = jnp.zeros((8, depth), jnp.float32)
    for index in range(6):
        value = jnp.sum(total[8 * index : 8 * index + 8], axis=1, keepdims=True)
        row = row + jnp.where(own_lane(8 * index), value, 0.0)
    message[...] = jnp.broadcast_to(jnp.sum(row, axis=0, keepdims=True), message.shape)


def product(left, right):
    a, b, c, d = left
    e, f, g, h = right
    return a * e + b * g, a * f + b * h, c * e + d * g, c * f + d * h


def first_column(h00, s01, h11):
    scale = tau_step / 2.0**squarings
    one = jnp.ones_like(h00)
    z1 = (scale * h00, scale * s01, scale * one, scale * h11)
    z2 = product(z1, z1)
    z3, z4 = product(z2, z1), product(z2, z2)
    weights = [1.0 / math.factorial(k + 1) for k in range(taylor_terms)]

    def block(first):
        w0, w1, w2, w3 = weights[first : first + 4]
        terms = [w1 * p + w2 * q + w3 * r for p, q, r in zip(z1, z2, z3)]
        return terms[0] + w0, terms[1], terms[2], terms[3] + w0

    phi = block(taylor_terms - 4)
    for first in range(taylor_terms - 8, -1, -4):
        phi = tuple(p + q for p, q in zip(product(z4, phi), block(first)))
    p00, p01, p10, p11 = product(z1, phi)
    p00, p11 = 1.0 + p00, 1.0 + p11
    q0, q1 = scale * phi[2], scale * phi[3]
    for _ in range(squarings):
        p00, p01, p10, p11, q0, q1 = (
            p00 * p00 + p01 * p10,
            p00 * p01 + p01 * p11,
            p10 * p00 + p11 * p10,
            p10 * p01 + p11 * p11,
            q0 * p00 + q1 * p10 + q0,
            q0 * p01 + q1 * p11 + q1,
        )
    return p00, p10, q0


def combine_kernel(gathered, field, image_one, image_two, columns_two, propagated, entries):
    members, rows, cols, depth = field.shape
    sums = jnp.broadcast_to(jnp.sum(gathered[...], axis=0, keepdims=True), (8, 128))
    g00, g01, g02, g11, g12, g22 = [
        jnp.broadcast_to(jnp.sum(jnp.where(own_lane(8 * index), sums, 0.0), axis=1, keepdims=True), (8, 128))
        for index in range(6)
    ]
    tiny = jnp.finfo(jnp.float32).tiny
    h00 = g01 / g00
    square_10 = jnp.maximum(g11 / g00 - h00 * h00, tiny)
    s01 = (g02 - h00 * g01) / g00
    h11 = ((g12 - h00 * g02) - h00 * (g11 - h00 * g01)) / (g00 * square_10)
    norm_2 = ((g22 - h00 * g12) - h00 * (g12 - h00 * g11)) / (g00 * square_10)
    h10 = jnp.sqrt(square_10)
    h01 = s01 / h10
    h21 = jnp.sqrt(jnp.maximum(norm_2 - h01 * h01 - h11 * h11, 0.0))
    e0, e1, e2 = first_column(h00, s01, h11)
    a2 = e2
    a1 = e1 - e2 * (h00 + h11)
    a0 = e0 - e1 * h00 - e2 * (s01 - h11 * h00)
    lane = lax.broadcasted_iota(jnp.int32, h00.shape, 1)
    table = h21
    for index, entry in enumerate((h00, h10, h01, h11)):
        table = jnp.where(lane == index, entry, table)
    entries[...] = (tau_step * table)[: entries.shape[0], : entries.shape[1]]
    place_j = lax.broadcasted_iota(jnp.int32, (cols, depth), 0)
    for member in range(members):
        b0, b1, b2 = [jnp.broadcast_to(a[member : member + 1], (cols, depth)) for a in (a0, a1, a2)]
        for row in range(rows):
            two = jnp.where(place_j == 0, columns_two[member, 0, row : row + 1], image_two[member, row])
            two = jnp.where(place_j == cols - 1, columns_two[member, 1, row : row + 1], two)
            propagated[member, row] = b0 * field[member, row] + b1 * image_one[member, row] + b2 * two


def shards(density, rate_table):
    members, rows, cols, depth = density.shape
    size_x, size_y = lax.axis_size("gx"), lax.axis_size("gy")
    devices = size_x * size_y
    vmem = pl.BlockSpec(memory_space=pltpu.VMEM)
    parity_x, parity_y = lax.axis_index("gx") % 2, lax.axis_index("gy") % 2

    def swap(axis, size, first, value):
        def partner(x, y):
            at = x if axis == "gx" else y
            other = at + 1 if (at - first) % 2 == 0 else at - 1
            if not 0 <= other < size:
                return (x, y ^ 1) if axis == "gx" else (x, other % size)
            return (other, y) if axis == "gx" else (x, other)

        pairs = [
            (x * size_y + y, partner(x, y)[0] * size_y + partner(x, y)[1])
            for x in range(size_x)
            for y in range(size_y)
        ]
        return lax.ppermute(value, ("gx", "gy"), pairs)

    assert size_x % 2 == 0 and size_y % 2 == 0

    def swaps(axis, size, parity, initial, last):
        if initial is last:
            return swap(axis, size, 0, last), swap(axis, size, 1, last)
        is_even = parity == 0
        return (
            swap(axis, size, 0, jnp.where(is_even, last, initial)),
            swap(axis, size, 1, jnp.where(is_even, initial, last)),
        )

    if rows == REACH:
        even_x, odd_x = swaps("gx", size_x, parity_x, density, density)
    else:
        even_x, odd_x = swaps("gx", size_x, parity_x, density[:, :REACH], density[:, rows - REACH :])

    edge = jax.ShapeDtypeStruct((members, rows, 2, depth), jnp.float32)
    block = jax.ShapeDtypeStruct(density.shape, jnp.float32)
    for_odd, for_even, field = pl.pallas_call(
        edges_kernel,
        out_shape=[edge, edge, block],
        in_specs=[pl.BlockSpec(memory_space=pl.ANY)],
        out_specs=[vmem] * 3,
        scratch_shapes=[pltpu.SemaphoreType.DMA],
        compiler_params=pltpu.CompilerParams(vmem_limit_bytes=4 * 2**20),
        name="edges",
    )(density)
    odd_y = swap("gy", size_y, 1, for_odd)
    even_y = swap("gy", size_y, 0, for_even)

    even_x, even_y, odd_y = lax.optimization_barrier((even_x, even_y, odd_y))

    def corners(first):
        even, odd = even_y[:, first : first + HALF], odd_y[:, first : first + HALF]
        left = jnp.where(parity_y == 0, odd, even)[:, :, 1:]
        right = jnp.where(parity_y == 0, even, odd)[:, :, :1]
        return jnp.concatenate([left, right], axis=2)

    even_corners, odd_corners = swaps("gx", size_x, parity_x, corners(0), corners(rows - HALF))

    lattice = (size_x * rows, size_y * cols)
    tall, span = rows + 2 * HALF, cols + 2 * GAP
    image_one, image_two, lines, parts = pl.pallas_call(
        functools.partial(images_kernel, lattice),
        out_shape=[
            block,
            block,
            jax.ShapeDtypeStruct((members, 10, tall, depth), jnp.float32),
            jax.ShapeDtypeStruct((48, depth), jnp.float32),
        ],
        in_specs=[vmem] * 6,
        out_specs=[vmem] * 4,
        scratch_shapes=[
            pltpu.VMEM((members, (rows + 2 * REACH) * span, depth), jnp.float32),
            pltpu.VMEM((members, tall * span, depth), jnp.float32),
        ],
        compiler_params=pltpu.CompilerParams(vmem_limit_bytes=8 * 2**20),
        name="images",
    )(rate_table, field, even_x, odd_x, even_y, odd_y)

    columns_two, message = pl.pallas_call(
        functools.partial(corners_kernel, lattice, cols),
        out_shape=[
            jax.ShapeDtypeStruct((members, 2, rows, depth), jnp.float32),
            jax.ShapeDtypeStruct((devices, 128), jnp.float32),
        ],
        in_specs=[vmem] * 5,
        out_specs=[vmem, vmem],
        scratch_shapes=[
            pltpu.VMEM((members, 2, 2, tall, depth), jnp.float32),
            pltpu.VMEM((48, depth), jnp.float32),
        ],
        compiler_params=pltpu.CompilerParams(vmem_limit_bytes=4 * 2**20),
        name="corners",
    )(rate_table, lines, odd_corners, even_corners, parts)

    gathered = lax.all_to_all(message, ("gy", "gx"), 0, 0, tiled=True)

    return pl.pallas_call(
        combine_kernel,
        out_shape=[block, jax.ShapeDtypeStruct((members, 5), jnp.float32)],
        in_specs=[vmem] * 5,
        out_specs=[vmem, vmem],
        compiler_params=pltpu.CompilerParams(vmem_limit_bytes=8 * 2**20),
        name="combine",
    )(gathered, field, image_one, image_two, columns_two)


def solution(mesh):
    in_specs = (P(None, "gx", "gy", None), P())
    out_specs = (P(None, "gx", "gy", None), P())
    return jax.shard_map(shards, mesh=mesh, in_specs=in_specs, out_specs=out_specs, check_vma=False)
```

```python
import functools
import math

import jax
import jax.numpy as jnp
from jax import lax
from jax.experimental import pallas as pl
from jax.experimental.pallas import tpu as pltpu
from jax.sharding import PartitionSpec as P

tau_step = 0.01
taylor_terms = 16
squarings = 4
REACH = 4
HALF = 2
GAP = 8


def parity_kernel(parity):
    parity[...] = jnp.full(parity.shape, lax.axis_index("gy") % 2, jnp.int32)


def edges_kernel(parity, field, for_odd, for_even):
    is_even = jnp.broadcast_to(parity[:1], for_odd.shape[1:3] + parity.shape[1:])[None] == 0
    cols = field.shape[2]
    low, high = field[:, :, :2], field[:, :, cols - 2 :]
    for_even[...] = jnp.where(is_even, high, low)
    for_odd[...] = jnp.where(is_even, low, high)


def own_lane(first):
    row = lax.broadcasted_iota(jnp.int32, (8, 128), 0)
    return lax.broadcasted_iota(jnp.int32, (8, 128), 1) == first + row


def lanes(depth):
    lane = lax.broadcasted_iota(jnp.int32, (1, depth), 1)
    amount_k = lane.astype(jnp.float32)
    return amount_k, jnp.where(lane < depth - 1, amount_k + 1.0, 0.0), jnp.where(lane > 0, 1.0, 0.0)


def apply(c, depth, i, make_u, make_v, lose_v, rest, centre, rows_by, left, right):
    _, above_k, inner_k = lanes(depth)
    value = make_u * rows_by(-1) + (c[1] * (i + 1.0)) * rows_by(1)
    value = value + make_v * left
    value = value + lose_v * right
    pair = pltpu.roll(rows_by(2), 1, 1)
    value = value + (inner_k * (0.5 * c[4] * (i + 2.0) * (i + 1.0))) * pair
    split = c[5] * rows_by(-2) + c[6] * centre
    value = value + above_k * pltpu.roll(split, depth - 1, 1)
    out = rest + (c[1] * i + 0.5 * c[4] * i * (i - 1.0))
    return value - out * centre


def constants(rates, member, depth, amount_j):
    c = [jnp.broadcast_to(rates[member : member + 1, r : r + 1], (1, depth)) for r in range(9)]
    amount_k = lanes(depth)[0]
    ratio_j, ratio_k = amount_j / c[7], amount_k / c[8]
    make_u = c[0] / (1.0 + ratio_j * ratio_j)
    make_v = c[2] / (1.0 + ratio_k * ratio_k)
    lose_v = c[3] * (amount_j + 1.0)
    rest = make_u + make_v + (c[3] * amount_j + (c[5] + c[6]) * amount_k)
    return c, make_u, make_v, lose_v, rest


def sides(even, odd, is_even, lower_inside, higher_inside):
    lower, higher = jnp.where(is_even, odd, even), jnp.where(is_even, even, odd)
    return jnp.where(lower_inside, lower, 0.0), jnp.where(higher_inside, higher, 0.0)


def images_kernel(
    lattice,
    rates,
    field,
    even_x,
    odd_x,
    even_y,
    odd_y,
    image_one,
    image_two,
    lines,
    parts,
    wide,
    wide_image,
):
    members, rows, cols, depth = field.shape
    span = cols + 2 * GAP
    tall = rows + 2 * HALF
    index_i, index_j = lax.axis_index("gx"), lax.axis_index("gy")
    first_i, first_j = index_i * rows, index_j * cols
    even_i, even_j = index_i % 2 == 0, index_j % 2 == 0
    count_i, count_j = lattice

    def place(row, start, values):
        for at in range(values.shape[1]):
            first = (row + REACH + at) * span + GAP + start
            wide[:, first : first + values.shape[2]] = values[:, at]

    place(0, 0, field[...])
    above, below = sides(even_x[...], odd_x[...], even_i, first_i > 0, first_i + rows < count_i)
    place(-REACH, 0, above)
    place(rows, 0, below)
    left, right = sides(even_y[...], odd_y[...], even_j, first_j > 0, first_j + cols < count_j)
    place(0, -2, left)
    place(0, cols, right)
    corner = jnp.zeros((members, HALF, 1, depth), jnp.float32)
    for row in (-HALF, rows):
        place(row, -1, corner)
        place(row, cols, corner)

    sublane = lax.broadcasted_iota(jnp.int32, (span, 1), 0)
    amount_j = (first_j - GAP + sublane).astype(jnp.float32)
    place_j = lax.broadcasted_iota(jnp.int32, (cols, depth), 0)
    inner_j = (place_j > 0) & (place_j < cols - 1)

    for member in range(members):
        c, make_u, make_v, lose_v, rest = constants(rates, member, depth, amount_j)
        make_u, lose_v, rest = [term[GAP : GAP + cols] for term in (make_u, lose_v, rest)]

        def image(read, row):
            i = (first_i + row).astype(jnp.float32)
            rows_by = lambda by: read(row + by, 0)
            return apply(c, depth, i, make_u, make_v, lose_v, rest, read(row, 0), rows_by, read(row, -1), read(row, 1))

        def read_field(row, start):
            return wide[member, pl.ds((row + REACH) * span + GAP + start, cols), :]

        def read_image(row, start):
            return wide_image[member, pl.ds((row + HALF) * span + GAP + start, cols), :]

        for row in range(-HALF, rows + HALF):
            inside = (first_i + row >= 0) & (first_i + row < count_i)
            value = image(read_field, row)
            if row < 0 or row >= rows:
                value = jnp.where(inside, value, 0.0)
            else:
                image_one[member, row] = value
            wide_image[member, pl.ds((row + HALF) * span + GAP, cols), :] = value

        products = [jnp.zeros((cols, depth), jnp.float32) for _ in range(6)]
        for row in range(rows):
            zero = field[member, row]
            one = image_one[member, row]
            two = jnp.where(inner_j, image(read_image, row), 0.0)
            image_two[member, row] = two
            terms = (zero * zero, zero * one, zero * two, one * one, one * two, two * two)
            products = [total + term for total, term in zip(products, terms)]
        for index, total in enumerate(products):
            parts[8 * index + member : 8 * index + member + 1, :] = jnp.sum(total, axis=0, keepdims=True)

        for at, column in enumerate((0, cols - 1, 1, cols - 2)):
            lines[member, at] = wide_image[member, pl.ds(GAP + column, tall, stride=span), :]
        for at, column in enumerate((0, cols - 1, -1, cols, -2, cols + 1)):
            lines[member, 4 + at] = wide[member, pl.ds(HALF * span + GAP + column, tall, stride=span), :]

    for index in range(6):
        parts[8 * index + members : 8 * index + 8, :] = jnp.zeros((8 - members, depth), jnp.float32)


def corners_kernel(lattice, cols, rates, lines, odd_corners, even_corners, parts, columns_two, message, edge, total):
    members, _, tall, depth = lines.shape
    rows = tall - 2 * HALF
    index_i, index_j = lax.axis_index("gx"), lax.axis_index("gy")
    first_i, first_j = index_i * rows, index_j * cols
    count_i, count_j = lattice
    upper, lower = sides(
        even_corners[...], odd_corners[...], index_i % 2 == 0, first_i > 0, first_i + rows < count_i
    )
    i = (first_i + lax.broadcasted_iota(jnp.int32, (rows, depth), 0)).astype(jnp.float32)
    total[...] = parts[...]
    for member in range(members):

        def line(at):
            return lines[member, at, pl.ds(HALF, rows), :]

        sums = [jnp.zeros((rows, depth), jnp.float32) for _ in range(3)]
        for side, column, beyond, inside in (
            (0, 0, -1, first_j > 0),
            (1, cols - 1, cols, first_j + cols < count_j),
        ):

            def at_column(column):
                amount_j = jnp.broadcast_to((first_j + column).astype(jnp.float32), (1, depth))
                return constants(rates, member, depth, amount_j)

            outer, fixed = edge.at[member, side, 0], edge.at[member, side, 1]
            outer[HALF : HALF + rows, :] = line(6 + side)
            for row in range(HALF):
                for first, corner in ((0, upper), (HALF + rows, lower)):
                    value = corner[member, row, side : side + 1, :]
                    outer[first + row : first + row + 1, :] = jnp.where(inside, value, 0.0)

            c, make_u, make_v, lose_v, rest = at_column(beyond)
            rows_by = lambda by: outer[pl.ds(HALF + by, rows), :]
            beside = (line(8), line(4)) if side == 0 else (line(5), line(9))
            value = apply(c, depth, i, make_u, make_v, lose_v, rest, rows_by(0), rows_by, *beside)
            image_beyond = jnp.where(inside, value, 0.0)

            c, make_u, make_v, lose_v, rest = at_column(column)
            gain = make_v if side == 0 else lose_v
            fixed[...] = lines[member, side]
            for first in (0, HALF + rows):
                fixed[first : first + HALF, :] = fixed[first : first + HALF, :] + gain * outer[first : first + HALF, :]

            rows_by = lambda by: fixed[pl.ds(HALF + by, rows), :]
            beside = (image_beyond, line(2)) if side == 0 else (line(3), image_beyond)
            two = apply(c, depth, i, make_u, make_v, lose_v, rest, rows_by(0), rows_by, *beside)
            columns_two[member, side] = two
            terms = (line(4 + side) * two, line(side) * two, two * two)
            sums = [value + term for value, term in zip(sums, terms)]
        for index, value in zip((2, 4, 5), sums):
            at = 8 * index + member
            total[at : at + 1, :] = total[at : at + 1, :] + jnp.sum(value, axis=0, keepdims=True)

    row = jnp.zeros((8, depth), jnp.float32)
    for index in range(6):
        value = jnp.sum(total[8 * index : 8 * index + 8], axis=1, keepdims=True)
        row = row + jnp.where(own_lane(8 * index), value, 0.0)
    message[...] = jnp.broadcast_to(jnp.sum(row, axis=0, keepdims=True), message.shape)


def product(left, right):
    a, b, c, d = left
    e, f, g, h = right
    return a * e + b * g, a * f + b * h, c * e + d * g, c * f + d * h


def first_column(h00, s01, h11):
    scale = tau_step / 2.0**squarings
    one = jnp.ones_like(h00)
    z1 = (scale * h00, scale * s01, scale * one, scale * h11)
    z2 = product(z1, z1)
    z3, z4 = product(z2, z1), product(z2, z2)
    weights = [1.0 / math.factorial(k + 1) for k in range(taylor_terms)]

    def block(first):
        w0, w1, w2, w3 = weights[first : first + 4]
        terms = [w1 * p + w2 * q + w3 * r for p, q, r in zip(z1, z2, z3)]
        return terms[0] + w0, terms[1], terms[2], terms[3] + w0

    phi = block(taylor_terms - 4)
    for first in range(taylor_terms - 8, -1, -4):
        phi = tuple(p + q for p, q in zip(product(z4, phi), block(first)))
    p00, p01, p10, p11 = product(z1, phi)
    p00, p11 = 1.0 + p00, 1.0 + p11
    q0, q1 = scale * phi[2], scale * phi[3]
    for _ in range(squarings):
        p00, p01, p10, p11, q0, q1 = (
            p00 * p00 + p01 * p10,
            p00 * p01 + p01 * p11,
            p10 * p00 + p11 * p10,
            p10 * p01 + p11 * p11,
            q0 * p00 + q1 * p10 + q0,
            q0 * p01 + q1 * p11 + q1,
        )
    return p00, p10, q0


def combine_kernel(gathered, field, image_one, image_two, columns_two, propagated, entries):
    members, rows, cols, depth = field.shape
    sums = jnp.broadcast_to(jnp.sum(gathered[...], axis=0, keepdims=True), (8, 128))
    g00, g01, g02, g11, g12, g22 = [
        jnp.broadcast_to(jnp.sum(jnp.where(own_lane(8 * index), sums, 0.0), axis=1, keepdims=True), (8, 128))
        for index in range(6)
    ]
    tiny = jnp.finfo(jnp.float32).tiny
    h00 = g01 / g00
    square_10 = jnp.maximum(g11 / g00 - h00 * h00, tiny)
    s01 = (g02 - h00 * g01) / g00
    h11 = ((g12 - h00 * g02) - h00 * (g11 - h00 * g01)) / (g00 * square_10)
    norm_2 = ((g22 - h00 * g12) - h00 * (g12 - h00 * g11)) / (g00 * square_10)
    h10 = jnp.sqrt(square_10)
    h01 = s01 / h10
    h21 = jnp.sqrt(jnp.maximum(norm_2 - h01 * h01 - h11 * h11, 0.0))
    e0, e1, e2 = first_column(h00, s01, h11)
    a2 = e2
    a1 = e1 - e2 * (h00 + h11)
    a0 = e0 - e1 * h00 - e2 * (s01 - h11 * h00)
    lane = lax.broadcasted_iota(jnp.int32, h00.shape, 1)
    table = h21
    for index, entry in enumerate((h00, h10, h01, h11)):
        table = jnp.where(lane == index, entry, table)
    entries[...] = (tau_step * table)[: entries.shape[0], : entries.shape[1]]
    place_j = lax.broadcasted_iota(jnp.int32, (cols, depth), 0)
    for member in range(members):
        b0, b1, b2 = [jnp.broadcast_to(a[member : member + 1], (cols, depth)) for a in (a0, a1, a2)]
        for row in range(rows):
            two = jnp.where(place_j == 0, columns_two[member, 0, row : row + 1], image_two[member, row])
            two = jnp.where(place_j == cols - 1, columns_two[member, 1, row : row + 1], two)
            propagated[member, row] = b0 * field[member, row] + b1 * image_one[member, row] + b2 * two


def shards(density, rate_table):
    members, rows, cols, depth = density.shape
    size_x, size_y = lax.axis_size("gx"), lax.axis_size("gy")
    devices = size_x * size_y
    vmem = pl.BlockSpec(memory_space=pltpu.VMEM)
    parity_x, parity_y = lax.axis_index("gx") % 2, lax.axis_index("gy") % 2

    def swap(axis, size, first, value):
        def partner(x, y):
            at = x if axis == "gx" else y
            other = at + 1 if (at - first) % 2 == 0 else at - 1
            if not 0 <= other < size:
                return (x, y ^ 1) if axis == "gx" else (x ^ 1, y)
            return (other, y) if axis == "gx" else (x, other)

        pairs = [
            (x * size_y + y, partner(x, y)[0] * size_y + partner(x, y)[1])
            for x in range(size_x)
            for y in range(size_y)
        ]
        return lax.ppermute(value, ("gx", "gy"), pairs)

    assert size_x % 2 == 0 and size_y % 2 == 0

    def swaps(axis, size, parity, initial, last):
        if initial is last:
            return swap(axis, size, 0, last), swap(axis, size, 1, last)
        is_even = parity == 0
        return (
            swap(axis, size, 0, jnp.where(is_even, last, initial)),
            swap(axis, size, 1, jnp.where(is_even, initial, last)),
        )

    if rows == REACH:
        even_x, odd_x = swaps("gx", size_x, parity_x, density, density)
    else:
        even_x, odd_x = swaps("gx", size_x, parity_x, density[:, :REACH], density[:, rows - REACH :])

    edge = jax.ShapeDtypeStruct((members, rows, 2, depth), jnp.float32)
    block = jax.ShapeDtypeStruct(density.shape, jnp.float32)
    parity = pl.pallas_call(
        parity_kernel,
        out_shape=jax.ShapeDtypeStruct((8, depth), jnp.int32),
        out_specs=vmem,
        compiler_params=pltpu.CompilerParams(vmem_limit_bytes=2**20),
        cost_estimate=pl.CostEstimate(flops=10**8, bytes_accessed=0, transcendentals=0),
        name="parity",
    )()
    for_odd, for_even = pl.pallas_call(
        edges_kernel,
        out_shape=[edge, edge],
        in_specs=[vmem, vmem],
        out_specs=[vmem] * 2,
        compiler_params=pltpu.CompilerParams(vmem_limit_bytes=2 * 2**20),
        name="edges",
    )(parity, density)
    odd_y = swap("gy", size_y, 1, for_odd)
    even_y = swap("gy", size_y, 0, for_even)

    even_x, odd_y, even_y = lax.optimization_barrier((even_x, odd_y, even_y))

    def corners(first):
        even, odd = even_y[:, first : first + HALF], odd_y[:, first : first + HALF]
        left = jnp.where(parity_y == 0, odd, even)[:, :, 1:]
        right = jnp.where(parity_y == 0, even, odd)[:, :, :1]
        return jnp.concatenate([left, right], axis=2)

    even_corners, odd_corners = swaps("gx", size_x, parity_x, corners(0), corners(rows - HALF))

    lattice = (size_x * rows, size_y * cols)
    tall, span = rows + 2 * HALF, cols + 2 * GAP
    image_one, image_two, lines, parts = pl.pallas_call(
        functools.partial(images_kernel, lattice),
        out_shape=[
            block,
            block,
            jax.ShapeDtypeStruct((members, 10, tall, depth), jnp.float32),
            jax.ShapeDtypeStruct((48, depth), jnp.float32),
        ],
        in_specs=[vmem] * 6,
        out_specs=[vmem] * 4,
        scratch_shapes=[
            pltpu.VMEM((members, (rows + 2 * REACH) * span, depth), jnp.float32),
            pltpu.VMEM((members, tall * span, depth), jnp.float32),
        ],
        compiler_params=pltpu.CompilerParams(vmem_limit_bytes=8 * 2**20),
        name="images",
    )(rate_table, density, even_x, odd_x, even_y, odd_y)

    columns_two, message = pl.pallas_call(
        functools.partial(corners_kernel, lattice, cols),
        out_shape=[
            jax.ShapeDtypeStruct((members, 2, rows, depth), jnp.float32),
            jax.ShapeDtypeStruct((devices, 128), jnp.float32),
        ],
        in_specs=[vmem] * 5,
        out_specs=[vmem, vmem],
        scratch_shapes=[
            pltpu.VMEM((members, 2, 2, tall, depth), jnp.float32),
            pltpu.VMEM((48, depth), jnp.float32),
        ],
        compiler_params=pltpu.CompilerParams(vmem_limit_bytes=4 * 2**20),
        name="corners",
    )(rate_table, lines, odd_corners, even_corners, parts)

    gathered = lax.all_to_all(message, ("gy", "gx"), 0, 0, tiled=True)

    return pl.pallas_call(
        combine_kernel,
        out_shape=[block, jax.ShapeDtypeStruct((members, 5), jnp.float32)],
        in_specs=[vmem] * 5,
        out_specs=[vmem, vmem],
        compiler_params=pltpu.CompilerParams(vmem_limit_bytes=8 * 2**20),
        name="combine",
    )(gathered, density, image_one, image_two, columns_two)


def solution(mesh):
    in_specs = (P(None, "gx", "gy", None), P())
    out_specs = (P(None, "gx", "gy", None), P())
    return jax.shard_map(shards, mesh=mesh, in_specs=in_specs, out_specs=out_specs, check_vma=False)
```

```python
import functools
import math

import jax
import jax.numpy as jnp
from jax import lax
from jax.experimental import pallas as pl
from jax.experimental.pallas import tpu as pltpu
from jax.sharding import PartitionSpec as P

tau_step = 0.01
taylor_terms = 16
squarings = 4
REACH = 4
HALF = 2
GAP = 8


def parity_kernel(parity):
    parity[...] = jnp.full(parity.shape, lax.axis_index("gy") % 2, jnp.int32)


def edges_kernel(parity, field, for_odd, for_even):
    is_even = jnp.broadcast_to(parity[:1], for_odd.shape[1:3] + parity.shape[1:])[None] == 0
    cols = field.shape[2]
    low, high = field[:, :, :2], field[:, :, cols - 2 :]
    for_even[...] = jnp.where(is_even, high, low)
    for_odd[...] = jnp.where(is_even, low, high)


def own_lane(first):
    row = lax.broadcasted_iota(jnp.int32, (8, 128), 0)
    return lax.broadcasted_iota(jnp.int32, (8, 128), 1) == first + row


def lanes(depth):
    lane = lax.broadcasted_iota(jnp.int32, (1, depth), 1)
    amount_k = lane.astype(jnp.float32)
    return amount_k, jnp.where(lane < depth - 1, amount_k + 1.0, 0.0), jnp.where(lane > 0, 1.0, 0.0)


def apply(c, depth, i, make_u, make_v, lose_v, rest, centre, rows_by, left, right):
    _, above_k, inner_k = lanes(depth)
    value = make_u * rows_by(-1) + (c[1] * (i + 1.0)) * rows_by(1)
    value = value + make_v * left
    value = value + lose_v * right
    pair = pltpu.roll(rows_by(2), 1, 1)
    value = value + (inner_k * (0.5 * c[4] * (i + 2.0) * (i + 1.0))) * pair
    split = c[5] * rows_by(-2) + c[6] * centre
    value = value + above_k * pltpu.roll(split, depth - 1, 1)
    out = rest + (c[1] * i + 0.5 * c[4] * i * (i - 1.0))
    return value - out * centre


def constants(rates, member, depth, amount_j):
    c = [jnp.broadcast_to(rates[member : member + 1, r : r + 1], (1, depth)) for r in range(9)]
    amount_k = lanes(depth)[0]
    ratio_j, ratio_k = amount_j / c[7], amount_k / c[8]
    make_u = c[0] / (1.0 + ratio_j * ratio_j)
    make_v = c[2] / (1.0 + ratio_k * ratio_k)
    lose_v = c[3] * (amount_j + 1.0)
    rest = make_u + make_v + (c[3] * amount_j + (c[5] + c[6]) * amount_k)
    return c, make_u, make_v, lose_v, rest


def sides(even, odd, is_even, lower_inside, higher_inside):
    lower, higher = jnp.where(is_even, odd, even), jnp.where(is_even, even, odd)
    return jnp.where(lower_inside, lower, 0.0), jnp.where(higher_inside, higher, 0.0)


def images_kernel(
    lattice,
    rates,
    field,
    even_x,
    odd_x,
    even_y,
    odd_y,
    image_one,
    image_two,
    lines,
    parts,
    wide,
    wide_image,
):
    members, rows, cols, depth = field.shape
    span = cols + 2 * GAP
    tall = rows + 2 * HALF
    index_i, index_j = lax.axis_index("gx"), lax.axis_index("gy")
    first_i, first_j = index_i * rows, index_j * cols
    even_i, even_j = index_i % 2 == 0, index_j % 2 == 0
    count_i, count_j = lattice

    def place(row, start, values):
        for at in range(values.shape[1]):
            first = (row + REACH + at) * span + GAP + start
            wide[:, first : first + values.shape[2]] = values[:, at]

    place(0, 0, field[...])
    above, below = sides(even_x[...], odd_x[...], even_i, first_i > 0, first_i + rows < count_i)
    place(-REACH, 0, above)
    place(rows, 0, below)
    left, right = sides(even_y[...], odd_y[...], even_j, first_j > 0, first_j + cols < count_j)
    place(0, -2, left)
    place(0, cols, right)
    corner = jnp.zeros((members, HALF, 1, depth), jnp.float32)
    for row in (-HALF, rows):
        place(row, -1, corner)
        place(row, cols, corner)

    sublane = lax.broadcasted_iota(jnp.int32, (span, 1), 0)
    amount_j = (first_j - GAP + sublane).astype(jnp.float32)
    place_j = lax.broadcasted_iota(jnp.int32, (cols, depth), 0)
    inner_j = (place_j > 0) & (place_j < cols - 1)

    for member in range(members):
        c, make_u, make_v, lose_v, rest = constants(rates, member, depth, amount_j)
        make_u, lose_v, rest = [term[GAP : GAP + cols] for term in (make_u, lose_v, rest)]

        def image(read, row):
            i = (first_i + row).astype(jnp.float32)
            rows_by = lambda by: read(row + by, 0)
            return apply(c, depth, i, make_u, make_v, lose_v, rest, read(row, 0), rows_by, read(row, -1), read(row, 1))

        def read_field(row, start):
            return wide[member, pl.ds((row + REACH) * span + GAP + start, cols), :]

        def read_image(row, start):
            return wide_image[member, pl.ds((row + HALF) * span + GAP + start, cols), :]

        for row in range(-HALF, rows + HALF):
            inside = (first_i + row >= 0) & (first_i + row < count_i)
            value = image(read_field, row)
            if row < 0 or row >= rows:
                value = jnp.where(inside, value, 0.0)
            else:
                image_one[member, row] = value
            wide_image[member, pl.ds((row + HALF) * span + GAP, cols), :] = value

        products = [jnp.zeros((cols, depth), jnp.float32) for _ in range(6)]
        for row in range(rows):
            zero = field[member, row]
            one = image_one[member, row]
            two = jnp.where(inner_j, image(read_image, row), 0.0)
            image_two[member, row] = two
            terms = (zero * zero, zero * one, zero * two, one * one, one * two, two * two)
            products = [total + term for total, term in zip(products, terms)]
        for index, total in enumerate(products):
            parts[8 * index + member : 8 * index + member + 1, :] = jnp.sum(total, axis=0, keepdims=True)

        for at, column in enumerate((0, cols - 1, 1, cols - 2)):
            lines[member, at] = wide_image[member, pl.ds(GAP + column, tall, stride=span), :]
        for at, column in enumerate((0, cols - 1, -1, cols, -2, cols + 1)):
            lines[member, 4 + at] = wide[member, pl.ds(HALF * span + GAP + column, tall, stride=span), :]

    for index in range(6):
        parts[8 * index + members : 8 * index + 8, :] = jnp.zeros((8 - members, depth), jnp.float32)


def corners_kernel(lattice, cols, rates, lines, odd_corners, even_corners, parts, columns_two, message, edge, total):
    members, _, tall, depth = lines.shape
    rows = tall - 2 * HALF
    index_i, index_j = lax.axis_index("gx"), lax.axis_index("gy")
    first_i, first_j = index_i * rows, index_j * cols
    count_i, count_j = lattice
    upper, lower = sides(
        even_corners[...], odd_corners[...], index_i % 2 == 0, first_i > 0, first_i + rows < count_i
    )
    i = (first_i + lax.broadcasted_iota(jnp.int32, (rows, depth), 0)).astype(jnp.float32)
    total[...] = parts[...]
    for member in range(members):

        def line(at):
            return lines[member, at, pl.ds(HALF, rows), :]

        sums = [jnp.zeros((rows, depth), jnp.float32) for _ in range(3)]
        for side, column, beyond, inside in (
            (0, 0, -1, first_j > 0),
            (1, cols - 1, cols, first_j + cols < count_j),
        ):

            def at_column(column):
                amount_j = jnp.broadcast_to((first_j + column).astype(jnp.float32), (1, depth))
                return constants(rates, member, depth, amount_j)

            outer, fixed = edge.at[member, side, 0], edge.at[member, side, 1]
            outer[HALF : HALF + rows, :] = line(6 + side)
            for row in range(HALF):
                for first, corner in ((0, upper), (HALF + rows, lower)):
                    value = corner[member, row, side : side + 1, :]
                    outer[first + row : first + row + 1, :] = jnp.where(inside, value, 0.0)

            c, make_u, make_v, lose_v, rest = at_column(beyond)
            rows_by = lambda by: outer[pl.ds(HALF + by, rows), :]
            beside = (line(8), line(4)) if side == 0 else (line(5), line(9))
            value = apply(c, depth, i, make_u, make_v, lose_v, rest, rows_by(0), rows_by, *beside)
            image_beyond = jnp.where(inside, value, 0.0)

            c, make_u, make_v, lose_v, rest = at_column(column)
            gain = make_v if side == 0 else lose_v
            fixed[...] = lines[member, side]
            for first in (0, HALF + rows):
                fixed[first : first + HALF, :] = fixed[first : first + HALF, :] + gain * outer[first : first + HALF, :]

            rows_by = lambda by: fixed[pl.ds(HALF + by, rows), :]
            beside = (image_beyond, line(2)) if side == 0 else (line(3), image_beyond)
            two = apply(c, depth, i, make_u, make_v, lose_v, rest, rows_by(0), rows_by, *beside)
            columns_two[member, side] = two
            terms = (line(4 + side) * two, line(side) * two, two * two)
            sums = [value + term for value, term in zip(sums, terms)]
        for index, value in zip((2, 4, 5), sums):
            at = 8 * index + member
            total[at : at + 1, :] = total[at : at + 1, :] + jnp.sum(value, axis=0, keepdims=True)

    row = jnp.zeros((8, depth), jnp.float32)
    for index in range(6):
        value = jnp.sum(total[8 * index : 8 * index + 8], axis=1, keepdims=True)
        row = row + jnp.where(own_lane(8 * index), value, 0.0)
    message[...] = jnp.broadcast_to(jnp.sum(row, axis=0, keepdims=True), message.shape)


def product(left, right):
    a, b, c, d = left
    e, f, g, h = right
    return a * e + b * g, a * f + b * h, c * e + d * g, c * f + d * h


def first_column(h00, s01, h11):
    scale = tau_step / 2.0**squarings
    one = jnp.ones_like(h00)
    z1 = (scale * h00, scale * s01, scale * one, scale * h11)
    z2 = product(z1, z1)
    z3, z4 = product(z2, z1), product(z2, z2)
    weights = [1.0 / math.factorial(k + 1) for k in range(taylor_terms)]

    def block(first):
        w0, w1, w2, w3 = weights[first : first + 4]
        terms = [w1 * p + w2 * q + w3 * r for p, q, r in zip(z1, z2, z3)]
        return terms[0] + w0, terms[1], terms[2], terms[3] + w0

    phi = block(taylor_terms - 4)
    for first in range(taylor_terms - 8, -1, -4):
        phi = tuple(p + q for p, q in zip(product(z4, phi), block(first)))
    p00, p01, p10, p11 = product(z1, phi)
    p00, p11 = 1.0 + p00, 1.0 + p11
    q0, q1 = scale * phi[2], scale * phi[3]
    for _ in range(squarings):
        p00, p01, p10, p11, q0, q1 = (
            p00 * p00 + p01 * p10,
            p00 * p01 + p01 * p11,
            p10 * p00 + p11 * p10,
            p10 * p01 + p11 * p11,
            q0 * p00 + q1 * p10 + q0,
            q0 * p01 + q1 * p11 + q1,
        )
    return p00, p10, q0


def combine_kernel(gathered, field, image_one, image_two, columns_two, propagated, entries):
    members, rows, cols, depth = field.shape
    sums = jnp.broadcast_to(jnp.sum(gathered[...], axis=0, keepdims=True), (8, 128))
    g00, g01, g02, g11, g12, g22 = [
        jnp.broadcast_to(jnp.sum(jnp.where(own_lane(8 * index), sums, 0.0), axis=1, keepdims=True), (8, 128))
        for index in range(6)
    ]
    tiny = jnp.finfo(jnp.float32).tiny
    h00 = g01 / g00
    square_10 = jnp.maximum(g11 / g00 - h00 * h00, tiny)
    s01 = (g02 - h00 * g01) / g00
    h11 = ((g12 - h00 * g02) - h00 * (g11 - h00 * g01)) / (g00 * square_10)
    norm_2 = ((g22 - h00 * g12) - h00 * (g12 - h00 * g11)) / (g00 * square_10)
    h10 = jnp.sqrt(square_10)
    h01 = s01 / h10
    h21 = jnp.sqrt(jnp.maximum(norm_2 - h01 * h01 - h11 * h11, 0.0))
    e0, e1, e2 = first_column(h00, s01, h11)
    a2 = e2
    a1 = e1 - e2 * (h00 + h11)
    a0 = e0 - e1 * h00 - e2 * (s01 - h11 * h00)
    lane = lax.broadcasted_iota(jnp.int32, h00.shape, 1)
    table = h21
    for index, entry in enumerate((h00, h10, h01, h11)):
        table = jnp.where(lane == index, entry, table)
    entries[...] = (tau_step * table)[: entries.shape[0], : entries.shape[1]]
    place_j = lax.broadcasted_iota(jnp.int32, (cols, depth), 0)
    for member in range(members):
        b0, b1, b2 = [jnp.broadcast_to(a[member : member + 1], (cols, depth)) for a in (a0, a1, a2)]
        for row in range(rows):
            two = jnp.where(place_j == 0, columns_two[member, 0, row : row + 1], image_two[member, row])
            two = jnp.where(place_j == cols - 1, columns_two[member, 1, row : row + 1], two)
            propagated[member, row] = b0 * field[member, row] + b1 * image_one[member, row] + b2 * two


def shards(density, rate_table):
    members, rows, cols, depth = density.shape
    size_x, size_y = lax.axis_size("gx"), lax.axis_size("gy")
    devices = size_x * size_y
    vmem = pl.BlockSpec(memory_space=pltpu.VMEM)
    parity_x, parity_y = lax.axis_index("gx") % 2, lax.axis_index("gy") % 2

    def swap(axis, size, first, value):
        def partner(x, y):
            at = x if axis == "gx" else y
            other = at + 1 if (at - first) % 2 == 0 else at - 1
            if not 0 <= other < size:
                return (x, y ^ 1) if axis == "gx" else (x ^ 1, y)
            return (other, y) if axis == "gx" else (x, other)

        pairs = [
            (x * size_y + y, partner(x, y)[0] * size_y + partner(x, y)[1])
            for x in range(size_x)
            for y in range(size_y)
        ]
        return lax.ppermute(value, ("gx", "gy"), pairs)

    assert size_x % 2 == 0 and size_y % 2 == 0

    def swaps(axis, size, parity, initial, last):
        if initial is last:
            return swap(axis, size, 0, last), swap(axis, size, 1, last)
        is_even = parity == 0
        return (
            swap(axis, size, 0, jnp.where(is_even, last, initial)),
            swap(axis, size, 1, jnp.where(is_even, initial, last)),
        )

    initial, last = (density, density) if rows == REACH else (density[:, :REACH], density[:, rows - REACH :])
    is_even = parity_x == 0
    even_x = swap("gx", size_x, 0, initial if rows == REACH else jnp.where(is_even, last, initial))

    edge = jax.ShapeDtypeStruct((members, rows, 2, depth), jnp.float32)
    block = jax.ShapeDtypeStruct(density.shape, jnp.float32)
    parity = pl.pallas_call(
        parity_kernel,
        out_shape=jax.ShapeDtypeStruct((8, depth), jnp.int32),
        out_specs=vmem,
        compiler_params=pltpu.CompilerParams(vmem_limit_bytes=2**20),
        cost_estimate=pl.CostEstimate(flops=10**8, bytes_accessed=0, transcendentals=0),
        name="parity",
    )()
    for_odd, for_even = pl.pallas_call(
        edges_kernel,
        out_shape=[edge, edge],
        in_specs=[vmem, vmem],
        out_specs=[vmem] * 2,
        compiler_params=pltpu.CompilerParams(vmem_limit_bytes=2 * 2**20),
        name="edges",
    )(parity, density)
    odd_y = swap("gy", size_y, 1, for_odd)
    even_y = swap("gy", size_y, 0, for_even)

    even_y, for_odd_x = lax.optimization_barrier((even_y, initial if rows == REACH else jnp.where(is_even, initial, last)))
    odd_x = swap("gx", size_x, 1, for_odd_x)
    even_x, odd_y, even_y = lax.optimization_barrier((even_x, odd_y, even_y))

    def corners(first):
        even, odd = even_y[:, first : first + HALF], odd_y[:, first : first + HALF]
        left = jnp.where(parity_y == 0, odd, even)[:, :, 1:]
        right = jnp.where(parity_y == 0, even, odd)[:, :, :1]
        return jnp.concatenate([left, right], axis=2)

    even_corners, odd_corners = swaps("gx", size_x, parity_x, corners(0), corners(rows - HALF))

    lattice = (size_x * rows, size_y * cols)
    tall, span = rows + 2 * HALF, cols + 2 * GAP
    image_one, image_two, lines, parts = pl.pallas_call(
        functools.partial(images_kernel, lattice),
        out_shape=[
            block,
            block,
            jax.ShapeDtypeStruct((members, 10, tall, depth), jnp.float32),
            jax.ShapeDtypeStruct((48, depth), jnp.float32),
        ],
        in_specs=[vmem] * 6,
        out_specs=[vmem] * 4,
        scratch_shapes=[
            pltpu.VMEM((members, (rows + 2 * REACH) * span, depth), jnp.float32),
            pltpu.VMEM((members, tall * span, depth), jnp.float32),
        ],
        compiler_params=pltpu.CompilerParams(vmem_limit_bytes=8 * 2**20),
        name="images",
    )(rate_table, density, even_x, odd_x, even_y, odd_y)

    columns_two, message = pl.pallas_call(
        functools.partial(corners_kernel, lattice, cols),
        out_shape=[
            jax.ShapeDtypeStruct((members, 2, rows, depth), jnp.float32),
            jax.ShapeDtypeStruct((devices, 128), jnp.float32),
        ],
        in_specs=[vmem] * 5,
        out_specs=[vmem, vmem],
        scratch_shapes=[
            pltpu.VMEM((members, 2, 2, tall, depth), jnp.float32),
            pltpu.VMEM((48, depth), jnp.float32),
        ],
        compiler_params=pltpu.CompilerParams(vmem_limit_bytes=4 * 2**20),
        name="corners",
    )(rate_table, lines, odd_corners, even_corners, parts)

    gathered = lax.all_to_all(message, ("gy", "gx"), 0, 0, tiled=True)

    return pl.pallas_call(
        combine_kernel,
        out_shape=[block, jax.ShapeDtypeStruct((members, 5), jnp.float32)],
        in_specs=[vmem] * 5,
        out_specs=[vmem, vmem],
        compiler_params=pltpu.CompilerParams(vmem_limit_bytes=8 * 2**20),
        name="combine",
    )(gathered, density, image_one, image_two, columns_two)


def solution(mesh):
    in_specs = (P(None, "gx", "gy", None), P())
    out_specs = (P(None, "gx", "gy", None), P())
    return jax.shard_map(shards, mesh=mesh, in_specs=in_specs, out_specs=out_specs, check_vma=False)
```

```python
import functools
import math

import jax
import jax.numpy as jnp
from jax import lax
from jax.experimental import pallas as pl
from jax.experimental.pallas import tpu as pltpu
from jax.sharding import PartitionSpec as P

tau_step = 0.01
taylor_terms = 16
squarings = 4
REACH = 4
HALF = 2
GAP = 8


def parity_kernel(parity):
    parity[...] = jnp.full(parity.shape, lax.axis_index("gy") % 2, jnp.int32)


def edges_kernel(parity, field, for_odd, for_even):
    is_even = jnp.broadcast_to(parity[:1], for_odd.shape[1:3] + parity.shape[1:])[None] == 0
    cols = field.shape[2]
    low, high = field[:, :, :2], field[:, :, cols - 2 :]
    for_even[...] = jnp.where(is_even, high, low)
    for_odd[...] = jnp.where(is_even, low, high)


def own_lane(first):
    row = lax.broadcasted_iota(jnp.int32, (8, 128), 0)
    return lax.broadcasted_iota(jnp.int32, (8, 128), 1) == first + row


def lanes(depth):
    lane = lax.broadcasted_iota(jnp.int32, (1, depth), 1)
    amount_k = lane.astype(jnp.float32)
    return amount_k, jnp.where(lane < depth - 1, amount_k + 1.0, 0.0), jnp.where(lane > 0, 1.0, 0.0)


def apply(c, depth, i, make_u, make_v, lose_v, rest, centre, rows_by, left, right):
    _, above_k, inner_k = lanes(depth)
    value = make_u * rows_by(-1) + (c[1] * (i + 1.0)) * rows_by(1)
    value = value + make_v * left
    value = value + lose_v * right
    pair = pltpu.roll(rows_by(2), 1, 1)
    value = value + (inner_k * (0.5 * c[4] * (i + 2.0) * (i + 1.0))) * pair
    split = c[5] * rows_by(-2) + c[6] * centre
    value = value + above_k * pltpu.roll(split, depth - 1, 1)
    out = rest + (c[1] * i + 0.5 * c[4] * i * (i - 1.0))
    return value - out * centre


def constants(rates, member, depth, amount_j):
    c = [jnp.broadcast_to(rates[member : member + 1, r : r + 1], (1, depth)) for r in range(9)]
    amount_k = lanes(depth)[0]
    ratio_j, ratio_k = amount_j / c[7], amount_k / c[8]
    make_u = c[0] / (1.0 + ratio_j * ratio_j)
    make_v = c[2] / (1.0 + ratio_k * ratio_k)
    lose_v = c[3] * (amount_j + 1.0)
    rest = make_u + make_v + (c[3] * amount_j + (c[5] + c[6]) * amount_k)
    return c, make_u, make_v, lose_v, rest


def sides(even, odd, is_even, lower_inside, higher_inside):
    lower, higher = jnp.where(is_even, odd, even), jnp.where(is_even, even, odd)
    return jnp.where(lower_inside, lower, 0.0), jnp.where(higher_inside, higher, 0.0)


def images_kernel(
    lattice,
    rates,
    field,
    even_x,
    odd_x,
    even_y,
    odd_y,
    image_one,
    image_two,
    lines,
    parts,
    wide,
    wide_image,
):
    members, rows, cols, depth = field.shape
    span = cols + 2 * GAP
    tall = rows + 2 * HALF
    index_i, index_j = lax.axis_index("gx"), lax.axis_index("gy")
    first_i, first_j = index_i * rows, index_j * cols
    even_i, even_j = index_i % 2 == 0, index_j % 2 == 0
    count_i, count_j = lattice

    def place(row, start, values):
        for at in range(values.shape[1]):
            first = (row + REACH + at) * span + GAP + start
            wide[:, first : first + values.shape[2]] = values[:, at]

    place(0, 0, field[...])
    above, below = sides(even_x[...], odd_x[...], even_i, first_i > 0, first_i + rows < count_i)
    place(-REACH, 0, above)
    place(rows, 0, below)
    left, right = sides(even_y[...], odd_y[...], even_j, first_j > 0, first_j + cols < count_j)
    place(0, -2, left)
    place(0, cols, right)
    corner = jnp.zeros((members, HALF, 1, depth), jnp.float32)
    for row in (-HALF, rows):
        place(row, -1, corner)
        place(row, cols, corner)

    sublane = lax.broadcasted_iota(jnp.int32, (span, 1), 0)
    amount_j = (first_j - GAP + sublane).astype(jnp.float32)
    place_j = lax.broadcasted_iota(jnp.int32, (cols, depth), 0)
    inner_j = (place_j > 0) & (place_j < cols - 1)

    for member in range(members):
        c, make_u, make_v, lose_v, rest = constants(rates, member, depth, amount_j)
        make_u, lose_v, rest = [term[GAP : GAP + cols] for term in (make_u, lose_v, rest)]

        def image(read, row):
            i = (first_i + row).astype(jnp.float32)
            rows_by = lambda by: read(row + by, 0)
            return apply(c, depth, i, make_u, make_v, lose_v, rest, read(row, 0), rows_by, read(row, -1), read(row, 1))

        def read_field(row, start):
            return wide[member, pl.ds((row + REACH) * span + GAP + start, cols), :]

        def read_image(row, start):
            return wide_image[member, pl.ds((row + HALF) * span + GAP + start, cols), :]

        for row in range(-HALF, rows + HALF):
            inside = (first_i + row >= 0) & (first_i + row < count_i)
            value = image(read_field, row)
            if row < 0 or row >= rows:
                value = jnp.where(inside, value, 0.0)
            else:
                image_one[member, row] = value
            wide_image[member, pl.ds((row + HALF) * span + GAP, cols), :] = value

        products = [jnp.zeros((cols, depth), jnp.float32) for _ in range(6)]
        for row in range(rows):
            zero = field[member, row]
            one = image_one[member, row]
            two = jnp.where(inner_j, image(read_image, row), 0.0)
            image_two[member, row] = two
            terms = (zero * zero, zero * one, zero * two, one * one, one * two, two * two)
            products = [total + term for total, term in zip(products, terms)]
        for index, total in enumerate(products):
            parts[8 * index + member : 8 * index + member + 1, :] = jnp.sum(total, axis=0, keepdims=True)

        for at, column in enumerate((0, cols - 1, 1, cols - 2)):
            lines[member, at] = wide_image[member, pl.ds(GAP + column, tall, stride=span), :]
        for at, column in enumerate((0, cols - 1, -1, cols, -2, cols + 1)):
            lines[member, 4 + at] = wide[member, pl.ds(HALF * span + GAP + column, tall, stride=span), :]

    for index in range(6):
        parts[8 * index + members : 8 * index + 8, :] = jnp.zeros((8 - members, depth), jnp.float32)


def corners_kernel(lattice, cols, rates, lines, odd_corners, even_corners, parts, columns_two, message, edge, total):
    members, _, tall, depth = lines.shape
    rows = tall - 2 * HALF
    index_i, index_j = lax.axis_index("gx"), lax.axis_index("gy")
    first_i, first_j = index_i * rows, index_j * cols
    count_i, count_j = lattice
    upper, lower = sides(
        even_corners[...], odd_corners[...], index_i % 2 == 0, first_i > 0, first_i + rows < count_i
    )
    i = (first_i + lax.broadcasted_iota(jnp.int32, (rows, depth), 0)).astype(jnp.float32)
    total[...] = parts[...]
    for member in range(members):

        def line(at):
            return lines[member, at, pl.ds(HALF, rows), :]

        sums = [jnp.zeros((rows, depth), jnp.float32) for _ in range(3)]
        for side, column, beyond, inside in (
            (0, 0, -1, first_j > 0),
            (1, cols - 1, cols, first_j + cols < count_j),
        ):

            def at_column(column):
                amount_j = jnp.broadcast_to((first_j + column).astype(jnp.float32), (1, depth))
                return constants(rates, member, depth, amount_j)

            outer, fixed = edge.at[member, side, 0], edge.at[member, side, 1]
            outer[HALF : HALF + rows, :] = line(6 + side)
            for row in range(HALF):
                for first, corner in ((0, upper), (HALF + rows, lower)):
                    value = corner[member, row, side : side + 1, :]
                    outer[first + row : first + row + 1, :] = jnp.where(inside, value, 0.0)

            c, make_u, make_v, lose_v, rest = at_column(beyond)
            rows_by = lambda by: outer[pl.ds(HALF + by, rows), :]
            beside = (line(8), line(4)) if side == 0 else (line(5), line(9))
            value = apply(c, depth, i, make_u, make_v, lose_v, rest, rows_by(0), rows_by, *beside)
            image_beyond = jnp.where(inside, value, 0.0)

            c, make_u, make_v, lose_v, rest = at_column(column)
            gain = make_v if side == 0 else lose_v
            fixed[...] = lines[member, side]
            for first in (0, HALF + rows):
                fixed[first : first + HALF, :] = fixed[first : first + HALF, :] + gain * outer[first : first + HALF, :]

            rows_by = lambda by: fixed[pl.ds(HALF + by, rows), :]
            beside = (image_beyond, line(2)) if side == 0 else (line(3), image_beyond)
            two = apply(c, depth, i, make_u, make_v, lose_v, rest, rows_by(0), rows_by, *beside)
            columns_two[member, side] = two
            terms = (line(4 + side) * two, line(side) * two, two * two)
            sums = [value + term for value, term in zip(sums, terms)]
        for index, value in zip((2, 4, 5), sums):
            at = 8 * index + member
            total[at : at + 1, :] = total[at : at + 1, :] + jnp.sum(value, axis=0, keepdims=True)

    row = jnp.zeros((8, depth), jnp.float32)
    for index in range(6):
        value = jnp.sum(total[8 * index : 8 * index + 8], axis=1, keepdims=True)
        row = row + jnp.where(own_lane(8 * index), value, 0.0)
    message[...] = jnp.broadcast_to(jnp.sum(row, axis=0, keepdims=True), message.shape)


def product(left, right):
    a, b, c, d = left
    e, f, g, h = right
    return a * e + b * g, a * f + b * h, c * e + d * g, c * f + d * h


def first_column(h00, s01, h11):
    scale = tau_step / 2.0**squarings
    one = jnp.ones_like(h00)
    z1 = (scale * h00, scale * s01, scale * one, scale * h11)
    z2 = product(z1, z1)
    z3, z4 = product(z2, z1), product(z2, z2)
    weights = [1.0 / math.factorial(k + 1) for k in range(taylor_terms)]

    def block(first):
        w0, w1, w2, w3 = weights[first : first + 4]
        terms = [w1 * p + w2 * q + w3 * r for p, q, r in zip(z1, z2, z3)]
        return terms[0] + w0, terms[1], terms[2], terms[3] + w0

    phi = block(taylor_terms - 4)
    for first in range(taylor_terms - 8, -1, -4):
        phi = tuple(p + q for p, q in zip(product(z4, phi), block(first)))
    p00, p01, p10, p11 = product(z1, phi)
    p00, p11 = 1.0 + p00, 1.0 + p11
    q0, q1 = scale * phi[2], scale * phi[3]
    for _ in range(squarings):
        p00, p01, p10, p11, q0, q1 = (
            p00 * p00 + p01 * p10,
            p00 * p01 + p01 * p11,
            p10 * p00 + p11 * p10,
            p10 * p01 + p11 * p11,
            q0 * p00 + q1 * p10 + q0,
            q0 * p01 + q1 * p11 + q1,
        )
    return p00, p10, q0


def combine_kernel(gathered, field, image_one, image_two, columns_two, propagated, entries):
    members, rows, cols, depth = field.shape
    sums = jnp.broadcast_to(jnp.sum(gathered[...], axis=0, keepdims=True), (8, 128))
    g00, g01, g02, g11, g12, g22 = [
        jnp.broadcast_to(jnp.sum(jnp.where(own_lane(8 * index), sums, 0.0), axis=1, keepdims=True), (8, 128))
        for index in range(6)
    ]
    tiny = jnp.finfo(jnp.float32).tiny
    h00 = g01 / g00
    square_10 = jnp.maximum(g11 / g00 - h00 * h00, tiny)
    s01 = (g02 - h00 * g01) / g00
    h11 = ((g12 - h00 * g02) - h00 * (g11 - h00 * g01)) / (g00 * square_10)
    norm_2 = ((g22 - h00 * g12) - h00 * (g12 - h00 * g11)) / (g00 * square_10)
    h10 = jnp.sqrt(square_10)
    h01 = s01 / h10
    h21 = jnp.sqrt(jnp.maximum(norm_2 - h01 * h01 - h11 * h11, 0.0))
    e0, e1, e2 = first_column(h00, s01, h11)
    a2 = e2
    a1 = e1 - e2 * (h00 + h11)
    a0 = e0 - e1 * h00 - e2 * (s01 - h11 * h00)
    lane = lax.broadcasted_iota(jnp.int32, h00.shape, 1)
    table = h21
    for index, entry in enumerate((h00, h10, h01, h11)):
        table = jnp.where(lane == index, entry, table)
    entries[...] = (tau_step * table)[: entries.shape[0], : entries.shape[1]]
    place_j = lax.broadcasted_iota(jnp.int32, (cols, depth), 0)
    for member in range(members):
        b0, b1, b2 = [jnp.broadcast_to(a[member : member + 1], (cols, depth)) for a in (a0, a1, a2)]
        for row in range(rows):
            two = jnp.where(place_j == 0, columns_two[member, 0, row : row + 1], image_two[member, row])
            two = jnp.where(place_j == cols - 1, columns_two[member, 1, row : row + 1], two)
            propagated[member, row] = b0 * field[member, row] + b1 * image_one[member, row] + b2 * two


def shards(density, rate_table):
    members, rows, cols, depth = density.shape
    size_x, size_y = lax.axis_size("gx"), lax.axis_size("gy")
    devices = size_x * size_y
    vmem = pl.BlockSpec(memory_space=pltpu.VMEM)
    parity_x, parity_y = lax.axis_index("gx") % 2, lax.axis_index("gy") % 2

    def swap(axis, size, first, value):
        def partner(x, y):
            at = x if axis == "gx" else y
            other = at + 1 if (at - first) % 2 == 0 else at - 1
            if not 0 <= other < size:
                return (x, y ^ 1) if axis == "gx" else (x ^ 1, y)
            return (other, y) if axis == "gx" else (x, other)

        pairs = [
            (x * size_y + y, partner(x, y)[0] * size_y + partner(x, y)[1])
            for x in range(size_x)
            for y in range(size_y)
        ]
        return lax.ppermute(value, ("gx", "gy"), pairs)

    assert size_x % 2 == 0 and size_y % 2 == 0

    def swaps(axis, size, parity, initial, last):
        if initial is last:
            return swap(axis, size, 0, last), swap(axis, size, 1, last)
        is_even = parity == 0
        return (
            swap(axis, size, 0, jnp.where(is_even, last, initial)),
            swap(axis, size, 1, jnp.where(is_even, initial, last)),
        )

    initial, last = (density, density) if rows == REACH else (density[:, :REACH], density[:, rows - REACH :])
    is_even = parity_x == 0
    even_x = swap("gx", size_x, 0, initial if rows == REACH else jnp.where(is_even, last, initial))

    edge = jax.ShapeDtypeStruct((members, rows, 2, depth), jnp.float32)
    block = jax.ShapeDtypeStruct(density.shape, jnp.float32)
    parity = pl.pallas_call(
        parity_kernel,
        out_shape=jax.ShapeDtypeStruct((8, depth), jnp.int32),
        out_specs=vmem,
        compiler_params=pltpu.CompilerParams(vmem_limit_bytes=2**20),
        cost_estimate=pl.CostEstimate(flops=10**8, bytes_accessed=0, transcendentals=0),
        name="parity",
    )()
    for_odd, for_even = pl.pallas_call(
        edges_kernel,
        out_shape=[edge, edge],
        in_specs=[vmem, vmem],
        out_specs=[vmem] * 2,
        compiler_params=pltpu.CompilerParams(vmem_limit_bytes=2 * 2**20),
        name="edges",
    )(parity, density)
    odd_y = swap("gy", size_y, 1, for_odd)
    even_y = swap("gy", size_y, 0, for_even)

    even_y, for_odd_x = lax.optimization_barrier((even_y, initial if rows == REACH else jnp.where(is_even, initial, last)))
    odd_x = swap("gx", size_x, 1, for_odd_x)
    even_x, odd_y, even_y = lax.optimization_barrier((even_x, odd_y, even_y))

    def corners(first):
        even, odd = even_y[:, first : first + HALF], odd_y[:, first : first + HALF]
        left = jnp.where(parity_y == 0, odd, even)[:, :, 1:]
        right = jnp.where(parity_y == 0, even, odd)[:, :, :1]
        return jnp.concatenate([left, right], axis=2)

    even_corners, odd_corners = swaps("gx", size_x, parity_x, corners(0), corners(rows - HALF))

    lattice = (size_x * rows, size_y * cols)
    tall, span = rows + 2 * HALF, cols + 2 * GAP
    image_one, image_two, lines, parts = pl.pallas_call(
        functools.partial(images_kernel, lattice),
        out_shape=[
            block,
            block,
            jax.ShapeDtypeStruct((members, 10, tall, depth), jnp.float32),
            jax.ShapeDtypeStruct((48, depth), jnp.float32),
        ],
        in_specs=[vmem] * 6,
        out_specs=[vmem] * 4,
        scratch_shapes=[
            pltpu.VMEM((members, (rows + 2 * REACH) * span, depth), jnp.float32),
            pltpu.VMEM((members, tall * span, depth), jnp.float32),
        ],
        compiler_params=pltpu.CompilerParams(vmem_limit_bytes=8 * 2**20),
        name="images",
    )(rate_table, density, even_x, odd_x, even_y, odd_y)

    columns_two, message = pl.pallas_call(
        functools.partial(corners_kernel, lattice, cols),
        out_shape=[
            jax.ShapeDtypeStruct((members, 2, rows, depth), jnp.float32),
            jax.ShapeDtypeStruct((devices, 128), jnp.float32),
        ],
        in_specs=[vmem] * 5,
        out_specs=[vmem, vmem],
        scratch_shapes=[
            pltpu.VMEM((members, 2, 2, tall, depth), jnp.float32),
            pltpu.VMEM((48, depth), jnp.float32),
        ],
        compiler_params=pltpu.CompilerParams(vmem_limit_bytes=4 * 2**20),
        name="corners",
    )(rate_table, lines, odd_corners, even_corners, parts)

    order = [0] + [i for i in range(devices - 1, 0, -1)]
    gathered = lax.all_to_all(message, ("gx", "gy"), 0, 0, axis_index_groups=[order], tiled=True)

    return pl.pallas_call(
        combine_kernel,
        out_shape=[block, jax.ShapeDtypeStruct((members, 5), jnp.float32)],
        in_specs=[vmem] * 5,
        out_specs=[vmem, vmem],
        compiler_params=pltpu.CompilerParams(vmem_limit_bytes=8 * 2**20),
        name="combine",
    )(gathered, density, image_one, image_two, columns_two)


def solution(mesh):
    in_specs = (P(None, "gx", "gy", None), P())
    out_specs = (P(None, "gx", "gy", None), P())
    return jax.shard_map(shards, mesh=mesh, in_specs=in_specs, out_specs=out_specs, check_vma=False)
```

```python
import functools
import math

import jax
import jax.numpy as jnp
from jax import lax
from jax.experimental import pallas as pl
from jax.experimental.pallas import tpu as pltpu
from jax.sharding import PartitionSpec as P

tau_step = 0.01
taylor_terms = 16
squarings = 4
REACH = 4
HALF = 2
GAP = 8


def parity_kernel(parity):
    parity[...] = jnp.full(parity.shape, lax.axis_index("gy") % 2, jnp.int32)


def edges_kernel(parity, field, for_odd, for_even):
    is_even = jnp.broadcast_to(parity[:1], for_odd.shape[1:3] + parity.shape[1:])[None] == 0
    cols = field.shape[2]
    low, high = field[:, :, :2], field[:, :, cols - 2 :]
    for_even[...] = jnp.where(is_even, high, low)
    for_odd[...] = jnp.where(is_even, low, high)


def own_lane(first):
    row = lax.broadcasted_iota(jnp.int32, (8, 128), 0)
    return lax.broadcasted_iota(jnp.int32, (8, 128), 1) == first + row


def lanes(depth):
    lane = lax.broadcasted_iota(jnp.int32, (1, depth), 1)
    amount_k = lane.astype(jnp.float32)
    return amount_k, jnp.where(lane < depth - 1, amount_k + 1.0, 0.0), jnp.where(lane > 0, 1.0, 0.0)


def apply(c, depth, i, make_u, make_v, lose_v, rest, centre, rows_by, left, right):
    _, above_k, inner_k = lanes(depth)
    value = make_u * rows_by(-1) + (c[1] * (i + 1.0)) * rows_by(1)
    value = value + make_v * left
    value = value + lose_v * right
    pair = pltpu.roll(rows_by(2), 1, 1)
    value = value + (inner_k * (0.5 * c[4] * (i + 2.0) * (i + 1.0))) * pair
    split = c[5] * rows_by(-2) + c[6] * centre
    value = value + above_k * pltpu.roll(split, depth - 1, 1)
    out = rest + (c[1] * i + 0.5 * c[4] * i * (i - 1.0))
    return value - out * centre


def constants(rates, member, depth, amount_j):
    c = [jnp.broadcast_to(rates[member : member + 1, r : r + 1], (1, depth)) for r in range(9)]
    amount_k = lanes(depth)[0]
    ratio_j, ratio_k = amount_j / c[7], amount_k / c[8]
    make_u = c[0] / (1.0 + ratio_j * ratio_j)
    make_v = c[2] / (1.0 + ratio_k * ratio_k)
    lose_v = c[3] * (amount_j + 1.0)
    rest = make_u + make_v + (c[3] * amount_j + (c[5] + c[6]) * amount_k)
    return c, make_u, make_v, lose_v, rest


def sides(even, odd, is_even, lower_inside, higher_inside):
    lower, higher = jnp.where(is_even, odd, even), jnp.where(is_even, even, odd)
    return jnp.where(lower_inside, lower, 0.0), jnp.where(higher_inside, higher, 0.0)


def images_kernel(
    lattice,
    rates,
    field,
    even_x,
    odd_x,
    even_y,
    odd_y,
    image_one,
    image_two,
    lines,
    parts,
    wide,
    wide_image,
):
    members, rows, cols, depth = field.shape
    span = cols + 2 * GAP
    tall = rows + 2 * HALF
    index_i, index_j = lax.axis_index("gx"), lax.axis_index("gy")
    first_i, first_j = index_i * rows, index_j * cols
    even_i, even_j = index_i % 2 == 0, index_j % 2 == 0
    count_i, count_j = lattice

    def place(row, start, values):
        for at in range(values.shape[1]):
            first = (row + REACH + at) * span + GAP + start
            wide[:, first : first + values.shape[2]] = values[:, at]

    place(0, 0, field[...])
    above, below = sides(even_x[...], odd_x[...], even_i, first_i > 0, first_i + rows < count_i)
    place(-REACH, 0, above)
    place(rows, 0, below)
    left, right = sides(even_y[...], odd_y[...], even_j, first_j > 0, first_j + cols < count_j)
    place(0, -2, left)
    place(0, cols, right)
    corner = jnp.zeros((members, HALF, 1, depth), jnp.float32)
    for row in (-HALF, rows):
        place(row, -1, corner)
        place(row, cols, corner)

    sublane = lax.broadcasted_iota(jnp.int32, (span, 1), 0)
    amount_j = (first_j - GAP + sublane).astype(jnp.float32)
    place_j = lax.broadcasted_iota(jnp.int32, (cols, depth), 0)
    inner_j = (place_j > 0) & (place_j < cols - 1)

    for member in range(members):
        c, make_u, make_v, lose_v, rest = constants(rates, member, depth, amount_j)
        make_u, lose_v, rest = [term[GAP : GAP + cols] for term in (make_u, lose_v, rest)]

        def image(read, row):
            i = (first_i + row).astype(jnp.float32)
            rows_by = lambda by: read(row + by, 0)
            return apply(c, depth, i, make_u, make_v, lose_v, rest, read(row, 0), rows_by, read(row, -1), read(row, 1))

        def read_field(row, start):
            return wide[member, pl.ds((row + REACH) * span + GAP + start, cols), :]

        def read_image(row, start):
            return wide_image[member, pl.ds((row + HALF) * span + GAP + start, cols), :]

        for row in range(-HALF, rows + HALF):
            inside = (first_i + row >= 0) & (first_i + row < count_i)
            value = image(read_field, row)
            if row < 0 or row >= rows:
                value = jnp.where(inside, value, 0.0)
            else:
                image_one[member, row] = value
            wide_image[member, pl.ds((row + HALF) * span + GAP, cols), :] = value

        products = [jnp.zeros((cols, depth), jnp.float32) for _ in range(6)]
        for row in range(rows):
            zero = field[member, row]
            one = image_one[member, row]
            two = jnp.where(inner_j, image(read_image, row), 0.0)
            image_two[member, row] = two
            terms = (zero * zero, zero * one, zero * two, one * one, one * two, two * two)
            products = [total + term for total, term in zip(products, terms)]
        for index, total in enumerate(products):
            parts[8 * index + member : 8 * index + member + 1, :] = jnp.sum(total, axis=0, keepdims=True)

        for at, column in enumerate((0, cols - 1, 1, cols - 2)):
            lines[member, at] = wide_image[member, pl.ds(GAP + column, tall, stride=span), :]
        for at, column in enumerate((0, cols - 1, -1, cols, -2, cols + 1)):
            lines[member, 4 + at] = wide[member, pl.ds(HALF * span + GAP + column, tall, stride=span), :]

    for index in range(6):
        parts[8 * index + members : 8 * index + 8, :] = jnp.zeros((8 - members, depth), jnp.float32)


def corners_kernel(lattice, cols, rates, lines, odd_corners, even_corners, parts, columns_two, message, edge, total):
    members, _, tall, depth = lines.shape
    rows = tall - 2 * HALF
    index_i, index_j = lax.axis_index("gx"), lax.axis_index("gy")
    first_i, first_j = index_i * rows, index_j * cols
    count_i, count_j = lattice
    upper, lower = sides(
        even_corners[...], odd_corners[...], index_i % 2 == 0, first_i > 0, first_i + rows < count_i
    )
    i = (first_i + lax.broadcasted_iota(jnp.int32, (rows, depth), 0)).astype(jnp.float32)
    total[...] = parts[...]
    for member in range(members):

        def line(at):
            return lines[member, at, pl.ds(HALF, rows), :]

        sums = [jnp.zeros((rows, depth), jnp.float32) for _ in range(3)]
        for side, column, beyond, inside in (
            (0, 0, -1, first_j > 0),
            (1, cols - 1, cols, first_j + cols < count_j),
        ):

            def at_column(column):
                amount_j = jnp.broadcast_to((first_j + column).astype(jnp.float32), (1, depth))
                return constants(rates, member, depth, amount_j)

            outer, fixed = edge.at[member, side, 0], edge.at[member, side, 1]
            outer[HALF : HALF + rows, :] = line(6 + side)
            for row in range(HALF):
                for first, corner in ((0, upper), (HALF + rows, lower)):
                    value = corner[member, row, side : side + 1, :]
                    outer[first + row : first + row + 1, :] = jnp.where(inside, value, 0.0)

            c, make_u, make_v, lose_v, rest = at_column(beyond)
            rows_by = lambda by: outer[pl.ds(HALF + by, rows), :]
            beside = (line(8), line(4)) if side == 0 else (line(5), line(9))
            value = apply(c, depth, i, make_u, make_v, lose_v, rest, rows_by(0), rows_by, *beside)
            image_beyond = jnp.where(inside, value, 0.0)

            c, make_u, make_v, lose_v, rest = at_column(column)
            gain = make_v if side == 0 else lose_v
            fixed[...] = lines[member, side]
            for first in (0, HALF + rows):
                fixed[first : first + HALF, :] = fixed[first : first + HALF, :] + gain * outer[first : first + HALF, :]

            rows_by = lambda by: fixed[pl.ds(HALF + by, rows), :]
            beside = (image_beyond, line(2)) if side == 0 else (line(3), image_beyond)
            two = apply(c, depth, i, make_u, make_v, lose_v, rest, rows_by(0), rows_by, *beside)
            columns_two[member, side] = two
            terms = (line(4 + side) * two, line(side) * two, two * two)
            sums = [value + term for value, term in zip(sums, terms)]
        for index, value in zip((2, 4, 5), sums):
            at = 8 * index + member
            total[at : at + 1, :] = total[at : at + 1, :] + jnp.sum(value, axis=0, keepdims=True)

    row = jnp.zeros((8, depth), jnp.float32)
    for index in range(6):
        value = jnp.sum(total[8 * index : 8 * index + 8], axis=1, keepdims=True)
        row = row + jnp.where(own_lane(8 * index), value, 0.0)
    message[...] = jnp.broadcast_to(jnp.sum(row, axis=0, keepdims=True), message.shape)


def product(left, right):
    a, b, c, d = left
    e, f, g, h = right
    return a * e + b * g, a * f + b * h, c * e + d * g, c * f + d * h


def first_column(h00, s01, h11):
    scale = tau_step / 2.0**squarings
    one = jnp.ones_like(h00)
    z1 = (scale * h00, scale * s01, scale * one, scale * h11)
    z2 = product(z1, z1)
    z3, z4 = product(z2, z1), product(z2, z2)
    weights = [1.0 / math.factorial(k + 1) for k in range(taylor_terms)]

    def block(first):
        w0, w1, w2, w3 = weights[first : first + 4]
        terms = [w1 * p + w2 * q + w3 * r for p, q, r in zip(z1, z2, z3)]
        return terms[0] + w0, terms[1], terms[2], terms[3] + w0

    phi = block(taylor_terms - 4)
    for first in range(taylor_terms - 8, -1, -4):
        phi = tuple(p + q for p, q in zip(product(z4, phi), block(first)))
    p00, p01, p10, p11 = product(z1, phi)
    p00, p11 = 1.0 + p00, 1.0 + p11
    q0, q1 = scale * phi[2], scale * phi[3]
    for _ in range(squarings):
        p00, p01, p10, p11, q0, q1 = (
            p00 * p00 + p01 * p10,
            p00 * p01 + p01 * p11,
            p10 * p00 + p11 * p10,
            p10 * p01 + p11 * p11,
            q0 * p00 + q1 * p10 + q0,
            q0 * p01 + q1 * p11 + q1,
        )
    return p00, p10, q0


def combine_kernel(gathered, field, image_one, image_two, columns_two, propagated, entries):
    members, rows, cols, depth = field.shape
    sums = jnp.broadcast_to(jnp.sum(gathered[...], axis=0, keepdims=True), (8, 128))
    g00, g01, g02, g11, g12, g22 = [
        jnp.broadcast_to(jnp.sum(jnp.where(own_lane(8 * index), sums, 0.0), axis=1, keepdims=True), (8, 128))
        for index in range(6)
    ]
    tiny = jnp.finfo(jnp.float32).tiny
    h00 = g01 / g00
    square_10 = jnp.maximum(g11 / g00 - h00 * h00, tiny)
    s01 = (g02 - h00 * g01) / g00
    h11 = ((g12 - h00 * g02) - h00 * (g11 - h00 * g01)) / (g00 * square_10)
    norm_2 = ((g22 - h00 * g12) - h00 * (g12 - h00 * g11)) / (g00 * square_10)
    h10 = jnp.sqrt(square_10)
    h01 = s01 / h10
    h21 = jnp.sqrt(jnp.maximum(norm_2 - h01 * h01 - h11 * h11, 0.0))
    e0, e1, e2 = first_column(h00, s01, h11)
    a2 = e2
    a1 = e1 - e2 * (h00 + h11)
    a0 = e0 - e1 * h00 - e2 * (s01 - h11 * h00)
    lane = lax.broadcasted_iota(jnp.int32, h00.shape, 1)
    table = h21
    for index, entry in enumerate((h00, h10, h01, h11)):
        table = jnp.where(lane == index, entry, table)
    entries[...] = (tau_step * table)[: entries.shape[0], : entries.shape[1]]
    place_j = lax.broadcasted_iota(jnp.int32, (cols, depth), 0)
    for member in range(members):
        b0, b1, b2 = [jnp.broadcast_to(a[member : member + 1], (cols, depth)) for a in (a0, a1, a2)]
        for row in range(rows):
            two = jnp.where(place_j == 0, columns_two[member, 0, row : row + 1], image_two[member, row])
            two = jnp.where(place_j == cols - 1, columns_two[member, 1, row : row + 1], two)
            propagated[member, row] = b0 * field[member, row] + b1 * image_one[member, row] + b2 * two


def shards(density, rate_table):
    members, rows, cols, depth = density.shape
    size_x, size_y = lax.axis_size("gx"), lax.axis_size("gy")
    devices = size_x * size_y
    vmem = pl.BlockSpec(memory_space=pltpu.VMEM)
    parity_x, parity_y = lax.axis_index("gx") % 2, lax.axis_index("gy") % 2

    def swap(axis, size, first, value):
        def partner(x, y):
            at = x if axis == "gx" else y
            other = at + 1 if (at - first) % 2 == 0 else at - 1
            if not 0 <= other < size:
                return (x, y ^ 1) if axis == "gx" else (x ^ 1, y)
            return (other, y) if axis == "gx" else (x, other)

        pairs = [
            (x * size_y + y, partner(x, y)[0] * size_y + partner(x, y)[1])
            for x in range(size_x)
            for y in range(size_y)
        ]
        return lax.ppermute(value, ("gx", "gy"), pairs)

    assert size_x % 2 == 0 and size_y % 2 == 0

    def swaps(axis, size, parity, initial, last):
        if initial is last:
            return swap(axis, size, 0, last), swap(axis, size, 1, last)
        is_even = parity == 0
        return (
            swap(axis, size, 0, jnp.where(is_even, last, initial)),
            swap(axis, size, 1, jnp.where(is_even, initial, last)),
        )

    initial, last = (density, density) if rows == REACH else (density[:, :REACH], density[:, rows - REACH :])
    is_even = parity_x == 0
    even_x = swap("gx", size_x, 0, initial if rows == REACH else jnp.where(is_even, last, initial))

    edge = jax.ShapeDtypeStruct((members, rows, 2, depth), jnp.float32)
    block = jax.ShapeDtypeStruct(density.shape, jnp.float32)
    parity = pl.pallas_call(
        parity_kernel,
        out_shape=jax.ShapeDtypeStruct((8, depth), jnp.int32),
        out_specs=vmem,
        compiler_params=pltpu.CompilerParams(vmem_limit_bytes=2**20),
        cost_estimate=pl.CostEstimate(flops=10**8, bytes_accessed=0, transcendentals=0),
        name="parity",
    )()
    for_odd, for_even = pl.pallas_call(
        edges_kernel,
        out_shape=[edge, edge],
        in_specs=[vmem, vmem],
        out_specs=[vmem] * 2,
        compiler_params=pltpu.CompilerParams(vmem_limit_bytes=2 * 2**20),
        name="edges",
    )(parity, density)
    odd_y = swap("gy", size_y, 1, for_odd)
    even_y = swap("gy", size_y, 0, for_even)

    even_y, for_odd_x = lax.optimization_barrier((even_y, initial if rows == REACH else jnp.where(is_even, initial, last)))
    odd_x = swap("gx", size_x, 1, for_odd_x)
    even_x, odd_y, even_y = lax.optimization_barrier((even_x, odd_y, even_y))

    def corners(first):
        even, odd = even_y[:, first : first + HALF], odd_y[:, first : first + HALF]
        left = jnp.where(parity_y == 0, odd, even)[:, :, 1:]
        right = jnp.where(parity_y == 0, even, odd)[:, :, :1]
        return jnp.concatenate([left, right], axis=2)

    even_corners, odd_corners = swaps("gx", size_x, parity_x, corners(0), corners(rows - HALF))

    lattice = (size_x * rows, size_y * cols)
    tall, span = rows + 2 * HALF, cols + 2 * GAP
    image_one, image_two, lines, parts = pl.pallas_call(
        functools.partial(images_kernel, lattice),
        out_shape=[
            block,
            block,
            jax.ShapeDtypeStruct((members, 10, tall, depth), jnp.float32),
            jax.ShapeDtypeStruct((48, depth), jnp.float32),
        ],
        in_specs=[vmem] * 6,
        out_specs=[vmem] * 4,
        scratch_shapes=[
            pltpu.VMEM((members, (rows + 2 * REACH) * span, depth), jnp.float32),
            pltpu.VMEM((members, tall * span, depth), jnp.float32),
        ],
        compiler_params=pltpu.CompilerParams(vmem_limit_bytes=8 * 2**20),
        name="images",
    )(rate_table, density, even_x, odd_x, even_y, odd_y)

    columns_two, message = pl.pallas_call(
        functools.partial(corners_kernel, lattice, cols),
        out_shape=[
            jax.ShapeDtypeStruct((members, 2, rows, depth), jnp.float32),
            jax.ShapeDtypeStruct((devices, 128), jnp.float32),
        ],
        in_specs=[vmem] * 5,
        out_specs=[vmem, vmem],
        scratch_shapes=[
            pltpu.VMEM((members, 2, 2, tall, depth), jnp.float32),
            pltpu.VMEM((48, depth), jnp.float32),
        ],
        compiler_params=pltpu.CompilerParams(vmem_limit_bytes=4 * 2**20),
        name="corners",
    )(rate_table, lines, odd_corners, even_corners, parts)

    order = list(range(devices - 1, -1, -1))
    gathered = lax.all_to_all(message, ("gx", "gy"), 0, 0, axis_index_groups=[order], tiled=True)

    return pl.pallas_call(
        combine_kernel,
        out_shape=[block, jax.ShapeDtypeStruct((members, 5), jnp.float32)],
        in_specs=[vmem] * 5,
        out_specs=[vmem, vmem],
        compiler_params=pltpu.CompilerParams(vmem_limit_bytes=8 * 2**20),
        name="combine",
    )(gathered, density, image_one, image_two, columns_two)


def solution(mesh):
    in_specs = (P(None, "gx", "gy", None), P())
    out_specs = (P(None, "gx", "gy", None), P())
    return jax.shard_map(shards, mesh=mesh, in_specs=in_specs, out_specs=out_specs, check_vma=False)
```

```python
import functools
import math

import jax
import jax.numpy as jnp
from jax import lax
from jax.experimental import pallas as pl
from jax.experimental.pallas import tpu as pltpu
from jax.sharding import PartitionSpec as P

tau_step = 0.01
taylor_terms = 16
squarings = 4
REACH = 4
HALF = 2
GAP = 8


def parity_kernel(parity):
    parity[...] = jnp.full(parity.shape, lax.axis_index("gy") % 2, jnp.int32)


def edges_kernel(parity, field, for_odd, for_even):
    is_even = jnp.broadcast_to(parity[:1], for_odd.shape[1:3] + parity.shape[1:])[None] == 0
    cols = field.shape[2]
    low, high = field[:, :, :2], field[:, :, cols - 2 :]
    for_even[...] = jnp.where(is_even, high, low)
    for_odd[...] = jnp.where(is_even, low, high)


def own_lane(first):
    row = lax.broadcasted_iota(jnp.int32, (8, 128), 0)
    return lax.broadcasted_iota(jnp.int32, (8, 128), 1) == first + row


def lanes(depth):
    lane = lax.broadcasted_iota(jnp.int32, (1, depth), 1)
    amount_k = lane.astype(jnp.float32)
    return amount_k, jnp.where(lane < depth - 1, amount_k + 1.0, 0.0), jnp.where(lane > 0, 1.0, 0.0)


def apply(c, depth, i, make_u, make_v, lose_v, rest, centre, rows_by, left, right):
    _, above_k, inner_k = lanes(depth)
    value = make_u * rows_by(-1) + (c[1] * (i + 1.0)) * rows_by(1)
    value = value + make_v * left
    value = value + lose_v * right
    pair = pltpu.roll(rows_by(2), 1, 1)
    value = value + (inner_k * (0.5 * c[4] * (i + 2.0) * (i + 1.0))) * pair
    split = c[5] * rows_by(-2) + c[6] * centre
    value = value + above_k * pltpu.roll(split, depth - 1, 1)
    out = rest + (c[1] * i + 0.5 * c[4] * i * (i - 1.0))
    return value - out * centre


def constants(rates, member, depth, amount_j):
    c = [jnp.broadcast_to(rates[member : member + 1, r : r + 1], (1, depth)) for r in range(9)]
    amount_k = lanes(depth)[0]
    ratio_j, ratio_k = amount_j / c[7], amount_k / c[8]
    make_u = c[0] / (1.0 + ratio_j * ratio_j)
    make_v = c[2] / (1.0 + ratio_k * ratio_k)
    lose_v = c[3] * (amount_j + 1.0)
    rest = make_u + make_v + (c[3] * amount_j + (c[5] + c[6]) * amount_k)
    return c, make_u, make_v, lose_v, rest


def sides(even, odd, is_even, lower_inside, higher_inside):
    lower, higher = jnp.where(is_even, odd, even), jnp.where(is_even, even, odd)
    return jnp.where(lower_inside, lower, 0.0), jnp.where(higher_inside, higher, 0.0)


def images_kernel(
    lattice,
    rates,
    field,
    even_x,
    odd_x,
    even_y,
    odd_y,
    image_one,
    image_two,
    lines,
    parts,
    wide,
    wide_image,
):
    members, rows, cols, depth = field.shape
    span = cols + 2 * GAP
    tall = rows + 2 * HALF
    index_i, index_j = lax.axis_index("gx"), lax.axis_index("gy")
    first_i, first_j = index_i * rows, index_j * cols
    even_i, even_j = index_i % 2 == 0, index_j % 2 == 0
    count_i, count_j = lattice

    def place(row, start, values):
        for at in range(values.shape[1]):
            first = (row + REACH + at) * span + GAP + start
            wide[:, first : first + values.shape[2]] = values[:, at]

    place(0, 0, field[...])
    above, below = sides(even_x[...], odd_x[...], even_i, first_i > 0, first_i + rows < count_i)
    place(-REACH, 0, above)
    place(rows, 0, below)
    left, right = sides(even_y[...], odd_y[...], even_j, first_j > 0, first_j + cols < count_j)
    place(0, -2, left)
    place(0, cols, right)
    corner = jnp.zeros((members, HALF, 1, depth), jnp.float32)
    for row in (-HALF, rows):
        place(row, -1, corner)
        place(row, cols, corner)

    sublane = lax.broadcasted_iota(jnp.int32, (span, 1), 0)
    amount_j = (first_j - GAP + sublane).astype(jnp.float32)
    place_j = lax.broadcasted_iota(jnp.int32, (cols, depth), 0)
    inner_j = (place_j > 0) & (place_j < cols - 1)

    for member in range(members):
        c, make_u, make_v, lose_v, rest = constants(rates, member, depth, amount_j)
        make_u, lose_v, rest = [term[GAP : GAP + cols] for term in (make_u, lose_v, rest)]

        def image(read, row):
            i = (first_i + row).astype(jnp.float32)
            rows_by = lambda by: read(row + by, 0)
            return apply(c, depth, i, make_u, make_v, lose_v, rest, read(row, 0), rows_by, read(row, -1), read(row, 1))

        def read_field(row, start):
            return wide[member, pl.ds((row + REACH) * span + GAP + start, cols), :]

        def read_image(row, start):
            return wide_image[member, pl.ds((row + HALF) * span + GAP + start, cols), :]

        for row in range(-HALF, rows + HALF):
            inside = (first_i + row >= 0) & (first_i + row < count_i)
            value = image(read_field, row)
            if row < 0 or row >= rows:
                value = jnp.where(inside, value, 0.0)
            else:
                image_one[member, row] = value
            wide_image[member, pl.ds((row + HALF) * span + GAP, cols), :] = value

        products = [jnp.zeros((cols, depth), jnp.float32) for _ in range(6)]
        for row in range(rows):
            zero = field[member, row]
            one = image_one[member, row]
            two = jnp.where(inner_j, image(read_image, row), 0.0)
            image_two[member, row] = two
            terms = (zero * zero, zero * one, zero * two, one * one, one * two, two * two)
            products = [total + term for total, term in zip(products, terms)]
        for index, total in enumerate(products):
            parts[8 * index + member : 8 * index + member + 1, :] = jnp.sum(total, axis=0, keepdims=True)

        for at, column in enumerate((0, cols - 1, 1, cols - 2)):
            lines[member, at] = wide_image[member, pl.ds(GAP + column, tall, stride=span), :]
        for at, column in enumerate((0, cols - 1, -1, cols, -2, cols + 1)):
            lines[member, 4 + at] = wide[member, pl.ds(HALF * span + GAP + column, tall, stride=span), :]

    for index in range(6):
        parts[8 * index + members : 8 * index + 8, :] = jnp.zeros((8 - members, depth), jnp.float32)


def corners_kernel(lattice, cols, rates, lines, odd_corners, even_corners, parts, columns_two, message, edge, total):
    members, _, tall, depth = lines.shape
    rows = tall - 2 * HALF
    index_i, index_j = lax.axis_index("gx"), lax.axis_index("gy")
    first_i, first_j = index_i * rows, index_j * cols
    count_i, count_j = lattice
    upper, lower = sides(
        even_corners[...], odd_corners[...], index_i % 2 == 0, first_i > 0, first_i + rows < count_i
    )
    i = (first_i + lax.broadcasted_iota(jnp.int32, (rows, depth), 0)).astype(jnp.float32)
    total[...] = parts[...]
    for member in range(members):

        def line(at):
            return lines[member, at, pl.ds(HALF, rows), :]

        sums = [jnp.zeros((rows, depth), jnp.float32) for _ in range(3)]
        for side, column, beyond, inside in (
            (0, 0, -1, first_j > 0),
            (1, cols - 1, cols, first_j + cols < count_j),
        ):

            def at_column(column):
                amount_j = jnp.broadcast_to((first_j + column).astype(jnp.float32), (1, depth))
                return constants(rates, member, depth, amount_j)

            outer, fixed = edge.at[member, side, 0], edge.at[member, side, 1]
            outer[HALF : HALF + rows, :] = line(6 + side)
            for row in range(HALF):
                for first, corner in ((0, upper), (HALF + rows, lower)):
                    value = corner[member, row, side : side + 1, :]
                    outer[first + row : first + row + 1, :] = jnp.where(inside, value, 0.0)

            c, make_u, make_v, lose_v, rest = at_column(beyond)
            rows_by = lambda by: outer[pl.ds(HALF + by, rows), :]
            beside = (line(8), line(4)) if side == 0 else (line(5), line(9))
            value = apply(c, depth, i, make_u, make_v, lose_v, rest, rows_by(0), rows_by, *beside)
            image_beyond = jnp.where(inside, value, 0.0)

            c, make_u, make_v, lose_v, rest = at_column(column)
            gain = make_v if side == 0 else lose_v
            fixed[:tall, :] = lines[member, side]
            for first in (0, HALF + rows):
                fixed[first : first + HALF, :] = fixed[first : first + HALF, :] + gain * outer[first : first + HALF, :]

            rows_by = lambda by: fixed[pl.ds(HALF + by, rows), :]
            beside = (image_beyond, line(2)) if side == 0 else (line(3), image_beyond)
            two = apply(c, depth, i, make_u, make_v, lose_v, rest, rows_by(0), rows_by, *beside)
            columns_two[member, side] = two
            terms = (line(4 + side) * two, line(side) * two, two * two)
            sums = [value + term for value, term in zip(sums, terms)]
        for index, value in zip((2, 4, 5), sums):
            at = 8 * index + member
            total[at : at + 1, :] = total[at : at + 1, :] + jnp.sum(value, axis=0, keepdims=True)

    row = jnp.zeros((8, depth), jnp.float32)
    for index in range(6):
        value = jnp.sum(total[8 * index : 8 * index + 8], axis=1, keepdims=True)
        row = row + jnp.where(own_lane(8 * index), value, 0.0)
    message[...] = jnp.broadcast_to(jnp.sum(row, axis=0, keepdims=True), message.shape)


def product(left, right):
    a, b, c, d = left
    e, f, g, h = right
    return a * e + b * g, a * f + b * h, c * e + d * g, c * f + d * h


def first_column(h00, s01, h11):
    scale = tau_step / 2.0**squarings
    one = jnp.ones_like(h00)
    z1 = (scale * h00, scale * s01, scale * one, scale * h11)
    z2 = product(z1, z1)
    z3, z4 = product(z2, z1), product(z2, z2)
    weights = [1.0 / math.factorial(k + 1) for k in range(taylor_terms)]

    def block(first):
        w0, w1, w2, w3 = weights[first : first + 4]
        terms = [w1 * p + w2 * q + w3 * r for p, q, r in zip(z1, z2, z3)]
        return terms[0] + w0, terms[1], terms[2], terms[3] + w0

    phi = block(taylor_terms - 4)
    for first in range(taylor_terms - 8, -1, -4):
        phi = tuple(p + q for p, q in zip(product(z4, phi), block(first)))
    p00, p01, p10, p11 = product(z1, phi)
    p00, p11 = 1.0 + p00, 1.0 + p11
    q0, q1 = scale * phi[2], scale * phi[3]
    for _ in range(squarings):
        p00, p01, p10, p11, q0, q1 = (
            p00 * p00 + p01 * p10,
            p00 * p01 + p01 * p11,
            p10 * p00 + p11 * p10,
            p10 * p01 + p11 * p11,
            q0 * p00 + q1 * p10 + q0,
            q0 * p01 + q1 * p11 + q1,
        )
    return p00, p10, q0


def combine_kernel(gathered, field, image_one, image_two, columns_two, propagated, entries):
    members, rows, cols, depth = field.shape
    sums = jnp.broadcast_to(jnp.sum(gathered[...], axis=0, keepdims=True), (8, 128))
    g00, g01, g02, g11, g12, g22 = [
        jnp.broadcast_to(jnp.sum(jnp.where(own_lane(8 * index), sums, 0.0), axis=1, keepdims=True), (8, 128))
        for index in range(6)
    ]
    tiny = jnp.finfo(jnp.float32).tiny
    h00 = g01 / g00
    square_10 = jnp.maximum(g11 / g00 - h00 * h00, tiny)
    s01 = (g02 - h00 * g01) / g00
    h11 = ((g12 - h00 * g02) - h00 * (g11 - h00 * g01)) / (g00 * square_10)
    norm_2 = ((g22 - h00 * g12) - h00 * (g12 - h00 * g11)) / (g00 * square_10)
    h10 = jnp.sqrt(square_10)
    h01 = s01 / h10
    h21 = jnp.sqrt(jnp.maximum(norm_2 - h01 * h01 - h11 * h11, 0.0))
    e0, e1, e2 = first_column(h00, s01, h11)
    a2 = e2
    a1 = e1 - e2 * (h00 + h11)
    a0 = e0 - e1 * h00 - e2 * (s01 - h11 * h00)
    lane = lax.broadcasted_iota(jnp.int32, h00.shape, 1)
    table = h21
    for index, entry in enumerate((h00, h10, h01, h11)):
        table = jnp.where(lane == index, entry, table)
    entries[...] = (tau_step * table)[: entries.shape[0], : entries.shape[1]]
    place_j = lax.broadcasted_iota(jnp.int32, (cols, depth), 0)
    for member in range(members):
        b0, b1, b2 = [jnp.broadcast_to(a[member : member + 1], (cols, depth)) for a in (a0, a1, a2)]
        for row in range(rows):
            two = jnp.where(place_j == 0, columns_two[member, 0, row : row + 1], image_two[member, row])
            two = jnp.where(place_j == cols - 1, columns_two[member, 1, row : row + 1], two)
            propagated[member, row] = b0 * field[member, row] + b1 * image_one[member, row] + b2 * two


def shards(density, rate_table):
    members, rows, cols, depth = density.shape
    size_x, size_y = lax.axis_size("gx"), lax.axis_size("gy")
    devices = size_x * size_y
    vmem = pl.BlockSpec(memory_space=pltpu.VMEM)
    parity_x, parity_y = lax.axis_index("gx") % 2, lax.axis_index("gy") % 2

    def swap(axis, size, first, value):
        def partner(x, y):
            at = x if axis == "gx" else y
            other = at + 1 if (at - first) % 2 == 0 else at - 1
            if not 0 <= other < size:
                return (x, y ^ 1) if axis == "gx" else (x ^ 1, y)
            return (other, y) if axis == "gx" else (x, other)

        pairs = [
            (x * size_y + y, partner(x, y)[0] * size_y + partner(x, y)[1])
            for x in range(size_x)
            for y in range(size_y)
        ]
        return lax.ppermute(value, ("gx", "gy"), pairs)

    assert size_x % 2 == 0 and size_y % 2 == 0

    def swaps(axis, size, parity, initial, last):
        if initial is last:
            return swap(axis, size, 0, last), swap(axis, size, 1, last)
        is_even = parity == 0
        return (
            swap(axis, size, 0, jnp.where(is_even, last, initial)),
            swap(axis, size, 1, jnp.where(is_even, initial, last)),
        )

    initial, last = (density, density) if rows == REACH else (density[:, :REACH], density[:, rows - REACH :])
    is_even = parity_x == 0
    even_x = swap("gx", size_x, 0, initial if rows == REACH else jnp.where(is_even, last, initial))

    edge = jax.ShapeDtypeStruct((members, rows, 2, depth), jnp.float32)
    block = jax.ShapeDtypeStruct(density.shape, jnp.float32)
    parity = pl.pallas_call(
        parity_kernel,
        out_shape=jax.ShapeDtypeStruct((8, depth), jnp.int32),
        out_specs=vmem,
        compiler_params=pltpu.CompilerParams(vmem_limit_bytes=2**20),
        cost_estimate=pl.CostEstimate(flops=10**8, bytes_accessed=0, transcendentals=0),
        name="parity",
    )()
    for_odd, for_even = pl.pallas_call(
        edges_kernel,
        out_shape=[edge, edge],
        in_specs=[vmem, vmem],
        out_specs=[vmem] * 2,
        compiler_params=pltpu.CompilerParams(vmem_limit_bytes=2 * 2**20),
        name="edges",
    )(parity, density)
    odd_y = swap("gy", size_y, 1, for_odd)
    even_y = swap("gy", size_y, 0, for_even)

    even_y, for_odd_x = lax.optimization_barrier((even_y, initial if rows == REACH else jnp.where(is_even, initial, last)))
    odd_x = swap("gx", size_x, 1, for_odd_x)
    even_x, odd_y, even_y = lax.optimization_barrier((even_x, odd_y, even_y))

    def corners(first):
        even, odd = even_y[:, first : first + HALF], odd_y[:, first : first + HALF]
        left = jnp.where(parity_y == 0, odd, even)[:, :, 1:]
        right = jnp.where(parity_y == 0, even, odd)[:, :, :1]
        return jnp.concatenate([left, right], axis=2)

    even_corners, odd_corners = swaps("gx", size_x, parity_x, corners(0), corners(rows - HALF))

    lattice = (size_x * rows, size_y * cols)
    tall, span = rows + 2 * HALF, cols + 2 * GAP
    image_one, image_two, lines, parts = pl.pallas_call(
        functools.partial(images_kernel, lattice),
        out_shape=[
            block,
            block,
            jax.ShapeDtypeStruct((members, 10, tall, depth), jnp.float32),
            jax.ShapeDtypeStruct((48, depth), jnp.float32),
        ],
        in_specs=[vmem] * 6,
        out_specs=[vmem] * 4,
        scratch_shapes=[
            pltpu.VMEM((members, (rows + 2 * REACH) * span, depth), jnp.float32),
            pltpu.VMEM((members, (tall + 1) * span, depth), jnp.float32),
        ],
        compiler_params=pltpu.CompilerParams(vmem_limit_bytes=8 * 2**20),
        name="images",
    )(rate_table, density, even_x, odd_x, even_y, odd_y)

    columns_two, message = pl.pallas_call(
        functools.partial(corners_kernel, lattice, cols),
        out_shape=[
            jax.ShapeDtypeStruct((members, 2, rows, depth), jnp.float32),
            jax.ShapeDtypeStruct((devices, 128), jnp.float32),
        ],
        in_specs=[vmem] * 5,
        out_specs=[vmem, vmem],
        scratch_shapes=[
            pltpu.VMEM((members, 2, 2, 2 * tall, depth), jnp.float32),
            pltpu.VMEM((48, depth), jnp.float32),
        ],
        compiler_params=pltpu.CompilerParams(vmem_limit_bytes=4 * 2**20),
        name="corners",
    )(rate_table, lines, odd_corners, even_corners, parts)

    gathered = lax.all_to_all(message, ("gy", "gx"), 0, 0, tiled=True)

    return pl.pallas_call(
        combine_kernel,
        out_shape=[block, jax.ShapeDtypeStruct((members, 5), jnp.float32)],
        in_specs=[vmem] * 5,
        out_specs=[vmem, vmem],
        compiler_params=pltpu.CompilerParams(vmem_limit_bytes=8 * 2**20),
        name="combine",
    )(gathered, density, image_one, image_two, columns_two)


def solution(mesh):
    in_specs = (P(None, "gx", "gy", None), P())
    out_specs = (P(None, "gx", "gy", None), P())
    return jax.shard_map(shards, mesh=mesh, in_specs=in_specs, out_specs=out_specs, check_vma=False)
```

```python
import functools
import math

import jax
import jax.numpy as jnp
from jax import lax
from jax.experimental import pallas as pl
from jax.experimental.pallas import tpu as pltpu
from jax.sharding import PartitionSpec as P

tau_step = 0.01
taylor_terms = 16
squarings = 4
REACH = 4
HALF = 2
GAP = 8


def parity_kernel(parity):
    parity[...] = jnp.full(parity.shape, lax.axis_index("gy") % 2, jnp.int32)


def edges_kernel(parity, field, for_odd, for_even):
    is_even = jnp.broadcast_to(parity[:1], for_odd.shape[1:3] + parity.shape[1:])[None] == 0
    cols = field.shape[2]
    low, high = field[:, :, :2], field[:, :, cols - 2 :]
    for_even[...] = jnp.where(is_even, high, low)
    for_odd[...] = jnp.where(is_even, low, high)


def own_lane(first):
    row = lax.broadcasted_iota(jnp.int32, (8, 128), 0)
    return lax.broadcasted_iota(jnp.int32, (8, 128), 1) == first + row


def lanes(depth):
    lane = lax.broadcasted_iota(jnp.int32, (1, depth), 1)
    amount_k = lane.astype(jnp.float32)
    return amount_k, jnp.where(lane < depth - 1, amount_k + 1.0, 0.0), jnp.where(lane > 0, 1.0, 0.0)


def apply(c, depth, i, make_u, make_v, lose_v, rest, centre, rows_by, left, right):
    _, above_k, inner_k = lanes(depth)
    value = make_u * rows_by(-1) + (c[1] * (i + 1.0)) * rows_by(1)
    value = value + make_v * left
    value = value + lose_v * right
    pair = pltpu.roll(rows_by(2), 1, 1)
    value = value + (inner_k * (0.5 * c[4] * (i + 2.0) * (i + 1.0))) * pair
    split = c[5] * rows_by(-2) + c[6] * centre
    value = value + above_k * pltpu.roll(split, depth - 1, 1)
    out = rest + (c[1] * i + 0.5 * c[4] * i * (i - 1.0))
    return value - out * centre


def constants(rates, member, depth, amount_j):
    c = [jnp.broadcast_to(rates[member : member + 1, r : r + 1], (1, depth)) for r in range(9)]
    amount_k = lanes(depth)[0]
    ratio_j, ratio_k = amount_j / c[7], amount_k / c[8]
    make_u = c[0] / (1.0 + ratio_j * ratio_j)
    make_v = c[2] / (1.0 + ratio_k * ratio_k)
    lose_v = c[3] * (amount_j + 1.0)
    rest = make_u + make_v + (c[3] * amount_j + (c[5] + c[6]) * amount_k)
    return c, make_u, make_v, lose_v, rest


def sides(even, odd, is_even, lower_inside, higher_inside):
    lower, higher = jnp.where(is_even, odd, even), jnp.where(is_even, even, odd)
    return jnp.where(lower_inside, lower, 0.0), jnp.where(higher_inside, higher, 0.0)


def images_kernel(
    lattice,
    rates,
    field,
    even_x,
    odd_x,
    even_y,
    odd_y,
    image_one,
    image_two,
    lines,
    parts,
    wide,
    wide_image,
):
    members, rows, cols, depth = field.shape
    span = cols + 2 * GAP
    tall = rows + 2 * HALF
    index_i, index_j = lax.axis_index("gx"), lax.axis_index("gy")
    first_i, first_j = index_i * rows, index_j * cols
    even_i, even_j = index_i % 2 == 0, index_j % 2 == 0
    count_i, count_j = lattice

    def place(row, start, values):
        for at in range(values.shape[1]):
            first = (row + REACH + at) * span + GAP + start
            wide[:, first : first + values.shape[2]] = values[:, at]

    place(0, 0, field[...])
    above, below = sides(even_x[...], odd_x[...], even_i, first_i > 0, first_i + rows < count_i)
    place(-REACH, 0, above)
    place(rows, 0, below)
    left, right = sides(even_y[...], odd_y[...], even_j, first_j > 0, first_j + cols < count_j)
    place(0, -2, left)
    place(0, cols, right)
    corner = jnp.zeros((members, HALF, 1, depth), jnp.float32)
    for row in (-HALF, rows):
        place(row, -1, corner)
        place(row, cols, corner)

    sublane = lax.broadcasted_iota(jnp.int32, (span, 1), 0)
    amount_j = (first_j - GAP + sublane).astype(jnp.float32)
    place_j = lax.broadcasted_iota(jnp.int32, (cols, depth), 0)
    inner_j = (place_j > 0) & (place_j < cols - 1)

    for member in range(members):
        c, make_u, make_v, lose_v, rest = constants(rates, member, depth, amount_j)
        make_u, lose_v, rest = [term[GAP : GAP + cols] for term in (make_u, lose_v, rest)]

        def image(read, row):
            i = (first_i + row).astype(jnp.float32)
            rows_by = lambda by: read(row + by, 0)
            return apply(c, depth, i, make_u, make_v, lose_v, rest, read(row, 0), rows_by, read(row, -1), read(row, 1))

        def read_field(row, start):
            return wide[member, pl.ds((row + REACH) * span + GAP + start, cols), :]

        def read_image(row, start):
            return wide_image[member, pl.ds((row + HALF) * span + GAP + start, cols), :]

        for row in range(-HALF, rows + HALF):
            inside = (first_i + row >= 0) & (first_i + row < count_i)
            value = image(read_field, row)
            if row < 0 or row >= rows:
                value = jnp.where(inside, value, 0.0)
            else:
                image_one[member, row] = value
            wide_image[member, pl.ds((row + HALF) * span + GAP, cols), :] = value

        products = [jnp.zeros((cols, depth), jnp.float32) for _ in range(6)]
        for row in range(rows):
            zero = field[member, row]
            one = image_one[member, row]
            two = jnp.where(inner_j, image(read_image, row), 0.0)
            image_two[member, row] = two
            terms = (zero * zero, zero * one, zero * two, one * one, one * two, two * two)
            products = [total + term for total, term in zip(products, terms)]
        for index, total in enumerate(products):
            parts[8 * index + member : 8 * index + member + 1, :] = jnp.sum(total, axis=0, keepdims=True)

        for at, column in enumerate((0, cols - 1, 1, cols - 2)):
            lines[member, at] = wide_image[member, pl.ds(GAP + column, tall, stride=span), :]
        for at, column in enumerate((0, cols - 1, -1, cols, -2, cols + 1)):
            lines[member, 4 + at] = wide[member, pl.ds(HALF * span + GAP + column, tall, stride=span), :]

    for index in range(6):
        parts[8 * index + members : 8 * index + 8, :] = jnp.zeros((8 - members, depth), jnp.float32)


def corners_kernel(lattice, cols, rates, lines, odd_corners, even_corners, parts, columns_two, message, edge, total):
    members, _, tall, depth = lines.shape
    rows = tall - 2 * HALF
    index_i, index_j = lax.axis_index("gx"), lax.axis_index("gy")
    first_i, first_j = index_i * rows, index_j * cols
    count_i, count_j = lattice
    upper, lower = sides(
        even_corners[...], odd_corners[...], index_i % 2 == 0, first_i > 0, first_i + rows < count_i
    )
    i = (first_i + lax.broadcasted_iota(jnp.int32, (rows, depth), 0)).astype(jnp.float32)
    total[...] = parts[...]
    for member in range(members):

        def line(at):
            return lines[member, at, pl.ds(HALF, rows), :]

        sums = [jnp.zeros((rows, depth), jnp.float32) for _ in range(3)]
        for side, column, beyond, inside in (
            (0, 0, -1, first_j > 0),
            (1, cols - 1, cols, first_j + cols < count_j),
        ):

            def at_column(column):
                amount_j = jnp.broadcast_to((first_j + column).astype(jnp.float32), (1, depth))
                return constants(rates, member, depth, amount_j)

            outer, fixed = edge.at[member, side, 0], edge.at[member, side, 1]
            outer[HALF : HALF + rows, :] = line(6 + side)
            for row in range(HALF):
                for first, corner in ((0, upper), (HALF + rows, lower)):
                    value = corner[member, row, side : side + 1, :]
                    outer[first + row : first + row + 1, :] = jnp.where(inside, value, 0.0)

            c, make_u, make_v, lose_v, rest = at_column(beyond)
            rows_by = lambda by: outer[pl.ds(HALF + by, rows), :]
            beside = (line(8), line(4)) if side == 0 else (line(5), line(9))
            value = apply(c, depth, i, make_u, make_v, lose_v, rest, rows_by(0), rows_by, *beside)
            image_beyond = jnp.where(inside, value, 0.0)

            c, make_u, make_v, lose_v, rest = at_column(column)
            gain = make_v if side == 0 else lose_v
            fixed[:tall, :] = lines[member, side]
            for first in (0, HALF + rows):
                fixed[first : first + HALF, :] = fixed[first : first + HALF, :] + gain * outer[first : first + HALF, :]

            rows_by = lambda by: fixed[pl.ds(HALF + by, rows), :]
            beside = (image_beyond, line(2)) if side == 0 else (line(3), image_beyond)
            two = apply(c, depth, i, make_u, make_v, lose_v, rest, rows_by(0), rows_by, *beside)
            columns_two[member, side] = two
            terms = (line(4 + side) * two, line(side) * two, two * two)
            sums = [value + term for value, term in zip(sums, terms)]
        for index, value in zip((2, 4, 5), sums):
            at = 8 * index + member
            total[at : at + 1, :] = total[at : at + 1, :] + jnp.sum(value, axis=0, keepdims=True)

    row = jnp.zeros((8, depth), jnp.float32)
    for index in range(6):
        value = jnp.sum(total[8 * index : 8 * index + 8], axis=1, keepdims=True)
        row = row + jnp.where(own_lane(8 * index), value, 0.0)
    message[...] = jnp.broadcast_to(jnp.sum(row, axis=0, keepdims=True), message.shape)


def product(left, right):
    a, b, c, d = left
    e, f, g, h = right
    return a * e + b * g, a * f + b * h, c * e + d * g, c * f + d * h


def first_column(h00, s01, h11):
    scale = tau_step / 2.0**squarings
    one = jnp.ones_like(h00)
    z1 = (scale * h00, scale * s01, scale * one, scale * h11)
    z2 = product(z1, z1)
    z3, z4 = product(z2, z1), product(z2, z2)
    weights = [1.0 / math.factorial(k + 1) for k in range(taylor_terms)]

    def block(first):
        w0, w1, w2, w3 = weights[first : first + 4]
        terms = [w1 * p + w2 * q + w3 * r for p, q, r in zip(z1, z2, z3)]
        return terms[0] + w0, terms[1], terms[2], terms[3] + w0

    phi = block(taylor_terms - 4)
    for first in range(taylor_terms - 8, -1, -4):
        phi = tuple(p + q for p, q in zip(product(z4, phi), block(first)))
    p00, p01, p10, p11 = product(z1, phi)
    p00, p11 = 1.0 + p00, 1.0 + p11
    q0, q1 = scale * phi[2], scale * phi[3]
    for _ in range(squarings):
        p00, p01, p10, p11, q0, q1 = (
            p00 * p00 + p01 * p10,
            p00 * p01 + p01 * p11,
            p10 * p00 + p11 * p10,
            p10 * p01 + p11 * p11,
            q0 * p00 + q1 * p10 + q0,
            q0 * p01 + q1 * p11 + q1,
        )
    return p00, p10, q0


def combine_kernel(gathered, field, image_one, image_two, columns_two, propagated, entries):
    members, rows, cols, depth = field.shape
    sums = jnp.broadcast_to(jnp.sum(gathered[...], axis=0, keepdims=True), (8, 128))
    g00, g01, g02, g11, g12, g22 = [
        jnp.broadcast_to(jnp.sum(jnp.where(own_lane(8 * index), sums, 0.0), axis=1, keepdims=True), (8, 128))
        for index in range(6)
    ]
    tiny = jnp.finfo(jnp.float32).tiny
    h00 = g01 / g00
    square_10 = jnp.maximum(g11 / g00 - h00 * h00, tiny)
    s01 = (g02 - h00 * g01) / g00
    h11 = ((g12 - h00 * g02) - h00 * (g11 - h00 * g01)) / (g00 * square_10)
    norm_2 = ((g22 - h00 * g12) - h00 * (g12 - h00 * g11)) / (g00 * square_10)
    h10 = jnp.sqrt(square_10)
    h01 = s01 / h10
    h21 = jnp.sqrt(jnp.maximum(norm_2 - h01 * h01 - h11 * h11, 0.0))
    e0, e1, e2 = first_column(h00, s01, h11)
    a2 = e2
    a1 = e1 - e2 * (h00 + h11)
    a0 = e0 - e1 * h00 - e2 * (s01 - h11 * h00)
    lane = lax.broadcasted_iota(jnp.int32, h00.shape, 1)
    table = h21
    for index, entry in enumerate((h00, h10, h01, h11)):
        table = jnp.where(lane == index, entry, table)
    entries[...] = (tau_step * table)[: entries.shape[0], : entries.shape[1]]
    place_j = lax.broadcasted_iota(jnp.int32, (cols, depth), 0)
    for member in range(members):
        b0, b1, b2 = [jnp.broadcast_to(a[member : member + 1], (cols, depth)) for a in (a0, a1, a2)]
        for row in range(rows):
            two = jnp.where(place_j == 0, columns_two[member, 0, row : row + 1], image_two[member, row])
            two = jnp.where(place_j == cols - 1, columns_two[member, 1, row : row + 1], two)
            propagated[member, row] = b0 * field[member, row] + b1 * image_one[member, row] + b2 * two


def shards(density, rate_table):
    members, rows, cols, depth = density.shape
    size_x, size_y = lax.axis_size("gx"), lax.axis_size("gy")
    devices = size_x * size_y
    vmem = pl.BlockSpec(memory_space=pltpu.VMEM)
    parity_x, parity_y = lax.axis_index("gx") % 2, lax.axis_index("gy") % 2

    def swap(axis, size, first, value):
        def partner(x, y):
            at = x if axis == "gx" else y
            other = at + 1 if (at - first) % 2 == 0 else at - 1
            if not 0 <= other < size:
                return (x, y ^ 1) if axis == "gx" else (x ^ 1, y)
            return (other, y) if axis == "gx" else (x, other)

        pairs = [
            (x * size_y + y, partner(x, y)[0] * size_y + partner(x, y)[1])
            for x in range(size_x)
            for y in range(size_y)
        ]
        return lax.ppermute(value, ("gx", "gy"), pairs)

    assert size_x % 2 == 0 and size_y % 2 == 0

    def swaps(axis, size, parity, initial, last):
        if initial is last:
            return swap(axis, size, 0, last), swap(axis, size, 1, last)
        is_even = parity == 0
        return (
            swap(axis, size, 0, jnp.where(is_even, last, initial)),
            swap(axis, size, 1, jnp.where(is_even, initial, last)),
        )

    initial, last = (density, density) if rows == REACH else (density[:, :REACH], density[:, rows - REACH :])
    is_even = parity_x == 0
    even_x = swap("gx", size_x, 0, initial if rows == REACH else jnp.where(is_even, last, initial))

    edge = jax.ShapeDtypeStruct((members, rows, 2, depth), jnp.float32)
    block = jax.ShapeDtypeStruct(density.shape, jnp.float32)
    parity = pl.pallas_call(
        parity_kernel,
        out_shape=jax.ShapeDtypeStruct((8, depth), jnp.int32),
        out_specs=vmem,
        compiler_params=pltpu.CompilerParams(vmem_limit_bytes=2**20),
        cost_estimate=pl.CostEstimate(flops=10**8, bytes_accessed=0, transcendentals=0),
        name="parity",
    )()
    for_odd, for_even = pl.pallas_call(
        edges_kernel,
        out_shape=[edge, edge],
        in_specs=[vmem, vmem],
        out_specs=[vmem] * 2,
        compiler_params=pltpu.CompilerParams(vmem_limit_bytes=2 * 2**20),
        name="edges",
    )(parity, density)
    odd_y = swap("gy", size_y, 1, for_odd)
    even_y = swap("gy", size_y, 0, for_even)

    even_y, for_odd_x = lax.optimization_barrier((even_y, initial if rows == REACH else jnp.where(is_even, initial, last)))
    odd_x = swap("gx", size_x, 1, for_odd_x)

    def corners(first):
        even, odd = even_y[:, first : first + HALF], odd_y[:, first : first + HALF]
        left = jnp.where(parity_y == 0, odd, even)[:, :, 1:]
        right = jnp.where(parity_y == 0, even, odd)[:, :, :1]
        return jnp.concatenate([left, right], axis=2)

    even_corners, odd_corners = swaps("gx", size_x, parity_x, corners(0), corners(rows - HALF))

    lattice = (size_x * rows, size_y * cols)
    tall, span = rows + 2 * HALF, cols + 2 * GAP
    image_one, image_two, lines, parts = pl.pallas_call(
        functools.partial(images_kernel, lattice),
        out_shape=[
            block,
            block,
            jax.ShapeDtypeStruct((members, 10, tall, depth), jnp.float32),
            jax.ShapeDtypeStruct((48, depth), jnp.float32),
        ],
        in_specs=[vmem] * 6,
        out_specs=[vmem] * 4,
        scratch_shapes=[
            pltpu.VMEM((members, (rows + 2 * REACH) * span, depth), jnp.float32),
            pltpu.VMEM((members, (tall + 1) * span, depth), jnp.float32),
        ],
        compiler_params=pltpu.CompilerParams(vmem_limit_bytes=8 * 2**20),
        name="images",
    )(rate_table, density, even_x, odd_x, even_y, odd_y)

    columns_two, message = pl.pallas_call(
        functools.partial(corners_kernel, lattice, cols),
        out_shape=[
            jax.ShapeDtypeStruct((members, 2, rows, depth), jnp.float32),
            jax.ShapeDtypeStruct((devices, 128), jnp.float32),
        ],
        in_specs=[vmem] * 5,
        out_specs=[vmem, vmem],
        scratch_shapes=[
            pltpu.VMEM((members, 2, 2, 2 * tall, depth), jnp.float32),
            pltpu.VMEM((48, depth), jnp.float32),
        ],
        compiler_params=pltpu.CompilerParams(vmem_limit_bytes=4 * 2**20),
        name="corners",
    )(rate_table, lines, odd_corners, even_corners, parts)

    gathered = lax.all_to_all(message, ("gy", "gx"), 0, 0, tiled=True)

    return pl.pallas_call(
        combine_kernel,
        out_shape=[block, jax.ShapeDtypeStruct((members, 5), jnp.float32)],
        in_specs=[vmem] * 5,
        out_specs=[vmem, vmem],
        compiler_params=pltpu.CompilerParams(vmem_limit_bytes=8 * 2**20),
        name="combine",
    )(gathered, density, image_one, image_two, columns_two)


def solution(mesh):
    in_specs = (P(None, "gx", "gy", None), P())
    out_specs = (P(None, "gx", "gy", None), P())
    return jax.shard_map(shards, mesh=mesh, in_specs=in_specs, out_specs=out_specs, check_vma=False)
```

```python
import functools
import math

import jax
import jax.numpy as jnp
from jax import lax
from jax.experimental import pallas as pl
from jax.experimental.pallas import tpu as pltpu
from jax.sharding import PartitionSpec as P

tau_step = 0.01
taylor_terms = 16
squarings = 4
REACH = 4
HALF = 2
GAP = 8


def parity_kernel(parity):
    parity[...] = jnp.full(parity.shape, lax.axis_index("gy") % 2, jnp.int32)


def edges_kernel(parity, field, for_odd, for_even):
    is_even = jnp.broadcast_to(parity[:1], for_odd.shape[1:3] + parity.shape[1:])[None] == 0
    cols = field.shape[2]
    low, high = field[:, :, :2], field[:, :, cols - 2 :]
    for_even[...] = jnp.where(is_even, high, low)
    for_odd[...] = jnp.where(is_even, low, high)


def own_lane(first):
    row = lax.broadcasted_iota(jnp.int32, (8, 128), 0)
    return lax.broadcasted_iota(jnp.int32, (8, 128), 1) == first + row


def lanes(depth):
    lane = lax.broadcasted_iota(jnp.int32, (1, depth), 1)
    amount_k = lane.astype(jnp.float32)
    return amount_k, jnp.where(lane < depth - 1, amount_k + 1.0, 0.0), jnp.where(lane > 0, 1.0, 0.0)


def apply(c, depth, i, make_u, make_v, lose_v, rest, centre, rows_by, left, right):
    _, above_k, inner_k = lanes(depth)
    value = make_u * rows_by(-1) + (c[1] * (i + 1.0)) * rows_by(1)
    value = value + make_v * left
    value = value + lose_v * right
    pair = pltpu.roll(rows_by(2), 1, 1)
    value = value + (inner_k * (0.5 * c[4] * (i + 2.0) * (i + 1.0))) * pair
    split = c[5] * rows_by(-2) + c[6] * centre
    value = value + above_k * pltpu.roll(split, depth - 1, 1)
    out = rest + (c[1] * i + 0.5 * c[4] * i * (i - 1.0))
    return value - out * centre


def constants(rates, member, depth, amount_j):
    c = [jnp.broadcast_to(rates[member : member + 1, r : r + 1], (1, depth)) for r in range(9)]
    amount_k = lanes(depth)[0]
    ratio_j, ratio_k = amount_j / c[7], amount_k / c[8]
    make_u = c[0] / (1.0 + ratio_j * ratio_j)
    make_v = c[2] / (1.0 + ratio_k * ratio_k)
    lose_v = c[3] * (amount_j + 1.0)
    rest = make_u + make_v + (c[3] * amount_j + (c[5] + c[6]) * amount_k)
    return c, make_u, make_v, lose_v, rest


def sides(even, odd, is_even, lower_inside, higher_inside):
    lower, higher = jnp.where(is_even, odd, even), jnp.where(is_even, even, odd)
    return jnp.where(lower_inside, lower, 0.0), jnp.where(higher_inside, higher, 0.0)


def images_kernel(
    lattice,
    rates,
    field,
    even_x,
    odd_x,
    even_y,
    odd_y,
    image_one,
    image_two,
    lines,
    parts,
    wide,
    wide_image,
):
    members, rows, cols, depth = field.shape
    span = cols + 2 * GAP
    tall = rows + 2 * HALF
    index_i, index_j = lax.axis_index("gx"), lax.axis_index("gy")
    first_i, first_j = index_i * rows, index_j * cols
    even_i, even_j = index_i % 2 == 0, index_j % 2 == 0
    count_i, count_j = lattice

    def place(row, start, values):
        for at in range(values.shape[1]):
            first = (row + REACH + at) * span + GAP + start
            wide[:, first : first + values.shape[2]] = values[:, at]

    place(0, 0, field[...])
    above, below = sides(even_x[...], odd_x[...], even_i, first_i > 0, first_i + rows < count_i)
    place(-REACH, 0, above)
    place(rows, 0, below)
    left, right = sides(even_y[...], odd_y[...], even_j, first_j > 0, first_j + cols < count_j)
    place(0, -2, left)
    place(0, cols, right)
    corner = jnp.zeros((members, HALF, 1, depth), jnp.float32)
    for row in (-HALF, rows):
        place(row, -1, corner)
        place(row, cols, corner)

    sublane = lax.broadcasted_iota(jnp.int32, (span, 1), 0)
    amount_j = (first_j - GAP + sublane).astype(jnp.float32)
    place_j = lax.broadcasted_iota(jnp.int32, (cols, depth), 0)
    inner_j = (place_j > 0) & (place_j < cols - 1)

    for member in range(members):
        c, make_u, make_v, lose_v, rest = constants(rates, member, depth, amount_j)
        make_u, lose_v, rest = [term[GAP : GAP + cols] for term in (make_u, lose_v, rest)]

        def image(read, row):
            i = (first_i + row).astype(jnp.float32)
            rows_by = lambda by: read(row + by, 0)
            return apply(c, depth, i, make_u, make_v, lose_v, rest, read(row, 0), rows_by, read(row, -1), read(row, 1))

        def read_field(row, start):
            return wide[member, pl.ds((row + REACH) * span + GAP + start, cols), :]

        def read_image(row, start):
            return wide_image[member, pl.ds((row + HALF) * span + GAP + start, cols), :]

        for row in range(-HALF, rows + HALF):
            inside = (first_i + row >= 0) & (first_i + row < count_i)
            value = image(read_field, row)
            if row < 0 or row >= rows:
                value = jnp.where(inside, value, 0.0)
            else:
                image_one[member, row] = value
            wide_image[member, pl.ds((row + HALF) * span + GAP, cols), :] = value

        products = [jnp.zeros((cols, depth), jnp.float32) for _ in range(6)]
        for row in range(rows):
            zero = field[member, row]
            one = image_one[member, row]
            two = jnp.where(inner_j, image(read_image, row), 0.0)
            image_two[member, row] = two
            terms = (zero * zero, zero * one, zero * two, one * one, one * two, two * two)
            products = [total + term for total, term in zip(products, terms)]
        for index, total in enumerate(products):
            parts[8 * index + member : 8 * index + member + 1, :] = jnp.sum(total, axis=0, keepdims=True)

        for at, column in enumerate((0, cols - 1, 1, cols - 2)):
            lines[member, at] = wide_image[member, pl.ds(GAP + column, tall, stride=span), :]
        for at, column in enumerate((0, cols - 1, -1, cols, -2, cols + 1)):
            lines[member, 4 + at] = wide[member, pl.ds(HALF * span + GAP + column, tall, stride=span), :]

    for index in range(6):
        parts[8 * index + members : 8 * index + 8, :] = jnp.zeros((8 - members, depth), jnp.float32)


def corners_kernel(lattice, cols, rates, lines, odd_corners, even_corners, parts, columns_two, message, edge, total):
    members, _, tall, depth = lines.shape
    rows = tall - 2 * HALF
    index_i, index_j = lax.axis_index("gx"), lax.axis_index("gy")
    first_i, first_j = index_i * rows, index_j * cols
    count_i, count_j = lattice
    upper, lower = sides(
        even_corners[...], odd_corners[...], index_i % 2 == 0, first_i > 0, first_i + rows < count_i
    )
    i = (first_i + lax.broadcasted_iota(jnp.int32, (rows, depth), 0)).astype(jnp.float32)
    total[...] = parts[...]
    for member in range(members):

        def line(at):
            return lines[member, at, pl.ds(HALF, rows), :]

        sums = [jnp.zeros((rows, depth), jnp.float32) for _ in range(3)]
        for side, column, beyond, inside in (
            (0, 0, -1, first_j > 0),
            (1, cols - 1, cols, first_j + cols < count_j),
        ):

            def at_column(column):
                amount_j = jnp.broadcast_to((first_j + column).astype(jnp.float32), (1, depth))
                return constants(rates, member, depth, amount_j)

            outer, fixed = edge.at[member, side, 0], edge.at[member, side, 1]
            outer[HALF : HALF + rows, :] = line(6 + side)
            for row in range(HALF):
                for first, corner in ((0, upper), (HALF + rows, lower)):
                    value = corner[member, row, side : side + 1, :]
                    outer[first + row : first + row + 1, :] = jnp.where(inside, value, 0.0)

            c, make_u, make_v, lose_v, rest = at_column(beyond)
            rows_by = lambda by: outer[pl.ds(HALF + by, rows), :]
            beside = (line(8), line(4)) if side == 0 else (line(5), line(9))
            value = apply(c, depth, i, make_u, make_v, lose_v, rest, rows_by(0), rows_by, *beside)
            image_beyond = jnp.where(inside, value, 0.0)

            c, make_u, make_v, lose_v, rest = at_column(column)
            gain = make_v if side == 0 else lose_v
            fixed[:tall, :] = lines[member, side]
            for first in (0, HALF + rows):
                fixed[first : first + HALF, :] = fixed[first : first + HALF, :] + gain * outer[first : first + HALF, :]

            rows_by = lambda by: fixed[pl.ds(HALF + by, rows), :]
            beside = (image_beyond, line(2)) if side == 0 else (line(3), image_beyond)
            two = apply(c, depth, i, make_u, make_v, lose_v, rest, rows_by(0), rows_by, *beside)
            columns_two[member, side] = two
            terms = (line(4 + side) * two, line(side) * two, two * two)
            sums = [value + term for value, term in zip(sums, terms)]
        for index, value in zip((2, 4, 5), sums):
            at = 8 * index + member
            total[at : at + 1, :] = total[at : at + 1, :] + jnp.sum(value, axis=0, keepdims=True)

    row = jnp.zeros((8, depth), jnp.float32)
    for index in range(6):
        value = jnp.sum(total[8 * index : 8 * index + 8], axis=1, keepdims=True)
        row = row + jnp.where(own_lane(8 * index), value, 0.0)
    message[...] = jnp.broadcast_to(jnp.sum(row, axis=0, keepdims=True), message.shape)


def product(left, right):
    a, b, c, d = left
    e, f, g, h = right
    return a * e + b * g, a * f + b * h, c * e + d * g, c * f + d * h


def first_column(h00, s01, h11):
    scale = tau_step / 2.0**squarings
    one = jnp.ones_like(h00)
    z1 = (scale * h00, scale * s01, scale * one, scale * h11)
    z2 = product(z1, z1)
    z3, z4 = product(z2, z1), product(z2, z2)
    weights = [1.0 / math.factorial(k + 1) for k in range(taylor_terms)]

    def block(first):
        w0, w1, w2, w3 = weights[first : first + 4]
        terms = [w1 * p + w2 * q + w3 * r for p, q, r in zip(z1, z2, z3)]
        return terms[0] + w0, terms[1], terms[2], terms[3] + w0

    phi = block(taylor_terms - 4)
    for first in range(taylor_terms - 8, -1, -4):
        phi = tuple(p + q for p, q in zip(product(z4, phi), block(first)))
    p00, p01, p10, p11 = product(z1, phi)
    p00, p11 = 1.0 + p00, 1.0 + p11
    q0, q1 = scale * phi[2], scale * phi[3]
    for _ in range(squarings):
        p00, p01, p10, p11, q0, q1 = (
            p00 * p00 + p01 * p10,
            p00 * p01 + p01 * p11,
            p10 * p00 + p11 * p10,
            p10 * p01 + p11 * p11,
            q0 * p00 + q1 * p10 + q0,
            q0 * p01 + q1 * p11 + q1,
        )
    return p00, p10, q0


def combine_kernel(gathered, field, image_one, image_two, columns_two, propagated, entries):
    members, rows, cols, depth = field.shape
    sums = jnp.broadcast_to(jnp.sum(gathered[...], axis=0, keepdims=True), (8, 128))
    g00, g01, g02, g11, g12, g22 = [
        jnp.broadcast_to(jnp.sum(jnp.where(own_lane(8 * index), sums, 0.0), axis=1, keepdims=True), (8, 128))
        for index in range(6)
    ]
    tiny = jnp.finfo(jnp.float32).tiny
    h00 = g01 / g00
    square_10 = jnp.maximum(g11 / g00 - h00 * h00, tiny)
    s01 = (g02 - h00 * g01) / g00
    h11 = ((g12 - h00 * g02) - h00 * (g11 - h00 * g01)) / (g00 * square_10)
    norm_2 = ((g22 - h00 * g12) - h00 * (g12 - h00 * g11)) / (g00 * square_10)
    h10 = jnp.sqrt(square_10)
    h01 = s01 / h10
    h21 = jnp.sqrt(jnp.maximum(norm_2 - h01 * h01 - h11 * h11, 0.0))
    e0, e1, e2 = first_column(h00, s01, h11)
    a2 = e2
    a1 = e1 - e2 * (h00 + h11)
    a0 = e0 - e1 * h00 - e2 * (s01 - h11 * h00)
    lane = lax.broadcasted_iota(jnp.int32, h00.shape, 1)
    table = h21
    for index, entry in enumerate((h00, h10, h01, h11)):
        table = jnp.where(lane == index, entry, table)
    entries[...] = (tau_step * table)[: entries.shape[0], : entries.shape[1]]
    place_j = lax.broadcasted_iota(jnp.int32, (cols, depth), 0)
    for member in range(members):
        b0, b1, b2 = [jnp.broadcast_to(a[member : member + 1], (cols, depth)) for a in (a0, a1, a2)]
        for row in range(rows):
            two = jnp.where(place_j == 0, columns_two[member, 0, row : row + 1], image_two[member, row])
            two = jnp.where(place_j == cols - 1, columns_two[member, 1, row : row + 1], two)
            propagated[member, row] = b0 * field[member, row] + b1 * image_one[member, row] + b2 * two


def shards(density, rate_table):
    members, rows, cols, depth = density.shape
    size_x, size_y = lax.axis_size("gx"), lax.axis_size("gy")
    devices = size_x * size_y
    vmem = pl.BlockSpec(memory_space=pltpu.VMEM)
    parity_x, parity_y = lax.axis_index("gx") % 2, lax.axis_index("gy") % 2

    def swap(axis, size, first, value):
        def partner(x, y):
            at = x if axis == "gx" else y
            other = at + 1 if (at - first) % 2 == 0 else at - 1
            if not 0 <= other < size:
                return (x, y ^ 1) if axis == "gx" else (x, other % size)
            return (other, y) if axis == "gx" else (x, other)

        pairs = [
            (x * size_y + y, partner(x, y)[0] * size_y + partner(x, y)[1])
            for x in range(size_x)
            for y in range(size_y)
        ]
        return lax.ppermute(value, ("gx", "gy"), pairs)

    assert size_x % 2 == 0 and size_y % 2 == 0

    def swaps(axis, size, parity, initial, last):
        if initial is last:
            return swap(axis, size, 0, last), swap(axis, size, 1, last)
        is_even = parity == 0
        return (
            swap(axis, size, 0, jnp.where(is_even, last, initial)),
            swap(axis, size, 1, jnp.where(is_even, initial, last)),
        )

    initial, last = (density, density) if rows == REACH else (density[:, :REACH], density[:, rows - REACH :])
    is_even = parity_x == 0
    even_x = swap("gx", size_x, 0, initial if rows == REACH else jnp.where(is_even, last, initial))

    edge = jax.ShapeDtypeStruct((members, rows, 2, depth), jnp.float32)
    block = jax.ShapeDtypeStruct(density.shape, jnp.float32)
    parity = pl.pallas_call(
        parity_kernel,
        out_shape=jax.ShapeDtypeStruct((8, depth), jnp.int32),
        out_specs=vmem,
        compiler_params=pltpu.CompilerParams(vmem_limit_bytes=2**20),
        cost_estimate=pl.CostEstimate(flops=10**8, bytes_accessed=0, transcendentals=0),
        name="parity",
    )()
    for_odd, for_even = pl.pallas_call(
        edges_kernel,
        out_shape=[edge, edge],
        in_specs=[vmem, vmem],
        out_specs=[vmem] * 2,
        compiler_params=pltpu.CompilerParams(vmem_limit_bytes=2 * 2**20),
        name="edges",
    )(parity, density)
    odd_y = swap("gy", size_y, 1, for_odd)
    even_y = swap("gy", size_y, 0, for_even)

    even_y, for_odd_x = lax.optimization_barrier((even_y, initial if rows == REACH else jnp.where(is_even, initial, last)))
    odd_x = swap("gx", size_x, 1, for_odd_x)

    def corners(first):
        even, odd = even_y[:, first : first + HALF], odd_y[:, first : first + HALF]
        left = jnp.where(parity_y == 0, odd, even)[:, :, 1:]
        right = jnp.where(parity_y == 0, even, odd)[:, :, :1]
        return jnp.concatenate([left, right], axis=2)

    even_corners, odd_corners = swaps("gx", size_x, parity_x, corners(0), corners(rows - HALF))

    lattice = (size_x * rows, size_y * cols)
    tall, span = rows + 2 * HALF, cols + 2 * GAP
    image_one, image_two, lines, parts = pl.pallas_call(
        functools.partial(images_kernel, lattice),
        out_shape=[
            block,
            block,
            jax.ShapeDtypeStruct((members, 10, tall, depth), jnp.float32),
            jax.ShapeDtypeStruct((48, depth), jnp.float32),
        ],
        in_specs=[vmem] * 6,
        out_specs=[vmem] * 4,
        scratch_shapes=[
            pltpu.VMEM((members, (rows + 2 * REACH) * span, depth), jnp.float32),
            pltpu.VMEM((members, (tall + 1) * span, depth), jnp.float32),
        ],
        compiler_params=pltpu.CompilerParams(vmem_limit_bytes=8 * 2**20),
        name="images",
    )(rate_table, density, even_x, odd_x, even_y, odd_y)

    columns_two, message = pl.pallas_call(
        functools.partial(corners_kernel, lattice, cols),
        out_shape=[
            jax.ShapeDtypeStruct((members, 2, rows, depth), jnp.float32),
            jax.ShapeDtypeStruct((devices, 128), jnp.float32),
        ],
        in_specs=[vmem] * 5,
        out_specs=[vmem, vmem],
        scratch_shapes=[
            pltpu.VMEM((members, 2, 2, 2 * tall, depth), jnp.float32),
            pltpu.VMEM((48, depth), jnp.float32),
        ],
        compiler_params=pltpu.CompilerParams(vmem_limit_bytes=4 * 2**20),
        name="corners",
    )(rate_table, lines, odd_corners, even_corners, parts)

    gathered = lax.all_to_all(message, ("gy", "gx"), 0, 0, tiled=True)

    return pl.pallas_call(
        combine_kernel,
        out_shape=[block, jax.ShapeDtypeStruct((members, 5), jnp.float32)],
        in_specs=[vmem] * 5,
        out_specs=[vmem, vmem],
        compiler_params=pltpu.CompilerParams(vmem_limit_bytes=8 * 2**20),
        name="combine",
    )(gathered, density, image_one, image_two, columns_two)


def solution(mesh):
    in_specs = (P(None, "gx", "gy", None), P())
    out_specs = (P(None, "gx", "gy", None), P())
    return jax.shard_map(shards, mesh=mesh, in_specs=in_specs, out_specs=out_specs, check_vma=False)
```

```python
import functools
import math

import jax
import jax.numpy as jnp
from jax import lax
from jax.experimental import pallas as pl
from jax.experimental.pallas import tpu as pltpu
from jax.sharding import PartitionSpec as P

tau_step = 0.01
taylor_terms = 16
squarings = 4
REACH = 4
HALF = 2
GAP = 8


def parity_kernel(parity):
    parity[...] = jnp.full(parity.shape, lax.axis_index("gy") % 2, jnp.int32)


def edges_kernel(parity, field, for_odd, for_even):
    is_even = jnp.broadcast_to(parity[:1], for_odd.shape[1:3] + parity.shape[1:])[None] == 0
    cols = field.shape[2]
    low, high = field[:, :, :2], field[:, :, cols - 2 :]
    for_even[...] = jnp.where(is_even, high, low)
    for_odd[...] = jnp.where(is_even, low, high)


def own_lane(first):
    row = lax.broadcasted_iota(jnp.int32, (8, 128), 0)
    return lax.broadcasted_iota(jnp.int32, (8, 128), 1) == first + row


def lanes(depth):
    lane = lax.broadcasted_iota(jnp.int32, (1, depth), 1)
    amount_k = lane.astype(jnp.float32)
    return amount_k, jnp.where(lane < depth - 1, amount_k + 1.0, 0.0), jnp.where(lane > 0, 1.0, 0.0)


def apply(c, depth, i, make_u, make_v, lose_v, rest, centre, rows_by, left, right):
    _, above_k, inner_k = lanes(depth)
    value = make_u * rows_by(-1) + (c[1] * (i + 1.0)) * rows_by(1)
    value = value + make_v * left
    value = value + lose_v * right
    pair = pltpu.roll(rows_by(2), 1, 1)
    value = value + (inner_k * (0.5 * c[4] * (i + 2.0) * (i + 1.0))) * pair
    split = c[5] * rows_by(-2) + c[6] * centre
    value = value + above_k * pltpu.roll(split, depth - 1, 1)
    out = rest + (c[1] * i + 0.5 * c[4] * i * (i - 1.0))
    return value - out * centre


def constants(rates, member, depth, amount_j):
    c = [jnp.broadcast_to(rates[member : member + 1, r : r + 1], (1, depth)) for r in range(9)]
    amount_k = lanes(depth)[0]
    ratio_j, ratio_k = amount_j / c[7], amount_k / c[8]
    make_u = c[0] / (1.0 + ratio_j * ratio_j)
    make_v = c[2] / (1.0 + ratio_k * ratio_k)
    lose_v = c[3] * (amount_j + 1.0)
    rest = make_u + make_v + (c[3] * amount_j + (c[5] + c[6]) * amount_k)
    return c, make_u, make_v, lose_v, rest


def sides(even, odd, is_even, lower_inside, higher_inside):
    lower, higher = jnp.where(is_even, odd, even), jnp.where(is_even, even, odd)
    return jnp.where(lower_inside, lower, 0.0), jnp.where(higher_inside, higher, 0.0)


def images_kernel(
    lattice,
    rates,
    field,
    even_x,
    odd_x,
    even_y,
    odd_y,
    image_one,
    image_two,
    lines,
    parts,
    wide,
    wide_image,
):
    members, rows, cols, depth = field.shape
    span = cols + 2 * GAP
    tall = rows + 2 * HALF
    index_i, index_j = lax.axis_index("gx"), lax.axis_index("gy")
    first_i, first_j = index_i * rows, index_j * cols
    even_i, even_j = index_i % 2 == 0, index_j % 2 == 0
    count_i, count_j = lattice

    def place(row, start, values):
        for at in range(values.shape[1]):
            first = (row + REACH + at) * span + GAP + start
            wide[:, first : first + values.shape[2]] = values[:, at]

    place(0, 0, field[...])
    above, below = sides(even_x[...], odd_x[...], even_i, first_i > 0, first_i + rows < count_i)
    place(-REACH, 0, above)
    place(rows, 0, below)
    left, right = sides(even_y[...], odd_y[...], even_j, first_j > 0, first_j + cols < count_j)
    place(0, -2, left)
    place(0, cols, right)
    corner = jnp.zeros((members, HALF, 1, depth), jnp.float32)
    for row in (-HALF, rows):
        place(row, -1, corner)
        place(row, cols, corner)

    sublane = lax.broadcasted_iota(jnp.int32, (span, 1), 0)
    amount_j = (first_j - GAP + sublane).astype(jnp.float32)
    place_j = lax.broadcasted_iota(jnp.int32, (cols, depth), 0)
    inner_j = (place_j > 0) & (place_j < cols - 1)

    for member in range(members):
        c, make_u, make_v, lose_v, rest = constants(rates, member, depth, amount_j)
        make_u, lose_v, rest = [term[GAP : GAP + cols] for term in (make_u, lose_v, rest)]

        def image(read, row):
            i = (first_i + row).astype(jnp.float32)
            rows_by = lambda by: read(row + by, 0)
            return apply(c, depth, i, make_u, make_v, lose_v, rest, read(row, 0), rows_by, read(row, -1), read(row, 1))

        def read_field(row, start):
            return wide[member, pl.ds((row + REACH) * span + GAP + start, cols), :]

        def read_image(row, start):
            return wide_image[member, pl.ds((row + HALF) * span + GAP + start, cols), :]

        for row in range(-HALF, rows + HALF):
            inside = (first_i + row >= 0) & (first_i + row < count_i)
            value = image(read_field, row)
            if row < 0 or row >= rows:
                value = jnp.where(inside, value, 0.0)
            else:
                image_one[member, row] = value
            wide_image[member, pl.ds((row + HALF) * span + GAP, cols), :] = value

        products = [jnp.zeros((cols, depth), jnp.float32) for _ in range(6)]
        for row in range(rows):
            zero = field[member, row]
            one = image_one[member, row]
            two = jnp.where(inner_j, image(read_image, row), 0.0)
            image_two[member, row] = two
            terms = (zero * zero, zero * one, zero * two, one * one, one * two, two * two)
            products = [total + term for total, term in zip(products, terms)]
        for index, total in enumerate(products):
            parts[8 * index + member : 8 * index + member + 1, :] = jnp.sum(total, axis=0, keepdims=True)

        for at, column in enumerate((0, cols - 1, 1, cols - 2)):
            lines[member, at] = wide_image[member, pl.ds(GAP + column, tall, stride=span), :]
        for at, column in enumerate((0, cols - 1, -1, cols, -2, cols + 1)):
            lines[member, 4 + at] = wide[member, pl.ds(HALF * span + GAP + column, tall, stride=span), :]

    for index in range(6):
        parts[8 * index + members : 8 * index + 8, :] = jnp.zeros((8 - members, depth), jnp.float32)


def corners_kernel(lattice, cols, rates, lines, odd_corners, even_corners, parts, columns_two, message, edge, total):
    members, _, tall, depth = lines.shape
    rows = tall - 2 * HALF
    index_i, index_j = lax.axis_index("gx"), lax.axis_index("gy")
    first_i, first_j = index_i * rows, index_j * cols
    count_i, count_j = lattice
    upper, lower = sides(
        even_corners[...], odd_corners[...], index_i % 2 == 0, first_i > 0, first_i + rows < count_i
    )
    i = (first_i + lax.broadcasted_iota(jnp.int32, (rows, depth), 0)).astype(jnp.float32)
    total[...] = parts[...]
    for member in range(members):

        def line(at):
            return lines[member, at, pl.ds(HALF, rows), :]

        sums = [jnp.zeros((rows, depth), jnp.float32) for _ in range(3)]
        for side, column, beyond, inside in (
            (0, 0, -1, first_j > 0),
            (1, cols - 1, cols, first_j + cols < count_j),
        ):

            def at_column(column):
                amount_j = jnp.broadcast_to((first_j + column).astype(jnp.float32), (1, depth))
                return constants(rates, member, depth, amount_j)

            outer, fixed = edge.at[member, side, 0], edge.at[member, side, 1]
            outer[HALF : HALF + rows, :] = line(6 + side)
            for row in range(HALF):
                for first, corner in ((0, upper), (HALF + rows, lower)):
                    value = corner[member, row, side : side + 1, :]
                    outer[first + row : first + row + 1, :] = jnp.where(inside, value, 0.0)

            c, make_u, make_v, lose_v, rest = at_column(beyond)
            rows_by = lambda by: outer[pl.ds(HALF + by, rows), :]
            beside = (line(8), line(4)) if side == 0 else (line(5), line(9))
            value = apply(c, depth, i, make_u, make_v, lose_v, rest, rows_by(0), rows_by, *beside)
            image_beyond = jnp.where(inside, value, 0.0)

            c, make_u, make_v, lose_v, rest = at_column(column)
            gain = make_v if side == 0 else lose_v
            fixed[:tall, :] = lines[member, side]
            for first in (0, HALF + rows):
                fixed[first : first + HALF, :] = fixed[first : first + HALF, :] + gain * outer[first : first + HALF, :]

            rows_by = lambda by: fixed[pl.ds(HALF + by, rows), :]
            beside = (image_beyond, line(2)) if side == 0 else (line(3), image_beyond)
            two = apply(c, depth, i, make_u, make_v, lose_v, rest, rows_by(0), rows_by, *beside)
            columns_two[member, side] = two
            terms = (line(4 + side) * two, line(side) * two, two * two)
            sums = [value + term for value, term in zip(sums, terms)]
        for index, value in zip((2, 4, 5), sums):
            at = 8 * index + member
            total[at : at + 1, :] = total[at : at + 1, :] + jnp.sum(value, axis=0, keepdims=True)

    row = jnp.zeros((8, depth), jnp.float32)
    for index in range(6):
        value = jnp.sum(total[8 * index : 8 * index + 8], axis=1, keepdims=True)
        row = row + jnp.where(own_lane(8 * index), value, 0.0)
    message[...] = jnp.broadcast_to(jnp.sum(row, axis=0, keepdims=True), message.shape)


def product(left, right):
    a, b, c, d = left
    e, f, g, h = right
    return a * e + b * g, a * f + b * h, c * e + d * g, c * f + d * h


def first_column(h00, s01, h11):
    scale = tau_step / 2.0**squarings
    one = jnp.ones_like(h00)
    z1 = (scale * h00, scale * s01, scale * one, scale * h11)
    z2 = product(z1, z1)
    z3, z4 = product(z2, z1), product(z2, z2)
    weights = [1.0 / math.factorial(k + 1) for k in range(taylor_terms)]

    def block(first):
        w0, w1, w2, w3 = weights[first : first + 4]
        terms = [w1 * p + w2 * q + w3 * r for p, q, r in zip(z1, z2, z3)]
        return terms[0] + w0, terms[1], terms[2], terms[3] + w0

    phi = block(taylor_terms - 4)
    for first in range(taylor_terms - 8, -1, -4):
        phi = tuple(p + q for p, q in zip(product(z4, phi), block(first)))
    p00, p01, p10, p11 = product(z1, phi)
    p00, p11 = 1.0 + p00, 1.0 + p11
    q0, q1 = scale * phi[2], scale * phi[3]
    for _ in range(squarings):
        p00, p01, p10, p11, q0, q1 = (
            p00 * p00 + p01 * p10,
            p00 * p01 + p01 * p11,
            p10 * p00 + p11 * p10,
            p10 * p01 + p11 * p11,
            q0 * p00 + q1 * p10 + q0,
            q0 * p01 + q1 * p11 + q1,
        )
    return p00, p10, q0


def combine_kernel(
    gathered, field, image_one, image_two, columns_two, propagated, entries, formed, sent
):
    members, rows, cols, depth = field.shape
    sums = jnp.broadcast_to(jnp.sum(gathered[...], axis=0, keepdims=True), (8, 128))
    g00, g01, g02, g11, g12, g22 = [
        jnp.broadcast_to(jnp.sum(jnp.where(own_lane(8 * index), sums, 0.0), axis=1, keepdims=True), (8, 128))
        for index in range(6)
    ]
    tiny = jnp.finfo(jnp.float32).tiny
    h00 = g01 / g00
    square_10 = jnp.maximum(g11 / g00 - h00 * h00, tiny)
    s01 = (g02 - h00 * g01) / g00
    h11 = ((g12 - h00 * g02) - h00 * (g11 - h00 * g01)) / (g00 * square_10)
    norm_2 = ((g22 - h00 * g12) - h00 * (g12 - h00 * g11)) / (g00 * square_10)
    h10 = jnp.sqrt(square_10)
    h01 = s01 / h10
    h21 = jnp.sqrt(jnp.maximum(norm_2 - h01 * h01 - h11 * h11, 0.0))
    e0, e1, e2 = first_column(h00, s01, h11)
    a2 = e2
    a1 = e1 - e2 * (h00 + h11)
    a0 = e0 - e1 * h00 - e2 * (s01 - h11 * h00)
    place_j = lax.broadcasted_iota(jnp.int32, (cols, depth), 0)
    copies = []
    for member in range(members):
        b0, b1, b2 = [jnp.broadcast_to(a[member : member + 1], (cols, depth)) for a in (a0, a1, a2)]
        for row in range(rows):
            two = jnp.where(place_j == 0, columns_two[member, 0, row : row + 1], image_two[member, row])
            two = jnp.where(place_j == cols - 1, columns_two[member, 1, row : row + 1], two)
            formed[member, row] = b0 * field[member, row] + b1 * image_one[member, row] + b2 * two
        copies.append(pltpu.make_async_copy(formed.at[member], propagated.at[member], sent.at[member]))
        copies[-1].start()
    lane = lax.broadcasted_iota(jnp.int32, h00.shape, 1)
    table = h21
    for index, entry in enumerate((h00, h10, h01, h11)):
        table = jnp.where(lane == index, entry, table)
    entries[...] = (tau_step * table)[: entries.shape[0], : entries.shape[1]]
    for copy in copies:
        copy.wait()


def shards(density, rate_table):
    members, rows, cols, depth = density.shape
    size_x, size_y = lax.axis_size("gx"), lax.axis_size("gy")
    devices = size_x * size_y
    vmem = pl.BlockSpec(memory_space=pltpu.VMEM)
    parity_x, parity_y = lax.axis_index("gx") % 2, lax.axis_index("gy") % 2

    def swap(axis, size, first, value):
        def partner(x, y):
            at = x if axis == "gx" else y
            other = at + 1 if (at - first) % 2 == 0 else at - 1
            if not 0 <= other < size:
                return (x, y ^ 1) if axis == "gx" else (x ^ 1, y)
            return (other, y) if axis == "gx" else (x, other)

        pairs = [
            (x * size_y + y, partner(x, y)[0] * size_y + partner(x, y)[1])
            for x in range(size_x)
            for y in range(size_y)
        ]
        return lax.ppermute(value, ("gx", "gy"), pairs)

    assert size_x % 2 == 0 and size_y % 2 == 0

    def swaps(axis, size, parity, initial, last):
        if initial is last:
            return swap(axis, size, 0, last), swap(axis, size, 1, last)
        is_even = parity == 0
        return (
            swap(axis, size, 0, jnp.where(is_even, last, initial)),
            swap(axis, size, 1, jnp.where(is_even, initial, last)),
        )

    initial, last = (density, density) if rows == REACH else (density[:, :REACH], density[:, rows - REACH :])
    is_even = parity_x == 0
    even_x = swap("gx", size_x, 0, initial if rows == REACH else jnp.where(is_even, last, initial))

    edge = jax.ShapeDtypeStruct((members, rows, 2, depth), jnp.float32)
    block = jax.ShapeDtypeStruct(density.shape, jnp.float32)
    parity = pl.pallas_call(
        parity_kernel,
        out_shape=jax.ShapeDtypeStruct((8, depth), jnp.int32),
        out_specs=vmem,
        compiler_params=pltpu.CompilerParams(vmem_limit_bytes=2**20),
        cost_estimate=pl.CostEstimate(flops=10**8, bytes_accessed=0, transcendentals=0),
        name="parity",
    )()
    for_odd, for_even = pl.pallas_call(
        edges_kernel,
        out_shape=[edge, edge],
        in_specs=[vmem, vmem],
        out_specs=[vmem] * 2,
        compiler_params=pltpu.CompilerParams(vmem_limit_bytes=2 * 2**20),
        name="edges",
    )(parity, density)
    odd_y = swap("gy", size_y, 1, for_odd)
    even_y = swap("gy", size_y, 0, for_even)

    even_y, for_odd_x = lax.optimization_barrier((even_y, initial if rows == REACH else jnp.where(is_even, initial, last)))
    odd_x = swap("gx", size_x, 1, for_odd_x)
    even_x, odd_y, even_y = lax.optimization_barrier((even_x, odd_y, even_y))

    def corners(first):
        even, odd = even_y[:, first : first + HALF], odd_y[:, first : first + HALF]
        left = jnp.where(parity_y == 0, odd, even)[:, :, 1:]
        right = jnp.where(parity_y == 0, even, odd)[:, :, :1]
        return jnp.concatenate([left, right], axis=2)

    even_corners, odd_corners = swaps("gx", size_x, parity_x, corners(0), corners(rows - HALF))

    lattice = (size_x * rows, size_y * cols)
    tall, span = rows + 2 * HALF, cols + 2 * GAP
    image_one, image_two, lines, parts = pl.pallas_call(
        functools.partial(images_kernel, lattice),
        out_shape=[
            block,
            block,
            jax.ShapeDtypeStruct((members, 10, tall, depth), jnp.float32),
            jax.ShapeDtypeStruct((48, depth), jnp.float32),
        ],
        in_specs=[vmem] * 6,
        out_specs=[vmem] * 4,
        scratch_shapes=[
            pltpu.VMEM((members, (rows + 2 * REACH) * span, depth), jnp.float32),
            pltpu.VMEM((members, (tall + 1) * span, depth), jnp.float32),
        ],
        compiler_params=pltpu.CompilerParams(vmem_limit_bytes=8 * 2**20),
        name="images",
    )(rate_table, density, even_x, odd_x, even_y, odd_y)

    columns_two, message = pl.pallas_call(
        functools.partial(corners_kernel, lattice, cols),
        out_shape=[
            jax.ShapeDtypeStruct((members, 2, rows, depth), jnp.float32),
            jax.ShapeDtypeStruct((devices, 128), jnp.float32),
        ],
        in_specs=[vmem] * 5,
        out_specs=[vmem, vmem],
        scratch_shapes=[
            pltpu.VMEM((members, 2, 2, 2 * tall, depth), jnp.float32),
            pltpu.VMEM((48, depth), jnp.float32),
        ],
        compiler_params=pltpu.CompilerParams(vmem_limit_bytes=4 * 2**20),
        name="corners",
    )(rate_table, lines, odd_corners, even_corners, parts)

    gathered = lax.all_to_all(message, ("gy", "gx"), 0, 0, tiled=True)

    return pl.pallas_call(
        combine_kernel,
        out_shape=[block, jax.ShapeDtypeStruct((members, 5), jnp.float32)],
        in_specs=[vmem] * 5,
        out_specs=[pl.BlockSpec(memory_space=pl.ANY), vmem],
        scratch_shapes=[pltpu.VMEM(density.shape, jnp.float32), pltpu.SemaphoreType.DMA((members,))],
        compiler_params=pltpu.CompilerParams(vmem_limit_bytes=8 * 2**20),
        name="combine",
    )(gathered, density, image_one, image_two, columns_two)


def solution(mesh):
    in_specs = (P(None, "gx", "gy", None), P())
    out_specs = (P(None, "gx", "gy", None), P())
    return jax.shard_map(shards, mesh=mesh, in_specs=in_specs, out_specs=out_specs, check_vma=False)
```

```python
import functools
import math

import jax
import jax.numpy as jnp
from jax import lax
from jax.experimental import pallas as pl
from jax.experimental.pallas import tpu as pltpu
from jax.sharding import PartitionSpec as P

tau_step = 0.01
taylor_terms = 16
squarings = 4
REACH = 4
HALF = 2
GAP = 8


def parity_kernel(parity):
    parity[...] = jnp.full(parity.shape, lax.axis_index("gy") % 2, jnp.int32)


def edges_kernel(parity, field, for_odd, for_even):
    is_even = jnp.broadcast_to(parity[:1], for_odd.shape[1:3] + parity.shape[1:])[None] == 0
    cols = field.shape[2]
    low, high = field[:, :, :2], field[:, :, cols - 2 :]
    for_even[...] = jnp.where(is_even, high, low)
    for_odd[...] = jnp.where(is_even, low, high)


def own_lane(first):
    row = lax.broadcasted_iota(jnp.int32, (8, 128), 0)
    return lax.broadcasted_iota(jnp.int32, (8, 128), 1) == first + row


def lanes(depth):
    lane = lax.broadcasted_iota(jnp.int32, (1, depth), 1)
    amount_k = lane.astype(jnp.float32)
    return amount_k, jnp.where(lane < depth - 1, amount_k + 1.0, 0.0), jnp.where(lane > 0, 1.0, 0.0)


def apply(c, depth, i, make_u, make_v, lose_v, rest, centre, rows_by, left, right):
    _, above_k, inner_k = lanes(depth)
    value = make_u * rows_by(-1) + (c[1] * (i + 1.0)) * rows_by(1)
    value = value + make_v * left
    value = value + lose_v * right
    pair = pltpu.roll(rows_by(2), 1, 1)
    value = value + (inner_k * (0.5 * c[4] * (i + 2.0) * (i + 1.0))) * pair
    split = c[5] * rows_by(-2) + c[6] * centre
    value = value + above_k * pltpu.roll(split, depth - 1, 1)
    out = rest + (c[1] * i + 0.5 * c[4] * i * (i - 1.0))
    return value - out * centre


def constants(rates, member, depth, amount_j):
    c = [jnp.broadcast_to(rates[member : member + 1, r : r + 1], (1, depth)) for r in range(9)]
    amount_k = lanes(depth)[0]
    ratio_j, ratio_k = amount_j / c[7], amount_k / c[8]
    make_u = c[0] / (1.0 + ratio_j * ratio_j)
    make_v = c[2] / (1.0 + ratio_k * ratio_k)
    lose_v = c[3] * (amount_j + 1.0)
    rest = make_u + make_v + (c[3] * amount_j + (c[5] + c[6]) * amount_k)
    return c, make_u, make_v, lose_v, rest


def sides(even, odd, is_even, lower_inside, higher_inside):
    lower, higher = jnp.where(is_even, odd, even), jnp.where(is_even, even, odd)
    return jnp.where(lower_inside, lower, 0.0), jnp.where(higher_inside, higher, 0.0)


def images_kernel(
    lattice,
    rates,
    field,
    even_x,
    odd_x,
    even_y,
    odd_y,
    image_one,
    image_two,
    lines,
    parts,
    wide,
    wide_image,
):
    members, rows, cols, depth = field.shape
    span = cols + 2 * GAP
    tall = rows + 2 * HALF
    index_i, index_j = lax.axis_index("gx"), lax.axis_index("gy")
    first_i, first_j = index_i * rows, index_j * cols
    even_i, even_j = index_i % 2 == 0, index_j % 2 == 0
    count_i, count_j = lattice

    def place(row, start, values):
        for at in range(values.shape[1]):
            first = (row + REACH + at) * span + GAP + start
            wide[:, first : first + values.shape[2]] = values[:, at]

    place(0, 0, field[...])
    above, below = sides(even_x[...], odd_x[...], even_i, first_i > 0, first_i + rows < count_i)
    place(-REACH, 0, above)
    place(rows, 0, below)
    left, right = sides(even_y[...], odd_y[...], even_j, first_j > 0, first_j + cols < count_j)
    place(0, -2, left)
    place(0, cols, right)
    corner = jnp.zeros((members, HALF, 1, depth), jnp.float32)
    for row in (-HALF, rows):
        place(row, -1, corner)
        place(row, cols, corner)

    sublane = lax.broadcasted_iota(jnp.int32, (span, 1), 0)
    amount_j = (first_j - GAP + sublane).astype(jnp.float32)
    place_j = lax.broadcasted_iota(jnp.int32, (cols, depth), 0)
    inner_j = (place_j > 0) & (place_j < cols - 1)

    for member in range(members):
        c, make_u, make_v, lose_v, rest = constants(rates, member, depth, amount_j)
        make_u, lose_v, rest = [term[GAP : GAP + cols] for term in (make_u, lose_v, rest)]

        def image(read, row):
            i = (first_i + row).astype(jnp.float32)
            rows_by = lambda by: read(row + by, 0)
            return apply(c, depth, i, make_u, make_v, lose_v, rest, read(row, 0), rows_by, read(row, -1), read(row, 1))

        def read_field(row, start):
            return wide[member, pl.ds((row + REACH) * span + GAP + start, cols), :]

        def read_image(row, start):
            return wide_image[member, pl.ds((row + HALF) * span + GAP + start, cols), :]

        for row in range(-HALF, rows + HALF):
            inside = (first_i + row >= 0) & (first_i + row < count_i)
            value = image(read_field, row)
            if row < 0 or row >= rows:
                value = jnp.where(inside, value, 0.0)
            else:
                image_one[member, row] = value
            wide_image[member, pl.ds((row + HALF) * span + GAP, cols), :] = value

        products = [jnp.zeros((cols, depth), jnp.float32) for _ in range(6)]
        for row in range(rows):
            zero = field[member, row]
            one = image_one[member, row]
            two = jnp.where(inner_j, image(read_image, row), 0.0)
            image_two[member, row] = two
            terms = (zero * zero, zero * one, zero * two, one * one, one * two, two * two)
            products = [total + term for total, term in zip(products, terms)]
        for index, total in enumerate(products):
            parts[8 * index + member : 8 * index + member + 1, :] = jnp.sum(total, axis=0, keepdims=True)

        for at, column in enumerate((0, cols - 1, 1, cols - 2)):
            lines[member, at] = wide_image[member, pl.ds(GAP + column, tall, stride=span), :]
        for at, column in enumerate((0, cols - 1, -1, cols, -2, cols + 1)):
            lines[member, 4 + at] = wide[member, pl.ds(HALF * span + GAP + column, tall, stride=span), :]

    for index in range(6):
        parts[8 * index + members : 8 * index + 8, :] = jnp.zeros((8 - members, depth), jnp.float32)


def corners_kernel(lattice, cols, rates, lines, odd_corners, even_corners, parts, columns_two, message, edge, total):
    members, _, tall, depth = lines.shape
    rows = tall - 2 * HALF
    index_i, index_j = lax.axis_index("gx"), lax.axis_index("gy")
    first_i, first_j = index_i * rows, index_j * cols
    count_i, count_j = lattice
    upper, lower = sides(
        even_corners[...], odd_corners[...], index_i % 2 == 0, first_i > 0, first_i + rows < count_i
    )
    i = (first_i + lax.broadcasted_iota(jnp.int32, (rows, depth), 0)).astype(jnp.float32)
    total[...] = parts[...]
    for member in range(members):

        def line(at):
            return lines[member, at, pl.ds(HALF, rows), :]

        sums = [jnp.zeros((rows, depth), jnp.float32) for _ in range(3)]
        for side, column, beyond, inside in (
            (0, 0, -1, first_j > 0),
            (1, cols - 1, cols, first_j + cols < count_j),
        ):

            def at_column(column):
                amount_j = jnp.broadcast_to((first_j + column).astype(jnp.float32), (1, depth))
                return constants(rates, member, depth, amount_j)

            outer, fixed = edge.at[member, side, 0], edge.at[member, side, 1]
            outer[HALF : HALF + rows, :] = line(6 + side)
            for row in range(HALF):
                for first, corner in ((0, upper), (HALF + rows, lower)):
                    value = corner[member, row, side : side + 1, :]
                    outer[first + row : first + row + 1, :] = jnp.where(inside, value, 0.0)

            c, make_u, make_v, lose_v, rest = at_column(beyond)
            rows_by = lambda by: outer[pl.ds(HALF + by, rows), :]
            beside = (line(8), line(4)) if side == 0 else (line(5), line(9))
            value = apply(c, depth, i, make_u, make_v, lose_v, rest, rows_by(0), rows_by, *beside)
            image_beyond = jnp.where(inside, value, 0.0)

            c, make_u, make_v, lose_v, rest = at_column(column)
            gain = make_v if side == 0 else lose_v
            fixed[:tall, :] = lines[member, side]
            for first in (0, HALF + rows):
                fixed[first : first + HALF, :] = fixed[first : first + HALF, :] + gain * outer[first : first + HALF, :]

            rows_by = lambda by: fixed[pl.ds(HALF + by, rows), :]
            beside = (image_beyond, line(2)) if side == 0 else (line(3), image_beyond)
            two = apply(c, depth, i, make_u, make_v, lose_v, rest, rows_by(0), rows_by, *beside)
            columns_two[member, side] = two
            terms = (line(4 + side) * two, line(side) * two, two * two)
            sums = [value + term for value, term in zip(sums, terms)]
        for index, value in zip((2, 4, 5), sums):
            at = 8 * index + member
            total[at : at + 1, :] = total[at : at + 1, :] + jnp.sum(value, axis=0, keepdims=True)

    row = jnp.zeros((8, depth), jnp.float32)
    for index in range(6):
        value = jnp.sum(total[8 * index : 8 * index + 8], axis=1, keepdims=True)
        row = row + jnp.where(own_lane(8 * index), value, 0.0)
    message[...] = jnp.broadcast_to(jnp.sum(row, axis=0, keepdims=True), message.shape)


def product(left, right):
    a, b, c, d = left
    e, f, g, h = right
    return a * e + b * g, a * f + b * h, c * e + d * g, c * f + d * h


def first_column(h00, s01, h11):
    scale = tau_step / 2.0**squarings
    one = jnp.ones_like(h00)
    z1 = (scale * h00, scale * s01, scale * one, scale * h11)
    z2 = product(z1, z1)
    z3, z4 = product(z2, z1), product(z2, z2)
    weights = [1.0 / math.factorial(k + 1) for k in range(taylor_terms)]

    def block(first):
        w0, w1, w2, w3 = weights[first : first + 4]
        terms = [w1 * p + w2 * q + w3 * r for p, q, r in zip(z1, z2, z3)]
        return terms[0] + w0, terms[1], terms[2], terms[3] + w0

    phi = block(taylor_terms - 4)
    for first in range(taylor_terms - 8, -1, -4):
        phi = tuple(p + q for p, q in zip(product(z4, phi), block(first)))
    p00, p01, p10, p11 = product(z1, phi)
    p00, p11 = 1.0 + p00, 1.0 + p11
    q0, q1 = scale * phi[2], scale * phi[3]
    for _ in range(squarings):
        p00, p01, p10, p11, q0, q1 = (
            p00 * p00 + p01 * p10,
            p00 * p01 + p01 * p11,
            p10 * p00 + p11 * p10,
            p10 * p01 + p11 * p11,
            q0 * p00 + q1 * p10 + q0,
            q0 * p01 + q1 * p11 + q1,
        )
    return p00, p10, q0


def combine_kernel(
    gathered, field, image_one, image_two, columns_two, propagated, entries, formed, table, sent
):
    members, rows, cols, depth = field.shape
    sums = jnp.broadcast_to(jnp.sum(gathered[...], axis=0, keepdims=True), (8, 128))
    g00, g01, g02, g11, g12, g22 = [
        jnp.broadcast_to(jnp.sum(jnp.where(own_lane(8 * index), sums, 0.0), axis=1, keepdims=True), (8, 128))
        for index in range(6)
    ]
    tiny = jnp.finfo(jnp.float32).tiny
    h00 = g01 / g00
    square_10 = jnp.maximum(g11 / g00 - h00 * h00, tiny)
    s01 = (g02 - h00 * g01) / g00
    h11 = ((g12 - h00 * g02) - h00 * (g11 - h00 * g01)) / (g00 * square_10)
    norm_2 = ((g22 - h00 * g12) - h00 * (g12 - h00 * g11)) / (g00 * square_10)
    h10 = jnp.sqrt(square_10)
    h01 = s01 / h10
    h21 = jnp.sqrt(jnp.maximum(norm_2 - h01 * h01 - h11 * h11, 0.0))
    e0, e1, e2 = first_column(h00, s01, h11)
    a2 = e2
    a1 = e1 - e2 * (h00 + h11)
    a0 = e0 - e1 * h00 - e2 * (s01 - h11 * h00)
    place_j = lax.broadcasted_iota(jnp.int32, (cols, depth), 0)
    copies = []
    for member in range(members):
        b0, b1, b2 = [jnp.broadcast_to(a[member : member + 1], (cols, depth)) for a in (a0, a1, a2)]
        for row in range(rows):
            two = jnp.where(place_j == 0, columns_two[member, 0, row : row + 1], image_two[member, row])
            two = jnp.where(place_j == cols - 1, columns_two[member, 1, row : row + 1], two)
            formed[member, row] = b0 * field[member, row] + b1 * image_one[member, row] + b2 * two
        copies.append(pltpu.make_async_copy(formed.at[member], propagated.at[member], sent.at[member]))
        copies[-1].start()
    lane = lax.broadcasted_iota(jnp.int32, h00.shape, 1)
    values = h21
    for index, entry in enumerate((h00, h10, h01, h11)):
        values = jnp.where(lane == index, entry, values)
    table[...] = (tau_step * values)[: table.shape[0], : table.shape[1]]
    copies.append(pltpu.make_async_copy(table, entries, sent.at[members]))
    copies[-1].start()
    for copy in copies:
        copy.wait()


def shards(density, rate_table):
    members, rows, cols, depth = density.shape
    size_x, size_y = lax.axis_size("gx"), lax.axis_size("gy")
    devices = size_x * size_y
    vmem = pl.BlockSpec(memory_space=pltpu.VMEM)
    parity_x, parity_y = lax.axis_index("gx") % 2, lax.axis_index("gy") % 2

    def swap(axis, size, first, value):
        def partner(x, y):
            at = x if axis == "gx" else y
            other = at + 1 if (at - first) % 2 == 0 else at - 1
            if not 0 <= other < size:
                return (x, y ^ 1) if axis == "gx" else (x ^ 1, y)
            return (other, y) if axis == "gx" else (x, other)

        pairs = [
            (x * size_y + y, partner(x, y)[0] * size_y + partner(x, y)[1])
            for x in range(size_x)
            for y in range(size_y)
        ]
        return lax.ppermute(value, ("gx", "gy"), pairs)

    assert size_x % 2 == 0 and size_y % 2 == 0

    def swaps(axis, size, parity, initial, last):
        if initial is last:
            return swap(axis, size, 0, last), swap(axis, size, 1, last)
        is_even = parity == 0
        return (
            swap(axis, size, 0, jnp.where(is_even, last, initial)),
            swap(axis, size, 1, jnp.where(is_even, initial, last)),
        )

    initial, last = (density, density) if rows == REACH else (density[:, :REACH], density[:, rows - REACH :])
    is_even = parity_x == 0
    even_x = swap("gx", size_x, 0, initial if rows == REACH else jnp.where(is_even, last, initial))

    edge = jax.ShapeDtypeStruct((members, rows, 2, depth), jnp.float32)
    block = jax.ShapeDtypeStruct(density.shape, jnp.float32)
    parity = pl.pallas_call(
        parity_kernel,
        out_shape=jax.ShapeDtypeStruct((8, depth), jnp.int32),
        out_specs=vmem,
        compiler_params=pltpu.CompilerParams(vmem_limit_bytes=2**20),
        cost_estimate=pl.CostEstimate(flops=10**8, bytes_accessed=0, transcendentals=0),
        name="parity",
    )()
    for_odd, for_even = pl.pallas_call(
        edges_kernel,
        out_shape=[edge, edge],
        in_specs=[vmem, vmem],
        out_specs=[vmem] * 2,
        compiler_params=pltpu.CompilerParams(vmem_limit_bytes=2 * 2**20),
        name="edges",
    )(parity, density)
    odd_y = swap("gy", size_y, 1, for_odd)
    even_y = swap("gy", size_y, 0, for_even)

    even_y, for_odd_x = lax.optimization_barrier((even_y, initial if rows == REACH else jnp.where(is_even, initial, last)))
    odd_x = swap("gx", size_x, 1, for_odd_x)
    even_x, odd_y, even_y = lax.optimization_barrier((even_x, odd_y, even_y))

    def corners(first):
        even, odd = even_y[:, first : first + HALF], odd_y[:, first : first + HALF]
        left = jnp.where(parity_y == 0, odd, even)[:, :, 1:]
        right = jnp.where(parity_y == 0, even, odd)[:, :, :1]
        return jnp.concatenate([left, right], axis=2)

    even_corners, odd_corners = swaps("gx", size_x, parity_x, corners(0), corners(rows - HALF))

    lattice = (size_x * rows, size_y * cols)
    tall, span = rows + 2 * HALF, cols + 2 * GAP
    image_one, image_two, lines, parts = pl.pallas_call(
        functools.partial(images_kernel, lattice),
        out_shape=[
            block,
            block,
            jax.ShapeDtypeStruct((members, 10, tall, depth), jnp.float32),
            jax.ShapeDtypeStruct((48, depth), jnp.float32),
        ],
        in_specs=[vmem] * 6,
        out_specs=[vmem] * 4,
        scratch_shapes=[
            pltpu.VMEM((members, (rows + 2 * REACH) * span, depth), jnp.float32),
            pltpu.VMEM((members, (tall + 1) * span, depth), jnp.float32),
        ],
        compiler_params=pltpu.CompilerParams(vmem_limit_bytes=8 * 2**20),
        name="images",
    )(rate_table, density, even_x, odd_x, even_y, odd_y)

    columns_two, message = pl.pallas_call(
        functools.partial(corners_kernel, lattice, cols),
        out_shape=[
            jax.ShapeDtypeStruct((members, 2, rows, depth), jnp.float32),
            jax.ShapeDtypeStruct((devices, 128), jnp.float32),
        ],
        in_specs=[vmem] * 5,
        out_specs=[vmem, vmem],
        scratch_shapes=[
            pltpu.VMEM((members, 2, 2, 2 * tall, depth), jnp.float32),
            pltpu.VMEM((48, depth), jnp.float32),
        ],
        compiler_params=pltpu.CompilerParams(vmem_limit_bytes=4 * 2**20),
        name="corners",
    )(rate_table, lines, odd_corners, even_corners, parts)

    gathered = lax.all_to_all(message, ("gy", "gx"), 0, 0, tiled=True)

    return pl.pallas_call(
        combine_kernel,
        out_shape=[block, jax.ShapeDtypeStruct((members, 5), jnp.float32)],
        in_specs=[vmem] * 5,
        out_specs=[pl.BlockSpec(memory_space=pl.ANY)] * 2,
        scratch_shapes=[
            pltpu.VMEM(density.shape, jnp.float32),
            pltpu.VMEM((members, 5), jnp.float32),
            pltpu.SemaphoreType.DMA((members + 1,)),
        ],
        compiler_params=pltpu.CompilerParams(vmem_limit_bytes=8 * 2**20),
        name="combine",
    )(gathered, density, image_one, image_two, columns_two)


def solution(mesh):
    in_specs = (P(None, "gx", "gy", None), P())
    out_specs = (P(None, "gx", "gy", None), P())
    return jax.shard_map(shards, mesh=mesh, in_specs=in_specs, out_specs=out_specs, check_vma=False)
```

```python
import functools
import math

import jax
import jax.numpy as jnp
from jax import lax
from jax.experimental import pallas as pl
from jax.experimental.pallas import tpu as pltpu
from jax.sharding import PartitionSpec as P

tau_step = 0.01
taylor_terms = 16
squarings = 4
REACH = 4
HALF = 2
GAP = 8


def parity_kernel(parity):
    parity[...] = jnp.full(parity.shape, lax.axis_index("gy") % 2, jnp.int32)


def edges_kernel(parity, field, for_odd, for_even):
    is_even = jnp.broadcast_to(parity[:1], for_odd.shape[1:3] + parity.shape[1:])[None] == 0
    cols = field.shape[2]
    low, high = field[:, :, :2], field[:, :, cols - 2 :]
    for_even[...] = jnp.where(is_even, high, low)
    for_odd[...] = jnp.where(is_even, low, high)


def own_lane(first):
    row = lax.broadcasted_iota(jnp.int32, (8, 128), 0)
    return lax.broadcasted_iota(jnp.int32, (8, 128), 1) == first + row


def lanes(depth):
    lane = lax.broadcasted_iota(jnp.int32, (1, depth), 1)
    amount_k = lane.astype(jnp.float32)
    return amount_k, jnp.where(lane < depth - 1, amount_k + 1.0, 0.0), jnp.where(lane > 0, 1.0, 0.0)


def apply(c, depth, i, make_u, make_v, lose_v, rest, centre, rows_by, left, right):
    _, above_k, inner_k = lanes(depth)
    value = make_u * rows_by(-1) + (c[1] * (i + 1.0)) * rows_by(1)
    value = value + make_v * left
    value = value + lose_v * right
    pair = pltpu.roll(rows_by(2), 1, 1)
    value = value + (inner_k * (0.5 * c[4] * (i + 2.0) * (i + 1.0))) * pair
    split = c[5] * rows_by(-2) + c[6] * centre
    value = value + above_k * pltpu.roll(split, depth - 1, 1)
    out = rest + (c[1] * i + 0.5 * c[4] * i * (i - 1.0))
    return value - out * centre


def constants(rates, member, depth, amount_j):
    c = [jnp.broadcast_to(rates[member : member + 1, r : r + 1], (1, depth)) for r in range(9)]
    amount_k = lanes(depth)[0]
    ratio_j, ratio_k = amount_j / c[7], amount_k / c[8]
    make_u = c[0] / (1.0 + ratio_j * ratio_j)
    make_v = c[2] / (1.0 + ratio_k * ratio_k)
    lose_v = c[3] * (amount_j + 1.0)
    rest = make_u + make_v + (c[3] * amount_j + (c[5] + c[6]) * amount_k)
    return c, make_u, make_v, lose_v, rest


def sides(even, odd, is_even, lower_inside, higher_inside):
    lower, higher = jnp.where(is_even, odd, even), jnp.where(is_even, even, odd)
    return jnp.where(lower_inside, lower, 0.0), jnp.where(higher_inside, higher, 0.0)


def images_kernel(
    lattice,
    rates,
    field,
    even_x,
    odd_x,
    even_y,
    odd_y,
    image_one,
    image_two,
    lines,
    parts,
    wide,
    wide_image,
):
    members, rows, cols, depth = field.shape
    span = cols + 2 * GAP
    tall = rows + 2 * HALF
    index_i, index_j = lax.axis_index("gx"), lax.axis_index("gy")
    first_i, first_j = index_i * rows, index_j * cols
    even_i, even_j = index_i % 2 == 0, index_j % 2 == 0
    count_i, count_j = lattice

    def place(row, start, values):
        for at in range(values.shape[1]):
            first = (row + REACH + at) * span + GAP + start
            wide[:, first : first + values.shape[2]] = values[:, at]

    place(0, 0, field[...])
    above, below = sides(even_x[...], odd_x[...], even_i, first_i > 0, first_i + rows < count_i)
    place(-REACH, 0, above)
    place(rows, 0, below)
    left, right = sides(even_y[...], odd_y[...], even_j, first_j > 0, first_j + cols < count_j)
    place(0, -2, left)
    place(0, cols, right)
    corner = jnp.zeros((members, HALF, 1, depth), jnp.float32)
    for row in (-HALF, rows):
        place(row, -1, corner)
        place(row, cols, corner)

    sublane = lax.broadcasted_iota(jnp.int32, (span, 1), 0)
    amount_j = (first_j - GAP + sublane).astype(jnp.float32)
    place_j = lax.broadcasted_iota(jnp.int32, (cols, depth), 0)
    inner_j = (place_j > 0) & (place_j < cols - 1)

    for member in range(members):
        c, make_u, make_v, lose_v, rest = constants(rates, member, depth, amount_j)
        make_u, lose_v, rest = [term[GAP : GAP + cols] for term in (make_u, lose_v, rest)]

        def image(read, row):
            i = (first_i + row).astype(jnp.float32)
            rows_by = lambda by: read(row + by, 0)
            return apply(c, depth, i, make_u, make_v, lose_v, rest, read(row, 0), rows_by, read(row, -1), read(row, 1))

        def read_field(row, start):
            return wide[member, pl.ds((row + REACH) * span + GAP + start, cols), :]

        def read_image(row, start):
            return wide_image[member, pl.ds((row + HALF) * span + GAP + start, cols), :]

        for row in range(-HALF, rows + HALF):
            inside = (first_i + row >= 0) & (first_i + row < count_i)
            value = image(read_field, row)
            if row < 0 or row >= rows:
                value = jnp.where(inside, value, 0.0)
            else:
                image_one[member, row] = value
            wide_image[member, pl.ds((row + HALF) * span + GAP, cols), :] = value

        products = [jnp.zeros((cols, depth), jnp.float32) for _ in range(6)]
        for row in range(rows):
            zero = field[member, row]
            one = image_one[member, row]
            two = jnp.where(inner_j, image(read_image, row), 0.0)
            image_two[member, row] = two
            terms = (zero * zero, zero * one, zero * two, one * one, one * two, two * two)
            products = [total + term for total, term in zip(products, terms)]
        for index, total in enumerate(products):
            parts[8 * index + member : 8 * index + member + 1, :] = jnp.sum(total, axis=0, keepdims=True)

        for at, column in enumerate((0, cols - 1, 1, cols - 2)):
            lines[member, at] = wide_image[member, pl.ds(GAP + column, tall, stride=span), :]
        for at, column in enumerate((0, cols - 1, -1, cols, -2, cols + 1)):
            lines[member, 4 + at] = wide[member, pl.ds(HALF * span + GAP + column, tall, stride=span), :]

    for index in range(6):
        parts[8 * index + members : 8 * index + 8, :] = jnp.zeros((8 - members, depth), jnp.float32)


def corners_kernel(lattice, cols, rates, lines, odd_corners, even_corners, parts, columns_two, message, edge, total):
    members, _, tall, depth = lines.shape
    rows = tall - 2 * HALF
    index_i, index_j = lax.axis_index("gx"), lax.axis_index("gy")
    first_i, first_j = index_i * rows, index_j * cols
    count_i, count_j = lattice
    upper, lower = sides(
        even_corners[...], odd_corners[...], index_i % 2 == 0, first_i > 0, first_i + rows < count_i
    )
    i = (first_i + lax.broadcasted_iota(jnp.int32, (rows, depth), 0)).astype(jnp.float32)
    total[...] = parts[...]
    for member in range(members):

        def line(at):
            return lines[member, at, pl.ds(HALF, rows), :]

        sums = [jnp.zeros((rows, depth), jnp.float32) for _ in range(3)]
        for side, column, beyond, inside in (
            (0, 0, -1, first_j > 0),
            (1, cols - 1, cols, first_j + cols < count_j),
        ):

            def at_column(column):
                amount_j = jnp.broadcast_to((first_j + column).astype(jnp.float32), (1, depth))
                return constants(rates, member, depth, amount_j)

            outer, fixed = edge.at[member, side, 0], edge.at[member, side, 1]
            outer[HALF : HALF + rows, :] = line(6 + side)
            for row in range(HALF):
                for first, corner in ((0, upper), (HALF + rows, lower)):
                    value = corner[member, row, side : side + 1, :]
                    outer[first + row : first + row + 1, :] = jnp.where(inside, value, 0.0)

            c, make_u, make_v, lose_v, rest = at_column(beyond)
            rows_by = lambda by: outer[pl.ds(HALF + by, rows), :]
            beside = (line(8), line(4)) if side == 0 else (line(5), line(9))
            value = apply(c, depth, i, make_u, make_v, lose_v, rest, rows_by(0), rows_by, *beside)
            image_beyond = jnp.where(inside, value, 0.0)

            c, make_u, make_v, lose_v, rest = at_column(column)
            gain = make_v if side == 0 else lose_v
            fixed[:tall, :] = lines[member, side]
            for first in (0, HALF + rows):
                fixed[first : first + HALF, :] = fixed[first : first + HALF, :] + gain * outer[first : first + HALF, :]

            rows_by = lambda by: fixed[pl.ds(HALF + by, rows), :]
            beside = (image_beyond, line(2)) if side == 0 else (line(3), image_beyond)
            two = apply(c, depth, i, make_u, make_v, lose_v, rest, rows_by(0), rows_by, *beside)
            columns_two[member, side] = two
            terms = (line(4 + side) * two, line(side) * two, two * two)
            sums = [value + term for value, term in zip(sums, terms)]
        for index, value in zip((2, 4, 5), sums):
            at = 8 * index + member
            total[at : at + 1, :] = total[at : at + 1, :] + jnp.sum(value, axis=0, keepdims=True)

    row = jnp.zeros((8, depth), jnp.float32)
    for index in range(6):
        value = jnp.sum(total[8 * index : 8 * index + 8], axis=1, keepdims=True)
        row = row + jnp.where(own_lane(8 * index), value, 0.0)
    message[...] = jnp.broadcast_to(jnp.sum(row, axis=0, keepdims=True), message.shape)


def product(left, right):
    a, b, c, d = left
    e, f, g, h = right
    return a * e + b * g, a * f + b * h, c * e + d * g, c * f + d * h


def first_column(h00, s01, h11):
    scale = tau_step / 2.0**squarings
    one = jnp.ones_like(h00)
    z1 = (scale * h00, scale * s01, scale * one, scale * h11)
    z2 = product(z1, z1)
    z3, z4 = product(z2, z1), product(z2, z2)
    weights = [1.0 / math.factorial(k + 1) for k in range(taylor_terms)]

    def block(first):
        w0, w1, w2, w3 = weights[first : first + 4]
        terms = [w1 * p + w2 * q + w3 * r for p, q, r in zip(z1, z2, z3)]
        return terms[0] + w0, terms[1], terms[2], terms[3] + w0

    phi = block(taylor_terms - 4)
    for first in range(taylor_terms - 8, -1, -4):
        phi = tuple(p + q for p, q in zip(product(z4, phi), block(first)))
    p00, p01, p10, p11 = product(z1, phi)
    p00, p11 = 1.0 + p00, 1.0 + p11
    q0, q1 = scale * phi[2], scale * phi[3]
    for _ in range(squarings):
        p00, p01, p10, p11, q0, q1 = (
            p00 * p00 + p01 * p10,
            p00 * p01 + p01 * p11,
            p10 * p00 + p11 * p10,
            p10 * p01 + p11 * p11,
            q0 * p00 + q1 * p10 + q0,
            q0 * p01 + q1 * p11 + q1,
        )
    return p00, p10, q0


def combine_kernel(gathered, field, image_one, image_two, columns_two, propagated, entries):
    members, rows, cols, depth = field.shape
    sums = jnp.broadcast_to(jnp.sum(gathered[...], axis=0, keepdims=True), (8, 128))
    g00, g01, g02, g11, g12, g22 = [
        jnp.broadcast_to(jnp.sum(jnp.where(own_lane(8 * index), sums, 0.0), axis=1, keepdims=True), (8, 128))
        for index in range(6)
    ]
    tiny = jnp.finfo(jnp.float32).tiny
    h00 = g01 / g00
    square_10 = jnp.maximum(g11 / g00 - h00 * h00, tiny)
    s01 = (g02 - h00 * g01) / g00
    h11 = ((g12 - h00 * g02) - h00 * (g11 - h00 * g01)) / (g00 * square_10)
    norm_2 = ((g22 - h00 * g12) - h00 * (g12 - h00 * g11)) / (g00 * square_10)
    h10 = jnp.sqrt(square_10)
    h01 = s01 / h10
    h21 = jnp.sqrt(jnp.maximum(norm_2 - h01 * h01 - h11 * h11, 0.0))
    e0, e1, e2 = first_column(h00, s01, h11)
    a2 = e2
    a1 = e1 - e2 * (h00 + h11)
    a0 = e0 - e1 * h00 - e2 * (s01 - h11 * h00)
    lane = lax.broadcasted_iota(jnp.int32, h00.shape, 1)
    table = h21
    for index, entry in enumerate((h00, h10, h01, h11)):
        table = jnp.where(lane == index, entry, table)
    entries[...] = (tau_step * table)[: entries.shape[0], : entries.shape[1]]
    place_j = lax.broadcasted_iota(jnp.int32, (cols, depth), 0)
    for member in range(members):
        b0, b1, b2 = [jnp.broadcast_to(a[member : member + 1], (cols, depth)) for a in (a0, a1, a2)]
        for row in range(rows):
            two = jnp.where(place_j == 0, columns_two[member, 0, row : row + 1], image_two[member, row])
            two = jnp.where(place_j == cols - 1, columns_two[member, 1, row : row + 1], two)
            propagated[member, row] = b0 * field[member, row] + b1 * image_one[member, row] + b2 * two


def shards(density, rate_table):
    members, rows, cols, depth = density.shape
    size_x, size_y = lax.axis_size("gx"), lax.axis_size("gy")
    devices = size_x * size_y
    vmem = pl.BlockSpec(memory_space=pltpu.VMEM)
    parity_x, parity_y = lax.axis_index("gx") % 2, lax.axis_index("gy") % 2

    def swap(axis, size, first, value):
        def partner(x, y):
            at = x if axis == "gx" else y
            other = at + 1 if (at - first) % 2 == 0 else at - 1
            if not 0 <= other < size:
                return (x, y ^ 1) if axis == "gx" else (x, other % size)
            return (other, y) if axis == "gx" else (x, other)

        pairs = [
            (x * size_y + y, partner(x, y)[0] * size_y + partner(x, y)[1])
            for x in range(size_x)
            for y in range(size_y)
        ]
        return lax.ppermute(value, ("gx", "gy"), pairs)

    assert size_x % 2 == 0 and size_y % 2 == 0

    def swaps(axis, size, parity, initial, last):
        if initial is last:
            return swap(axis, size, 0, last), swap(axis, size, 1, last)
        is_even = parity == 0
        return (
            swap(axis, size, 0, jnp.where(is_even, last, initial)),
            swap(axis, size, 1, jnp.where(is_even, initial, last)),
        )

    initial, last = (density, density) if rows == REACH else (density[:, :REACH], density[:, rows - REACH :])
    is_even = parity_x == 0
    even_x = swap("gx", size_x, 0, initial if rows == REACH else jnp.where(is_even, last, initial))

    edge = jax.ShapeDtypeStruct((members, rows, 2, depth), jnp.float32)
    block = jax.ShapeDtypeStruct(density.shape, jnp.float32)
    parity = pl.pallas_call(
        parity_kernel,
        out_shape=jax.ShapeDtypeStruct((8, depth), jnp.int32),
        out_specs=vmem,
        compiler_params=pltpu.CompilerParams(vmem_limit_bytes=2**20),
        cost_estimate=pl.CostEstimate(flops=10**8, bytes_accessed=0, transcendentals=0),
        name="parity",
    )()
    for_odd, for_even = pl.pallas_call(
        edges_kernel,
        out_shape=[edge, edge],
        in_specs=[vmem, vmem],
        out_specs=[vmem] * 2,
        compiler_params=pltpu.CompilerParams(vmem_limit_bytes=2 * 2**20),
        name="edges",
    )(parity, density)
    odd_y = swap("gy", size_y, 1, for_odd)
    even_y = swap("gy", size_y, 0, for_even)

    even_y, for_odd_x = lax.optimization_barrier((even_y, initial if rows == REACH else jnp.where(is_even, initial, last)))
    odd_x = swap("gx", size_x, 1, for_odd_x)
    even_x, odd_y, even_y = lax.optimization_barrier((even_x, odd_y, even_y))

    def corners(first):
        even, odd = even_y[:, first : first + HALF], odd_y[:, first : first + HALF]
        left = jnp.where(parity_y == 0, odd, even)[:, :, 1:]
        right = jnp.where(parity_y == 0, even, odd)[:, :, :1]
        return jnp.concatenate([left, right], axis=2)

    even_corners, odd_corners = swaps("gx", size_x, parity_x, corners(0), corners(rows - HALF))

    lattice = (size_x * rows, size_y * cols)
    tall, span = rows + 2 * HALF, cols + 2 * GAP
    image_one, image_two, lines, parts = pl.pallas_call(
        functools.partial(images_kernel, lattice),
        out_shape=[
            block,
            block,
            jax.ShapeDtypeStruct((members, 10, tall, depth), jnp.float32),
            jax.ShapeDtypeStruct((48, depth), jnp.float32),
        ],
        in_specs=[vmem] * 6,
        out_specs=[vmem] * 4,
        scratch_shapes=[
            pltpu.VMEM((members, (rows + 2 * REACH) * span, depth), jnp.float32),
            pltpu.VMEM((members, (tall + 1) * span, depth), jnp.float32),
        ],
        compiler_params=pltpu.CompilerParams(vmem_limit_bytes=8 * 2**20),
        name="images",
    )(rate_table, density, even_x, odd_x, even_y, odd_y)

    columns_two, message = pl.pallas_call(
        functools.partial(corners_kernel, lattice, cols),
        out_shape=[
            jax.ShapeDtypeStruct((members, 2, rows, depth), jnp.float32),
            jax.ShapeDtypeStruct((devices, 128), jnp.float32),
        ],
        in_specs=[vmem] * 5,
        out_specs=[vmem, vmem],
        scratch_shapes=[
            pltpu.VMEM((members, 2, 2, 2 * tall, depth), jnp.float32),
            pltpu.VMEM((48, depth), jnp.float32),
        ],
        compiler_params=pltpu.CompilerParams(vmem_limit_bytes=4 * 2**20),
        name="corners",
    )(rate_table, lines, odd_corners, even_corners, parts)

    gathered = lax.all_to_all(message, ("gy", "gx"), 0, 0, tiled=True)

    return pl.pallas_call(
        combine_kernel,
        out_shape=[block, jax.ShapeDtypeStruct((members, 5), jnp.float32)],
        in_specs=[vmem] * 5,
        out_specs=[vmem, vmem],
        compiler_params=pltpu.CompilerParams(vmem_limit_bytes=8 * 2**20),
        name="combine",
    )(gathered, density, image_one, image_two, columns_two)


def solution(mesh):
    in_specs = (P(None, "gx", "gy", None), P())
    out_specs = (P(None, "gx", "gy", None), P())
    return jax.shard_map(shards, mesh=mesh, in_specs=in_specs, out_specs=out_specs, check_vma=False)
```

```python
import functools
import math

import jax
import jax.numpy as jnp
from jax import lax
from jax.experimental import pallas as pl
from jax.experimental.pallas import tpu as pltpu
from jax.sharding import PartitionSpec as P

tau_step = 0.01
taylor_terms = 16
squarings = 4
REACH = 4
HALF = 2
GAP = 8


def parity_kernel(parity):
    parity[...] = jnp.full(parity.shape, lax.axis_index("gy") % 2, jnp.int32)


def edges_kernel(parity, field, for_odd, for_even):
    is_even = jnp.broadcast_to(parity[:1], for_odd.shape[1:3] + parity.shape[1:])[None] == 0
    cols = field.shape[2]
    low, high = field[:, :, :2], field[:, :, cols - 2 :]
    for_even[...] = jnp.where(is_even, high, low)
    for_odd[...] = jnp.where(is_even, low, high)


def own_lane(first):
    row = lax.broadcasted_iota(jnp.int32, (8, 128), 0)
    return lax.broadcasted_iota(jnp.int32, (8, 128), 1) == first + row


def lanes(depth):
    lane = lax.broadcasted_iota(jnp.int32, (1, depth), 1)
    amount_k = lane.astype(jnp.float32)
    return amount_k, jnp.where(lane < depth - 1, amount_k + 1.0, 0.0), jnp.where(lane > 0, 1.0, 0.0)


def apply(c, depth, i, make_u, make_v, lose_v, rest, centre, rows_by, left, right):
    _, above_k, inner_k = lanes(depth)
    value = make_u * rows_by(-1) + (c[1] * (i + 1.0)) * rows_by(1)
    value = value + make_v * left
    value = value + lose_v * right
    pair = pltpu.roll(rows_by(2), 1, 1)
    value = value + (inner_k * (0.5 * c[4] * (i + 2.0) * (i + 1.0))) * pair
    split = c[5] * rows_by(-2) + c[6] * centre
    value = value + above_k * pltpu.roll(split, depth - 1, 1)
    out = rest + (c[1] * i + 0.5 * c[4] * i * (i - 1.0))
    return value - out * centre


def constants(rates, member, depth, amount_j):
    c = [jnp.broadcast_to(rates[member : member + 1, r : r + 1], (1, depth)) for r in range(9)]
    amount_k = lanes(depth)[0]
    ratio_j, ratio_k = amount_j / c[7], amount_k / c[8]
    make_u = c[0] / (1.0 + ratio_j * ratio_j)
    make_v = c[2] / (1.0 + ratio_k * ratio_k)
    lose_v = c[3] * (amount_j + 1.0)
    rest = make_u + make_v + (c[3] * amount_j + (c[5] + c[6]) * amount_k)
    return c, make_u, make_v, lose_v, rest


def sides(even, odd, is_even, lower_inside, higher_inside):
    lower, higher = jnp.where(is_even, odd, even), jnp.where(is_even, even, odd)
    return jnp.where(lower_inside, lower, 0.0), jnp.where(higher_inside, higher, 0.0)


def images_kernel(
    lattice,
    rates,
    field,
    even_x,
    odd_x,
    even_y,
    odd_y,
    image_one,
    image_two,
    lines,
    parts,
    wide,
    wide_image,
):
    members, rows, cols, depth = field.shape
    span = cols + 2 * GAP
    tall = rows + 2 * HALF
    index_i, index_j = lax.axis_index("gx"), lax.axis_index("gy")
    first_i, first_j = index_i * rows, index_j * cols
    even_i, even_j = index_i % 2 == 0, index_j % 2 == 0
    count_i, count_j = lattice

    def place(row, start, values):
        for at in range(values.shape[1]):
            first = (row + REACH + at) * span + GAP + start
            wide[:, first : first + values.shape[2]] = values[:, at]

    place(0, 0, field[...])
    above, below = sides(even_x[...], odd_x[...], even_i, first_i > 0, first_i + rows < count_i)
    place(-REACH, 0, above)
    place(rows, 0, below)
    left, right = sides(even_y[...], odd_y[...], even_j, first_j > 0, first_j + cols < count_j)
    place(0, -2, left)
    place(0, cols, right)
    corner = jnp.zeros((members, HALF, 1, depth), jnp.float32)
    for row in (-HALF, rows):
        place(row, -1, corner)
        place(row, cols, corner)

    sublane = lax.broadcasted_iota(jnp.int32, (span, 1), 0)
    amount_j = (first_j - GAP + sublane).astype(jnp.float32)
    place_j = lax.broadcasted_iota(jnp.int32, (cols, depth), 0)
    inner_j = (place_j > 0) & (place_j < cols - 1)

    for member in range(members):
        c, make_u, make_v, lose_v, rest = constants(rates, member, depth, amount_j)
        make_u, lose_v, rest = [term[GAP : GAP + cols] for term in (make_u, lose_v, rest)]

        def image(read, row):
            i = (first_i + row).astype(jnp.float32)
            rows_by = lambda by: read(row + by, 0)
            return apply(c, depth, i, make_u, make_v, lose_v, rest, read(row, 0), rows_by, read(row, -1), read(row, 1))

        def read_field(row, start):
            return wide[member, pl.ds((row + REACH) * span + GAP + start, cols), :]

        def read_image(row, start):
            return wide_image[member, pl.ds((row + HALF) * span + GAP + start, cols), :]

        for row in range(-HALF, rows + HALF):
            inside = (first_i + row >= 0) & (first_i + row < count_i)
            value = image(read_field, row)
            if row < 0 or row >= rows:
                value = jnp.where(inside, value, 0.0)
            else:
                image_one[member, row] = value
            wide_image[member, pl.ds((row + HALF) * span + GAP, cols), :] = value

        products = [jnp.zeros((cols, depth), jnp.float32) for _ in range(6)]
        for row in range(rows):
            zero = field[member, row]
            one = image_one[member, row]
            two = jnp.where(inner_j, image(read_image, row), 0.0)
            image_two[member, row] = two
            terms = (zero * zero, zero * one, zero * two, one * one, one * two, two * two)
            products = [total + term for total, term in zip(products, terms)]
        for index, total in enumerate(products):
            parts[8 * index + member : 8 * index + member + 1, :] = jnp.sum(total, axis=0, keepdims=True)

        for at, column in enumerate((0, cols - 1, 1, cols - 2)):
            lines[member, at] = wide_image[member, pl.ds(GAP + column, tall, stride=span), :]
        for at, column in enumerate((0, cols - 1, -1, cols, -2, cols + 1)):
            lines[member, 4 + at] = wide[member, pl.ds(HALF * span + GAP + column, tall, stride=span), :]

    for index in range(6):
        parts[8 * index + members : 8 * index + 8, :] = jnp.zeros((8 - members, depth), jnp.float32)


def corners_kernel(lattice, cols, rates, lines, odd_corners, even_corners, parts, columns_two, message, edge, total):
    members, _, tall, depth = lines.shape
    rows = tall - 2 * HALF
    index_i, index_j = lax.axis_index("gx"), lax.axis_index("gy")
    first_i, first_j = index_i * rows, index_j * cols
    count_i, count_j = lattice
    upper, lower = sides(
        even_corners[...], odd_corners[...], index_i % 2 == 0, first_i > 0, first_i + rows < count_i
    )
    i = (first_i + lax.broadcasted_iota(jnp.int32, (rows, depth), 0)).astype(jnp.float32)
    total[...] = parts[...]
    for member in range(members):

        def line(at):
            return lines[member, at, pl.ds(HALF, rows), :]

        sums = [jnp.zeros((rows, depth), jnp.float32) for _ in range(3)]
        for side, column, beyond, inside in (
            (0, 0, -1, first_j > 0),
            (1, cols - 1, cols, first_j + cols < count_j),
        ):

            def at_column(column):
                amount_j = jnp.broadcast_to((first_j + column).astype(jnp.float32), (1, depth))
                return constants(rates, member, depth, amount_j)

            outer, fixed = edge.at[member, side, 0], edge.at[member, side, 1]
            outer[HALF : HALF + rows, :] = line(6 + side)
            for row in range(HALF):
                for first, corner in ((0, upper), (HALF + rows, lower)):
                    value = corner[member, row, side : side + 1, :]
                    outer[first + row : first + row + 1, :] = jnp.where(inside, value, 0.0)

            c, make_u, make_v, lose_v, rest = at_column(beyond)
            rows_by = lambda by: outer[pl.ds(HALF + by, rows), :]
            beside = (line(8), line(4)) if side == 0 else (line(5), line(9))
            value = apply(c, depth, i, make_u, make_v, lose_v, rest, rows_by(0), rows_by, *beside)
            image_beyond = jnp.where(inside, value, 0.0)

            c, make_u, make_v, lose_v, rest = at_column(column)
            gain = make_v if side == 0 else lose_v
            fixed[:tall, :] = lines[member, side]
            for first in (0, HALF + rows):
                fixed[first : first + HALF, :] = fixed[first : first + HALF, :] + gain * outer[first : first + HALF, :]

            rows_by = lambda by: fixed[pl.ds(HALF + by, rows), :]
            beside = (image_beyond, line(2)) if side == 0 else (line(3), image_beyond)
            two = apply(c, depth, i, make_u, make_v, lose_v, rest, rows_by(0), rows_by, *beside)
            columns_two[member, side] = two
            terms = (line(4 + side) * two, line(side) * two, two * two)
            sums = [value + term for value, term in zip(sums, terms)]
        for index, value in zip((2, 4, 5), sums):
            at = 8 * index + member
            total[at : at + 1, :] = total[at : at + 1, :] + jnp.sum(value, axis=0, keepdims=True)

    row = jnp.zeros((8, depth), jnp.float32)
    for index in range(6):
        value = jnp.sum(total[8 * index : 8 * index + 8], axis=1, keepdims=True)
        row = row + jnp.where(own_lane(8 * index), value, 0.0)
    message[...] = jnp.broadcast_to(jnp.sum(row, axis=0, keepdims=True), message.shape)


def product(left, right):
    a, b, c, d = left
    e, f, g, h = right
    return a * e + b * g, a * f + b * h, c * e + d * g, c * f + d * h


def first_column(h00, s01, h11):
    scale = tau_step / 2.0**squarings
    one = jnp.ones_like(h00)
    z1 = (scale * h00, scale * s01, scale * one, scale * h11)
    z2 = product(z1, z1)
    z3, z4 = product(z2, z1), product(z2, z2)
    weights = [1.0 / math.factorial(k + 1) for k in range(taylor_terms)]

    def block(first):
        w0, w1, w2, w3 = weights[first : first + 4]
        terms = [w1 * p + w2 * q + w3 * r for p, q, r in zip(z1, z2, z3)]
        return terms[0] + w0, terms[1], terms[2], terms[3] + w0

    phi = block(taylor_terms - 4)
    for first in range(taylor_terms - 8, -1, -4):
        phi = tuple(p + q for p, q in zip(product(z4, phi), block(first)))
    p00, p01, p10, p11 = product(z1, phi)
    p00, p11 = 1.0 + p00, 1.0 + p11
    q0, q1 = scale * phi[2], scale * phi[3]
    for _ in range(squarings):
        p00, p01, p10, p11, q0, q1 = (
            p00 * p00 + p01 * p10,
            p00 * p01 + p01 * p11,
            p10 * p00 + p11 * p10,
            p10 * p01 + p11 * p11,
            q0 * p00 + q1 * p10 + q0,
            q0 * p01 + q1 * p11 + q1,
        )
    return p00, p10, q0


def combine_kernel(gathered, field, image_one, image_two, columns_two, propagated, entries):
    members, rows, cols, depth = field.shape
    sums = jnp.broadcast_to(jnp.sum(gathered[...], axis=0, keepdims=True), (8, 128))
    g00, g01, g02, g11, g12, g22 = [
        jnp.broadcast_to(jnp.sum(jnp.where(own_lane(8 * index), sums, 0.0), axis=1, keepdims=True), (8, 128))
        for index in range(6)
    ]
    tiny = jnp.finfo(jnp.float32).tiny
    h00 = g01 / g00
    square_10 = jnp.maximum(g11 / g00 - h00 * h00, tiny)
    s01 = (g02 - h00 * g01) / g00
    h11 = ((g12 - h00 * g02) - h00 * (g11 - h00 * g01)) / (g00 * square_10)
    norm_2 = ((g22 - h00 * g12) - h00 * (g12 - h00 * g11)) / (g00 * square_10)
    h10 = jnp.sqrt(square_10)
    h01 = s01 / h10
    h21 = jnp.sqrt(jnp.maximum(norm_2 - h01 * h01 - h11 * h11, 0.0))
    e0, e1, e2 = first_column(h00, s01, h11)
    a2 = e2
    a1 = e1 - e2 * (h00 + h11)
    a0 = e0 - e1 * h00 - e2 * (s01 - h11 * h00)
    lane = lax.broadcasted_iota(jnp.int32, h00.shape, 1)
    table = h21
    for index, entry in enumerate((h00, h10, h01, h11)):
        table = jnp.where(lane == index, entry, table)
    entries[...] = (tau_step * table)[: entries.shape[0], : entries.shape[1]]
    place_j = lax.broadcasted_iota(jnp.int32, (cols, depth), 0)
    for member in range(members):
        b0, b1, b2 = [jnp.broadcast_to(a[member : member + 1], (cols, depth)) for a in (a0, a1, a2)]
        for row in range(rows):
            two = jnp.where(place_j == 0, columns_two[member, 0, row : row + 1], image_two[member, row])
            two = jnp.where(place_j == cols - 1, columns_two[member, 1, row : row + 1], two)
            propagated[member, row] = b0 * field[member, row] + b1 * image_one[member, row] + b2 * two


def shards(density, rate_table):
    members, rows, cols, depth = density.shape
    size_x, size_y = lax.axis_size("gx"), lax.axis_size("gy")
    devices = size_x * size_y
    vmem = pl.BlockSpec(memory_space=pltpu.VMEM)
    parity_x, parity_y = lax.axis_index("gx") % 2, lax.axis_index("gy") % 2

    def swap(axis, size, first, value):
        def partner(x, y):
            at = x if axis == "gx" else y
            other = at + 1 if (at - first) % 2 == 0 else at - 1
            if not 0 <= other < size:
                return (x, y ^ 1) if axis == "gx" else (x, other % size)
            return (other, y) if axis == "gx" else (x, other)

        pairs = [
            (x * size_y + y, partner(x, y)[0] * size_y + partner(x, y)[1])
            for x in range(size_x)
            for y in range(size_y)
        ]
        return lax.ppermute(value, ("gx", "gy"), pairs)

    assert size_x % 2 == 0 and size_y % 2 == 0

    def swaps(axis, size, parity, initial, last):
        if initial is last:
            return swap(axis, size, 0, last), swap(axis, size, 1, last)
        is_even = parity == 0
        return (
            swap(axis, size, 0, jnp.where(is_even, last, initial)),
            swap(axis, size, 1, jnp.where(is_even, initial, last)),
        )

    initial, last = (density, density) if rows == REACH else (density[:, :REACH], density[:, rows - REACH :])
    is_even = parity_x == 0
    even_x = swap("gx", size_x, 0, initial if rows == REACH else jnp.where(is_even, last, initial))

    edge = jax.ShapeDtypeStruct((members, rows, 2, depth), jnp.float32)
    block = jax.ShapeDtypeStruct(density.shape, jnp.float32)
    parity = pl.pallas_call(
        parity_kernel,
        out_shape=jax.ShapeDtypeStruct((8, depth), jnp.int32),
        out_specs=vmem,
        compiler_params=pltpu.CompilerParams(vmem_limit_bytes=2**20),
        cost_estimate=pl.CostEstimate(flops=10**8, bytes_accessed=0, transcendentals=0),
        name="parity",
    )()
    for_odd, for_even = pl.pallas_call(
        edges_kernel,
        out_shape=[edge, edge],
        in_specs=[vmem, vmem],
        out_specs=[vmem] * 2,
        compiler_params=pltpu.CompilerParams(vmem_limit_bytes=2 * 2**20),
        name="edges",
    )(parity, density)
    odd_y = swap("gy", size_y, 1, for_odd)
    even_y = swap("gy", size_y, 0, for_even)

    even_y, for_odd_x = lax.optimization_barrier((even_y, initial if rows == REACH else jnp.where(is_even, initial, last)))
    odd_x = swap("gx", size_x, 1, for_odd_x)
    even_x, odd_y, even_y = lax.optimization_barrier((even_x, odd_y, even_y))

    def corners(first):
        even, odd = even_y[:, first : first + HALF], odd_y[:, first : first + HALF]
        left = jnp.where(parity_y == 0, odd, even)[:, :, 1:]
        right = jnp.where(parity_y == 0, even, odd)[:, :, :1]
        return jnp.concatenate([left, right], axis=2)

    even_corners, odd_corners = swaps("gx", size_x, parity_x, corners(0), corners(rows - HALF))

    lattice = (size_x * rows, size_y * cols)
    tall, span = rows + 2 * HALF, cols + 2 * GAP
    image_one, image_two, lines, parts = pl.pallas_call(
        functools.partial(images_kernel, lattice),
        out_shape=[
            block,
            block,
            jax.ShapeDtypeStruct((members, 10, tall, depth), jnp.float32),
            jax.ShapeDtypeStruct((48, depth), jnp.float32),
        ],
        in_specs=[vmem] * 6,
        out_specs=[vmem] * 4,
        scratch_shapes=[
            pltpu.VMEM((members, (rows + 2 * REACH) * span, depth), jnp.float32),
            pltpu.VMEM((members, (tall + 1) * span, depth), jnp.float32),
        ],
        compiler_params=pltpu.CompilerParams(vmem_limit_bytes=8 * 2**20),
        name="images",
    )(rate_table, density, even_x, odd_x, even_y, odd_y)

    columns_two, message = pl.pallas_call(
        functools.partial(corners_kernel, lattice, cols),
        out_shape=[
            jax.ShapeDtypeStruct((members, 2, rows, depth), jnp.float32),
            jax.ShapeDtypeStruct((devices, 128), jnp.float32),
        ],
        in_specs=[vmem] * 5,
        out_specs=[vmem, vmem],
        scratch_shapes=[
            pltpu.VMEM((members, 2, 2, 2 * tall, depth), jnp.float32),
            pltpu.VMEM((48, depth), jnp.float32),
        ],
        compiler_params=pltpu.CompilerParams(vmem_limit_bytes=4 * 2**20),
        name="corners",
    )(rate_table, lines, odd_corners, even_corners, parts)

    order = [0] + [i for i in range(devices - 1, 0, -1)]
    gathered = lax.all_to_all(message, ("gx", "gy"), 0, 0, axis_index_groups=[order], tiled=True)

    return pl.pallas_call(
        combine_kernel,
        out_shape=[block, jax.ShapeDtypeStruct((members, 5), jnp.float32)],
        in_specs=[vmem] * 5,
        out_specs=[vmem, vmem],
        compiler_params=pltpu.CompilerParams(vmem_limit_bytes=8 * 2**20),
        name="combine",
    )(gathered, density, image_one, image_two, columns_two)


def solution(mesh):
    in_specs = (P(None, "gx", "gy", None), P())
    out_specs = (P(None, "gx", "gy", None), P())
    return jax.shard_map(shards, mesh=mesh, in_specs=in_specs, out_specs=out_specs, check_vma=False)
```

```python
import functools
import math

import jax
import jax.numpy as jnp
from jax import lax
from jax.experimental import pallas as pl
from jax.experimental.pallas import tpu as pltpu
from jax.sharding import PartitionSpec as P

tau_step = 0.01
taylor_terms = 16
squarings = 4
REACH = 4
HALF = 2
GAP = 8


def parity_kernel(parity):
    parity[...] = jnp.full(parity.shape, lax.axis_index("gy") % 2, jnp.int32)


def edges_kernel(parity, field, for_odd, for_even):
    is_even = jnp.broadcast_to(parity[:1], for_odd.shape[1:3] + parity.shape[1:])[None] == 0
    cols = field.shape[2]
    low, high = field[:, :, :2], field[:, :, cols - 2 :]
    for_even[...] = jnp.where(is_even, high, low)
    for_odd[...] = jnp.where(is_even, low, high)


def own_lane(first):
    row = lax.broadcasted_iota(jnp.int32, (8, 128), 0)
    return lax.broadcasted_iota(jnp.int32, (8, 128), 1) == first + row


def lanes(depth):
    lane = lax.broadcasted_iota(jnp.int32, (1, depth), 1)
    amount_k = lane.astype(jnp.float32)
    return amount_k, jnp.where(lane < depth - 1, amount_k + 1.0, 0.0), jnp.where(lane > 0, 1.0, 0.0)


def apply(c, depth, i, make_u, make_v, lose_v, rest, centre, rows_by, left, right):
    _, above_k, inner_k = lanes(depth)
    value = make_u * rows_by(-1) + (c[1] * (i + 1.0)) * rows_by(1)
    value = value + make_v * left
    value = value + lose_v * right
    pair = pltpu.roll(rows_by(2), 1, 1)
    value = value + (inner_k * (0.5 * c[4] * (i + 2.0) * (i + 1.0))) * pair
    split = c[5] * rows_by(-2) + c[6] * centre
    value = value + above_k * pltpu.roll(split, depth - 1, 1)
    out = rest + (c[1] * i + 0.5 * c[4] * i * (i - 1.0))
    return value - out * centre


def constants(rates, member, depth, amount_j):
    c = [jnp.broadcast_to(rates[member : member + 1, r : r + 1], (1, depth)) for r in range(9)]
    amount_k = lanes(depth)[0]
    ratio_j, ratio_k = amount_j / c[7], amount_k / c[8]
    make_u = c[0] / (1.0 + ratio_j * ratio_j)
    make_v = c[2] / (1.0 + ratio_k * ratio_k)
    lose_v = c[3] * (amount_j + 1.0)
    rest = make_u + make_v + (c[3] * amount_j + (c[5] + c[6]) * amount_k)
    return c, make_u, make_v, lose_v, rest


def sides(even, odd, is_even, lower_inside, higher_inside):
    lower, higher = jnp.where(is_even, odd, even), jnp.where(is_even, even, odd)
    return jnp.where(lower_inside, lower, 0.0), jnp.where(higher_inside, higher, 0.0)


def images_kernel(
    lattice,
    rates,
    field,
    even_x,
    odd_x,
    even_y,
    odd_y,
    image_one,
    image_two,
    lines,
    parts,
    wide,
    wide_image,
):
    members, rows, cols, depth = field.shape
    span = cols + 2 * GAP
    tall = rows + 2 * HALF
    index_i, index_j = lax.axis_index("gx"), lax.axis_index("gy")
    first_i, first_j = index_i * rows, index_j * cols
    even_i, even_j = index_i % 2 == 0, index_j % 2 == 0
    count_i, count_j = lattice

    def place(row, start, values):
        for at in range(values.shape[1]):
            first = (row + REACH + at) * span + GAP + start
            wide[:, first : first + values.shape[2]] = values[:, at]

    place(0, 0, field[...])
    above, below = sides(even_x[...], odd_x[...], even_i, first_i > 0, first_i + rows < count_i)
    place(-REACH, 0, above)
    place(rows, 0, below)
    left, right = sides(even_y[...], odd_y[...], even_j, first_j > 0, first_j + cols < count_j)
    place(0, -2, left)
    place(0, cols, right)
    corner = jnp.zeros((members, HALF, 1, depth), jnp.float32)
    for row in (-HALF, rows):
        place(row, -1, corner)
        place(row, cols, corner)

    sublane = lax.broadcasted_iota(jnp.int32, (span, 1), 0)
    amount_j = (first_j - GAP + sublane).astype(jnp.float32)
    place_j = lax.broadcasted_iota(jnp.int32, (cols, depth), 0)
    inner_j = (place_j > 0) & (place_j < cols - 1)

    for member in range(members):
        c, make_u, make_v, lose_v, rest = constants(rates, member, depth, amount_j)
        make_u, lose_v, rest = [term[GAP : GAP + cols] for term in (make_u, lose_v, rest)]

        def image(read, row):
            i = (first_i + row).astype(jnp.float32)
            rows_by = lambda by: read(row + by, 0)
            return apply(c, depth, i, make_u, make_v, lose_v, rest, read(row, 0), rows_by, read(row, -1), read(row, 1))

        def read_field(row, start):
            return wide[member, pl.ds((row + REACH) * span + GAP + start, cols), :]

        def read_image(row, start):
            return wide_image[member, pl.ds((row + HALF) * span + GAP + start, cols), :]

        for row in range(-HALF, rows + HALF):
            inside = (first_i + row >= 0) & (first_i + row < count_i)
            value = image(read_field, row)
            if row < 0 or row >= rows:
                value = jnp.where(inside, value, 0.0)
            else:
                image_one[member, row] = value
            wide_image[member, pl.ds((row + HALF) * span + GAP, cols), :] = value

        products = [jnp.zeros((cols, depth), jnp.float32) for _ in range(6)]
        for row in range(rows):
            zero = field[member, row]
            one = image_one[member, row]
            two = jnp.where(inner_j, image(read_image, row), 0.0)
            image_two[member, row] = two
            terms = (zero * zero, zero * one, zero * two, one * one, one * two, two * two)
            products = [total + term for total, term in zip(products, terms)]
        for index, total in enumerate(products):
            parts[8 * index + member : 8 * index + member + 1, :] = jnp.sum(total, axis=0, keepdims=True)

        for at, column in enumerate((0, cols - 1, 1, cols - 2)):
            lines[member, at] = wide_image[member, pl.ds(GAP + column, tall, stride=span), :]
        for at, column in enumerate((0, cols - 1, -1, cols, -2, cols + 1)):
            lines[member, 4 + at] = wide[member, pl.ds(HALF * span + GAP + column, tall, stride=span), :]

    for index in range(6):
        parts[8 * index + members : 8 * index + 8, :] = jnp.zeros((8 - members, depth), jnp.float32)


def corners_kernel(lattice, cols, rates, lines, odd_corners, even_corners, parts, columns_two, message, edge, total):
    members, _, tall, depth = lines.shape
    rows = tall - 2 * HALF
    index_i, index_j = lax.axis_index("gx"), lax.axis_index("gy")
    first_i, first_j = index_i * rows, index_j * cols
    count_i, count_j = lattice
    upper, lower = sides(
        even_corners[...], odd_corners[...], index_i % 2 == 0, first_i > 0, first_i + rows < count_i
    )
    i = (first_i + lax.broadcasted_iota(jnp.int32, (rows, depth), 0)).astype(jnp.float32)
    total[...] = parts[...]
    for member in range(members):

        def line(at):
            return lines[member, at, pl.ds(HALF, rows), :]

        sums = [jnp.zeros((rows, depth), jnp.float32) for _ in range(3)]
        for side, column, beyond, inside in (
            (0, 0, -1, first_j > 0),
            (1, cols - 1, cols, first_j + cols < count_j),
        ):

            def at_column(column):
                amount_j = jnp.broadcast_to((first_j + column).astype(jnp.float32), (1, depth))
                return constants(rates, member, depth, amount_j)

            outer, fixed = edge.at[member, side, 0], edge.at[member, side, 1]
            outer[HALF : HALF + rows, :] = line(6 + side)
            for row in range(HALF):
                for first, corner in ((0, upper), (HALF + rows, lower)):
                    value = corner[member, row, side : side + 1, :]
                    outer[first + row : first + row + 1, :] = jnp.where(inside, value, 0.0)

            c, make_u, make_v, lose_v, rest = at_column(beyond)
            rows_by = lambda by: outer[pl.ds(HALF + by, rows), :]
            beside = (line(8), line(4)) if side == 0 else (line(5), line(9))
            value = apply(c, depth, i, make_u, make_v, lose_v, rest, rows_by(0), rows_by, *beside)
            image_beyond = jnp.where(inside, value, 0.0)

            c, make_u, make_v, lose_v, rest = at_column(column)
            gain = make_v if side == 0 else lose_v
            fixed[:tall, :] = lines[member, side]
            for first in (0, HALF + rows):
                fixed[first : first + HALF, :] = fixed[first : first + HALF, :] + gain * outer[first : first + HALF, :]

            rows_by = lambda by: fixed[pl.ds(HALF + by, rows), :]
            beside = (image_beyond, line(2)) if side == 0 else (line(3), image_beyond)
            two = apply(c, depth, i, make_u, make_v, lose_v, rest, rows_by(0), rows_by, *beside)
            columns_two[member, side] = two
            terms = (line(4 + side) * two, line(side) * two, two * two)
            sums = [value + term for value, term in zip(sums, terms)]
        for index, value in zip((2, 4, 5), sums):
            at = 8 * index + member
            total[at : at + 1, :] = total[at : at + 1, :] + jnp.sum(value, axis=0, keepdims=True)

    row = jnp.zeros((8, depth), jnp.float32)
    for index in range(6):
        value = jnp.sum(total[8 * index : 8 * index + 8], axis=1, keepdims=True)
        row = row + jnp.where(own_lane(8 * index), value, 0.0)
    message[...] = jnp.broadcast_to(jnp.sum(row, axis=0, keepdims=True), message.shape)


def product(left, right):
    a, b, c, d = left
    e, f, g, h = right
    return a * e + b * g, a * f + b * h, c * e + d * g, c * f + d * h


def first_column(h00, s01, h11):
    scale = tau_step / 2.0**squarings
    one = jnp.ones_like(h00)
    z1 = (scale * h00, scale * s01, scale * one, scale * h11)
    z2 = product(z1, z1)
    z3, z4 = product(z2, z1), product(z2, z2)
    weights = [1.0 / math.factorial(k + 1) for k in range(taylor_terms)]

    def block(first):
        w0, w1, w2, w3 = weights[first : first + 4]
        terms = [w1 * p + w2 * q + w3 * r for p, q, r in zip(z1, z2, z3)]
        return terms[0] + w0, terms[1], terms[2], terms[3] + w0

    phi = block(taylor_terms - 4)
    for first in range(taylor_terms - 8, -1, -4):
        phi = tuple(p + q for p, q in zip(product(z4, phi), block(first)))
    p00, p01, p10, p11 = product(z1, phi)
    p00, p11 = 1.0 + p00, 1.0 + p11
    q0, q1 = scale * phi[2], scale * phi[3]
    for _ in range(squarings):
        p00, p01, p10, p11, q0, q1 = (
            p00 * p00 + p01 * p10,
            p00 * p01 + p01 * p11,
            p10 * p00 + p11 * p10,
            p10 * p01 + p11 * p11,
            q0 * p00 + q1 * p10 + q0,
            q0 * p01 + q1 * p11 + q1,
        )
    return p00, p10, q0


def combine_kernel(gathered, field, image_one, image_two, columns_two, propagated, entries):
    members, rows, cols, depth = field.shape
    sums = jnp.broadcast_to(jnp.sum(gathered[...], axis=0, keepdims=True), (8, 128))
    g00, g01, g02, g11, g12, g22 = [
        jnp.broadcast_to(jnp.sum(jnp.where(own_lane(8 * index), sums, 0.0), axis=1, keepdims=True), (8, 128))
        for index in range(6)
    ]
    tiny = jnp.finfo(jnp.float32).tiny
    h00 = g01 / g00
    square_10 = jnp.maximum(g11 / g00 - h00 * h00, tiny)
    s01 = (g02 - h00 * g01) / g00
    h11 = ((g12 - h00 * g02) - h00 * (g11 - h00 * g01)) / (g00 * square_10)
    norm_2 = ((g22 - h00 * g12) - h00 * (g12 - h00 * g11)) / (g00 * square_10)
    h10 = jnp.sqrt(square_10)
    h01 = s01 / h10
    h21 = jnp.sqrt(jnp.maximum(norm_2 - h01 * h01 - h11 * h11, 0.0))
    e0, e1, e2 = first_column(h00, s01, h11)
    a2 = e2
    a1 = e1 - e2 * (h00 + h11)
    a0 = e0 - e1 * h00 - e2 * (s01 - h11 * h00)
    lane = lax.broadcasted_iota(jnp.int32, h00.shape, 1)
    table = h21
    for index, entry in enumerate((h00, h10, h01, h11)):
        table = jnp.where(lane == index, entry, table)
    entries[...] = (tau_step * table)[: entries.shape[0], : entries.shape[1]]
    place_j = lax.broadcasted_iota(jnp.int32, (cols, depth), 0)
    for member in range(members):
        b0, b1, b2 = [jnp.broadcast_to(a[member : member + 1], (cols, depth)) for a in (a0, a1, a2)]
        for row in range(rows):
            two = jnp.where(place_j == 0, columns_two[member, 0, row : row + 1], image_two[member, row])
            two = jnp.where(place_j == cols - 1, columns_two[member, 1, row : row + 1], two)
            propagated[member, row] = b0 * field[member, row] + b1 * image_one[member, row] + b2 * two


def shards(density, rate_table):
    members, rows, cols, depth = density.shape
    size_x, size_y = lax.axis_size("gx"), lax.axis_size("gy")
    devices = size_x * size_y
    vmem = pl.BlockSpec(memory_space=pltpu.VMEM)
    parity_x, parity_y = lax.axis_index("gx") % 2, lax.axis_index("gy") % 2

    def swap(axis, size, first, value):
        def partner(x, y):
            at = x if axis == "gx" else y
            other = at + 1 if (at - first) % 2 == 0 else at - 1
            if not 0 <= other < size:
                return (x, y ^ 1) if axis == "gx" else (x, other % size)
            return (other, y) if axis == "gx" else (x, other)

        pairs = [
            (x * size_y + y, partner(x, y)[0] * size_y + partner(x, y)[1])
            for x in range(size_x)
            for y in range(size_y)
        ]
        return lax.ppermute(value, ("gx", "gy"), pairs)

    assert size_x % 2 == 0 and size_y % 2 == 0

    def swaps(axis, size, parity, initial, last):
        if initial is last:
            return swap(axis, size, 0, last), swap(axis, size, 1, last)
        is_even = parity == 0
        return (
            swap(axis, size, 0, jnp.where(is_even, last, initial)),
            swap(axis, size, 1, jnp.where(is_even, initial, last)),
        )

    initial, last = (density, density) if rows == REACH else (density[:, :REACH], density[:, rows - REACH :])
    is_even = parity_x == 0
    even_x = swap("gx", size_x, 0, initial if rows == REACH else jnp.where(is_even, last, initial))

    edge = jax.ShapeDtypeStruct((members, rows, 2, depth), jnp.float32)
    block = jax.ShapeDtypeStruct(density.shape, jnp.float32)
    parity = pl.pallas_call(
        parity_kernel,
        out_shape=jax.ShapeDtypeStruct((8, depth), jnp.int32),
        out_specs=vmem,
        compiler_params=pltpu.CompilerParams(vmem_limit_bytes=2**20),
        cost_estimate=pl.CostEstimate(flops=10**8, bytes_accessed=0, transcendentals=0),
        name="parity",
    )()
    for_odd, for_even = pl.pallas_call(
        edges_kernel,
        out_shape=[edge, edge],
        in_specs=[vmem, vmem],
        out_specs=[vmem] * 2,
        compiler_params=pltpu.CompilerParams(vmem_limit_bytes=2 * 2**20),
        name="edges",
    )(parity, density)
    odd_y = swap("gy", size_y, 1, for_odd)
    even_y = swap("gy", size_y, 0, for_even)

    even_y, for_odd_x = lax.optimization_barrier((even_y, initial if rows == REACH else jnp.where(is_even, initial, last)))
    odd_x = swap("gx", size_x, 1, for_odd_x)
    odd_y, even_y, even_x = lax.optimization_barrier((odd_y, even_y, even_x))

    def corners(first):
        even, odd = even_y[:, first : first + HALF], odd_y[:, first : first + HALF]
        left = jnp.where(parity_y == 0, odd, even)[:, :, 1:]
        right = jnp.where(parity_y == 0, even, odd)[:, :, :1]
        return jnp.concatenate([left, right], axis=2)

    even_corners, odd_corners = swaps("gx", size_x, parity_x, corners(0), corners(rows - HALF))

    lattice = (size_x * rows, size_y * cols)
    tall, span = rows + 2 * HALF, cols + 2 * GAP
    image_one, image_two, lines, parts = pl.pallas_call(
        functools.partial(images_kernel, lattice),
        out_shape=[
            block,
            block,
            jax.ShapeDtypeStruct((members, 10, tall, depth), jnp.float32),
            jax.ShapeDtypeStruct((48, depth), jnp.float32),
        ],
        in_specs=[vmem] * 6,
        out_specs=[vmem] * 4,
        scratch_shapes=[
            pltpu.VMEM((members, (rows + 2 * REACH) * span, depth), jnp.float32),
            pltpu.VMEM((members, (tall + 1) * span, depth), jnp.float32),
        ],
        compiler_params=pltpu.CompilerParams(vmem_limit_bytes=8 * 2**20),
        name="images",
    )(rate_table, density, even_x, odd_x, even_y, odd_y)

    columns_two, message = pl.pallas_call(
        functools.partial(corners_kernel, lattice, cols),
        out_shape=[
            jax.ShapeDtypeStruct((members, 2, rows, depth), jnp.float32),
            jax.ShapeDtypeStruct((devices, 128), jnp.float32),
        ],
        in_specs=[vmem] * 5,
        out_specs=[vmem, vmem],
        scratch_shapes=[
            pltpu.VMEM((members, 2, 2, 2 * tall, depth), jnp.float32),
            pltpu.VMEM((48, depth), jnp.float32),
        ],
        compiler_params=pltpu.CompilerParams(vmem_limit_bytes=4 * 2**20),
        name="corners",
    )(rate_table, lines, odd_corners, even_corners, parts)

    gathered = lax.all_to_all(message, ("gy", "gx"), 0, 0, tiled=True)

    return pl.pallas_call(
        combine_kernel,
        out_shape=[block, jax.ShapeDtypeStruct((members, 5), jnp.float32)],
        in_specs=[vmem] * 5,
        out_specs=[vmem, vmem],
        compiler_params=pltpu.CompilerParams(vmem_limit_bytes=8 * 2**20),
        name="combine",
    )(gathered, density, image_one, image_two, columns_two)


def solution(mesh):
    in_specs = (P(None, "gx", "gy", None), P())
    out_specs = (P(None, "gx", "gy", None), P())
    return jax.shard_map(shards, mesh=mesh, in_specs=in_specs, out_specs=out_specs, check_vma=False)
```
